32 devices in a mesh: row: 8 (over z, y), col: 4 (over x, core).
Axes of the slice: x: 2, y: 2, z: 4, core: 2. Of those that a mesh axis runs over, the one named last changes fastest.
Arguments:
- brick_velocity_stress: float32 [128, 9, 16, 256], P(('row', 'col')), may hold values from -6 to 6
- brick_relaxation_memory: float32 [128, 18, 16, 256], P(('row', 'col')), may hold values from -2 to 2
- brick_cell_material: int32 [128, 16, 256], P(('row', 'col')), may hold values from 0 to 7
- brick_live: int32 [128], P(('row', 'col')), may hold values from 0 to 1, as said below
- water_state: float32 [4, 256, 128, 128], P(None, 'row', 'col'), may hold values from -6 to 6
- water_material: int32 [256, 128, 128], P('row', 'col'), may hold values from 0 to 7
- material_table: float32 [8, 8], replicated, may hold values from 0.01 to 0.95, as said below
Outputs:
- motion_out: float32 [128, 9, 16, 256], P(('row', 'col'))
- memory_out: float32 [128, 18, 16, 256], P(('row', 'col'))
- water_out: float32 [4, 256, 128, 128], P(None, 'row', 'col')
The draws below stay inside these ranges and needn't reach their ends.
Inputs may be any that keep to these rules, and one draw needn't show every extreme that they name: `brick_live`: tiles j and j + 2 of one row of tiles hold 4 live bricks together; in every row some tile holds 4 or none. `material_table`: column 0 is the buoyancy, 1 the first Lame constant (the bulk modulus of water cells), 2 the shear modulus, 3 to 5 the retentions of the three mechanisms, 6 and 7 the anelastic Lame constant and shear modulus.
All inputs are finite; a program needn't handle non-finite values.
Results may differ from the reference program's by a relative error of at most 0.00011.
Values sent between devices are 32-bit elements; how exact they have to be, the bound alone decides.
No kernel may reach another device: no remote copies, remote signals or barrier semaphores. Data moves between devices by JAX's collectives and lax.ppermute only.
A program may use at most 128 MiB of HBM per device.

```python
import jax
import jax.numpy as jnp
from jax import lax

BRICK_EDGE_CELLS = 16
NZ = 128
STEPS = 3
MATERIAL_COUNT = 8
TILE_COUNT_X = 8
TILE_COUNT_Y = 4
NX = 256
NY = 128
BRICK_SLOT_COUNT = 128
BRICK_FACE_CELLS = 256


def draw_brick_live(key, part):
    keys = jax.random.split(jax.random.fold_in(key, 17), 4)
    half_count = TILE_COUNT_Y // 2
    lower = jax.random.randint(keys[0], (TILE_COUNT_X, half_count), 0, 5)
    chosen = jax.random.randint(keys[1], (TILE_COUNT_X,), 0, half_count)
    extreme = jax.random.randint(keys[2], (TILE_COUNT_X,), 0, 2) * 4
    places = jnp.arange(half_count, dtype=jnp.int32)
    lower = jnp.where(places[None, :] == chosen[:, None], extreme[:, None], lower)
    counts = jnp.concatenate([lower, 4 - lower], axis=1)
    scores = jax.random.randint(keys[3], (TILE_COUNT_X, TILE_COUNT_Y, 4), 0, 1 << 20) * 4 + jnp.arange(4, dtype=jnp.int32)
    ranks = jnp.argsort(jnp.argsort(scores, axis=-1), axis=-1)
    alive = (ranks < counts[..., None]).astype(jnp.int32)
    return alive.reshape((-1,))


def draw_material_table(key, part):
    lower = jnp.array([0.4, 0.05, 0.02, 0.3, 0.5, 0.7, 0.01, 0.01], jnp.float32)
    upper = jnp.array([0.8, 0.15, 0.08, 0.6, 0.8, 0.95, 0.05, 0.03], jnp.float32)
    spread = jax.random.uniform(jax.random.fold_in(key, 29), (MATERIAL_COUNT, 8), jnp.float32)
    return lower[None, :] + (upper - lower)[None, :] * spread


def plant(result, own_key, least, top_value):
    longest = result.shape.index(max(result.shape))
    spots = []
    for shift in (0, 1):
        where = [jax.random.randint(jax.random.fold_in(own_key, axis), (), 0, length) for axis, length in enumerate(result.shape)]
        where[longest] = (where[longest] + shift) % result.shape[longest]
        spots.append(tuple(where))
    return result.at[spots[0]].set(least).at[spots[1]].set(top_value)


def shard_levels(key, dims, cuts, low, largest):
    gain, own = 1.0, jax.random.fold_in(key, 6)
    for position, shards_of in cuts:
        steps = jnp.exp(jax.random.uniform(jax.random.fold_in(own, position), (shards_of,), jnp.float32, low / len(cuts), largest / len(cuts)))
        gain = gain * jnp.repeat(steps, dims[position] // shards_of).reshape([-1 if axis == position else 1 for axis in range(len(dims))])
    return gain


def normal_values(own_key, shape, deviation, bound, shards=(), kind=jnp.bfloat16):
    loudness = shard_levels(own_key, shape, shards, -0.22, 0.18) if shards else 1.0
    drawn = jax.random.normal(own_key, shape, jnp.float32) * deviation * loudness
    return jnp.minimum(jnp.maximum(drawn, -bound), bound).astype(kind)


def setup_inputs(seed: int = 0) -> dict:
    seeds = jax.random.split(jax.random.key(seed), 8)
    brick_velocity_stress = normal_values(seeds[0], (BRICK_SLOT_COUNT, 9, BRICK_EDGE_CELLS, BRICK_FACE_CELLS), 1.0, 6.0, ((0, 32),), jnp.float32)
    brick_relaxation_memory = normal_values(seeds[1], (BRICK_SLOT_COUNT, 18, BRICK_EDGE_CELLS, BRICK_FACE_CELLS), 0.3, 2.0, ((0, 32),), jnp.float32)
    brick_cell_material = plant(jax.random.randint(seeds[2], (BRICK_SLOT_COUNT, BRICK_EDGE_CELLS, BRICK_FACE_CELLS), 0, MATERIAL_COUNT), jax.random.fold_in(seeds[2], 1), 0, MATERIAL_COUNT - 1).astype(jnp.int32)
    brick_live = draw_brick_live(jax.random.fold_in(seeds[7], 71), 0)
    water_state = normal_values(seeds[4], (4, NX, NY, NZ), 1.0, 6.0, ((1, 8), (2, 4)), jnp.float32)
    water_material = plant(jax.random.randint(seeds[5], (NX, NY, NZ), 0, MATERIAL_COUNT), jax.random.fold_in(seeds[5], 1), 0, MATERIAL_COUNT - 1).astype(jnp.int32)
    material_table = draw_material_table(jax.random.fold_in(seeds[7], 71), 0)
    return {"brick_velocity_stress": brick_velocity_stress, "brick_relaxation_memory": brick_relaxation_memory, "brick_cell_material": brick_cell_material, "brick_live": brick_live, "water_state": water_state, "water_material": water_material, "material_table": material_table}


def lookup(indices, values_table, first, stop):
    levels = jnp.arange(values_table.shape[0], dtype=jnp.int32)
    onehot = (indices[None] == levels.reshape((-1,) + (1,) * indices.ndim)).astype(jnp.float32)
    return jnp.einsum('mk,m...->k...', values_table[:, first:stop], onehot, precision=lax.Precision.HIGHEST)


def along_x(field, before, beyond):
    forward = jnp.concatenate([field[..., 1:, :], beyond[..., None, :]], axis=-2)
    backward = jnp.concatenate([before[..., None, :], field[..., :-1, :]], axis=-2)
    return 0.5 * (forward - backward)


def along_y(field, before, beyond):
    extent = before.shape[-1]
    padded = jnp.concatenate([before, field, beyond], axis=-1)
    return 0.5 * (padded[..., 2 * extent:] - padded[..., :-2 * extent])


def along_z(field, before, beyond):
    extent = before.shape[-1]
    depth_pos = lax.broadcasted_iota(jnp.int32, field.shape, field.ndim - 1) % extent
    nothing = jnp.zeros_like(field[..., :1])
    forward = jnp.where(depth_pos == extent - 1, jnp.repeat(beyond, extent, axis=-1), jnp.concatenate([field[..., 1:], nothing], axis=-1))
    backward = jnp.where(depth_pos == 0, jnp.repeat(before, extent, axis=-1), jnp.concatenate([nothing, field[..., :-1]], axis=-1))
    return 0.5 * (forward - backward)


def face_layers(fields):
    extent = fields.shape[2]
    first_y = fields[..., :extent].reshape(fields.shape[:2] + (-1,))
    last_y = fields[..., -extent:].reshape(fields.shape[:2] + (-1,))
    return jnp.stack([fields[:, :, 0], fields[:, :, -1], first_y, last_y], axis=1)


def top_layer(fields):
    extent = fields.shape[2]
    return fields[..., extent - 1::extent].reshape(fields.shape[:2] + (-1,))


def brick_velocity(motion, params, nearby_cells, top_p):
    stress = motion[:, 3:9]
    extent = motion.shape[2]
    leading_axes = (motion.shape[0], extent, extent)
    blank = jnp.zeros(leading_axes, jnp.float32)

    def diff_x(comp):
        return along_x(stress[:, comp], nearby_cells[:, 0, comp], nearby_cells[:, 1, comp])

    def diff_y(comp):
        return along_y(stress[:, comp], nearby_cells[:, 2, comp].reshape(leading_axes), nearby_cells[:, 3, comp].reshape(leading_axes))

    def diff_z(comp, beyond):
        return along_z(stress[:, comp], blank, beyond)

    upper_stress = -top_p.reshape(leading_axes)
    forcing = jnp.stack([diff_x(0) + diff_y(3) + diff_z(4, blank), diff_x(3) + diff_y(1) + diff_z(5, blank), diff_x(4) + diff_y(5) + diff_z(2, upper_stress)], axis=1)
    velocity = motion[:, 0:3] + params[:, 0:1] * forcing
    return jnp.concatenate([velocity, stress], axis=1)


def brick_stress(motion, memory, params, nearby_cells, top_u):
    velocity = motion[:, 0:3]
    extent = motion.shape[2]
    leading_axes = (motion.shape[0], extent, extent)
    blank = jnp.zeros(leading_axes, jnp.float32)

    def diff_x(comp):
        return along_x(velocity[:, comp], nearby_cells[:, 0, comp], nearby_cells[:, 1, comp])

    def diff_y(comp):
        return along_y(velocity[:, comp], nearby_cells[:, 2, comp].reshape(leading_axes), nearby_cells[:, 3, comp].reshape(leading_axes))

    def diff_z(comp):
        return along_z(velocity[:, comp], blank, top_u[:, comp].reshape(leading_axes))

    strain = [diff_x(0), diff_y(1), diff_z(2), 0.5 * (diff_y(0) + diff_x(1)), 0.5 * (diff_z(0) + diff_x(2)), 0.5 * (diff_z(1) + diff_y(2))]
    dilation = strain[0] + strain[1] + strain[2]
    lame_first, shear_mod = params[:, 1], params[:, 2]
    spring_lame, spring_shear = params[:, 6], params[:, 7]
    memories = {}
    stresses = []
    for comp in range(6):
        elastic = 2.0 * shear_mod * strain[comp]
        relaxed = 2.0 * spring_shear * strain[comp]
        if comp < 3:
            elastic = elastic + lame_first * dilation
            relaxed = relaxed + spring_lame * dilation
        summed = jnp.zeros(leading_axes[:1] + (extent, extent * extent), jnp.float32)
        for mechanism in range(3):
            retain = params[:, 3 + mechanism]
            updated = retain * memory[:, 6 * mechanism + comp] + (1.0 - retain) * relaxed
            memories[6 * mechanism + comp] = updated
            summed = summed + updated
        stresses.append(motion[:, 3 + comp] + elastic - summed)
    new_memory = jnp.stack([memories[place] for place in range(18)], axis=1)
    return jnp.concatenate([velocity, jnp.stack(stresses, axis=1)], axis=1), new_memory


def vertical(field, bottom):
    nothing = jnp.zeros_like(field[..., :1])
    forward = jnp.concatenate([field[..., 1:], nothing], axis=-1)
    backward = jnp.concatenate([bottom[..., None], field[..., :-1]], axis=-1)
    return 0.5 * (forward - backward)


def water_velocity(water, buoyancy, p_padded, bottom_p):
    grad_x = 0.5 * (p_padded[2:, 1:-1] - p_padded[:-2, 1:-1])
    grad_y = 0.5 * (p_padded[1:-1, 2:] - p_padded[1:-1, :-2])
    grad_z = vertical(water[0], bottom_p)
    velocity = water[1:4] - buoyancy[None] * jnp.stack([grad_x, grad_y, grad_z])
    return jnp.concatenate([water[0:1], velocity], axis=0)


def water_pressure(water, bulk_modulus, ux_padded, uy_padded, bottom_u):
    divergence = 0.5 * (ux_padded[2:, 1:-1] - ux_padded[:-2, 1:-1]) + 0.5 * (uy_padded[1:-1, 2:] - uy_padded[1:-1, :-2]) + vertical(water[3], bottom_u)
    pressure = water[0] - bulk_modulus * divergence
    return jnp.concatenate([pressure[None], water[1:4]], axis=0)


def surface_to_slots(surface):
    leading_axes = surface.shape[:-2]
    count_lead = len(leading_axes)
    reshaped_array = surface.reshape(leading_axes + (TILE_COUNT_X, 2, BRICK_EDGE_CELLS, TILE_COUNT_Y, 2, BRICK_EDGE_CELLS))
    axis_permutation = tuple(range(count_lead)) + tuple(count_lead + place for place in (0, 3, 1, 4, 2, 5))
    return reshaped_array.transpose(axis_permutation).reshape(leading_axes + (BRICK_SLOT_COUNT, BRICK_EDGE_CELLS * BRICK_EDGE_CELLS))


def slots_to_surface(slots):
    reshaped_array = slots.reshape((TILE_COUNT_X, TILE_COUNT_Y, 2, 2, BRICK_EDGE_CELLS, BRICK_EDGE_CELLS))
    return reshaped_array.transpose((0, 2, 4, 1, 3, 5)).reshape((NX, NY))


def neighbours(side_faces):
    trailing_axes = side_faces.shape[1:]
    patch_grid = side_faces.reshape((TILE_COUNT_X, TILE_COUNT_Y, 2, 2) + trailing_axes).transpose((0, 2, 1, 3, 4, 5, 6)).reshape((2 * TILE_COUNT_X, 2 * TILE_COUNT_Y) + trailing_axes)
    padded = jnp.pad(patch_grid, ((1, 1), (1, 1), (0, 0), (0, 0), (0, 0)))
    nearby_cells = jnp.stack([padded[:-2, 1:-1, 1], padded[2:, 1:-1, 0], padded[1:-1, :-2, 3], padded[1:-1, 2:, 2]], axis=2)
    return nearby_cells.reshape((TILE_COUNT_X, 2, TILE_COUNT_Y, 2) + trailing_axes).transpose((0, 2, 1, 3, 4, 5, 6)).reshape((BRICK_SLOT_COUNT,) + trailing_axes)


def pad_plane(field):
    return jnp.pad(field, ((1, 1), (1, 1), (0, 0)))


def reference(brick_velocity_stress, brick_relaxation_memory, brick_cell_material, brick_live, water_state, water_material, material_table):
    alive_mask = brick_live.astype(jnp.float32)[:, None, None, None]
    motion = brick_velocity_stress * alive_mask
    memory = brick_relaxation_memory * alive_mask
    params = jnp.moveaxis(lookup(brick_cell_material, material_table, 0, 8), 0, 1)
    coefficients = lookup(water_material, material_table, 0, 2)
    buoyancy, bulk_modulus = coefficients[0], coefficients[1]
    water = water_state
    for instant in range(STEPS):
        nearby_cells = neighbours(face_layers(motion[:, 3:9]))
        upper_face = top_layer(motion[:, 5:6])
        bottom_p = -slots_to_surface(upper_face[:, 0])
        p_slots = surface_to_slots(water[0, :, :, 0])
        water = water_velocity(water, buoyancy, pad_plane(water[0]), bottom_p)
        motion = brick_velocity(motion, params, nearby_cells, p_slots) * alive_mask
        nearby_cells = neighbours(face_layers(motion[:, 0:3]))
        upper_face = top_layer(motion[:, 0:3])
        bottom_u = slots_to_surface(upper_face[:, 2])
        u_slots = jnp.moveaxis(surface_to_slots(water[1:4, :, :, 0]), 0, 1)
        water = water_pressure(water, bulk_modulus, pad_plane(water[1]), pad_plane(water[2]), bottom_u)
        motion, memory = brick_stress(motion, memory, params, nearby_cells, u_slots)
        motion = motion * alive_mask
        memory = memory * alive_mask
    return motion, memory, water
```

```python
import functools

import jax
import jax.numpy as jnp
from jax import lax
from jax.experimental import pallas as pl
from jax.experimental.pallas import tpu as pltpu
from jax.sharding import PartitionSpec as P

STEPS = 3
LANES = 128
SUB = 8
VX, VY, VZ, XX, YY, ZZ, XY, XZ, YZ = range(9)
PAD = 8
P_NEAR, P_FAR, U_NEAR, BRICKS = 0, 32, 64, 96
CORNERS = 160
ROW_CONST, COL_CONST = 160, 176
ROW_LAYERS = [("n", f) for f in (XX, YY, ZZ, XY, XZ, YZ, VX, VY, VZ)] + [("f", f) for f in (XX, XY, XZ)]
COL_LAYERS = [("n", f) for f in (XX, YY, ZZ, XY, XZ, YZ, VX, VY, VZ)] + [("f", f) for f in (XY, YY, YZ)]


def lane_ids():
    return lax.broadcasted_iota(jnp.int32, (SUB, LANES), 1)


def sub_ids():
    return lax.broadcasted_iota(jnp.int32, (SUB, LANES), 0)


def roll(value, shift):
    shift = shift % LANES
    return value if shift == 0 else pltpu.roll(value, shift, 1)


def pick(values, indices):
    return jnp.take_along_axis(values, indices, axis=1, mode="promise_in_bounds")


class Shape:
    def __init__(self, nx, ny, edge):
        self.nx, self.ny, self.edge = nx, ny, edge
        self.across = ny * edge // LANES
        self.yper = LANES // edge
        self.half = self.across // 2
        self.px = ny + 2 * PAD

    def slot(self, ti, tj):
        per = self.edge // SUB
        return 2 * (ti // per) + tj // self.half

    def place(self, ti, tj):
        per = self.edge // SUB
        row = (ti % per) * SUB
        if not isinstance(row, int):
            row = pl.multiple_of(row, SUB)
        lane = (tj % self.half) * LANES
        return pl.ds(row, SUB), pl.ds(lane, LANES)

    def layer(self, x, tj):
        return 2 * (x // self.edge) + tj // self.half, x % self.edge, (tj % self.half) * LANES


def pack(g, water, motion, live, hb_tile, row_first, row_last, col_first, col_last, edge_b=None):
    nx, ny = g.nx, g.ny
    plane = nx * ny
    lane = lane_ids()

    def scale(slot):
        return None if live is None else live[slot].astype(jnp.float32)

    for out, near, far in ((row_first, 0, 1), (row_last, nx - 1, nx - 2)):
        for first, comp, x in ((P_NEAR, 0, near), (P_FAR, 0, far), (U_NEAR, 1, near)):
            for t in range(ny // SUB):
                out[pl.ds(first + SUB * t, SUB), :] = water[pl.ds(comp * plane + x * ny + SUB * t, SUB), :]
        for tj in range(g.across):
            block = BRICKS + 16 * tj
            for k, (which, field) in enumerate(ROW_LAYERS):
                slot, row, lanes = g.layer(near if which == "n" else far, tj)
                value = motion[slot, field, pl.ds(row, 1), pl.ds(lanes, LANES)]
                factor = scale(slot)
                out[pl.ds(block + k, 1), :] = value if factor is None else value * factor
            ti = near // SUB
            value = hb_tile(ti, tj)
            out[pl.ds(block + 12, 1), :] = value[near % SUB : near % SUB + 1, :]
        if edge_b is not None:
            for t in range(ny // SUB):
                out[pl.ds(ROW_CONST + SUB * t, SUB), :] = edge_b(pl.ds(near * ny + SUB * t, SUB))
    for out, near, far, tj in ((col_first, 0, 1, 0), (col_last, ny - 1, ny - 2, g.across - 1)):
        for first, comp, y in ((P_NEAR, 0, near), (P_FAR, 0, far), (U_NEAR, 2, near)):
            for t in range(nx // SUB):
                out[pl.ds(first + SUB * t, SUB), :] = water[pl.ds(comp * plane + SUB * t * ny + y, SUB, stride=ny), :]
        for ti in range(nx // SUB):
            slot = g.slot(ti, tj)
            rows, lanes = g.place(ti, tj)
            factor = scale(slot)
            tiles = {}
            for which, field in COL_LAYERS:
                if field not in tiles:
                    value = motion[slot, field, rows, lanes]
                    tiles[field] = value if factor is None else value * factor
            pieces = [(tiles[field], near if which == "n" else far) for which, field in COL_LAYERS]
            pieces.append((hb_tile(ti, tj), near))
            for column in range(2):
                packed = None
                for k, (value, y) in enumerate(pieces[8 * column : 8 * column + 8]):
                    moved = roll(value, g.edge * k - g.edge * (y % g.yper))
                    packed = moved if packed is None else jnp.where(lane >= g.edge * k, moved, packed)
                out[pl.ds(BRICKS + 32 * column + SUB * ti, SUB), :] = packed
        if edge_b is not None:
            for t in range(nx // SUB):
                out[pl.ds(COL_CONST + SUB * t, SUB), :] = edge_b(pl.ds(SUB * t * ny + near, SUB, stride=ny))


def first_kernel(g, live, table, water, material, motion, brick_material, row_first, row_last, col_first, col_last):
    def hb_tile(ti, tj):
        slot = g.slot(ti, tj)
        rows, lanes = g.place(ti, tj)
        return pick(table[0], brick_material[slot, rows, lanes]) * live[slot].astype(jnp.float32)

    def edge_b(rows):
        return pick(table[0], material[rows, :])

    for out in (col_first, col_last):
        out[pl.ds(CORNERS, 16), :] = jnp.zeros((16, LANES), jnp.float32)
    pack(g, water, motion, live, hb_tile, row_first, row_last, col_first, col_last, edge_b)


def step_kernel(g, first, last, *refs):
    refs = list(refs)

    def take(count):
        taken = refs[:count]
        del refs[:count]
        return taken

    live, table, water, material, motion, memory, brick_material = take(7)
    row_before, row_after, col_before, col_after = take(4)
    if not first:
        (const_in,) = take(1)
    water_out, motion_out, memory_out = take(3)
    if not last:
        sends = take(4)
    if first:
        (const_out,) = take(1)
    press, uy_pad, ux_halo, bricks, hb_pad = take(5)

    nx, ny, edge, across, yper = g.nx, g.ny, g.edge, g.across, g.yper
    plane, px = nx * ny, g.px
    width = across + 2
    lane, sub = lane_ids(), sub_ids()
    depth = lane % edge
    zero = jnp.zeros((SUB, LANES), jnp.float32)
    origin = lane * 0
    top_pick = sub * edge + (edge - 1)
    ytiles, xtiles = ny // SUB, nx // SUB
    BX = 16

    def at(x, y):
        return (x + PAD) * px + y + PAD

    def const(side, t):
        if first:
            ref, start = ((row_before, ROW_CONST), (row_after, ROW_CONST), (col_before, COL_CONST), (col_after, COL_CONST))[side]
            value = ref[pl.ds(start + SUB * t, SUB), :]
            const_out[pl.ds(32 * side + SUB * t, SUB), :] = value
            return value
        return const_in[pl.ds(32 * side + SUB * t, SUB), :]

    @pl.loop(0, nx)
    def _(x):
        for t in range(ytiles):
            row = pl.multiple_of(at(x, SUB * t), SUB)
            press[pl.ds(row, SUB), :] = water[pl.ds(pl.multiple_of(x * ny + SUB * t, SUB), SUB), :]

    for ref, near, far in ((row_before, -1, -2), (row_after, nx, nx + 1)):
        for t in range(ytiles):
            press[pl.ds(at(near, SUB * t), SUB), :] = ref[pl.ds(P_NEAR + SUB * t, SUB), :]
            press[pl.ds(at(far, SUB * t), SUB), :] = ref[pl.ds(P_FAR + SUB * t, SUB), :]
    for ref, near, far in ((col_before, -1, -2), (col_after, ny, ny + 1)):
        for t in range(xtiles):
            press[pl.ds(at(SUB * t, near), SUB, stride=px), :] = ref[pl.ds(P_NEAR + SUB * t, SUB), :]
            press[pl.ds(at(SUB * t, far), SUB, stride=px), :] = ref[pl.ds(P_FAR + SUB * t, SUB), :]

    for ti in range(xtiles):
        for tj in range(across):
            slot = g.slot(ti, tj)
            rows, lanes = g.place(ti, tj)
            alive = live[slot].astype(jnp.float32)
            for field in range(9):
                value = motion[slot, field, rows, lanes]
                if first:
                    value = value * alive
                bricks[field * width + 1 + tj, pl.ds(BX + SUB * ti, SUB), :] = value
            hb_pad[1 + tj, pl.ds(BX + SUB * ti, SUB), :] = pick(table[0], brick_material[slot, rows, lanes]) * alive
    for ref, near, far in ((row_before, -1, -2), (row_after, nx, nx + 1)):
        for tj in range(across):
            block = BRICKS + 16 * tj
            for k, (which, field) in enumerate(ROW_LAYERS):
                x = near if which == "n" else far
                bricks[field * width + 1 + tj, pl.ds(BX + x, 1), :] = ref[pl.ds(block + k, 1), :]
            hb_pad[1 + tj, pl.ds(BX + near, 1), :] = ref[pl.ds(block + 12, 1), :]
    for ref, tj, near, far in ((col_before, 0, yper - 1, yper - 2), (col_after, width - 1, 0, 1)):
        for ti in range(xtiles):
            columns = [ref[pl.ds(BRICKS + 32 * c + SUB * ti, SUB), :] for c in range(2)]
            found = {}
            for k, (which, field) in enumerate(COL_LAYERS):
                y = near if which == "n" else far
                moved = roll(columns[k // 8], edge * (y - k % 8))
                if which == "n":
                    found[field] = moved
                else:
                    found[field] = jnp.where(lane // edge == far, moved, found[field])
            for field, value in found.items():
                bricks[field * width + tj, pl.ds(BX + SUB * ti, SUB), :] = value
            hb_pad[tj, pl.ds(BX + SUB * ti, SUB), :] = roll(columns[1], edge * (near - 4))
        for k, x in ((0, -1), (1, nx)):
            for c in range(6):
                bricks[(XX + c) * width + tj, pl.ds(BX + x, 1), :] = ref[pl.ds(CORNERS + 8 * k + c, 1), :]

    @pl.loop(0, nx)
    def _(x):
        for t in range(ytiles):
            own = pl.ds(pl.multiple_of(x * ny + SUB * t, SUB), SUB)
            row = at(x, SUB * t)
            here = press[pl.ds(pl.multiple_of(row, SUB), SUB), :]
            dx = press[pl.ds(pl.multiple_of(row + px, SUB), SUB), :] - press[pl.ds(pl.multiple_of(row - px, SUB), SUB), :]
            dy = press[pl.ds(row + 1, SUB), :] - press[pl.ds(row - 1, SUB), :]
            surface = jnp.broadcast_to(bricks[ZZ * width + 1 + t, pl.ds(BX + x, 1), :], (SUB, LANES))
            below = -pick(surface, top_pick)
            dz = jnp.where(lane == LANES - 1, zero, roll(here, -1)) - jnp.where(lane == 0, below, roll(here, 1))
            hb = pick(table[0], material[own, :])
            for k, change in ((1, dx), (2, dy), (3, dz)):
                place = pl.ds(pl.multiple_of(k * plane + x * ny + SUB * t, SUB), SUB)
                value = water[place, :] - hb * change
                water_out[place, :] = value
                if k == 2:
                    uy_pad[pl.ds(pl.multiple_of(x * px + PAD + SUB * t, SUB), SUB), :] = value

    for side, (ref, x) in enumerate(((row_before, -1), (row_after, nx))):
        for t in range(ytiles):
            change = press[pl.ds(at(x + 1, SUB * t), SUB), :] - press[pl.ds(at(x - 1, SUB * t), SUB), :]
            ux_halo[pl.ds(side * ny + SUB * t, SUB), :] = ref[pl.ds(U_NEAR + SUB * t, SUB), :] - const(side, t) * change
    for side, (ref, y) in enumerate(((col_before, -1), (col_after, ny))):
        for t in range(xtiles):
            change = press[pl.ds(at(SUB * t, y + 1), SUB, stride=px), :] - press[pl.ds(at(SUB * t, y - 1), SUB, stride=px), :]
            uy_pad[pl.ds(SUB * t * px + PAD + y, SUB, stride=px), :] = (
                ref[pl.ds(U_NEAR + SUB * t, SUB), :] - const(2 + side, t) * change
            )

    def beyond_top(load, ys):
        top = None
        for k, y in ys:
            value = pick(load(y), origin)
            top = value if top is None else jnp.where(lane >= edge * k, value, top)
        return top

    def tile_rows(tj):
        if tj == 0:
            return [(0, -1)]
        if tj == width - 1:
            return [(0, ny)]
        return [(k, yper * (tj - 1) + k) for k in range(yper)]

    def along_y(rolled, tj):
        ahead = rolled[tj][1] if tj == width - 1 else jnp.where(lane < LANES - edge, rolled[tj][1], rolled[tj + 1][1])
        behind = rolled[tj][0] if tj == 0 else jnp.where(lane >= edge, rolled[tj][0], rolled[tj - 1][0])
        return ahead - behind

    def along_z(value, beyond):
        return jnp.where(depth == edge - 1, beyond, roll(value, -1)) - jnp.where(depth == 0, zero, roll(value, 1))

    @pl.loop(0, xtiles + 2)
    def _(ti):
        row = pl.multiple_of(BX - SUB + SUB * ti, SUB)
        here = pl.ds(row, SUB)

        def load(field, tj):
            return bricks[field * width + tj, here, :]

        def along_x(field, tj):
            return bricks[field * width + tj, pl.ds(row + 1, SUB), :] - bricks[field * width + tj, pl.ds(row - 1, SUB), :]

        for target, fx, fy, fz in ((VX, XX, XY, XZ), (VY, XY, YY, YZ), (VZ, XZ, YZ, ZZ)):
            rolled = [(roll(value, edge), roll(value, -edge)) for value in (load(fy, tj) for tj in range(width))]
            for tj in range(width):
                beyond = zero
                if fz == ZZ:
                    beyond = -beyond_top(
                        lambda y: press[pl.ds(SUB * ti * px + y + PAD, SUB, stride=px), :], tile_rows(tj)
                    )
                change = along_x(fx, tj) + along_y(rolled, tj) + along_z(load(fz, tj), beyond)
                bricks[target * width + tj, here, :] = load(target, tj) + hb_pad[tj, here, :] * change

    def water_pressure(x, before, after):
        for t in range(ytiles):
            own = pl.ds(pl.multiple_of(x * ny + SUB * t, SUB), SUB)
            row = x * px + PAD + SUB * t
            dy = uy_pad[pl.ds(row + 1, SUB), :] - uy_pad[pl.ds(row - 1, SUB), :]
            uz = water_out[pl.ds(pl.multiple_of(3 * plane + x * ny + SUB * t, SUB), SUB), :]
            surface = jnp.broadcast_to(bricks[VZ * width + 1 + t, pl.ds(BX + x, 1), :], (SUB, LANES))
            below = pick(surface, top_pick)
            dz = jnp.where(lane == LANES - 1, zero, roll(uz, -1)) - jnp.where(lane == 0, below, roll(uz, 1))
            hk = pick(table[1], material[own, :])
            water_out[own, :] = water[own, :] - hk * ((after(t) - before(t)) + dy + dz)

    def ux_at(x):
        return lambda t: water_out[pl.ds(pl.multiple_of(plane + x * ny + SUB * t, SUB), SUB), :]

    def ux_beyond(side):
        return lambda t: ux_halo[pl.ds(side * ny + SUB * t, SUB), :]

    water_pressure(0, ux_beyond(0), ux_at(1))
    water_pressure(nx - 1, ux_at(nx - 2), ux_beyond(1))

    @pl.loop(1, nx - 1)
    def _(x):
        water_pressure(x, ux_at(x - 1), ux_at(x + 1))

    @pl.loop(0, xtiles)
    def _(ti):
        row = pl.multiple_of(BX + SUB * ti, SUB)
        here = pl.ds(row, SUB)
        rolled = []
        for field in (VX, VY, VZ):
            values = [bricks[field * width + tj, here, :] for tj in range(width)]
            rolled.append([(roll(value, edge), roll(value, -edge)) for value in values])
        for tj in range(1, across + 1):
            slot = g.slot(ti, tj - 1)
            rows, lanes = g.place(ti, tj - 1)
            alive = live[slot].astype(jnp.float32)
            dx, dy, dz = [], [], []
            for field in (VX, VY, VZ):
                key = field * width + tj
                value = bricks[key, here, :]
                motion_out[slot, field, rows, lanes] = value
                dx.append(bricks[key, pl.ds(row + 1, SUB), :] - bricks[key, pl.ds(row - 1, SUB), :])
                dy.append(along_y(rolled[field], tj))
                beyond = beyond_top(
                    lambda y: water_out[pl.ds((1 + field) * plane + SUB * ti * ny + y, SUB, stride=ny), :], tile_rows(tj)
                )
                dz.append(along_z(value, beyond))
            strain = [dx[0], dy[1], dz[2], dy[0] + dx[1], dz[0] + dx[2], dz[1] + dy[2]]
            dilation = strain[0] + strain[1] + strain[2]
            kinds = brick_material[slot, rows, lanes]
            lame = pick(table[1], kinds) * alive * dilation
            shear = pick(table[2], kinds) * alive
            retain = [pick(table[3 + l], kinds) for l in range(3)]
            spring_lame = pick(table[6], kinds) * alive * dilation
            spring_shear = pick(table[7], kinds) * alive
            half_shear, half_spring = 0.5 * shear, 0.5 * spring_shear
            for comp in range(6):
                if comp < 3:
                    elastic = shear * strain[comp] + lame
                    relaxed = spring_shear * strain[comp] + spring_lame
                else:
                    elastic = half_shear * strain[comp]
                    relaxed = half_spring * strain[comp]
                summed = None
                for l in range(3):
                    old = memory[slot, 6 * l + comp, rows, lanes]
                    if first:
                        old = old * alive
                    new = relaxed + retain[l] * (old - relaxed)
                    memory_out[slot, 6 * l + comp, rows, lanes] = new
                    summed = new if summed is None else summed + new
                motion_out[slot, XX + comp, rows, lanes] = bricks[(XX + comp) * width + tj, here, :] + elastic - summed

    if not last:
        def hb_tile(ti, tj):
            return hb_pad[1 + tj, pl.ds(BX + SUB * ti, SUB), :]

        for out in sends[2:]:
            out[pl.ds(CORNERS, 16), :] = jnp.zeros((16, LANES), jnp.float32)
        pack(g, water_out, motion_out, None, hb_tile, *sends)


def exchange(sends):
    row_first, row_last, col_first, col_last = sends

    def shift(value, axis, up):
        count = lax.axis_size(axis)
        pairs = [(i, i + 1) for i in range(count - 1)]
        return lax.ppermute(value, axis, pairs if up else [(j, i) for i, j in pairs])

    row_before = shift(row_last, "row", True)
    row_after = shift(row_first, "row", False)

    def with_corners(message, tile):
        start = BRICKS + 16 * tile
        corners = jnp.concatenate([row_before[start : start + 8], row_after[start : start + 8]])
        return lax.dynamic_update_slice(message, corners, (CORNERS, 0))

    col_before = shift(with_corners(col_last, 3), "col", True)
    col_after = shift(with_corners(col_first, 0), "col", False)
    return row_before, row_after, col_before, col_after


def body(
    brick_velocity_stress,
    brick_relaxation_memory,
    brick_cell_material,
    brick_live,
    water_state,
    water_material,
    material_table,
):
    _, nx, ny, nz = water_state.shape
    g = Shape(nx, ny, brick_cell_material.shape[1])
    halves = jnp.array([0.5, 0.5, 1.0, 1.0, 1.0, 1.0, 0.5, 1.0], jnp.float32)
    columns = (material_table * halves).T
    table = jnp.broadcast_to(
        jnp.tile(columns, (1, LANES // columns.shape[1]))[:, None, :], (columns.shape[0], SUB, LANES)
    )
    water = water_state.reshape((-1, nz))
    material = water_material.reshape((-1, nz))
    motion, memory = brick_velocity_stress, brick_relaxation_memory

    def f32(*shape):
        return jax.ShapeDtypeStruct(shape, jnp.float32)

    smem = pl.BlockSpec(memory_space=pltpu.SMEM)
    vmem = pl.BlockSpec(memory_space=pltpu.VMEM)
    params = pltpu.CompilerParams(vmem_limit_bytes=48 * 1024 * 1024)

    def messages(constants):
        extra = 32 if constants else 0
        return (f32(160 + extra, LANES), f32(160 + extra, LANES), f32(176 + extra, LANES), f32(176 + extra, LANES))

    sends = pl.pallas_call(
        functools.partial(first_kernel, g),
        out_shape=messages(True),
        in_specs=[smem] + [vmem] * 5,
        out_specs=[vmem] * 4,
        compiler_params=params,
        name="pack_edges",
    )(brick_live, table, water, material, motion, brick_cell_material)
    constants = ()
    for step in range(STEPS):
        first, last = step == 0, step == STEPS - 1
        received = exchange(sends)
        out_shape = [f32(*water.shape), f32(*motion.shape), f32(*memory.shape)]
        if not last:
            out_shape += list(messages(False))
        if first:
            out_shape += [f32(128, LANES)]
        results = pl.pallas_call(
            functools.partial(step_kernel, g, first, last),
            out_shape=out_shape,
            in_specs=[smem] + [vmem] * (10 + len(constants)),
            out_specs=[vmem] * len(out_shape),
            scratch_shapes=[
                pltpu.VMEM(((nx + 2 * PAD) * g.px, LANES), jnp.float32),
                pltpu.VMEM((nx * g.px, LANES), jnp.float32),
                pltpu.VMEM((2 * ny, LANES), jnp.float32),
                pltpu.VMEM((9 * (g.across + 2), nx + 32, LANES), jnp.float32),
                pltpu.VMEM((g.across + 2, nx + 32, LANES), jnp.float32),
            ],
            compiler_params=params,
            name="time_step",
        )(brick_live, table, water, material, motion, memory, brick_cell_material, *received, *constants)
        water, motion, memory = results[:3]
        if not last:
            sends = results[3:7]
        if first:
            constants = (results[7],)
    return motion, memory, water.reshape(water_state.shape)


def solution(mesh):
    return jax.shard_map(
        body,
        mesh=mesh,
        in_specs=(
            P(("row", "col"), None, None, None),
            P(("row", "col"), None, None, None),
            P(("row", "col"), None, None),
            P(("row", "col")),
            P(None, "row", "col", None),
            P("row", "col", None),
            P(),
        ),
        out_specs=(
            P(("row", "col"), None, None, None),
            P(("row", "col"), None, None, None),
            P(None, "row", "col", None),
        ),
        check_vma=False,
    )
```

```python
import functools

import jax
import jax.numpy as jnp
from jax import lax
from jax.experimental import pallas as pl
from jax.experimental.pallas import tpu as pltpu
from jax.sharding import PartitionSpec as P

STEPS = 3
LANES = 128
SUB = 8
PAD = 8
VX, VY, VZ, XX, YY, ZZ, XY, XZ, YZ = range(9)
HB, LAME, SHEAR, RETAIN, SPRING_LAME, SPRING_SHEAR = 0, 1, 2, 3, 6, 7
ALONG_X = (XX, XY, XZ)
ALONG_Y = (XY, YY, YZ)
ALONG_Z = (XZ, YZ, ZZ)
M_P, M_U, M_BRICK, M_CORNER = 0, 32, 64, 96
ROW_CONST, COL_CONST = 96, 112


def lane_ids():
    return lax.broadcasted_iota(jnp.int32, (SUB, LANES), 1)


def roll(value, shift):
    shift = shift % LANES
    return value if shift == 0 else pltpu.roll(value, shift, 1)


def roll_row(row, shift):
    shift = shift % LANES
    if shift == 0:
        return row
    return pltpu.roll(jnp.broadcast_to(row, (SUB, LANES)), shift, 1)[0:1, :]


def pick(values, indices):
    return jnp.take_along_axis(values, indices, axis=1, mode="promise_in_bounds")


def aligned(start, size=SUB):
    return pl.ds(start if isinstance(start, int) else pl.multiple_of(start, SUB), size)


class Grid:
    def __init__(self, nx, ny, edge):
        self.nx, self.ny, self.edge = nx, ny, edge
        self.plane = nx * ny
        self.across = ny * edge // LANES
        self.yper = LANES // edge
        self.half = self.across // 2
        self.xtiles, self.ytiles = nx // SUB, ny // SUB
        self.per = edge // SUB

    def slot(self, ti, tj):
        return 2 * (ti // self.per) + tj // self.half

    def place(self, ti, tj):
        return aligned((ti % self.per) * SUB), pl.ds((tj % self.half) * LANES, LANES)


def set_zero_pads(g, press, stress):
    zero = jnp.zeros((SUB, LANES), jnp.float32)
    for t in range(g.ytiles):
        press[0, pl.ds(PAD + SUB * t, SUB), :] = zero
        press[g.nx + 1, pl.ds(PAD + SUB * t, SUB), :] = zero

    @pl.loop(1, g.nx + 1)
    def _(x):
        press[x, pl.ds(0, SUB), :] = zero
        press[x, pl.ds(PAD + g.ny, SUB), :] = zero

    for field in ALONG_X:
        for tj in range(g.across):
            key = (field - XX) * g.across + tj
            stress[key, pl.ds(0, SUB), :] = zero
            stress[key, pl.ds(PAD + g.nx, SUB), :] = zero


def shifted_top(g, load, ys, lane):
    top = None
    for k, y in enumerate(ys):
        value = roll(load(y), g.edge * k + g.edge - 1)
        top = value if top is None else jnp.where(lane >= g.edge * k, value, top)
    return top


def along_y(g, rolled, tj, lane):
    zero = jnp.zeros((SUB, LANES), jnp.float32)
    after = rolled[tj + 1][1] if tj + 1 < len(rolled) else zero
    before = rolled[tj - 1][0] if tj > 0 else zero
    ahead = jnp.where(lane < LANES - g.edge, rolled[tj][1], after)
    behind = jnp.where(lane >= g.edge, rolled[tj][0], before)
    return ahead - behind


def along_z(g, value, beyond, depth):
    zero = jnp.zeros((SUB, LANES), jnp.float32)
    return jnp.where(depth == g.edge - 1, beyond, roll(value, -1)) - jnp.where(depth == 0, zero, roll(value, 1))


def water_z(g, value, below, lane):
    zero = jnp.zeros((SUB, LANES), jnp.float32)
    return jnp.where(lane == LANES - 1, zero, roll(value, -1)) - jnp.where(lane == 0, below, roll(value, 1))


def surface_pick():
    return lax.broadcasted_iota(jnp.int32, (SUB, LANES), 0)


def velocity_part(g, water_out, press, stress, hb_water, load_u, load_v, bricks_out, load_hb):
    lane = lane_ids()
    depth = lane % g.edge
    zero = jnp.zeros((SUB, LANES), jnp.float32)
    top_pick = surface_pick() * g.edge + (g.edge - 1)
    plane, ny, across = g.plane, g.ny, g.across

    def water_layer(x):
        results = []
        for t in range(g.ytiles):
            rows = pl.ds(PAD + SUB * t, SUB)
            here = press[x + 1, rows, :]
            dx = press[x + 2, rows, :] - press[x, rows, :]
            dy = press[x + 1, pl.ds(PAD + SUB * t + 1, SUB), :] - press[x + 1, pl.ds(PAD + SUB * t - 1, SUB), :]
            surface = jnp.broadcast_to(stress[(ZZ - XX) * across + t, pl.ds(PAD + x, 1), :], (SUB, LANES))
            dz = water_z(g, here, -pick(surface, top_pick), lane)
            own = x * ny + SUB * t
            hb = hb_water[aligned(own), :]
            for k, change in ((1, dx), (2, dy), (3, dz)):
                results.append((k * plane + own, load_u(k, x, t) - hb * change))
        return results

    @pl.loop(0, g.nx // 2)
    def _(pair):
        for row, value in water_layer(2 * pair) + water_layer(2 * pair + 1):
            water_out[aligned(row), :] = value

    @pl.loop(0, g.xtiles)
    def _(ti):
        row = pl.multiple_of(SUB * ti, SUB)
        here = pl.ds(pl.multiple_of(row + PAD, SUB), SUB)

        def load(field, tj):
            return stress[(field - XX) * across + tj, here, :]

        def along_x(field, tj):
            key = (field - XX) * across + tj
            return stress[key, pl.ds(row + PAD + 1, SUB), :] - stress[key, pl.ds(row + PAD - 1, SUB), :]

        results = []
        for target, fx, fy, fz in zip((VX, VY, VZ), ALONG_X, ALONG_Y, ALONG_Z):
            rolled = [(roll(value, g.edge), roll(value, -g.edge)) for value in (load(fy, tj) for tj in range(across))]
            for tj in range(across):
                beyond = zero
                if fz == ZZ:
                    ys = [g.yper * tj + k for k in range(g.yper)]
                    beyond = -shifted_top(g, lambda y: water_out[pl.ds(row * ny + y, SUB, stride=ny), :], ys, lane)
                change = along_x(fx, tj) + along_y(g, rolled, tj, lane) + along_z(g, load(fz, tj), beyond, depth)
                results.append((target * across + tj, load_v(target, ti, tj) + load_hb(ti, tj) * change))
        for key, value in results:
            bricks_out[key, pl.ds(row, SUB), :] = value


def pack(g, water, bricks, params, hb_water, row_first, row_last, col_first, col_last, first):
    nx, ny, plane, across, edge = g.nx, g.ny, g.plane, g.across, g.edge
    lane = lane_ids()
    for out, x in ((row_first, 0), (row_last, nx - 1)):
        for t in range(g.ytiles):
            own = x * ny + SUB * t
            out[pl.ds(M_P + SUB * t, SUB), :] = water[pl.ds(own, SUB), :]
            out[pl.ds(M_U + SUB * t, SUB), :] = water[pl.ds(plane + own, SUB), :]
            if first:
                out[pl.ds(ROW_CONST + SUB * t, SUB), :] = hb_water[pl.ds(own, SUB), :]
        for tj in range(across):
            block = M_BRICK + SUB * tj
            for k, field in enumerate(ALONG_X + (VX, VY, VZ)):
                out[pl.ds(block + k, 1), :] = bricks[field * across + tj, pl.ds(x, 1), :]
            out[pl.ds(block + 6, 1), :] = params[HB * across + tj, pl.ds(x, 1), :]
            spare = bricks[YY * across + tj, pl.ds(x, 1), :]
            shear = bricks[YZ * across + tj, pl.ds(x, 1), :]
            if tj == 0:
                spare = jnp.where(lane[0:1, :] < edge, spare, roll_row(shear, edge))
            elif tj == across - 1:
                spare = jnp.where(lane[0:1, :] >= LANES - edge, spare, roll_row(shear, -edge))
            out[pl.ds(block + 7, 1), :] = spare
    for out, y, tj in ((col_first, 0, 0), (col_last, ny - 1, across - 1)):
        for t in range(g.xtiles):
            own = SUB * t * ny + y
            out[pl.ds(M_P + SUB * t, SUB), :] = water[pl.ds(own, SUB, stride=ny), :]
            out[pl.ds(M_U + SUB * t, SUB), :] = water[pl.ds(2 * plane + own, SUB, stride=ny), :]
            if first:
                out[pl.ds(COL_CONST + SUB * t, SUB), :] = hb_water[pl.ds(own, SUB, stride=ny), :]
            rows = pl.ds(SUB * t, SUB)
            pieces = [bricks[field * across + tj, rows, :] for field in ALONG_Y + (VX, VY, VZ)]
            pieces.append(params[HB * across + tj, rows, :])
            packed = None
            for k, value in enumerate(pieces):
                moved = roll(value, edge * (k - y % g.yper))
                packed = moved if packed is None else jnp.where(lane >= edge * k, moved, packed)
            out[pl.ds(M_BRICK + SUB * t, SUB), :] = packed
        out[pl.ds(M_CORNER, 2 * SUB), :] = jnp.zeros((2 * SUB, LANES), jnp.float32)


def first_kernel(
    g, live, table, water_hbm, material_hbm, motion_hbm, kinds_hbm,
    water_out, bricks_out, params, hb_water, hk_water, row_first, row_last, col_first, col_last,
    press, stress, water, material, motion, kinds, sems,
):
    nx, ny, plane, across = g.nx, g.ny, g.plane, g.across
    copies = [
        pltpu.make_async_copy(motion_hbm, motion, sems.at[0]),
        pltpu.make_async_copy(kinds_hbm, kinds, sems.at[1]),
        pltpu.make_async_copy(water_hbm.at[0], press.at[pl.ds(1, nx), pl.ds(PAD, ny), :], sems.at[2]),
        pltpu.make_async_copy(material_hbm, material, sems.at[3]),
        pltpu.make_async_copy(water_hbm.at[pl.ds(1, 3)], water, sems.at[4]),
    ]
    for copy in copies:
        copy.start()
    lane = lane_ids()
    levels = table.shape[0]
    scales = (0.5, 0.5, 1.0, 1.0, 1.0, 1.0, 0.5, 1.0)
    columns = []
    for c, factor in enumerate(scales):
        column = jnp.zeros((SUB, LANES), jnp.float32)
        for level in range(levels):
            column = jnp.where(lane == level, table[level, c], column)
        columns.append(column * factor)
    set_zero_pads(g, press, stress)

    copies[0].wait()
    copies[1].wait()

    @pl.loop(0, g.xtiles)
    def _(ti):
        for tj in range(across):
            slot = g.slot(ti, tj)
            rows, lanes = g.place(ti, tj)
            alive = live[slot].astype(jnp.float32)
            here = aligned(SUB * ti)
            index = kinds[slot, rows, lanes]
            for c in range(8):
                value = pick(columns[c], index)
                params[c * across + tj, here, :] = value if 3 <= c < 6 else value * alive
            for field in range(XX, YZ + 1):
                value = motion[slot, field, rows, lanes] * alive
                bricks_out[field * across + tj, here, :] = value
                stress[(field - XX) * across + tj, aligned(PAD + SUB * ti), :] = value

    copies[2].wait()
    copies[3].wait()

    @pl.loop(0, nx)
    def _(x):
        results = []
        for t in range(g.ytiles):
            own = x * ny + SUB * t
            index = material[x, pl.ds(SUB * t, SUB), :]
            results.append((own, pick(columns[0], index), pick(columns[1], index), press[x + 1, pl.ds(PAD + SUB * t, SUB), :]))
        for own, hb, hk, p in results:
            hb_water[aligned(own), :] = hb
            hk_water[aligned(own), :] = hk
            water_out[aligned(own), :] = p

    copies[4].wait()

    def load_u(k, x, t):
        return water[k - 1, x, pl.ds(SUB * t, SUB), :]

    def load_v(field, ti, tj):
        slot = g.slot(ti, tj)
        rows, lanes = g.place(ti, tj)
        return motion[slot, field, rows, lanes] * live[slot].astype(jnp.float32)

    def load_hb(ti, tj):
        return params[HB * across + tj, aligned(SUB * ti), :]

    velocity_part(g, water_out, press, stress, hb_water, load_u, load_v, bricks_out, load_hb)
    pack(g, water_out, bricks_out, params, hb_water, row_first, row_last, col_first, col_last, True)


def step_kernel(g, first, last, *refs):
    refs = list(refs)

    def take(count):
        taken = refs[:count]
        del refs[:count]
        return taken

    if first:
        (live,) = take(1)
    water, bricks, memory, params, hb_water, hk_water = take(6)
    row_before, row_after, col_before, col_after = take(4)
    if not first:
        (const_in,) = take(1)
    water_out, bricks_out, memory_out = take(3)
    if not last:
        sends = take(4)
    if first:
        (const_out,) = take(1)
    press, stress, ux, uy, speed = take(5)

    nx, ny, edge, across, plane = g.nx, g.ny, g.edge, g.across, g.plane
    wide = across + 2
    lane = lane_ids()
    depth = lane % edge
    top_pick = surface_pick() * edge + (edge - 1)
    py = ny + 2 * PAD

    def const(side, t):
        if first:
            ref, start = ((row_before, ROW_CONST), (row_after, ROW_CONST), (col_before, COL_CONST), (col_after, COL_CONST))[side]
            value = ref[pl.ds(start + SUB * t, SUB), :]
            const_out[pl.ds(32 * side + SUB * t, SUB), :] = value
            return value
        return const_in[pl.ds(32 * side + SUB * t, SUB), :]

    if not last:
        set_zero_pads(g, press, stress)

    @pl.loop(0, nx)
    def _(x):
        for t in range(g.ytiles):
            own = x * ny + SUB * t
            ux[aligned(ny + own), :] = water[aligned(plane + own), :]
            uy[aligned(x * py + PAD + SUB * t), :] = water[aligned(2 * plane + own), :]

    for side, (ref, x, halo, sign) in enumerate(((row_before, 0, -1, 1.0), (row_after, nx - 1, nx, -1.0))):
        for t in range(g.ytiles):
            own = x * ny + SUB * t
            here = pl.ds(ny + own, SUB)
            ux[here, :] = ux[here, :] + sign * hb_water[pl.ds(own, SUB), :] * ref[pl.ds(M_P + SUB * t, SUB), :]
            ux[pl.ds((halo + 1) * ny + SUB * t, SUB), :] = (
                ref[pl.ds(M_U + SUB * t, SUB), :] - sign * const(side, t) * water[pl.ds(own, SUB), :]
            )
    for side, (ref, y, halo, sign) in enumerate(((col_before, 0, -1, 1.0), (col_after, ny - 1, ny, -1.0))):
        for t in range(g.xtiles):
            own = pl.ds(SUB * t * ny + y, SUB, stride=ny)
            here = pl.ds(SUB * t * py + PAD + y, SUB, stride=py)
            uy[here, :] = uy[here, :] + sign * hb_water[own, :] * ref[pl.ds(M_P + SUB * t, SUB), :]
            uy[pl.ds(SUB * t * py + PAD + halo, SUB, stride=py), :] = (
                ref[pl.ds(M_U + SUB * t, SUB), :] - sign * const(2 + side, t) * water[own, :]
            )

    for field in (VX, VY, VZ):
        for tj in range(across):
            for ti in range(g.xtiles):
                speed[field * wide + 1 + tj, pl.ds(PAD + SUB * ti, SUB), :] = bricks[field * across + tj, pl.ds(SUB * ti, SUB), :]
    for ref, x, halo, sign in ((row_before, 0, -1, 1.0), (row_after, nx - 1, nx, -1.0)):
        for tj in range(across):
            block = M_BRICK + SUB * tj
            own_hb = sign * params[HB * across + tj, pl.ds(x, 1), :]
            their_hb = sign * ref[pl.ds(block + 6, 1), :]
            for c in (VX, VY, VZ):
                here = pl.ds(PAD + x, 1)
                key = c * wide + 1 + tj
                speed[key, here, :] = speed[key, here, :] - own_hb * ref[pl.ds(block + c, 1), :]
                speed[key, pl.ds(PAD + halo, 1), :] = (
                    ref[pl.ds(block + 3 + c, 1), :] + their_hb * bricks[ALONG_X[c] * across + tj, pl.ds(x, 1), :]
                )
    for ref, tj, halo, sign in ((col_before, 0, 0, 1.0), (col_after, across - 1, wide - 1, -1.0)):
        near = 0 if tj == 0 else LANES - edge
        far = LANES - edge - near
        inside = (lane >= near) & (lane < near + edge)
        for ti in range(g.xtiles):
            column = ref[pl.ds(M_BRICK + SUB * ti, SUB), :]
            own_hb = jnp.where(inside, sign * params[HB * across + tj, pl.ds(SUB * ti, SUB), :], 0.0)
            their_hb = sign * roll(column, far - 6 * edge)
            here = pl.ds(PAD + SUB * ti, SUB)
            for c in (VX, VY, VZ):
                key = c * wide + 1 + tj
                speed[key, here, :] = speed[key, here, :] - own_hb * roll(column, near - c * edge)
                own = bricks[ALONG_Y[c] * across + tj, pl.ds(SUB * ti, SUB), :]
                speed[c * wide + halo, here, :] = roll(column, far - (3 + c) * edge) + their_hb * roll(own, far - near)
        for k, (row_ref, x, x_halo, x_sign) in enumerate(((row_before, 0, -1, 1.0), (row_after, nx - 1, nx, -1.0))):
            corner = M_CORNER + SUB * k
            spare = ref[pl.ds(corner + 7, 1), :]
            toward = near - far
            inward = edge if far == 0 else -edge
            along = (
                roll_row(ref[pl.ds(corner + 1, 1), :], toward),
                roll_row(spare, toward),
                roll_row(spare, toward - inward),
            )
            row_hb = jnp.where(inside[0:1, :], sign * row_ref[pl.ds(M_BRICK + SUB * tj + 6, 1), :], 0.0)
            col_hb = x_sign * roll_row(ref[pl.ds(M_BRICK + x, 1), :], far - 6 * edge)
            for c in (VX, VY, VZ):
                key, here = c * wide + 1 + tj, pl.ds(PAD + x_halo, 1)
                speed[key, here, :] = speed[key, here, :] - row_hb * along[c]
                key, here = c * wide + halo, pl.ds(PAD + x, 1)
                speed[key, here, :] = speed[key, here, :] - col_hb * ref[pl.ds(corner + c, 1), :]

    @pl.loop(0, g.xtiles)
    def _(ti):
        row = pl.multiple_of(SUB * ti, SUB)
        here = pl.ds(row, SUB)
        inner = pl.ds(pl.multiple_of(row + PAD, SUB), SUB)
        rolled = []
        for field in (VX, VY, VZ):
            values = [speed[field * wide + tj, inner, :] for tj in range(wide)]
            rolled.append([(roll(value, edge), roll(value, -edge)) for value in values])
        tops = (
            lambda y: ux[pl.ds(ny + row * ny + y, SUB, stride=ny), :],
            lambda y: uy[pl.ds(row * py + PAD + y, SUB, stride=py), :],
            lambda y: water[pl.ds(3 * plane + row * ny + y, SUB, stride=ny), :],
        )
        for tj in range(across):
            ys = [g.yper * tj + k for k in range(g.yper)]
            dx, dy, dz, speeds = [], [], [], []
            for field in (VX, VY, VZ):
                key = field * wide + 1 + tj
                value = speed[key, inner, :]
                speeds.append(value)
                dx.append(speed[key, pl.ds(row + PAD + 1, SUB), :] - speed[key, pl.ds(row + PAD - 1, SUB), :])
                dy.append(along_y(g, rolled[field], tj + 1, lane))
                dz.append(along_z(g, value, shifted_top(g, tops[field], ys, lane), depth))
            strain = [dx[0], dy[1], dz[2], dy[0] + dx[1], dz[0] + dx[2], dz[1] + dy[2]]
            dilation = strain[0] + strain[1] + strain[2]

            def param(c):
                return params[c * across + tj, here, :]

            lame, shear = param(LAME) * dilation, param(SHEAR)
            spring_lame, spring_shear = param(SPRING_LAME) * dilation, param(SPRING_SHEAR)
            retain = [param(RETAIN + l) for l in range(3)]
            half_shear, half_spring = 0.5 * shear, 0.5 * spring_shear
            slot = g.slot(ti, tj)
            rows, lanes = g.place(ti, tj)
            if first:
                alive = live[slot].astype(jnp.float32)
            stresses, memories = [], {}
            for comp in range(6):
                if comp < 3:
                    elastic = shear * strain[comp] + lame
                    relaxed = spring_shear * strain[comp] + spring_lame
                else:
                    elastic = half_shear * strain[comp]
                    relaxed = half_spring * strain[comp]
                summed = None
                for l in range(3):
                    place = 6 * l + comp
                    if first:
                        old = memory[slot, place, rows, lanes] * alive
                    else:
                        old = memory[place * across + tj, here, :]
                    new = relaxed + retain[l] * (old - relaxed)
                    memories[place] = new
                    summed = new if summed is None else summed + new
                stresses.append(bricks[(XX + comp) * across + tj, here, :] + elastic - summed)
            for place, value in memories.items():
                if last:
                    memory_out[slot, place, rows, lanes] = value
                else:
                    memory_out[place * across + tj, here, :] = value
            for comp, value in enumerate(stresses):
                if last:
                    bricks_out[slot, XX + comp, rows, lanes] = value
                else:
                    bricks_out[(XX + comp) * across + tj, here, :] = value
                    stress[comp * across + tj, inner, :] = value
            if last:
                for field in (VX, VY, VZ):
                    bricks_out[slot, field, rows, lanes] = speeds[field]

    def water_layer(x):
        results = []
        for t in range(g.ytiles):
            own = x * ny + SUB * t
            dx = ux[aligned((x + 2) * ny + SUB * t), :] - ux[aligned(x * ny + SUB * t), :]
            row = x * py + PAD + SUB * t
            dy = uy[pl.ds(row + 1, SUB), :] - uy[pl.ds(row - 1, SUB), :]
            surface = jnp.broadcast_to(speed[VZ * wide + 1 + t, pl.ds(PAD + x, 1), :], (SUB, LANES))
            uz = water[aligned(3 * plane + own), :]
            dz = water_z(g, uz, pick(surface, top_pick), lane)
            value = water[aligned(own), :] - hk_water[aligned(own), :] * (dx + dy + dz)
            results.append((own, t, value, uz, row))
        return x, results

    @pl.loop(0, nx // 2)
    def _(pair):
        for x, results in (water_layer(2 * pair), water_layer(2 * pair + 1)):
            for own, t, value, uz, row in results:
                water_out[aligned(own), :] = value
                if last:
                    water_out[aligned(plane + own), :] = ux[aligned(ny + own), :]
                    water_out[aligned(2 * plane + own), :] = uy[aligned(row), :]
                    water_out[aligned(3 * plane + own), :] = uz
                else:
                    press[x + 1, pl.ds(PAD + SUB * t, SUB), :] = value

    if not last:
        def load_u(k, x, t):
            if k == 1:
                return ux[aligned((x + 1) * ny + SUB * t), :]
            if k == 2:
                return uy[aligned(x * py + PAD + SUB * t), :]
            return water[aligned(3 * plane + x * ny + SUB * t), :]

        def load_v(field, ti, tj):
            return speed[field * wide + 1 + tj, aligned(PAD + SUB * ti), :]

        def load_hb(ti, tj):
            return params[HB * across + tj, aligned(SUB * ti), :]

        velocity_part(g, water_out, press, stress, hb_water, load_u, load_v, bricks_out, load_hb)
        pack(g, water_out, bricks_out, params, hb_water, *sends, False)


def exchange(g, sends):
    row_first, row_last, col_first, col_last = sends

    def shift(value, axis, up):
        count = lax.axis_size(axis)
        pairs = [(i, i + 1) for i in range(count - 1)]
        return lax.ppermute(value, axis, pairs if up else [(j, i) for i, j in pairs])

    row_before = shift(row_last, "row", True)
    row_after = shift(row_first, "row", False)

    def with_corners(message, tile):
        start = M_BRICK + SUB * tile
        corners = jnp.concatenate([row_before[start : start + SUB], row_after[start : start + SUB]])
        return lax.dynamic_update_slice(message, corners, (M_CORNER, 0))

    col_before = shift(with_corners(col_last, g.across - 1), "col", True)
    col_after = shift(with_corners(col_first, 0), "col", False)
    return row_before, row_after, col_before, col_after


def body(
    brick_velocity_stress,
    brick_relaxation_memory,
    brick_cell_material,
    brick_live,
    water_state,
    water_material,
    material_table,
):
    _, nx, ny, nz = water_state.shape
    g = Grid(nx, ny, brick_cell_material.shape[1])
    across, plane = g.across, g.plane

    def f32(*shape):
        return jax.ShapeDtypeStruct(shape, jnp.float32)

    smem = pl.BlockSpec(memory_space=pltpu.SMEM)
    vmem = pl.BlockSpec(memory_space=pltpu.VMEM)
    hbm = pl.BlockSpec(memory_space=pltpu.HBM)
    params = pltpu.CompilerParams(vmem_limit_bytes=24 * 1024 * 1024)
    press = pltpu.VMEM((nx + 2, ny + 2 * PAD, nz), jnp.float32)
    stress = pltpu.VMEM((6 * across, nx + 2 * PAD, LANES), jnp.float32)

    def messages(first):
        extra = 32 if first else 0
        return [f32(96 + extra, LANES)] * 2 + [f32(112 + extra, LANES)] * 2

    results = pl.pallas_call(
        functools.partial(first_kernel, g),
        out_shape=[
            f32(4 * plane, nz), f32(9 * across, nx, LANES), f32(8 * across, nx, LANES), f32(plane, nz), f32(plane, nz),
        ] + messages(True),
        in_specs=[smem] * 2 + [hbm] * 4,
        out_specs=[vmem] * 9,
        scratch_shapes=[
            press,
            stress,
            pltpu.VMEM((3, nx, ny, nz), jnp.float32),
            pltpu.VMEM(water_material.shape, jnp.int32),
            pltpu.VMEM(brick_velocity_stress.shape, jnp.float32),
            pltpu.VMEM(brick_cell_material.shape, jnp.int32),
            pltpu.SemaphoreType.DMA((5,)),
        ],
        compiler_params=params,
        name="first_velocity",
    )(brick_live, material_table, water_state, water_material, brick_velocity_stress, brick_cell_material)
    water, bricks, coefficients, hb_water, hk_water = results[:5]
    sends = results[5:]
    memory = brick_relaxation_memory
    constants = ()
    for step in range(STEPS):
        first, last = step == 0, step == STEPS - 1
        received = exchange(g, sends)
        if last:
            out_shape = [f32(4 * plane, nz), f32(*brick_velocity_stress.shape), f32(*memory_shape)]
        else:
            memory_shape = brick_relaxation_memory.shape
            out_shape = [f32(4 * plane, nz), f32(9 * across, nx, LANES), f32(18 * across, nx, LANES)] + messages(False)
        if first:
            out_shape += [f32(128, LANES)]
        alive = (brick_live,) if first else ()
        results = pl.pallas_call(
            functools.partial(step_kernel, g, first, last),
            out_shape=out_shape,
            in_specs=[smem] * len(alive) + [vmem] * (10 + len(constants)),
            out_specs=[vmem] * len(out_shape),
            scratch_shapes=[
                press,
                stress,
                pltpu.VMEM(((nx + 2) * ny, nz), jnp.float32),
                pltpu.VMEM((nx * (ny + 2 * PAD), nz), jnp.float32),
                pltpu.VMEM((3 * (across + 2), nx + 2 * PAD, LANES), jnp.float32),
            ],
            compiler_params=params,
            name="time_step",
        )(*alive, water, bricks, memory, coefficients, hb_water, hk_water, *received, *constants)
        water, bricks, memory = results[:3]
        if not last:
            sends = results[3:7]
        if first:
            constants = (results[7],)
    return bricks, memory, water.reshape(water_state.shape)


def solution(mesh):
    return jax.shard_map(
        body,
        mesh=mesh,
        in_specs=(
            P(("row", "col"), None, None, None),
            P(("row", "col"), None, None, None),
            P(("row", "col"), None, None),
            P(("row", "col")),
            P(None, "row", "col", None),
            P("row", "col", None),
            P(),
        ),
        out_specs=(
            P(("row", "col"), None, None, None),
            P(("row", "col"), None, None, None),
            P(None, "row", "col", None),
        ),
        check_vma=False,
    )
```

```python
import functools

import jax
import jax.numpy as jnp
from jax import lax
from jax.experimental import pallas as pl
from jax.experimental.pallas import tpu as pltpu
from jax.sharding import PartitionSpec as P

STEPS = 3
LANES = 128
SUB = 8
PAD = 8
VX, VY, VZ, XX, YY, ZZ, XY, XZ, YZ = range(9)
HB, LAME, SHEAR, RETAIN, SPRING_LAME, SPRING_SHEAR, ALIVE = 0, 1, 2, 3, 6, 7, 8
ALONG_X = (XX, XY, XZ)
ALONG_Y = (XY, YY, YZ)
ALONG_Z = (XZ, YZ, ZZ)
M_P, M_U, M_BRICK, M_CORNER = 0, 32, 64, 96
ROW_CONST, COL_CONST = 96, 112


def lane_ids():
    return lax.broadcasted_iota(jnp.int32, (SUB, LANES), 1)


def roll(value, shift):
    shift = shift % LANES
    return value if shift == 0 else pltpu.roll(value, shift, 1)


def roll_row(row, shift):
    shift = shift % LANES
    if shift == 0:
        return row
    return pltpu.roll(jnp.broadcast_to(row, (SUB, LANES)), shift, 1)[0:1, :]


def pick(values, indices):
    return jnp.take_along_axis(values, indices, axis=1, mode="promise_in_bounds")


def aligned(start, size=SUB):
    return pl.ds(start if isinstance(start, int) else pl.multiple_of(start, SUB), size)


class Grid:
    def __init__(self, nx, ny, edge):
        self.nx, self.ny, self.edge = nx, ny, edge
        self.plane = nx * ny
        self.across = ny * edge // LANES
        self.yper = LANES // edge
        self.half = self.across // 2
        self.xtiles, self.ytiles = nx // SUB, ny // SUB
        self.per = edge // SUB

    def slot(self, ti, tj):
        return 2 * (ti // self.per) + tj // self.half

    def place(self, ti, tj):
        return aligned((ti % self.per) * SUB), pl.ds((tj % self.half) * LANES, LANES)


def set_zero_pads(g, press, stress):
    zero = jnp.zeros((SUB, LANES), jnp.float32)
    for t in range(g.ytiles):
        press[0, pl.ds(PAD + SUB * t, SUB), :] = zero
        press[g.nx + 1, pl.ds(PAD + SUB * t, SUB), :] = zero

    @pl.loop(1, g.nx + 1)
    def _(x):
        press[x, pl.ds(0, SUB), :] = zero
        press[x, pl.ds(PAD + g.ny, SUB), :] = zero

    for field in ALONG_X:
        for tj in range(g.across):
            key = (field - XX) * g.across + tj
            stress[key, pl.ds(0, SUB), :] = zero
            stress[key, pl.ds(PAD + g.nx, SUB), :] = zero


def shifted_top(g, load, ys, lane):
    top = None
    for k, y in enumerate(ys):
        value = roll(load(y), g.edge * k + g.edge - 1)
        top = value if top is None else jnp.where(lane >= g.edge * k, value, top)
    return top


def along_y(g, rolled, tj, lane):
    zero = jnp.zeros((SUB, LANES), jnp.float32)
    after = rolled[tj + 1][1] if tj + 1 < len(rolled) else zero
    before = rolled[tj - 1][0] if tj > 0 else zero
    ahead = jnp.where(lane < LANES - g.edge, rolled[tj][1], after)
    behind = jnp.where(lane >= g.edge, rolled[tj][0], before)
    return ahead - behind


def along_z(g, value, beyond, depth):
    zero = jnp.zeros((SUB, LANES), jnp.float32)
    return jnp.where(depth == g.edge - 1, beyond, roll(value, -1)) - jnp.where(depth == 0, zero, roll(value, 1))


def water_z(g, value, below, lane):
    zero = jnp.zeros((SUB, LANES), jnp.float32)
    return jnp.where(lane == LANES - 1, zero, roll(value, -1)) - jnp.where(lane == 0, below, roll(value, 1))


def surface_pick():
    return lax.broadcasted_iota(jnp.int32, (SUB, LANES), 0)


def velocity_part(g, water_out, press, stress, hb_water, load_u, load_v, bricks_out, load_hb):
    lane = lane_ids()
    depth = lane % g.edge
    zero = jnp.zeros((SUB, LANES), jnp.float32)
    top_pick = surface_pick() * g.edge + (g.edge - 1)
    plane, ny, across = g.plane, g.ny, g.across

    def water_layer(x):
        results = []
        for t in range(g.ytiles):
            rows = pl.ds(PAD + SUB * t, SUB)
            here = press[x + 1, rows, :]
            dx = press[x + 2, rows, :] - press[x, rows, :]
            dy = press[x + 1, pl.ds(PAD + SUB * t + 1, SUB), :] - press[x + 1, pl.ds(PAD + SUB * t - 1, SUB), :]
            surface = jnp.broadcast_to(stress[(ZZ - XX) * across + t, pl.ds(PAD + x, 1), :], (SUB, LANES))
            dz = water_z(g, here, -pick(surface, top_pick), lane)
            own = x * ny + SUB * t
            hb = hb_water[aligned(own), :]
            for k, change in ((1, dx), (2, dy), (3, dz)):
                results.append((k * plane + own, load_u(k, x, t) - hb * change))
        return results

    @pl.loop(0, g.nx // 2)
    def _(pair):
        for row, value in water_layer(2 * pair) + water_layer(2 * pair + 1):
            water_out[aligned(row), :] = value

    @pl.loop(0, g.xtiles)
    def _(ti):
        row = pl.multiple_of(SUB * ti, SUB)
        here = pl.ds(pl.multiple_of(row + PAD, SUB), SUB)

        def load(field, tj):
            return stress[(field - XX) * across + tj, here, :]

        def along_x(field, tj):
            key = (field - XX) * across + tj
            return stress[key, pl.ds(row + PAD + 1, SUB), :] - stress[key, pl.ds(row + PAD - 1, SUB), :]

        results = []
        for target, fx, fy, fz in zip((VX, VY, VZ), ALONG_X, ALONG_Y, ALONG_Z):
            rolled = [(roll(value, g.edge), roll(value, -g.edge)) for value in (load(fy, tj) for tj in range(across))]
            for tj in range(across):
                beyond = zero
                if fz == ZZ:
                    ys = [g.yper * tj + k for k in range(g.yper)]
                    beyond = -shifted_top(g, lambda y: water_out[pl.ds(row * ny + y, SUB, stride=ny), :], ys, lane)
                change = along_x(fx, tj) + along_y(g, rolled, tj, lane) + along_z(g, load(fz, tj), beyond, depth)
                results.append((target * across + tj, load_v(target, ti, tj) + load_hb(ti, tj) * change))
        for key, value in results:
            bricks_out[key, pl.ds(row, SUB), :] = value


def pack(g, water, bricks, params, hb_water, row_first, row_last, col_first, col_last, first):
    nx, ny, plane, across, edge = g.nx, g.ny, g.plane, g.across, g.edge
    lane = lane_ids()
    for out, x in ((row_first, 0), (row_last, nx - 1)):
        for t in range(g.ytiles):
            own = x * ny + SUB * t
            out[pl.ds(M_P + SUB * t, SUB), :] = water[pl.ds(own, SUB), :]
            out[pl.ds(M_U + SUB * t, SUB), :] = water[pl.ds(plane + own, SUB), :]
            if first:
                out[pl.ds(ROW_CONST + SUB * t, SUB), :] = hb_water[pl.ds(own, SUB), :]
        for tj in range(across):
            block = M_BRICK + SUB * tj
            for k, field in enumerate(ALONG_X + (VX, VY, VZ)):
                out[pl.ds(block + k, 1), :] = bricks[field * across + tj, pl.ds(x, 1), :]
            out[pl.ds(block + 6, 1), :] = params[HB * across + tj, pl.ds(x, 1), :]
            spare = bricks[YY * across + tj, pl.ds(x, 1), :]
            shear = bricks[YZ * across + tj, pl.ds(x, 1), :]
            if tj == 0:
                spare = jnp.where(lane[0:1, :] < edge, spare, roll_row(shear, edge))
            elif tj == across - 1:
                spare = jnp.where(lane[0:1, :] >= LANES - edge, spare, roll_row(shear, -edge))
            out[pl.ds(block + 7, 1), :] = spare
    for out, y, tj in ((col_first, 0, 0), (col_last, ny - 1, across - 1)):
        for t in range(g.xtiles):
            own = SUB * t * ny + y
            out[pl.ds(M_P + SUB * t, SUB), :] = water[pl.ds(own, SUB, stride=ny), :]
            out[pl.ds(M_U + SUB * t, SUB), :] = water[pl.ds(2 * plane + own, SUB, stride=ny), :]
            if first:
                out[pl.ds(COL_CONST + SUB * t, SUB), :] = hb_water[pl.ds(own, SUB, stride=ny), :]
            rows = pl.ds(SUB * t, SUB)
            pieces = [bricks[field * across + tj, rows, :] for field in ALONG_Y + (VX, VY, VZ)]
            pieces.append(params[HB * across + tj, rows, :])
            packed = None
            for k, value in enumerate(pieces):
                moved = roll(value, edge * (k - y % g.yper))
                packed = moved if packed is None else jnp.where(lane >= edge * k, moved, packed)
            out[pl.ds(M_BRICK + SUB * t, SUB), :] = packed
        out[pl.ds(M_CORNER, 2 * SUB), :] = jnp.zeros((2 * SUB, LANES), jnp.float32)


def first_kernel(
    g, live_hbm, table_hbm, water_hbm, material_hbm, motion_hbm, kinds_hbm,
    water_out, bricks_out, params, hb_water, hk_water, row_first, row_last, col_first, col_last,
    press, stress, water, material, motion, kinds, live, table, sems,
):
    nx, ny, plane, across = g.nx, g.ny, g.plane, g.across
    copies = [
        pltpu.make_async_copy(motion_hbm, motion, sems.at[0]),
        pltpu.make_async_copy(kinds_hbm, kinds, sems.at[1]),
        pltpu.make_async_copy(water_hbm.at[0], press.at[pl.ds(1, nx), pl.ds(PAD, ny), :], sems.at[2]),
        pltpu.make_async_copy(material_hbm, material, sems.at[3]),
        pltpu.make_async_copy(water_hbm.at[pl.ds(1, 3)], water, sems.at[4]),
        pltpu.make_async_copy(live_hbm, live, sems.at[5]),
        pltpu.make_async_copy(table_hbm, table, sems.at[6]),
    ]
    for copy in copies:
        copy.start()
    lane = lane_ids()
    set_zero_pads(g, press, stress)
    copies[5].wait()
    copies[6].wait()
    levels = table.shape[0]
    scales = (0.5, 0.5, 1.0, 1.0, 1.0, 1.0, 0.5, 1.0)
    columns = []
    for c, factor in enumerate(scales):
        column = jnp.zeros((SUB, LANES), jnp.float32)
        for level in range(levels):
            column = jnp.where(lane == level, table[level, c], column)
        columns.append(column * factor)

    copies[0].wait()
    copies[1].wait()

    @pl.loop(0, g.xtiles)
    def _(ti):
        for tj in range(across):
            slot = g.slot(ti, tj)
            rows, lanes = g.place(ti, tj)
            alive = live[slot].astype(jnp.float32)
            here = aligned(SUB * ti)
            index = kinds[slot, rows, lanes]
            for c in range(8):
                value = pick(columns[c], index)
                params[c * across + tj, here, :] = value if 3 <= c < 6 else value * alive
            params[ALIVE * across + tj, here, :] = jnp.zeros((SUB, LANES), jnp.float32) + alive
            for field in range(XX, YZ + 1):
                value = motion[slot, field, rows, lanes] * alive
                bricks_out[field * across + tj, here, :] = value
                stress[(field - XX) * across + tj, aligned(PAD + SUB * ti), :] = value

    copies[2].wait()
    copies[3].wait()

    @pl.loop(0, nx)
    def _(x):
        results = []
        for t in range(g.ytiles):
            own = x * ny + SUB * t
            index = material[x, pl.ds(SUB * t, SUB), :]
            results.append((own, pick(columns[0], index), pick(columns[1], index), press[x + 1, pl.ds(PAD + SUB * t, SUB), :]))
        for own, hb, hk, p in results:
            hb_water[aligned(own), :] = hb
            hk_water[aligned(own), :] = hk
            water_out[aligned(own), :] = p

    copies[4].wait()

    def load_u(k, x, t):
        return water[k - 1, x, pl.ds(SUB * t, SUB), :]

    def load_v(field, ti, tj):
        slot = g.slot(ti, tj)
        rows, lanes = g.place(ti, tj)
        return motion[slot, field, rows, lanes] * live[slot].astype(jnp.float32)

    def load_hb(ti, tj):
        return params[HB * across + tj, aligned(SUB * ti), :]

    velocity_part(g, water_out, press, stress, hb_water, load_u, load_v, bricks_out, load_hb)
    pack(g, water_out, bricks_out, params, hb_water, row_first, row_last, col_first, col_last, True)


def step_kernel(g, first, last, *refs):
    refs = list(refs)

    def take(count):
        taken = refs[:count]
        del refs[:count]
        return taken

    water, bricks, memory, params, hb_water, hk_water = take(6)
    row_before, row_after, col_before, col_after = take(4)
    if not first:
        (const_in,) = take(1)
    water_out, bricks_out, memory_out = take(3)
    if not last:
        sends = take(4)
    if first:
        (const_out,) = take(1)
    press, stress, ux, uy, speed = take(5)

    nx, ny, edge, across, plane = g.nx, g.ny, g.edge, g.across, g.plane
    wide = across + 2
    lane = lane_ids()
    depth = lane % edge
    top_pick = surface_pick() * edge + (edge - 1)
    py = ny + 2 * PAD

    def const(side, t):
        if first:
            ref, start = ((row_before, ROW_CONST), (row_after, ROW_CONST), (col_before, COL_CONST), (col_after, COL_CONST))[side]
            value = ref[pl.ds(start + SUB * t, SUB), :]
            const_out[pl.ds(32 * side + SUB * t, SUB), :] = value
            return value
        return const_in[pl.ds(32 * side + SUB * t, SUB), :]

    if not last:
        set_zero_pads(g, press, stress)

    @pl.loop(0, nx)
    def _(x):
        for t in range(g.ytiles):
            own = x * ny + SUB * t
            ux[aligned(ny + own), :] = water[aligned(plane + own), :]
            uy[aligned(x * py + PAD + SUB * t), :] = water[aligned(2 * plane + own), :]

    for side, (ref, x, halo, sign) in enumerate(((row_before, 0, -1, 1.0), (row_after, nx - 1, nx, -1.0))):
        for t in range(g.ytiles):
            own = x * ny + SUB * t
            here = pl.ds(ny + own, SUB)
            ux[here, :] = ux[here, :] + sign * hb_water[pl.ds(own, SUB), :] * ref[pl.ds(M_P + SUB * t, SUB), :]
            ux[pl.ds((halo + 1) * ny + SUB * t, SUB), :] = (
                ref[pl.ds(M_U + SUB * t, SUB), :] - sign * const(side, t) * water[pl.ds(own, SUB), :]
            )
    for side, (ref, y, halo, sign) in enumerate(((col_before, 0, -1, 1.0), (col_after, ny - 1, ny, -1.0))):
        for t in range(g.xtiles):
            own = pl.ds(SUB * t * ny + y, SUB, stride=ny)
            here = pl.ds(SUB * t * py + PAD + y, SUB, stride=py)
            uy[here, :] = uy[here, :] + sign * hb_water[own, :] * ref[pl.ds(M_P + SUB * t, SUB), :]
            uy[pl.ds(SUB * t * py + PAD + halo, SUB, stride=py), :] = (
                ref[pl.ds(M_U + SUB * t, SUB), :] - sign * const(2 + side, t) * water[own, :]
            )

    for field in (VX, VY, VZ):
        for tj in range(across):
            for ti in range(g.xtiles):
                speed[field * wide + 1 + tj, pl.ds(PAD + SUB * ti, SUB), :] = bricks[field * across + tj, pl.ds(SUB * ti, SUB), :]
    for ref, x, halo, sign in ((row_before, 0, -1, 1.0), (row_after, nx - 1, nx, -1.0)):
        for tj in range(across):
            block = M_BRICK + SUB * tj
            own_hb = sign * params[HB * across + tj, pl.ds(x, 1), :]
            their_hb = sign * ref[pl.ds(block + 6, 1), :]
            for c in (VX, VY, VZ):
                here = pl.ds(PAD + x, 1)
                key = c * wide + 1 + tj
                speed[key, here, :] = speed[key, here, :] - own_hb * ref[pl.ds(block + c, 1), :]
                speed[key, pl.ds(PAD + halo, 1), :] = (
                    ref[pl.ds(block + 3 + c, 1), :] + their_hb * bricks[ALONG_X[c] * across + tj, pl.ds(x, 1), :]
                )
    for ref, tj, halo, sign in ((col_before, 0, 0, 1.0), (col_after, across - 1, wide - 1, -1.0)):
        near = 0 if tj == 0 else LANES - edge
        far = LANES - edge - near
        inside = (lane >= near) & (lane < near + edge)
        for ti in range(g.xtiles):
            column = ref[pl.ds(M_BRICK + SUB * ti, SUB), :]
            own_hb = jnp.where(inside, sign * params[HB * across + tj, pl.ds(SUB * ti, SUB), :], 0.0)
            their_hb = sign * roll(column, far - 6 * edge)
            here = pl.ds(PAD + SUB * ti, SUB)
            for c in (VX, VY, VZ):
                key = c * wide + 1 + tj
                speed[key, here, :] = speed[key, here, :] - own_hb * roll(column, near - c * edge)
                own = bricks[ALONG_Y[c] * across + tj, pl.ds(SUB * ti, SUB), :]
                speed[c * wide + halo, here, :] = roll(column, far - (3 + c) * edge) + their_hb * roll(own, far - near)
        for k, (row_ref, x, x_halo, x_sign) in enumerate(((row_before, 0, -1, 1.0), (row_after, nx - 1, nx, -1.0))):
            corner = M_CORNER + SUB * k
            spare = ref[pl.ds(corner + 7, 1), :]
            toward = near - far
            inward = edge if far == 0 else -edge
            along = (
                roll_row(ref[pl.ds(corner + 1, 1), :], toward),
                roll_row(spare, toward),
                roll_row(spare, toward - inward),
            )
            row_hb = jnp.where(inside[0:1, :], sign * row_ref[pl.ds(M_BRICK + SUB * tj + 6, 1), :], 0.0)
            col_hb = x_sign * roll_row(ref[pl.ds(M_BRICK + x, 1), :], far - 6 * edge)
            for c in (VX, VY, VZ):
                key, here = c * wide + 1 + tj, pl.ds(PAD + x_halo, 1)
                speed[key, here, :] = speed[key, here, :] - row_hb * along[c]
                key, here = c * wide + halo, pl.ds(PAD + x, 1)
                speed[key, here, :] = speed[key, here, :] - col_hb * ref[pl.ds(corner + c, 1), :]

    @pl.loop(0, g.xtiles)
    def _(ti):
        row = pl.multiple_of(SUB * ti, SUB)
        here = pl.ds(row, SUB)
        inner = pl.ds(pl.multiple_of(row + PAD, SUB), SUB)
        rolled = []
        for field in (VX, VY, VZ):
            values = [speed[field * wide + tj, inner, :] for tj in range(wide)]
            rolled.append([(roll(value, edge), roll(value, -edge)) for value in values])
        tops = (
            lambda y: ux[pl.ds(ny + row * ny + y, SUB, stride=ny), :],
            lambda y: uy[pl.ds(row * py + PAD + y, SUB, stride=py), :],
            lambda y: water[pl.ds(3 * plane + row * ny + y, SUB, stride=ny), :],
        )
        for tj in range(across):
            ys = [g.yper * tj + k for k in range(g.yper)]
            dx, dy, dz, speeds = [], [], [], []
            for field in (VX, VY, VZ):
                key = field * wide + 1 + tj
                value = speed[key, inner, :]
                speeds.append(value)
                dx.append(speed[key, pl.ds(row + PAD + 1, SUB), :] - speed[key, pl.ds(row + PAD - 1, SUB), :])
                dy.append(along_y(g, rolled[field], tj + 1, lane))
                dz.append(along_z(g, value, shifted_top(g, tops[field], ys, lane), depth))
            strain = [dx[0], dy[1], dz[2], dy[0] + dx[1], dz[0] + dx[2], dz[1] + dy[2]]
            dilation = strain[0] + strain[1] + strain[2]

            def param(c):
                return params[c * across + tj, here, :]

            lame, shear = param(LAME) * dilation, param(SHEAR)
            spring_lame, spring_shear = param(SPRING_LAME) * dilation, param(SPRING_SHEAR)
            retain = [param(RETAIN + l) for l in range(3)]
            half_shear, half_spring = 0.5 * shear, 0.5 * spring_shear
            slot = g.slot(ti, tj)
            rows, lanes = g.place(ti, tj)
            if first:
                alive = param(ALIVE)
            stresses, memories = [], {}
            for comp in range(6):
                if comp < 3:
                    elastic = shear * strain[comp] + lame
                    relaxed = spring_shear * strain[comp] + spring_lame
                else:
                    elastic = half_shear * strain[comp]
                    relaxed = half_spring * strain[comp]
                summed = None
                for l in range(3):
                    place = 6 * l + comp
                    if first:
                        old = memory[slot, place, rows, lanes] * alive
                    else:
                        old = memory[place * across + tj, here, :]
                    new = relaxed + retain[l] * (old - relaxed)
                    memories[place] = new
                    summed = new if summed is None else summed + new
                stresses.append(bricks[(XX + comp) * across + tj, here, :] + elastic - summed)
            for place, value in memories.items():
                if last:
                    memory_out[slot, place, rows, lanes] = value
                else:
                    memory_out[place * across + tj, here, :] = value
            for comp, value in enumerate(stresses):
                if last:
                    bricks_out[slot, XX + comp, rows, lanes] = value
                else:
                    bricks_out[(XX + comp) * across + tj, here, :] = value
                    stress[comp * across + tj, inner, :] = value
            if last:
                for field in (VX, VY, VZ):
                    bricks_out[slot, field, rows, lanes] = speeds[field]

    def water_layer(x):
        results = []
        for t in range(g.ytiles):
            own = x * ny + SUB * t
            dx = ux[aligned((x + 2) * ny + SUB * t), :] - ux[aligned(x * ny + SUB * t), :]
            row = x * py + PAD + SUB * t
            dy = uy[pl.ds(row + 1, SUB), :] - uy[pl.ds(row - 1, SUB), :]
            surface = jnp.broadcast_to(speed[VZ * wide + 1 + t, pl.ds(PAD + x, 1), :], (SUB, LANES))
            uz = water[aligned(3 * plane + own), :]
            dz = water_z(g, uz, pick(surface, top_pick), lane)
            value = water[aligned(own), :] - hk_water[aligned(own), :] * (dx + dy + dz)
            results.append((own, t, value, uz, row))
        return x, results

    @pl.loop(0, nx // 2)
    def _(pair):
        for x, results in (water_layer(2 * pair), water_layer(2 * pair + 1)):
            for own, t, value, uz, row in results:
                water_out[aligned(own), :] = value
                if last:
                    water_out[aligned(plane + own), :] = ux[aligned(ny + own), :]
                    water_out[aligned(2 * plane + own), :] = uy[aligned(row), :]
                    water_out[aligned(3 * plane + own), :] = uz
                else:
                    press[x + 1, pl.ds(PAD + SUB * t, SUB), :] = value

    if not last:
        def load_u(k, x, t):
            if k == 1:
                return ux[aligned((x + 1) * ny + SUB * t), :]
            if k == 2:
                return uy[aligned(x * py + PAD + SUB * t), :]
            return water[aligned(3 * plane + x * ny + SUB * t), :]

        def load_v(field, ti, tj):
            return speed[field * wide + 1 + tj, aligned(PAD + SUB * ti), :]

        def load_hb(ti, tj):
            return params[HB * across + tj, aligned(SUB * ti), :]

        velocity_part(g, water_out, press, stress, hb_water, load_u, load_v, bricks_out, load_hb)
        pack(g, water_out, bricks_out, params, hb_water, *sends, False)


def exchange(g, sends):
    row_first, row_last, col_first, col_last = sends

    def shift(value, axis, up):
        count = lax.axis_size(axis)
        pairs = [(i, i + 1) for i in range(count - 1)]
        return lax.ppermute(value, axis, pairs if up else [(j, i) for i, j in pairs])

    row_before = shift(row_last, "row", True)
    row_after = shift(row_first, "row", False)

    def with_corners(message, tile):
        start = M_BRICK + SUB * tile
        corners = jnp.concatenate([row_before[start : start + SUB], row_after[start : start + SUB]])
        return lax.dynamic_update_slice(message, corners, (M_CORNER, 0))

    col_before = shift(with_corners(col_last, g.across - 1), "col", True)
    col_after = shift(with_corners(col_first, 0), "col", False)
    return row_before, row_after, col_before, col_after


def body(
    brick_velocity_stress,
    brick_relaxation_memory,
    brick_cell_material,
    brick_live,
    water_state,
    water_material,
    material_table,
):
    _, nx, ny, nz = water_state.shape
    g = Grid(nx, ny, brick_cell_material.shape[1])
    across, plane = g.across, g.plane

    def f32(*shape):
        return jax.ShapeDtypeStruct(shape, jnp.float32)

    vmem = pl.BlockSpec(memory_space=pltpu.VMEM)
    hbm = pl.BlockSpec(memory_space=pltpu.HBM)
    params = pltpu.CompilerParams(vmem_limit_bytes=24 * 1024 * 1024)
    press = pltpu.VMEM((nx + 2, ny + 2 * PAD, nz), jnp.float32)
    stress = pltpu.VMEM((6 * across, nx + 2 * PAD, LANES), jnp.float32)

    def messages(first):
        extra = 32 if first else 0
        return [f32(96 + extra, LANES)] * 2 + [f32(112 + extra, LANES)] * 2

    results = pl.pallas_call(
        functools.partial(first_kernel, g),
        out_shape=[
            f32(4 * plane, nz), f32(9 * across, nx, LANES), f32(9 * across, nx, LANES), f32(plane, nz), f32(plane, nz),
        ] + messages(True),
        in_specs=[hbm] * 6,
        out_specs=[vmem] * 9,
        scratch_shapes=[
            press,
            stress,
            pltpu.VMEM((3, nx, ny, nz), jnp.float32),
            pltpu.VMEM(water_material.shape, jnp.int32),
            pltpu.VMEM(brick_velocity_stress.shape, jnp.float32),
            pltpu.VMEM(brick_cell_material.shape, jnp.int32),
            pltpu.SMEM(brick_live.shape, jnp.int32),
            pltpu.SMEM(material_table.shape, jnp.float32),
            pltpu.SemaphoreType.DMA((7,)),
        ],
        compiler_params=params,
        name="first_velocity",
    )(*[
        pltpu.with_memory_space_constraint(value, pltpu.HBM)
        for value in (
            brick_live, material_table, water_state, water_material, brick_velocity_stress, brick_cell_material,
        )
    ])
    water, bricks, coefficients, hb_water, hk_water = results[:5]
    sends = results[5:]
    memory = brick_relaxation_memory
    constants = ()
    for step in range(STEPS):
        first, last = step == 0, step == STEPS - 1
        received = exchange(g, sends)
        if last:
            out_shape = [f32(4 * plane, nz), f32(*brick_velocity_stress.shape), f32(*memory_shape)]
        else:
            memory_shape = brick_relaxation_memory.shape
            out_shape = [f32(4 * plane, nz), f32(9 * across, nx, LANES), f32(18 * across, nx, LANES)] + messages(False)
        if first:
            out_shape += [f32(128, LANES)]
        results = pl.pallas_call(
            functools.partial(step_kernel, g, first, last),
            out_shape=out_shape,
            in_specs=[vmem] * (10 + len(constants)),
            out_specs=[vmem] * len(out_shape),
            scratch_shapes=[
                press,
                stress,
                pltpu.VMEM(((nx + 2) * ny, nz), jnp.float32),
                pltpu.VMEM((nx * (ny + 2 * PAD), nz), jnp.float32),
                pltpu.VMEM((3 * (across + 2), nx + 2 * PAD, LANES), jnp.float32),
            ],
            compiler_params=params,
            name="time_step",
        )(water, bricks, memory, coefficients, hb_water, hk_water, *received, *constants)
        water, bricks, memory = results[:3]
        if not last:
            sends = results[3:7]
        if first:
            constants = (results[7],)
    return bricks, memory, water.reshape(water_state.shape)


def solution(mesh):
    return jax.shard_map(
        body,
        mesh=mesh,
        in_specs=(
            P(("row", "col"), None, None, None),
            P(("row", "col"), None, None, None),
            P(("row", "col"), None, None),
            P(("row", "col")),
            P(None, "row", "col", None),
            P("row", "col", None),
            P(),
        ),
        out_specs=(
            P(("row", "col"), None, None, None),
            P(("row", "col"), None, None, None),
            P(None, "row", "col", None),
        ),
        check_vma=False,
    )
```

```python
import functools

import jax
import jax.numpy as jnp
from jax import lax
from jax.experimental import pallas as pl
from jax.experimental.pallas import tpu as pltpu
from jax.sharding import PartitionSpec as P

STEPS = 3
LANES = 128
SUB = 8
PAD = 8
VX, VY, VZ, XX, YY, ZZ, XY, XZ, YZ = range(9)
HB, LAME, SHEAR, RETAIN, SPRING_LAME, SPRING_SHEAR, ALIVE = 0, 1, 2, 3, 6, 7, 8
ALONG_X = (XX, XY, XZ)
ALONG_Y = (XY, YY, YZ)
ALONG_Z = (XZ, YZ, ZZ)
M_P, M_U, M_BRICK, M_CORNER = 0, 32, 64, 96
COL_CONST, ROW_CONST = 96, 112


def lane_ids():
    return lax.broadcasted_iota(jnp.int32, (SUB, LANES), 1)


def roll(value, shift):
    shift = shift % LANES
    return value if shift == 0 else pltpu.roll(value, shift, 1)


def roll_row(row, shift):
    shift = shift % LANES
    if shift == 0:
        return row
    return pltpu.roll(jnp.broadcast_to(row, (SUB, LANES)), shift, 1)[0:1, :]


def pick(values, indices):
    return jnp.take_along_axis(values, indices, axis=1, mode="promise_in_bounds")


def aligned(start, size=SUB):
    return pl.ds(start if isinstance(start, int) else pl.multiple_of(start, SUB), size)


class Grid:
    def __init__(self, nx, ny, edge):
        self.nx, self.ny, self.edge = nx, ny, edge
        self.plane = nx * ny
        self.across = ny * edge // LANES
        self.yper = LANES // edge
        self.half = self.across // 2
        self.xtiles, self.ytiles = nx // SUB, ny // SUB
        self.per = edge // SUB

    def slot(self, ti, tj):
        return 2 * (ti // self.per) + tj // self.half

    def place(self, ti, tj):
        return aligned((ti % self.per) * SUB), pl.ds((tj % self.half) * LANES, LANES)


def set_zero_pads(g, press, stress):
    zero = jnp.zeros((SUB, LANES), jnp.float32)
    for t in range(g.ytiles):
        press[0, pl.ds(PAD + SUB * t, SUB), :] = zero
        press[g.nx + 1, pl.ds(PAD + SUB * t, SUB), :] = zero

    @pl.loop(1, g.nx + 1)
    def _(x):
        press[x, pl.ds(0, SUB), :] = zero
        press[x, pl.ds(PAD + g.ny, SUB), :] = zero

    for field in ALONG_X:
        for tj in range(g.across):
            key = (field - XX) * g.across + tj
            stress[key, pl.ds(0, SUB), :] = zero
            stress[key, pl.ds(PAD + g.nx, SUB), :] = zero


def shifted_top(g, load, ys, lane):
    top = None
    for k, y in enumerate(ys):
        value = roll(load(y), g.edge * k + g.edge - 1)
        top = value if top is None else jnp.where(lane >= g.edge * k, value, top)
    return top


def along_y(g, rolled, tj, lane):
    zero = jnp.zeros((SUB, LANES), jnp.float32)
    after = rolled[tj + 1][1] if tj + 1 < len(rolled) else zero
    before = rolled[tj - 1][0] if tj > 0 else zero
    ahead = jnp.where(lane < LANES - g.edge, rolled[tj][1], after)
    behind = jnp.where(lane >= g.edge, rolled[tj][0], before)
    return ahead - behind


def along_z(g, value, beyond, depth):
    zero = jnp.zeros((SUB, LANES), jnp.float32)
    return jnp.where(depth == g.edge - 1, beyond, roll(value, -1)) - jnp.where(depth == 0, zero, roll(value, 1))


def water_z(g, value, below, lane):
    zero = jnp.zeros((SUB, LANES), jnp.float32)
    return jnp.where(lane == LANES - 1, zero, roll(value, -1)) - jnp.where(lane == 0, below, roll(value, 1))


def surface_pick():
    return lax.broadcasted_iota(jnp.int32, (SUB, LANES), 0)


def water_velocity(g, layers, water_out, press, stress, hb_water, load_u):
    lane = lane_ids()
    top_pick = surface_pick() * g.edge + (g.edge - 1)

    def water_layer(x):
        results = []
        for t in range(g.ytiles):
            rows = pl.ds(PAD + SUB * t, SUB)
            here = press[x + 1, rows, :]
            dx = press[x + 2, rows, :] - press[x, rows, :]
            dy = press[x + 1, pl.ds(PAD + SUB * t + 1, SUB), :] - press[x + 1, pl.ds(PAD + SUB * t - 1, SUB), :]
            surface = jnp.broadcast_to(stress[(ZZ - XX) * g.across + t, pl.ds(PAD + x, 1), :], (SUB, LANES))
            dz = water_z(g, here, -pick(surface, top_pick), lane)
            own = x * g.ny + SUB * t
            hb = hb_water[aligned(own), :]
            for k, change in ((1, dx), (2, dy), (3, dz)):
                results.append((k * g.plane + own, load_u(k, x, t) - hb * change))
        return results

    turns, layer = layers

    @pl.loop(0, turns)
    def _(turn):
        x = layer(turn)
        for row, value in water_layer(x) + water_layer(x + 1):
            water_out[aligned(row), :] = value


def brick_velocity(g, water_out, stress, load_v, bricks_out, load_hb):
    lane = lane_ids()
    depth = lane % g.edge
    zero = jnp.zeros((SUB, LANES), jnp.float32)
    across, ny = g.across, g.ny

    @pl.loop(0, g.xtiles)
    def _(ti):
        row = pl.multiple_of(SUB * ti, SUB)
        here = pl.ds(pl.multiple_of(row + PAD, SUB), SUB)

        def load(field, tj):
            return stress[(field - XX) * across + tj, here, :]

        def along_x(field, tj):
            key = (field - XX) * across + tj
            return stress[key, pl.ds(row + PAD + 1, SUB), :] - stress[key, pl.ds(row + PAD - 1, SUB), :]

        results = []
        for target, fx, fy, fz in zip((VX, VY, VZ), ALONG_X, ALONG_Y, ALONG_Z):
            rolled = [(roll(value, g.edge), roll(value, -g.edge)) for value in (load(fy, tj) for tj in range(across))]
            for tj in range(across):
                beyond = zero
                if fz == ZZ:
                    ys = [g.yper * tj + k for k in range(g.yper)]
                    beyond = -shifted_top(g, lambda y: water_out[pl.ds(row * ny + y, SUB, stride=ny), :], ys, lane)
                change = along_x(fx, tj) + along_y(g, rolled, tj, lane) + along_z(g, load(fz, tj), beyond, depth)
                results.append((target * across + tj, load_v(target, ti, tj) + load_hb(ti, tj) * change))
        for key, value in results:
            bricks_out[key, pl.ds(row, SUB), :] = value


def brick_stress(g, ti, first, bricks, memory, params, speed, tops, store):
    edge, across = g.edge, g.across
    wide = across + 2
    lane = lane_ids()
    depth = lane % edge
    row = SUB * ti if isinstance(ti, int) else pl.multiple_of(SUB * ti, SUB)
    here, inner = aligned(row), aligned(row + PAD)
    rolled = []
    for field in (VX, VY, VZ):
        values = [speed[field * wide + tj, inner, :] for tj in range(wide)]
        rolled.append([(roll(value, edge), roll(value, -edge)) for value in values])
    for tj in range(across):
        ys = [g.yper * tj + k for k in range(g.yper)]
        dx, dy, dz, speeds = [], [], [], []
        for field in (VX, VY, VZ):
            key = field * wide + 1 + tj
            value = speed[key, inner, :]
            speeds.append(value)
            dx.append(speed[key, pl.ds(row + PAD + 1, SUB), :] - speed[key, pl.ds(row + PAD - 1, SUB), :])
            dy.append(along_y(g, rolled[field], tj + 1, lane))
            dz.append(along_z(g, value, shifted_top(g, tops[field], ys, lane), depth))
        strain = [dx[0], dy[1], dz[2], dy[0] + dx[1], dz[0] + dx[2], dz[1] + dy[2]]
        dilation = strain[0] + strain[1] + strain[2]

        def param(c):
            return params[c * across + tj, here, :]

        lame, shear = param(LAME) * dilation, param(SHEAR)
        spring_lame, spring_shear = param(SPRING_LAME) * dilation, param(SPRING_SHEAR)
        retain = [param(RETAIN + l) for l in range(3)]
        half_shear, half_spring = 0.5 * shear, 0.5 * spring_shear
        slot = g.slot(ti, tj)
        rows, lanes = g.place(ti, tj)
        if first:
            alive = param(ALIVE)
        stresses, memories = [], {}
        for comp in range(6):
            if comp < 3:
                elastic = shear * strain[comp] + lame
                relaxed = spring_shear * strain[comp] + spring_lame
            else:
                elastic = half_shear * strain[comp]
                relaxed = half_spring * strain[comp]
            summed = None
            for l in range(3):
                place = 6 * l + comp
                if first:
                    old = memory[slot, place, rows, lanes] * alive
                else:
                    old = memory[place * across + tj, here, :]
                new = relaxed + retain[l] * (old - relaxed)
                memories[place] = new
                summed = new if summed is None else summed + new
            stresses.append(bricks[(XX + comp) * across + tj, here, :] + elastic - summed)
        store(ti, tj, here, inner, speeds, stresses, memories)


def store_planes(g, bricks_out, memory_out, stress):
    def store(ti, tj, here, inner, speeds, stresses, memories):
        for place, value in memories.items():
            memory_out[place * g.across + tj, here, :] = value
        for comp, value in enumerate(stresses):
            bricks_out[(XX + comp) * g.across + tj, here, :] = value
            stress[comp * g.across + tj, inner, :] = value

    return store


def store_slots(g, motion, memory):
    def store(ti, tj, here, inner, speeds, stresses, memories):
        slot = g.slot(ti, tj)
        rows, lanes = g.place(ti, tj)
        for place, value in memories.items():
            memory[slot, place, rows, lanes] = value
        for field, value in enumerate(speeds + stresses):
            motion[slot, field, rows, lanes] = value

    return store


def pack(g, water, bricks, params, hb_water, row_first, row_last, col_first, col_last, first):
    nx, ny, plane, across, edge = g.nx, g.ny, g.plane, g.across, g.edge
    lane = lane_ids()
    for out, x in ((row_first, 0), (row_last, nx - 1)):
        for t in range(g.ytiles):
            own = x * ny + SUB * t
            out[pl.ds(M_P + SUB * t, SUB), :] = water[pl.ds(own, SUB), :]
            out[pl.ds(M_U + SUB * t, SUB), :] = water[pl.ds(plane + own, SUB), :]
            if first:
                out[pl.ds(ROW_CONST + SUB * t, SUB), :] = hb_water[pl.ds(own, SUB), :]
        for tj in range(across):
            block = M_BRICK + SUB * tj
            for k, field in enumerate(ALONG_X + (VX, VY, VZ)):
                out[pl.ds(block + k, 1), :] = bricks[field * across + tj, pl.ds(x, 1), :]
            out[pl.ds(block + 6, 1), :] = params[HB * across + tj, pl.ds(x, 1), :]
            out[pl.ds(block + 7, 1), :] = jnp.zeros((1, LANES), jnp.float32)
        out[pl.ds(M_CORNER, 2 * SUB), :] = jnp.zeros((2 * SUB, LANES), jnp.float32)
    for out, y, tj in ((col_first, 0, 0), (col_last, ny - 1, across - 1)):
        for t in range(g.xtiles):
            own = SUB * t * ny + y
            out[pl.ds(M_P + SUB * t, SUB), :] = water[pl.ds(own, SUB, stride=ny), :]
            out[pl.ds(M_U + SUB * t, SUB), :] = water[pl.ds(2 * plane + own, SUB, stride=ny), :]
            if first:
                out[pl.ds(COL_CONST + SUB * t, SUB), :] = hb_water[pl.ds(own, SUB, stride=ny), :]
            rows = pl.ds(SUB * t, SUB)
            pieces = [bricks[field * across + tj, rows, :] for field in ALONG_Y + (VX, VY, VZ)]
            pieces.append(params[HB * across + tj, rows, :])
            beside = (1, 0) if t == 0 else (SUB - 2, SUB - 1)
            shear = bricks[XZ * across + tj, rows, :]
            if t == 0 or t == g.xtiles - 1:
                shear = pltpu.roll(shear, 1 if t == 0 else SUB - 1, 0)
            sub = lax.broadcasted_iota(jnp.int32, (SUB, LANES), 0)
            pieces.append(jnp.where(sub == beside[0], shear, bricks[XX * across + tj, rows, :]))
            packed = None
            for k, value in enumerate(pieces):
                moved = roll(value, edge * (k - y % g.yper))
                packed = moved if packed is None else jnp.where(lane >= edge * k, moved, packed)
            out[pl.ds(M_BRICK + SUB * t, SUB), :] = packed


def first_kernel(
    g, live_hbm, table_hbm, water_hbm, material_hbm, motion_hbm, kinds_hbm,
    water_out, bricks_out, params, hb_water, hk_water, row_first, row_last, col_first, col_last,
    press, stress, water, material, motion, kinds, live, table, sems,
):
    nx, ny, plane, across = g.nx, g.ny, g.plane, g.across
    copies = [
        pltpu.make_async_copy(motion_hbm, motion, sems.at[0]),
        pltpu.make_async_copy(kinds_hbm, kinds, sems.at[1]),
        pltpu.make_async_copy(water_hbm.at[0], press.at[pl.ds(1, nx), pl.ds(PAD, ny), :], sems.at[2]),
        pltpu.make_async_copy(material_hbm, material, sems.at[3]),
        pltpu.make_async_copy(water_hbm.at[pl.ds(1, 3)], water, sems.at[4]),
        pltpu.make_async_copy(live_hbm, live, sems.at[5]),
        pltpu.make_async_copy(table_hbm, table, sems.at[6]),
    ]
    for copy in copies:
        copy.start()
    lane = lane_ids()
    set_zero_pads(g, press, stress)
    copies[5].wait()
    copies[6].wait()
    levels = table.shape[0]
    scales = (0.5, 0.5, 1.0, 1.0, 1.0, 1.0, 0.5, 1.0)
    columns = []
    for c, factor in enumerate(scales):
        column = jnp.zeros((SUB, LANES), jnp.float32)
        for level in range(levels):
            column = jnp.where(lane == level, table[level, c], column)
        columns.append(column * factor)

    copies[0].wait()
    copies[1].wait()

    @pl.loop(0, g.xtiles)
    def _(ti):
        for tj in range(across):
            slot = g.slot(ti, tj)
            rows, lanes = g.place(ti, tj)
            alive = live[slot].astype(jnp.float32)
            here = aligned(SUB * ti)
            index = kinds[slot, rows, lanes]
            for c in range(8):
                value = pick(columns[c], index)
                params[c * across + tj, here, :] = value if 3 <= c < 6 else value * alive
            params[ALIVE * across + tj, here, :] = jnp.zeros((SUB, LANES), jnp.float32) + alive
            for field in range(XX, YZ + 1):
                value = motion[slot, field, rows, lanes] * alive
                bricks_out[field * across + tj, here, :] = value
                stress[(field - XX) * across + tj, aligned(PAD + SUB * ti), :] = value

    copies[2].wait()
    copies[3].wait()

    @pl.loop(0, nx)
    def _(x):
        results = []
        for t in range(g.ytiles):
            own = x * ny + SUB * t
            index = material[x, pl.ds(SUB * t, SUB), :]
            results.append((own, pick(columns[0], index), pick(columns[1], index), press[x + 1, pl.ds(PAD + SUB * t, SUB), :]))
        for own, hb, hk, p in results:
            hb_water[aligned(own), :] = hb
            hk_water[aligned(own), :] = hk
            water_out[aligned(own), :] = p

    copies[4].wait()

    def load_u(k, x, t):
        return water[k - 1, x, pl.ds(SUB * t, SUB), :]

    def load_v(field, ti, tj):
        slot = g.slot(ti, tj)
        rows, lanes = g.place(ti, tj)
        return motion[slot, field, rows, lanes] * live[slot].astype(jnp.float32)

    def load_hb(ti, tj):
        return params[HB * across + tj, aligned(SUB * ti), :]

    water_velocity(g, (nx // 2, lambda turn: 2 * turn), water_out, press, stress, hb_water, load_u)
    brick_velocity(g, water_out, stress, load_v, bricks_out, load_hb)
    pack(g, water_out, bricks_out, params, hb_water, row_first, row_last, col_first, col_last, True)


def slots_of(g, array, ti):
    slot = g.slot(ti, 0)
    return array.at[pl.ds(slot, 2), :, pl.ds((ti % g.per) * SUB, SUB), :]


class Refs:
    def __init__(self, refs):
        self.refs = list(refs)

    def take(self, count):
        taken, self.refs = self.refs[:count], self.refs[count:]
        return taken


def inner_kernel(g, first, last, *refs):
    refs = Refs(refs)
    water, bricks, memory, params, hb_water, hk_water, col_before, col_after = refs.take(8)
    if not first:
        (const_in,) = refs.take(1)
    uy, speed = refs.take(2)
    if last:
        water_hbm, motion_hbm, memory_hbm = refs.take(3)
    else:
        water_out, press, stress, bricks_out, memory_out = refs.take(5)
    if first:
        (const_out,) = refs.take(1)
    if last:
        press_buf, uy_buf, motion_buf, memory_buf, sems = refs.take(5)

    nx, ny, edge, across, plane = g.nx, g.ny, g.edge, g.across, g.plane
    wide = across + 2
    lane = lane_ids()
    top_pick = surface_pick() * edge + (edge - 1)
    py = ny + 2 * PAD
    low, high = SUB, nx - SUB
    copies = []

    def send(source, target):
        copies.append(pltpu.make_async_copy(source, target, sems.at[len(copies)]))
        copies[-1].start()

    def part(component, start, stop):
        return pl.ds(component * plane + start * ny, (stop - start) * ny)

    if last:
        send(water.at[part(3, 0, nx), :], water_hbm.at[part(3, 0, nx), :])
        send(water.at[part(1, 1, nx - 1), :], water_hbm.at[part(1, 1, nx - 1), :])
    else:
        set_zero_pads(g, press, stress)

    @pl.loop(0, nx)
    def _(x):
        for t in range(g.ytiles):
            own = x * ny + SUB * t
            uy[aligned(x * py + PAD + SUB * t), :] = water[aligned(2 * plane + own), :]
            if last:
                uy_buf[aligned(own), :] = water[aligned(2 * plane + own), :]

    for side, (ref, y, halo, sign) in enumerate(((col_before, 0, -1, 1.0), (col_after, ny - 1, ny, -1.0))):
        for t in range(g.xtiles):
            own = pl.ds(SUB * t * ny + y, SUB, stride=ny)
            here = pl.ds(SUB * t * py + PAD + y, SUB, stride=py)
            place = pl.ds(32 * side + SUB * t, SUB)
            if first:
                theirs = ref[pl.ds(COL_CONST + SUB * t, SUB), :]
                const_out[place, :] = theirs
            else:
                theirs = const_in[place, :]
            value = uy[here, :] + sign * hb_water[own, :] * ref[pl.ds(M_P + SUB * t, SUB), :]
            uy[here, :] = value
            if last:
                uy_buf[own, :] = value
            uy[pl.ds(SUB * t * py + PAD + halo, SUB, stride=py), :] = (
                ref[pl.ds(M_U + SUB * t, SUB), :] - sign * theirs * water[own, :]
            )
    if last:
        send(uy_buf, water_hbm.at[part(2, 0, nx), :])

    for field in (VX, VY, VZ):
        for tj in range(across):
            for ti in range(g.xtiles):
                speed[field * wide + 1 + tj, pl.ds(PAD + SUB * ti, SUB), :] = bricks[field * across + tj, pl.ds(SUB * ti, SUB), :]
    for ref, tj, halo, sign in ((col_before, 0, 0, 1.0), (col_after, across - 1, wide - 1, -1.0)):
        near = 0 if tj == 0 else LANES - edge
        far = LANES - edge - near
        inside = (lane >= near) & (lane < near + edge)
        for ti in range(g.xtiles):
            column = ref[pl.ds(M_BRICK + SUB * ti, SUB), :]
            own_hb = jnp.where(inside, sign * params[HB * across + tj, pl.ds(SUB * ti, SUB), :], 0.0)
            their_hb = sign * roll(column, far - 6 * edge)
            here = pl.ds(PAD + SUB * ti, SUB)
            for c in (VX, VY, VZ):
                key = c * wide + 1 + tj
                speed[key, here, :] = bricks[c * across + tj, pl.ds(SUB * ti, SUB), :] - own_hb * roll(column, near - c * edge)
                own = bricks[ALONG_Y[c] * across + tj, pl.ds(SUB * ti, SUB), :]
                speed[c * wide + halo, here, :] = roll(column, far - (3 + c) * edge) + their_hb * roll(own, far - near)

    store = store_slots(g, motion_buf, memory_buf) if last else store_planes(g, bricks_out, memory_out, stress)

    @pl.loop(1, g.xtiles - 1)
    def _(ti):
        row = pl.multiple_of(SUB * ti, SUB)
        tops = (
            lambda y: water[pl.ds(plane + row * ny + y, SUB, stride=ny), :],
            lambda y: uy[pl.ds(row * py + PAD + y, SUB, stride=py), :],
            lambda y: water[pl.ds(3 * plane + row * ny + y, SUB, stride=ny), :],
        )
        brick_stress(g, ti, first, bricks, memory, params, speed, tops, store)

    if last:
        for ti in range(1, g.xtiles - 1):
            send(slots_of(g, motion_buf, ti), slots_of(g, motion_hbm, ti))
            send(slots_of(g, memory_buf, ti), slots_of(g, memory_hbm, ti))

    def layer(x):
        results = []
        for t in range(g.ytiles):
            own = x * ny + SUB * t
            dx = water[aligned(plane + own + ny), :] - water[aligned(plane + own - ny), :]
            results.append(
                (x, t, own, water_stress(g, x, t, dx, water, uy, speed, hk_water, lane, top_pick))
            )
        return results

    @pl.loop(0, (nx - 4) // 2)
    def _(turn):
        for x, t, own, value in layer(2 + 2 * turn) + layer(3 + 2 * turn):
            if last:
                press_buf[aligned(own), :] = value
            else:
                water_out[aligned(own), :] = value
                press[x + 1, pl.ds(PAD + SUB * t, SUB), :] = value

    if last:
        send(press_buf.at[part(0, 2, nx - 2), :], water_hbm.at[part(0, 2, nx - 2), :])
        for copy in copies:
            copy.wait()
    else:
        def load_u(k, x, t):
            if k == 2:
                return uy[aligned(x * py + PAD + SUB * t), :]
            return water[aligned(k * plane + x * ny + SUB * t), :]

        layers = ((high - low) // 2, lambda turn: low + 2 * turn)
        water_velocity(g, layers, water_out, press, stress, hb_water, load_u)


def water_stress(g, x, t, dx, water, uy, speed, hk_water, lane, top_pick):
    row = x * (g.ny + 2 * PAD) + PAD + SUB * t
    own = x * g.ny + SUB * t
    dy = uy[pl.ds(row + 1, SUB), :] - uy[pl.ds(row - 1, SUB), :]
    surface = jnp.broadcast_to(speed[VZ * (g.across + 2) + 1 + t, pl.ds(PAD + x, 1), :], (SUB, LANES))
    dz = water_z(g, water[aligned(3 * g.plane + own), :], pick(surface, top_pick), lane)
    return water[aligned(own), :] - hk_water[aligned(own), :] * (dx + dy + dz)


def edge_kernel(g, first, last, *refs):
    refs = Refs(refs)
    water, bricks, memory, params, hb_water, hk_water, col_before, col_after, row_before, row_after = refs.take(10)
    if not first:
        (const_in,) = refs.take(1)
    (uy,) = refs.take(1)
    refs.take(4 if last else 6)
    (speed,) = refs.take(1)
    if last:
        water_hbm, motion_hbm, memory_hbm = refs.take(3)
    else:
        water_out, press, stress, bricks_out, memory_out = refs.take(5)
        sends = refs.take(4)
    if first:
        (const_out,) = refs.take(1)
    (ux,) = refs.take(1)
    if last:
        press_buf, motion_buf, memory_buf, sems = refs.take(4)

    nx, ny, edge, across, plane = g.nx, g.ny, g.edge, g.across, g.plane
    wide = across + 2
    lane = lane_ids()
    top_pick = surface_pick() * edge + (edge - 1)
    py = ny + 2 * PAD
    copies = []

    def send(source, target):
        copies.append(pltpu.make_async_copy(source, target, sems.at[len(copies)]))
        copies[-1].start()

    @pl.loop(0, SUB)
    def _(x):
        for t in range(g.ytiles):
            own = x * ny + SUB * t
            ux[aligned(ny + own), :] = water[aligned(plane + own), :]
            ux[aligned((1 + SUB) * ny + own), :] = water[aligned(plane + (nx - SUB) * ny + own), :]

    sides = ((row_before, 0, -1, 1.0, 1, 0), (row_after, nx - 1, nx, -1.0, 2 * SUB, 2 * SUB + 1))
    for side, (ref, x, halo, sign, own_layer, halo_layer) in enumerate(sides):
        for t in range(g.ytiles):
            own = pl.ds(x * ny + SUB * t, SUB)
            place = pl.ds(32 * side + SUB * t, SUB)
            if first:
                theirs = ref[pl.ds(ROW_CONST + SUB * t, SUB), :]
                const_out[place, :] = theirs
            else:
                theirs = const_in[place, :]
            here = pl.ds(own_layer * ny + SUB * t, SUB)
            ux[here, :] = ux[here, :] + sign * hb_water[own, :] * ref[pl.ds(M_P + SUB * t, SUB), :]
            ux[pl.ds(halo_layer * ny + SUB * t, SUB), :] = ref[pl.ds(M_U + SUB * t, SUB), :] - sign * theirs * water[own, :]
    if last:
        for layer, x in ((1, 0), (2 * SUB, nx - 1)):
            send(ux.at[pl.ds(layer * ny, ny), :], water_hbm.at[pl.ds(plane + x * ny, ny), :])

    for ref, x, halo, sign, _, _ in sides:
        for tj in range(across):
            block = M_BRICK + SUB * tj
            own_hb = sign * params[HB * across + tj, pl.ds(x, 1), :]
            their_hb = sign * ref[pl.ds(block + 6, 1), :]
            for c in (VX, VY, VZ):
                here = pl.ds(PAD + x, 1)
                key = c * wide + 1 + tj
                speed[key, here, :] = speed[key, here, :] - own_hb * ref[pl.ds(block + c, 1), :]
                speed[key, pl.ds(PAD + halo, 1), :] = (
                    ref[pl.ds(block + 3 + c, 1), :] + their_hb * bricks[ALONG_X[c] * across + tj, pl.ds(x, 1), :]
                )
        edge_row = SUB - 1 if x == 0 else 0
        beside_row = SUB - 2 if x == 0 else 1
        for k, (col_ref, tj, col_halo, col_sign) in enumerate(((col_before, 0, 0, 1.0), (col_after, across - 1, wide - 1, -1.0))):
            near = 0 if tj == 0 else LANES - edge
            far = LANES - edge - near
            inside = (lane[0:1, :] >= near) & (lane[0:1, :] < near + edge)
            corner = ref[pl.ds(M_CORNER + SUB * k + edge_row, 1), :]
            beside = ref[pl.ds(M_CORNER + SUB * k + beside_row, 1), :]
            across_y = [roll_row(corner, near - c * edge) for c in range(3)]
            across_x = (roll_row(corner, far - 7 * edge), roll_row(corner, far), roll_row(beside, far - 7 * edge))
            row_hb = jnp.where(inside, col_sign * ref[pl.ds(M_BRICK + SUB * tj + 6, 1), :], 0.0)
            col_hb = sign * roll_row(col_ref[pl.ds(M_BRICK + x, 1), :], far - 6 * edge)
            for c in (VX, VY, VZ):
                key, here = c * wide + 1 + tj, pl.ds(PAD + halo, 1)
                speed[key, here, :] = speed[key, here, :] - row_hb * across_y[c]
                key, here = c * wide + col_halo, pl.ds(PAD + x, 1)
                speed[key, here, :] = speed[key, here, :] - col_hb * across_x[c]

    store = store_slots(g, motion_buf, memory_buf) if last else store_planes(g, bricks_out, memory_out, stress)

    @pl.loop(0, 2)
    def _(turn):
        ti = turn * (g.xtiles - 1)
        row = pl.multiple_of(SUB * ti, SUB)
        above = pl.multiple_of((1 + SUB * turn) * ny, SUB)
        tops = (
            lambda y: ux[pl.ds(above + y, SUB, stride=ny), :],
            lambda y: uy[pl.ds(row * py + PAD + y, SUB, stride=py), :],
            lambda y: water[pl.ds(3 * plane + row * ny + y, SUB, stride=ny), :],
        )
        brick_stress(g, ti, first, bricks, memory, params, speed, tops, store)

    if last:
        for ti in (0, g.xtiles - 1):
            send(slots_of(g, motion_buf, ti), slots_of(g, motion_hbm, ti))
            send(slots_of(g, memory_buf, ti), slots_of(g, memory_hbm, ti))

    for pair, (x, layer) in enumerate(((0, 1), (nx - 2, 2 * SUB - 1))):
        for step in range(2):
            for t in range(g.ytiles):
                dx = (
                    ux[pl.ds((layer + step + 1) * ny + SUB * t, SUB), :] - ux[pl.ds((layer + step - 1) * ny + SUB * t, SUB), :]
                )
                value = water_stress(g, x + step, t, dx, water, uy, speed, hk_water, lane, top_pick)
                if last:
                    press_buf[pl.ds((2 * pair + step) * ny + SUB * t, SUB), :] = value
                else:
                    water_out[pl.ds((x + step) * ny + SUB * t, SUB), :] = value
                    press[x + step + 1, pl.ds(PAD + SUB * t, SUB), :] = value

    if last:
        for pair, x in enumerate((0, nx - 2)):
            send(press_buf.at[pl.ds(2 * pair * ny, 2 * ny), :], water_hbm.at[pl.ds(x * ny, 2 * ny), :])
        for copy in copies:
            copy.wait()
    else:
        def load_u(k, x, t):
            if k == 1:
                layer = x - (x // (nx - SUB)) * (nx - 2 * SUB) + 1
                return ux[aligned(layer * ny + SUB * t), :]
            if k == 2:
                return uy[aligned(x * py + PAD + SUB * t), :]
            return water[aligned(3 * plane + x * ny + SUB * t), :]

        def load_v(field, ti, tj):
            return speed[field * wide + 1 + tj, aligned(PAD + SUB * ti), :]

        def load_hb(ti, tj):
            return params[HB * across + tj, aligned(SUB * ti), :]

        layers = (SUB, lambda turn: 2 * turn + (turn // (SUB // 2)) * (nx - 2 * SUB))
        water_velocity(g, layers, water_out, press, stress, hb_water, load_u)
        brick_velocity(g, water_out, stress, load_v, bricks_out, load_hb)
        pack(g, water_out, bricks_out, params, hb_water, *sends, False)


def shift(value, axis, up):
    count = lax.axis_size(axis)
    pairs = [(i, i + 1) for i in range(count - 1)]
    return lax.ppermute(value, axis, pairs if up else [(j, i) for i, j in pairs])


def exchange(g, sends):
    row_first, row_last, col_first, col_last = sends
    col_before = shift(col_last, "col", True)
    col_after = shift(col_first, "col", False)

    def with_corners(message, start):
        start += M_BRICK
        corners = jnp.concatenate([col_before[start : start + SUB], col_after[start : start + SUB]])
        return lax.dynamic_update_slice(message, corners, (M_CORNER, 0))

    row_before = shift(with_corners(row_last, g.nx - SUB), "row", True)
    row_after = shift(with_corners(row_first, 0), "row", False)
    return col_before, col_after, row_before, row_after


def body(
    brick_velocity_stress,
    brick_relaxation_memory,
    brick_cell_material,
    brick_live,
    water_state,
    water_material,
    material_table,
):
    _, nx, ny, nz = water_state.shape
    g = Grid(nx, ny, brick_cell_material.shape[1])
    across, plane = g.across, g.plane

    def f32(*shape):
        return jax.ShapeDtypeStruct(shape, jnp.float32)

    vmem = pl.BlockSpec(memory_space=pltpu.VMEM)
    hbm = pl.BlockSpec(memory_space=pltpu.HBM)
    params = pltpu.CompilerParams(vmem_limit_bytes=24 * 1024 * 1024)
    press = pltpu.VMEM((nx + 2, ny + 2 * PAD, nz), jnp.float32)
    stress = pltpu.VMEM((6 * across, nx + 2 * PAD, LANES), jnp.float32)

    def messages(first):
        extra = 32 if first else 0
        return [f32(112 + extra, LANES)] * 2 + [f32(96 + extra, LANES)] * 2

    def buffer(*shape):
        return pltpu.VMEM(shape, jnp.float32)

    def held(*values):
        return [pltpu.with_memory_space_constraint(value, pltpu.VMEM) for value in values]

    results = pl.pallas_call(
        functools.partial(first_kernel, g),
        out_shape=[
            f32(4 * plane, nz), f32(9 * across, nx, LANES), f32(9 * across, nx, LANES), f32(plane, nz), f32(plane, nz),
        ] + messages(True),
        in_specs=[hbm] * 6,
        out_specs=[vmem] * 9,
        scratch_shapes=[
            press,
            stress,
            pltpu.VMEM((3, nx, ny, nz), jnp.float32),
            pltpu.VMEM(water_material.shape, jnp.int32),
            pltpu.VMEM(brick_velocity_stress.shape, jnp.float32),
            pltpu.VMEM(brick_cell_material.shape, jnp.int32),
            pltpu.SMEM(brick_live.shape, jnp.int32),
            pltpu.SMEM(material_table.shape, jnp.float32),
            pltpu.SemaphoreType.DMA((7,)),
        ],
        compiler_params=params,
        name="first_velocity",
    )(*[
        pltpu.with_memory_space_constraint(value, pltpu.HBM)
        for value in (
            brick_live, material_table, water_state, water_material, brick_velocity_stress, brick_cell_material,
        )
    ])
    water, bricks, coefficients, hb_water, hk_water = results[:5]
    sends = results[5:]
    memory = brick_relaxation_memory
    col_const, row_const = (), ()
    uy_shape = (nx * (ny + 2 * PAD), nz)
    speed_shape = (3 * (across + 2), nx + 2 * PAD, LANES)
    ux = buffer((2 * SUB + 2) * ny, nz)
    slot_buffers = [
        pltpu.VMEM(brick_velocity_stress.shape, jnp.float32),
        pltpu.VMEM(brick_relaxation_memory.shape, jnp.float32),
    ]
    finals = [f32(4 * plane, nz), f32(*brick_velocity_stress.shape), f32(*brick_relaxation_memory.shape)]
    planes = [
        buffer(4 * plane, nz),
        buffer(nx + 2, ny + 2 * PAD, nz),
        buffer(6 * across, nx + 2 * PAD, LANES),
        buffer(9 * across, nx, LANES),
        buffer(18 * across, nx, LANES),
    ]
    for step in range(STEPS):
        first, last = step == 0, step == STEPS - 1
        *columns, row_before, row_after = exchange(g, sends)
        state = (water, bricks, memory, coefficients, hb_water, hk_water)
        shapes = finals if last else planes
        spaces = [hbm if last else vmem] * len(shapes)
        inner = pl.pallas_call(
            functools.partial(inner_kernel, g, first, last),
            out_shape=[buffer(*uy_shape), buffer(*speed_shape)] + shapes + ([buffer(64, LANES)] if first else []),
            in_specs=[vmem] * (8 + len(col_const)),
            out_specs=[vmem] * 2 + spaces + ([vmem] if first else []),
            scratch_shapes=[buffer(plane, nz), buffer(plane, nz)] + slot_buffers + [pltpu.SemaphoreType.DMA((8,))] if last else [],
            compiler_params=params,
            cost_estimate=pl.CostEstimate(flops=20_000_000, bytes_accessed=8_000_000, transcendentals=0),
            name="inner",
        )(*held(*state), *columns, *col_const)
        if first:
            col_const = (inner[-1],)
            inner = inner[:-1]
        uy, *partial = inner
        count = 10 + len(row_const) + 1
        results = pl.pallas_call(
            functools.partial(edge_kernel, g, first, last),
            out_shape=[buffer(*speed_shape)] + shapes + ([] if last else messages(False)) + ([buffer(64, LANES)] if first else []),
            in_specs=[vmem] * (count + 1) + spaces,
            out_specs=[vmem] + spaces + [vmem] * (0 if last else 4) + ([vmem] if first else []),
            input_output_aliases={count + k: k for k in range(1 + len(shapes))},
            scratch_shapes=[ux] + ([buffer(4 * ny, nz)] + slot_buffers + [pltpu.SemaphoreType.DMA((8,))] if last else []),
            compiler_params=params,
            name="edges",
        )(*held(*state), *columns, row_before, row_after, *row_const, *held(uy), *(held(partial[0]) + (list(partial[1:]) if last else held(*partial[1:]))))
        if last:
            return results[2], results[3], results[1].reshape(water_state.shape)
        _, water, _, _, bricks, memory = results[:6]
        sends = results[6:10]
        if first:
            row_const = (results[10],)


def solution(mesh):
    return jax.shard_map(
        body,
        mesh=mesh,
        in_specs=(
            P(("row", "col"), None, None, None),
            P(("row", "col"), None, None, None),
            P(("row", "col"), None, None),
            P(("row", "col")),
            P(None, "row", "col", None),
            P("row", "col", None),
            P(),
        ),
        out_specs=(
            P(("row", "col"), None, None, None),
            P(("row", "col"), None, None, None),
            P(None, "row", "col", None),
        ),
        check_vma=False,
    )
```

```python
import functools

import jax
import jax.numpy as jnp
from jax import lax
from jax.experimental import pallas as pl
from jax.experimental.pallas import tpu as pltpu
from jax.sharding import PartitionSpec as P

STEPS = 3
LANES = 128
SUB = 8
PAD = 8
VX, VY, VZ, XX, YY, ZZ, XY, XZ, YZ = range(9)
HB, LAME, SHEAR, RETAIN, SPRING_LAME, SPRING_SHEAR, ALIVE = 0, 1, 2, 3, 6, 7, 8
ALONG_X = (XX, XY, XZ)
ALONG_Y = (XY, YY, YZ)
ALONG_Z = (XZ, YZ, ZZ)
M_P, M_U, M_BRICK, M_CORNER = 0, 32, 64, 96
COL_CONST, ROW_CONST = 96, 112


def lane_ids():
    return lax.broadcasted_iota(jnp.int32, (SUB, LANES), 1)


def roll(value, shift):
    shift = shift % LANES
    return value if shift == 0 else pltpu.roll(value, shift, 1)


def roll_row(row, shift):
    shift = shift % LANES
    if shift == 0:
        return row
    return pltpu.roll(jnp.broadcast_to(row, (SUB, LANES)), shift, 1)[0:1, :]


def pick(values, indices):
    return jnp.take_along_axis(values, indices, axis=1, mode="promise_in_bounds")


def aligned(start, size=SUB):
    return pl.ds(start if isinstance(start, int) else pl.multiple_of(start, SUB), size)


class Grid:
    def __init__(self, nx, ny, edge):
        self.nx, self.ny, self.edge = nx, ny, edge
        self.plane = nx * ny
        self.across = ny * edge // LANES
        self.yper = LANES // edge
        self.half = self.across // 2
        self.xtiles, self.ytiles = nx // SUB, ny // SUB
        self.per = edge // SUB

    def slot(self, ti, tj):
        return 2 * (ti // self.per) + tj // self.half

    def place(self, ti, tj):
        return aligned((ti % self.per) * SUB), pl.ds((tj % self.half) * LANES, LANES)


def zero_press_pads(g, press):
    zero = jnp.zeros((SUB, LANES), jnp.float32)
    for t in range(g.ytiles):
        press[0, pl.ds(PAD + SUB * t, SUB), :] = zero
        press[g.nx + 1, pl.ds(PAD + SUB * t, SUB), :] = zero

    @pl.loop(1, g.nx + 1)
    def _(x):
        press[x, pl.ds(0, SUB), :] = zero
        press[x, pl.ds(PAD + g.ny, SUB), :] = zero


def zero_stress_pads(g, stress):
    zero = jnp.zeros((SUB, LANES), jnp.float32)
    for field in ALONG_X:
        for tj in range(g.across):
            key = (field - XX) * g.across + tj
            stress[key, pl.ds(0, SUB), :] = zero
            stress[key, pl.ds(PAD + g.nx, SUB), :] = zero


def shifted_top(g, load, ys, lane):
    top = None
    for k, y in enumerate(ys):
        value = roll(load(y), g.edge * k + g.edge - 1)
        top = value if top is None else jnp.where(lane >= g.edge * k, value, top)
    return top


def along_y(g, rolled, tj, lane):
    zero = jnp.zeros((SUB, LANES), jnp.float32)
    after = rolled[tj + 1][1] if tj + 1 < len(rolled) else zero
    before = rolled[tj - 1][0] if tj > 0 else zero
    ahead = jnp.where(lane < LANES - g.edge, rolled[tj][1], after)
    behind = jnp.where(lane >= g.edge, rolled[tj][0], before)
    return ahead - behind


def along_z(g, value, beyond, depth):
    zero = jnp.zeros((SUB, LANES), jnp.float32)
    return jnp.where(depth == g.edge - 1, beyond, roll(value, -1)) - jnp.where(depth == 0, zero, roll(value, 1))


def water_z(g, value, below, lane):
    zero = jnp.zeros((SUB, LANES), jnp.float32)
    return jnp.where(lane == LANES - 1, zero, roll(value, -1)) - jnp.where(lane == 0, below, roll(value, 1))


def surface_pick():
    return lax.broadcasted_iota(jnp.int32, (SUB, LANES), 0)


def water_velocity(g, layers, water_out, press, surface_row, load_hb, load_u):
    lane = lane_ids()
    top_pick = surface_pick() * g.edge + (g.edge - 1)

    def water_layer(x):
        results = []
        for t in range(g.ytiles):
            rows = pl.ds(PAD + SUB * t, SUB)
            here = press[x + 1, rows, :]
            dx = press[x + 2, rows, :] - press[x, rows, :]
            dy = press[x + 1, pl.ds(PAD + SUB * t + 1, SUB), :] - press[x + 1, pl.ds(PAD + SUB * t - 1, SUB), :]
            surface = jnp.broadcast_to(surface_row(t, x), (SUB, LANES))
            dz = water_z(g, here, -pick(surface, top_pick), lane)
            own = x * g.ny + SUB * t
            hb = load_hb(x, t)
            for k, change in ((1, dx), (2, dy), (3, dz)):
                results.append((k * g.plane + own, load_u(k, x, t) - hb * change))
        return results

    turns, layer = layers

    @pl.loop(0, turns)
    def _(turn):
        x = layer(turn)
        for row, value in water_layer(x) + water_layer(x + 1):
            water_out[aligned(row), :] = value


def brick_velocity(g, water_out, stress, load_v, bricks_out, load_hb):
    lane = lane_ids()
    depth = lane % g.edge
    zero = jnp.zeros((SUB, LANES), jnp.float32)
    across, ny = g.across, g.ny

    @pl.loop(0, g.xtiles)
    def _(ti):
        row = pl.multiple_of(SUB * ti, SUB)
        here = pl.ds(pl.multiple_of(row + PAD, SUB), SUB)

        def load(field, tj):
            return stress[(field - XX) * across + tj, here, :]

        def along_x(field, tj):
            key = (field - XX) * across + tj
            return stress[key, pl.ds(row + PAD + 1, SUB), :] - stress[key, pl.ds(row + PAD - 1, SUB), :]

        results = []
        for target, fx, fy, fz in zip((VX, VY, VZ), ALONG_X, ALONG_Y, ALONG_Z):
            rolled = [(roll(value, g.edge), roll(value, -g.edge)) for value in (load(fy, tj) for tj in range(across))]
            for tj in range(across):
                beyond = zero
                if fz == ZZ:
                    ys = [g.yper * tj + k for k in range(g.yper)]
                    beyond = -shifted_top(g, lambda y: water_out[pl.ds(row * ny + y, SUB, stride=ny), :], ys, lane)
                change = along_x(fx, tj) + along_y(g, rolled, tj, lane) + along_z(g, load(fz, tj), beyond, depth)
                results.append((target * across + tj, load_v(target, ti, tj) + load_hb(ti, tj) * change))
        for key, value in results:
            bricks_out[key, pl.ds(row, SUB), :] = value


def brick_stress(g, ti, first, bricks, memory, params, speed, tops, store):
    edge, across = g.edge, g.across
    wide = across + 2
    lane = lane_ids()
    depth = lane % edge
    row = SUB * ti if isinstance(ti, int) else pl.multiple_of(SUB * ti, SUB)
    here, inner = aligned(row), aligned(row + PAD)
    rolled = []
    for field in (VX, VY, VZ):
        values = [speed[field * wide + tj, inner, :] for tj in range(wide)]
        rolled.append([(roll(value, edge), roll(value, -edge)) for value in values])
    for tj in range(across):
        ys = [g.yper * tj + k for k in range(g.yper)]
        dx, dy, dz, speeds = [], [], [], []
        for field in (VX, VY, VZ):
            key = field * wide + 1 + tj
            value = speed[key, inner, :]
            speeds.append(value)
            dx.append(speed[key, pl.ds(row + PAD + 1, SUB), :] - speed[key, pl.ds(row + PAD - 1, SUB), :])
            dy.append(along_y(g, rolled[field], tj + 1, lane))
            dz.append(along_z(g, value, shifted_top(g, tops[field], ys, lane), depth))
        strain = [dx[0], dy[1], dz[2], dy[0] + dx[1], dz[0] + dx[2], dz[1] + dy[2]]
        dilation = strain[0] + strain[1] + strain[2]

        def param(c):
            return params[c * across + tj, here, :]

        lame, shear = param(LAME) * dilation, param(SHEAR)
        spring_lame, spring_shear = param(SPRING_LAME) * dilation, param(SPRING_SHEAR)
        retain = [param(RETAIN + l) for l in range(3)]
        half_shear, half_spring = 0.5 * shear, 0.5 * spring_shear
        slot = g.slot(ti, tj)
        rows, lanes = g.place(ti, tj)
        if first:
            alive = param(ALIVE)
        stresses, memories = [], {}
        for comp in range(6):
            if comp < 3:
                elastic = shear * strain[comp] + lame
                relaxed = spring_shear * strain[comp] + spring_lame
            else:
                elastic = half_shear * strain[comp]
                relaxed = half_spring * strain[comp]
            summed = None
            for l in range(3):
                place = 6 * l + comp
                if first:
                    old = memory[slot, place, rows, lanes] * alive
                else:
                    old = memory[place * across + tj, here, :]
                new = relaxed + retain[l] * (old - relaxed)
                memories[place] = new
                summed = new if summed is None else summed + new
            stresses.append(bricks[(XX + comp) * across + tj, here, :] + elastic - summed)
        store(ti, tj, here, inner, speeds, stresses, memories)


def store_planes(g, bricks_out, memory_out, stress):
    def store(ti, tj, here, inner, speeds, stresses, memories):
        for place, value in memories.items():
            memory_out[place * g.across + tj, here, :] = value
        for comp, value in enumerate(stresses):
            bricks_out[(XX + comp) * g.across + tj, here, :] = value
            stress[comp * g.across + tj, inner, :] = value

    return store


def store_slots(g, motion, memory):
    def store(ti, tj, here, inner, speeds, stresses, memories):
        slot = g.slot(ti, tj)
        rows, lanes = g.place(ti, tj)
        for place, value in memories.items():
            memory[slot, place, rows, lanes] = value
        for field, value in enumerate(speeds + stresses):
            motion[slot, field, rows, lanes] = value

    return store


def pack(g, water, bricks, params, edges, row_first, row_last, col_first, col_last, first):
    row_u, row_hb, col_u, col_hb = edges
    nx, ny, across, edge = g.nx, g.ny, g.across, g.edge
    lane = lane_ids()
    for side, (out, x, inward, sign) in enumerate(((row_first, 0, 1, 1.0), (row_last, nx - 1, nx - 2, -1.0))):
        for t in range(g.ytiles):
            own = x * ny + SUB * t
            hb = row_hb(side, t)
            out[pl.ds(M_P + SUB * t, SUB), :] = water[pl.ds(own, SUB), :]
            out[pl.ds(M_U + SUB * t, SUB), :] = row_u(side, t) - sign * hb * water[pl.ds(inward * ny + SUB * t, SUB), :]
            if first:
                out[pl.ds(ROW_CONST + SUB * t, SUB), :] = hb
        for tj in range(across):
            block = M_BRICK + SUB * tj
            for k, field in enumerate(ALONG_X + (VX, VY, VZ)):
                out[pl.ds(block + k, 1), :] = bricks[field * across + tj, pl.ds(x, 1), :]
            out[pl.ds(block + 6, 1), :] = params[HB * across + tj, pl.ds(x, 1), :]
            out[pl.ds(block + 7, 1), :] = jnp.zeros((1, LANES), jnp.float32)
        out[pl.ds(M_CORNER, 2 * SUB), :] = jnp.zeros((2 * SUB, LANES), jnp.float32)
    sides = ((col_first, 0, 1, 0, 1.0), (col_last, ny - 1, ny - 2, across - 1, -1.0))
    for side, (out, y, inward, tj, sign) in enumerate(sides):
        for t in range(g.xtiles):
            own = SUB * t * ny + y
            hb = col_hb(side, t)
            out[pl.ds(M_P + SUB * t, SUB), :] = water[pl.ds(own, SUB, stride=ny), :]
            out[pl.ds(M_U + SUB * t, SUB), :] = (
                col_u(side, t) - sign * hb * water[pl.ds(SUB * t * ny + inward, SUB, stride=ny), :]
            )
            if first:
                out[pl.ds(COL_CONST + SUB * t, SUB), :] = hb
            rows = pl.ds(SUB * t, SUB)
            pieces = [bricks[field * across + tj, rows, :] for field in ALONG_Y + (VX, VY, VZ)]
            pieces.append(params[HB * across + tj, rows, :])
            beside = (1, 0) if t == 0 else (SUB - 2, SUB - 1)
            shear = bricks[XZ * across + tj, rows, :]
            if t == 0 or t == g.xtiles - 1:
                shear = pltpu.roll(shear, 1 if t == 0 else SUB - 1, 0)
            sub = lax.broadcasted_iota(jnp.int32, (SUB, LANES), 0)
            pieces.append(jnp.where(sub == beside[0], shear, bricks[XX * across + tj, rows, :]))
            packed = None
            for k, value in enumerate(pieces):
                moved = roll(value, edge * (k - y % g.yper))
                packed = moved if packed is None else jnp.where(lane >= edge * k, moved, packed)
            out[pl.ds(M_BRICK + SUB * t, SUB), :] = packed


def first_kernel(
    g, live_hbm, table_hbm, water_hbm, material_hbm, motion_hbm, kinds_hbm,
    water_out, bricks_out, params, columns, row_first, row_last, col_first, col_last,
    stress, pressure, ux_edge, uy_edge, material_x, material_y, motion, kinds, live, table, sems,
):
    nx, ny, across = g.nx, g.ny, g.across
    copies = []

    def fetch(source, target):
        copies.append(pltpu.make_async_copy(source, target, sems.at[len(copies)]))
        copies[-1].start()

    fetch(live_hbm, live)
    fetch(table_hbm, table)
    fetch(kinds_hbm, kinds)
    fetch(motion_hbm, motion)
    fetch(water_hbm.at[0], pressure)
    for side, (x, y) in enumerate(((0, 0), (nx - 1, ny - SUB))):
        fetch(water_hbm.at[1, x], ux_edge.at[side])
        fetch(material_hbm.at[x], material_x.at[side])
        fetch(water_hbm.at[2, :, pl.ds(y, SUB), :], uy_edge.at[side])
        fetch(material_hbm.at[:, pl.ds(y, SUB), :], material_y.at[side])
    lane = lane_ids()
    zero_stress_pads(g, stress)
    copies[0].wait()
    copies[1].wait()
    scales = (0.5, 0.5, 1.0, 1.0, 1.0, 1.0, 0.5, 1.0)
    for c, factor in enumerate(scales):
        column = jnp.zeros((SUB, LANES), jnp.float32)
        for level in range(table.shape[0]):
            column = jnp.where(lane == level, table[level, c], column)
        columns[c] = column * factor
    copies[2].wait()
    copies[3].wait()

    @pl.loop(0, g.xtiles)
    def _(ti):
        for tj in range(across):
            slot = g.slot(ti, tj)
            rows, lanes = g.place(ti, tj)
            alive = live[slot].astype(jnp.float32)
            here = aligned(SUB * ti)
            index = kinds[slot, rows, lanes]
            for c in range(8):
                value = pick(columns[c], index)
                params[c * across + tj, here, :] = value if 3 <= c < 6 else value * alive
            params[ALIVE * across + tj, here, :] = jnp.zeros((SUB, LANES), jnp.float32) + alive
            for field in range(XX, YZ + 1):
                value = motion[slot, field, rows, lanes] * alive
                bricks_out[field * across + tj, here, :] = value
                stress[(field - XX) * across + tj, aligned(PAD + SUB * ti), :] = value

    copies[4].wait()

    @pl.loop(0, nx // 2)
    def _(turn):
        results = []
        for x in (2 * turn, 2 * turn + 1):
            for t in range(g.ytiles):
                results.append((x * ny + SUB * t, pressure[x, pl.ds(SUB * t, SUB), :]))
        for own, value in results:
            water_out[aligned(own), :] = value

    def load_v(field, ti, tj):
        slot = g.slot(ti, tj)
        rows, lanes = g.place(ti, tj)
        return motion[slot, field, rows, lanes] * live[slot].astype(jnp.float32)

    def load_hb(ti, tj):
        return params[HB * across + tj, aligned(SUB * ti), :]

    brick_velocity(g, water_out, stress, load_v, bricks_out, load_hb)
    for copy in copies[5:]:
        copy.wait()

    def rows_of(side, t):
        return side, pl.ds(SUB * t, SUB), side * (SUB - 1)

    edges = (
        lambda side, t: ux_edge[side, pl.ds(SUB * t, SUB), :],
        lambda side, t: pick(columns[0], material_x[side, pl.ds(SUB * t, SUB), :]),
        lambda side, t: uy_edge[(*rows_of(side, t), slice(None))],
        lambda side, t: pick(columns[0], material_y[(*rows_of(side, t), slice(None))]),
    )
    pack(g, water_out, bricks_out, params, edges, row_first, row_last, col_first, col_last, True)


def first_water_kernel(
    g, pressure, row_first, row_last, bricks, columns, state, material, water_out, first_same, last_same, hb_water, hk_water, press
):
    nx, ny = g.nx, g.ny
    zero_press_pads(g, press)

    @pl.loop(0, nx // 2)
    def _(turn):
        results = []
        for x in (2 * turn, 2 * turn + 1):
            for t in range(g.ytiles):
                own = x * ny + SUB * t
                index = material[x, pl.ds(SUB * t, SUB), :]
                results.append((x, t, own, pick(columns[0], index), pick(columns[1], index), pressure[aligned(own), :]))
        for x, t, own, hb, hk, value in results:
            hb_water[aligned(own), :] = hb
            hk_water[aligned(own), :] = hk
            press[x + 1, pl.ds(PAD + SUB * t, SUB), :] = value

    water_velocity(
        g,
        (nx // 2, lambda turn: 2 * turn),
        water_out,
        press,
        lambda t, x: bricks[ZZ * g.across + t, pl.ds(x, 1), :],
        lambda x, t: hb_water[aligned(x * ny + SUB * t), :],
        lambda k, x, t: state[k, x, pl.ds(SUB * t, SUB), :],
    )


def edge_water_kernel(
    g, same, row_first, row_last, water, press, stress, hb_water, ux, uy, water_out, first_same, last_same
):
    nx, ny, plane = g.nx, g.ny, g.plane

    def load_u(k, x, t):
        if k == 1:
            layer = x - (x // (nx - SUB)) * (nx - 2 * SUB) + 1
            return ux[aligned(layer * ny + SUB * t), :]
        if k == 2:
            return uy[aligned(x * (ny + 2 * PAD) + PAD + SUB * t), :]
        return water[aligned(3 * plane + x * ny + SUB * t), :]

    water_velocity(
        g,
        (SUB, lambda turn: 2 * turn + (turn // (SUB // 2)) * (nx - 2 * SUB)),
        water_out,
        press,
        lambda t, x: stress[(ZZ - XX) * g.across + t, pl.ds(PAD + x, 1), :],
        lambda x, t: hb_water[aligned(x * ny + SUB * t), :],
        load_u,
    )


def slots_of(g, array, ti):
    slot = g.slot(ti, 0)
    return array.at[pl.ds(slot, 2), :, pl.ds((ti % g.per) * SUB, SUB), :]


class Refs:
    def __init__(self, refs):
        self.refs = list(refs)

    def take(self, count):
        taken, self.refs = self.refs[:count], self.refs[count:]
        return taken


def inner_kernel(g, first, last, *refs):
    refs = Refs(refs)
    water, bricks, memory, params, hb_water, hk_water, col_before, col_after = refs.take(8)
    if not first:
        (const_in,) = refs.take(1)
    uy, speed = refs.take(2)
    if last:
        water_hbm, motion_hbm, memory_hbm = refs.take(3)
    else:
        water_out, press, stress, bricks_out, memory_out = refs.take(5)
    if first:
        (const_out,) = refs.take(1)
    if last:
        press_buf, uy_buf, motion_buf, memory_buf, sems = refs.take(5)

    nx, ny, edge, across, plane = g.nx, g.ny, g.edge, g.across, g.plane
    wide = across + 2
    lane = lane_ids()
    top_pick = surface_pick() * edge + (edge - 1)
    py = ny + 2 * PAD
    low, high = SUB, nx - SUB
    copies = []

    def send(source, target):
        copies.append(pltpu.make_async_copy(source, target, sems.at[len(copies)]))
        copies[-1].start()

    def part(component, start, stop):
        return pl.ds(component * plane + start * ny, (stop - start) * ny)

    if last:
        send(water.at[part(3, 0, nx), :], water_hbm.at[part(3, 0, nx), :])
        send(water.at[part(1, 1, nx - 1), :], water_hbm.at[part(1, 1, nx - 1), :])
    else:
        zero_press_pads(g, press)
        zero_stress_pads(g, stress)

    @pl.loop(0, nx)
    def _(x):
        for t in range(g.ytiles):
            own = x * ny + SUB * t
            uy[aligned(x * py + PAD + SUB * t), :] = water[aligned(2 * plane + own), :]
            if last:
                uy_buf[aligned(own), :] = water[aligned(2 * plane + own), :]

    for side, (ref, y, halo, sign) in enumerate(((col_before, 0, -1, 1.0), (col_after, ny - 1, ny, -1.0))):
        for t in range(g.xtiles):
            own = pl.ds(SUB * t * ny + y, SUB, stride=ny)
            here = pl.ds(SUB * t * py + PAD + y, SUB, stride=py)
            place = pl.ds(32 * side + SUB * t, SUB)
            if first:
                theirs = ref[pl.ds(COL_CONST + SUB * t, SUB), :]
                const_out[place, :] = theirs
            else:
                theirs = const_in[place, :]
            value = uy[here, :] + sign * hb_water[own, :] * ref[pl.ds(M_P + SUB * t, SUB), :]
            uy[here, :] = value
            if last:
                uy_buf[own, :] = value
            uy[pl.ds(SUB * t * py + PAD + halo, SUB, stride=py), :] = (
                ref[pl.ds(M_U + SUB * t, SUB), :] - sign * theirs * water[own, :]
            )
    if last:
        send(uy_buf, water_hbm.at[part(2, 0, nx), :])

    for field in (VX, VY, VZ):
        for tj in range(across):
            for ti in range(g.xtiles):
                speed[field * wide + 1 + tj, pl.ds(PAD + SUB * ti, SUB), :] = bricks[field * across + tj, pl.ds(SUB * ti, SUB), :]
    for ref, tj, halo, sign in ((col_before, 0, 0, 1.0), (col_after, across - 1, wide - 1, -1.0)):
        near = 0 if tj == 0 else LANES - edge
        far = LANES - edge - near
        inside = (lane >= near) & (lane < near + edge)
        for ti in range(g.xtiles):
            column = ref[pl.ds(M_BRICK + SUB * ti, SUB), :]
            own_hb = jnp.where(inside, sign * params[HB * across + tj, pl.ds(SUB * ti, SUB), :], 0.0)
            their_hb = sign * roll(column, far - 6 * edge)
            here = pl.ds(PAD + SUB * ti, SUB)
            for c in (VX, VY, VZ):
                key = c * wide + 1 + tj
                speed[key, here, :] = bricks[c * across + tj, pl.ds(SUB * ti, SUB), :] - own_hb * roll(column, near - c * edge)
                own = bricks[ALONG_Y[c] * across + tj, pl.ds(SUB * ti, SUB), :]
                speed[c * wide + halo, here, :] = roll(column, far - (3 + c) * edge) + their_hb * roll(own, far - near)

    store = store_slots(g, motion_buf, memory_buf) if last else store_planes(g, bricks_out, memory_out, stress)

    @pl.loop(1, g.xtiles - 1)
    def _(ti):
        row = pl.multiple_of(SUB * ti, SUB)
        tops = (
            lambda y: water[pl.ds(plane + row * ny + y, SUB, stride=ny), :],
            lambda y: uy[pl.ds(row * py + PAD + y, SUB, stride=py), :],
            lambda y: water[pl.ds(3 * plane + row * ny + y, SUB, stride=ny), :],
        )
        brick_stress(g, ti, first, bricks, memory, params, speed, tops, store)

    if last:
        for ti in range(1, g.xtiles - 1):
            send(slots_of(g, motion_buf, ti), slots_of(g, motion_hbm, ti))
            send(slots_of(g, memory_buf, ti), slots_of(g, memory_hbm, ti))

    def layer(x):
        results = []
        for t in range(g.ytiles):
            own = x * ny + SUB * t
            dx = water[aligned(plane + own + ny), :] - water[aligned(plane + own - ny), :]
            results.append(
                (x, t, own, water_stress(g, x, t, dx, water, uy, speed, hk_water, lane, top_pick))
            )
        return results

    @pl.loop(0, (nx - 4) // 2)
    def _(turn):
        for x, t, own, value in layer(2 + 2 * turn) + layer(3 + 2 * turn):
            if last:
                press_buf[aligned(own), :] = value
            else:
                water_out[aligned(own), :] = value
                press[x + 1, pl.ds(PAD + SUB * t, SUB), :] = value

    if last:
        send(press_buf.at[part(0, 2, nx - 2), :], water_hbm.at[part(0, 2, nx - 2), :])
        for copy in copies:
            copy.wait()
    else:
        def load_u(k, x, t):
            if k == 2:
                return uy[aligned(x * py + PAD + SUB * t), :]
            return water[aligned(k * plane + x * ny + SUB * t), :]

        layers = ((high - low) // 2, lambda turn: low + 2 * turn)
        water_velocity(
            g,
            layers,
            water_out,
            press,
            lambda t, x: stress[(ZZ - XX) * across + t, pl.ds(PAD + x, 1), :],
            lambda x, t: hb_water[aligned(x * ny + SUB * t), :],
            load_u,
        )


def water_stress(g, x, t, dx, water, uy, speed, hk_water, lane, top_pick):
    row = x * (g.ny + 2 * PAD) + PAD + SUB * t
    own = x * g.ny + SUB * t
    dy = uy[pl.ds(row + 1, SUB), :] - uy[pl.ds(row - 1, SUB), :]
    surface = jnp.broadcast_to(speed[VZ * (g.across + 2) + 1 + t, pl.ds(PAD + x, 1), :], (SUB, LANES))
    dz = water_z(g, water[aligned(3 * g.plane + own), :], pick(surface, top_pick), lane)
    return water[aligned(own), :] - hk_water[aligned(own), :] * (dx + dy + dz)


def edge_kernel(g, first, last, *refs):
    refs = Refs(refs)
    water, bricks, memory, params, hb_water, hk_water, col_before, col_after, row_before, row_after = refs.take(10)
    if not first:
        (const_in,) = refs.take(1)
    (uy,) = refs.take(1)
    refs.take(4 if last else 6)
    (speed,) = refs.take(1)
    if last:
        water_hbm, motion_hbm, memory_hbm = refs.take(3)
    else:
        water_out, press, stress, bricks_out, memory_out = refs.take(5)
        sends = refs.take(4)
    (ux,) = refs.take(1)
    if first:
        (const_out,) = refs.take(1)
    if last:
        press_buf, motion_buf, memory_buf, sems = refs.take(4)

    nx, ny, edge, across, plane = g.nx, g.ny, g.edge, g.across, g.plane
    wide = across + 2
    lane = lane_ids()
    top_pick = surface_pick() * edge + (edge - 1)
    py = ny + 2 * PAD
    copies = []

    def send(source, target):
        copies.append(pltpu.make_async_copy(source, target, sems.at[len(copies)]))
        copies[-1].start()

    @pl.loop(0, SUB)
    def _(x):
        for t in range(g.ytiles):
            own = x * ny + SUB * t
            ux[aligned(ny + own), :] = water[aligned(plane + own), :]
            ux[aligned((1 + SUB) * ny + own), :] = water[aligned(plane + (nx - SUB) * ny + own), :]

    sides = ((row_before, 0, -1, 1.0, 1, 0), (row_after, nx - 1, nx, -1.0, 2 * SUB, 2 * SUB + 1))
    for side, (ref, x, halo, sign, own_layer, halo_layer) in enumerate(sides):
        for t in range(g.ytiles):
            own = pl.ds(x * ny + SUB * t, SUB)
            place = pl.ds(32 * side + SUB * t, SUB)
            if first:
                theirs = ref[pl.ds(ROW_CONST + SUB * t, SUB), :]
                const_out[place, :] = theirs
            else:
                theirs = const_in[place, :]
            here = pl.ds(own_layer * ny + SUB * t, SUB)
            ux[here, :] = ux[here, :] + sign * hb_water[own, :] * ref[pl.ds(M_P + SUB * t, SUB), :]
            ux[pl.ds(halo_layer * ny + SUB * t, SUB), :] = ref[pl.ds(M_U + SUB * t, SUB), :] - sign * theirs * water[own, :]
    if last:
        for layer, x in ((1, 0), (2 * SUB, nx - 1)):
            send(ux.at[pl.ds(layer * ny, ny), :], water_hbm.at[pl.ds(plane + x * ny, ny), :])

    for ref, x, halo, sign, _, _ in sides:
        for tj in range(across):
            block = M_BRICK + SUB * tj
            own_hb = sign * params[HB * across + tj, pl.ds(x, 1), :]
            their_hb = sign * ref[pl.ds(block + 6, 1), :]
            for c in (VX, VY, VZ):
                here = pl.ds(PAD + x, 1)
                key = c * wide + 1 + tj
                speed[key, here, :] = speed[key, here, :] - own_hb * ref[pl.ds(block + c, 1), :]
                speed[key, pl.ds(PAD + halo, 1), :] = (
                    ref[pl.ds(block + 3 + c, 1), :] + their_hb * bricks[ALONG_X[c] * across + tj, pl.ds(x, 1), :]
                )
        edge_row = SUB - 1 if x == 0 else 0
        beside_row = SUB - 2 if x == 0 else 1
        for k, (col_ref, tj, col_halo, col_sign) in enumerate(((col_before, 0, 0, 1.0), (col_after, across - 1, wide - 1, -1.0))):
            near = 0 if tj == 0 else LANES - edge
            far = LANES - edge - near
            inside = (lane[0:1, :] >= near) & (lane[0:1, :] < near + edge)
            corner = ref[pl.ds(M_CORNER + SUB * k + edge_row, 1), :]
            beside = ref[pl.ds(M_CORNER + SUB * k + beside_row, 1), :]
            across_y = [roll_row(corner, near - c * edge) for c in range(3)]
            across_x = (roll_row(corner, far - 7 * edge), roll_row(corner, far), roll_row(beside, far - 7 * edge))
            row_hb = jnp.where(inside, col_sign * ref[pl.ds(M_BRICK + SUB * tj + 6, 1), :], 0.0)
            col_hb = sign * roll_row(col_ref[pl.ds(M_BRICK + x, 1), :], far - 6 * edge)
            for c in (VX, VY, VZ):
                key, here = c * wide + 1 + tj, pl.ds(PAD + halo, 1)
                speed[key, here, :] = speed[key, here, :] - row_hb * across_y[c]
                key, here = c * wide + col_halo, pl.ds(PAD + x, 1)
                speed[key, here, :] = speed[key, here, :] - col_hb * across_x[c]

    store = store_slots(g, motion_buf, memory_buf) if last else store_planes(g, bricks_out, memory_out, stress)

    @pl.loop(0, 2)
    def _(turn):
        ti = turn * (g.xtiles - 1)
        row = pl.multiple_of(SUB * ti, SUB)
        above = pl.multiple_of((1 + SUB * turn) * ny, SUB)
        tops = (
            lambda y: ux[pl.ds(above + y, SUB, stride=ny), :],
            lambda y: uy[pl.ds(row * py + PAD + y, SUB, stride=py), :],
            lambda y: water[pl.ds(3 * plane + row * ny + y, SUB, stride=ny), :],
        )
        brick_stress(g, ti, first, bricks, memory, params, speed, tops, store)

    if last:
        for ti in (0, g.xtiles - 1):
            send(slots_of(g, motion_buf, ti), slots_of(g, motion_hbm, ti))
            send(slots_of(g, memory_buf, ti), slots_of(g, memory_hbm, ti))

    for pair, (x, layer) in enumerate(((0, 1), (nx - 2, 2 * SUB - 1))):
        for step in range(2):
            for t in range(g.ytiles):
                dx = (
                    ux[pl.ds((layer + step + 1) * ny + SUB * t, SUB), :] - ux[pl.ds((layer + step - 1) * ny + SUB * t, SUB), :]
                )
                value = water_stress(g, x + step, t, dx, water, uy, speed, hk_water, lane, top_pick)
                if last:
                    press_buf[pl.ds((2 * pair + step) * ny + SUB * t, SUB), :] = value
                else:
                    water_out[pl.ds((x + step) * ny + SUB * t, SUB), :] = value
                    press[x + step + 1, pl.ds(PAD + SUB * t, SUB), :] = value

    if last:
        for pair, x in enumerate((0, nx - 2)):
            send(press_buf.at[pl.ds(2 * pair * ny, 2 * ny), :], water_hbm.at[pl.ds(x * ny, 2 * ny), :])
        for copy in copies:
            copy.wait()
    else:
        def load_v(field, ti, tj):
            return speed[field * wide + 1 + tj, aligned(PAD + SUB * ti), :]

        def load_hb(ti, tj):
            return params[HB * across + tj, aligned(SUB * ti), :]

        def column(side, t):
            return pl.ds(SUB * t * ny + side * (ny - 1), SUB, stride=ny)

        faces = (
            lambda side, t: ux[pl.ds((1 + side * (2 * SUB - 1)) * ny + SUB * t, SUB), :],
            lambda side, t: hb_water[pl.ds(side * (nx - 1) * ny + SUB * t, SUB), :],
            lambda side, t: uy[pl.ds(SUB * t * py + PAD + side * (ny - 1), SUB, stride=py), :],
            lambda side, t: hb_water[column(side, t), :],
        )
        brick_velocity(g, water_out, stress, load_v, bricks_out, load_hb)
        pack(g, water_out, bricks_out, params, faces, *sends, False)


def shift(value, axis, up):
    count = lax.axis_size(axis)
    pairs = [(i, i + 1) for i in range(count - 1)]
    return lax.ppermute(value, axis, pairs if up else [(j, i) for i, j in pairs])


def exchange(g, sends):
    row_first, row_last, col_first, col_last = sends
    col_before = shift(col_last, "col", True)
    col_after = shift(col_first, "col", False)

    def with_corners(message, start):
        start += M_BRICK
        corners = jnp.concatenate([col_before[start : start + SUB], col_after[start : start + SUB]])
        return lax.dynamic_update_slice(message, corners, (M_CORNER, 0))

    row_before = shift(with_corners(row_last, g.nx - SUB), "row", True)
    row_after = shift(with_corners(row_first, 0), "row", False)
    return col_before, col_after, row_before, row_after


def body(
    brick_velocity_stress,
    brick_relaxation_memory,
    brick_cell_material,
    brick_live,
    water_state,
    water_material,
    material_table,
):
    _, nx, ny, nz = water_state.shape
    g = Grid(nx, ny, brick_cell_material.shape[1])
    across, plane = g.across, g.plane

    def f32(*shape):
        return jax.ShapeDtypeStruct(shape, jnp.float32)

    vmem = pl.BlockSpec(memory_space=pltpu.VMEM)
    hbm = pl.BlockSpec(memory_space=pltpu.HBM)
    params = pltpu.CompilerParams(vmem_limit_bytes=24 * 1024 * 1024)
    def messages(first):
        extra = 32 if first else 0
        return [f32(112 + extra, LANES)] * 2 + [f32(96 + extra, LANES)] * 2

    def buffer(*shape):
        return pltpu.VMEM(shape, jnp.float32)

    def held(*values):
        return [pltpu.with_memory_space_constraint(value, pltpu.VMEM) for value in values]

    def pinned(*values):
        return [pltpu.with_memory_space_constraint(value, pltpu.HBM) for value in values]

    press = buffer(nx + 2, ny + 2 * PAD, nz)
    stress = buffer(6 * across, nx + 2 * PAD, LANES)
    work = pl.CostEstimate(flops=20_000_000, bytes_accessed=8_000_000, transcendentals=0)
    water, bricks, coefficients, columns, *sends = pl.pallas_call(
        functools.partial(first_kernel, g),
        out_shape=[
            buffer(4 * plane, nz), f32(9 * across, nx, LANES), f32(9 * across, nx, LANES), f32(8, SUB, LANES),
        ] + messages(True),
        in_specs=[hbm] * 6,
        out_specs=[vmem] * 8,
        scratch_shapes=[
            stress,
            buffer(nx, ny, nz),
            buffer(2, ny, nz),
            buffer(2, nx, SUB, nz),
            pltpu.VMEM((2, ny, nz), jnp.int32),
            pltpu.VMEM((2, nx, SUB, nz), jnp.int32),
            pltpu.VMEM(brick_velocity_stress.shape, jnp.float32),
            pltpu.VMEM(brick_cell_material.shape, jnp.int32),
            pltpu.SMEM(brick_live.shape, jnp.int32),
            pltpu.SMEM(material_table.shape, jnp.float32),
            pltpu.SemaphoreType.DMA((13,)),
        ],
        compiler_params=params,
        name="first_bricks",
    )(*pinned(brick_live, material_table, water_state, water_material, brick_velocity_stress, brick_cell_material))

    def passed(*messages):
        return [buffer(*message.shape) for message in messages]

    water, sends[0], sends[1], hb_water, hk_water = pl.pallas_call(
        functools.partial(first_water_kernel, g),
        out_shape=[buffer(4 * plane, nz)] + passed(*sends[:2]) + [f32(plane, nz), f32(plane, nz)],
        in_specs=[vmem] * 7,
        out_specs=[vmem] * 5,
        input_output_aliases={0: 0, 1: 1, 2: 2},
        scratch_shapes=[press],
        compiler_params=params,
        cost_estimate=work,
        name="first_water",
    )(*held(water, *sends[:2], bricks, columns, water_state, water_material))
    memory = brick_relaxation_memory
    col_const, row_const = (), ()
    uy_shape = (nx * (ny + 2 * PAD), nz)
    speed_shape = (3 * (across + 2), nx + 2 * PAD, LANES)
    ux_buffer = buffer((2 * SUB + 2) * ny, nz)
    slot_buffers = [
        pltpu.VMEM(brick_velocity_stress.shape, jnp.float32),
        pltpu.VMEM(brick_relaxation_memory.shape, jnp.float32),
    ]
    finals = [f32(4 * plane, nz), f32(*brick_velocity_stress.shape), f32(*brick_relaxation_memory.shape)]
    planes = [
        buffer(4 * plane, nz),
        buffer(nx + 2, ny + 2 * PAD, nz),
        buffer(6 * across, nx + 2 * PAD, LANES),
        buffer(9 * across, nx, LANES),
        buffer(18 * across, nx, LANES),
    ]
    for step in range(STEPS):
        first, last = step == 0, step == STEPS - 1
        *columns, row_before, row_after = exchange(g, sends)
        state = (water, bricks, memory, coefficients, hb_water, hk_water)
        shapes = finals if last else planes
        spaces = [hbm if last else vmem] * len(shapes)
        inner = pl.pallas_call(
            functools.partial(inner_kernel, g, first, last),
            out_shape=[buffer(*uy_shape), buffer(*speed_shape)] + shapes + ([buffer(64, LANES)] if first else []),
            in_specs=[vmem] * (8 + len(col_const)),
            out_specs=[vmem] * 2 + spaces + ([vmem] if first else []),
            scratch_shapes=[buffer(plane, nz), buffer(plane, nz)] + slot_buffers + [pltpu.SemaphoreType.DMA((8,))] if last else [],
            compiler_params=params,
            cost_estimate=work,
            name="inner",
        )(*held(*state), *columns, *col_const)
        if first:
            col_const = (inner[-1],)
            inner = inner[:-1]
        uy, *partial = inner
        count = 10 + len(row_const) + 1
        results = pl.pallas_call(
            functools.partial(edge_kernel, g, first, last),
            out_shape=[buffer(*speed_shape)]
            + shapes
            + ([] if last else messages(False) + [ux_buffer])
            + ([buffer(64, LANES)] if first else []),
            in_specs=[vmem] * (count + 1) + spaces,
            out_specs=[vmem] + spaces + [vmem] * (0 if last else 5) + ([vmem] if first else []),
            input_output_aliases={count + k: k for k in range(1 + len(shapes))},
            scratch_shapes=[ux_buffer, buffer(4 * ny, nz)] + slot_buffers + [pltpu.SemaphoreType.DMA((8,))] if last else [],
            compiler_params=params,
            name="edges",
        )(*held(*state), *columns, row_before, row_after, *row_const, *held(uy), *(held(partial[0]) + (list(partial[1:]) if last else held(*partial[1:]))))
        if last:
            return results[2], results[3], results[1].reshape(water_state.shape)
        old_water = water
        _, water, pressed, stressed, bricks, memory = results[:6]
        sends = list(results[6:10])
        if first:
            row_const = (results[11],)
        water, sends[0], sends[1] = pl.pallas_call(
            functools.partial(edge_water_kernel, g),
            out_shape=[buffer(4 * plane, nz)] + passed(*sends[:2]),
            in_specs=[vmem] * 9,
            out_specs=[vmem] * 3,
            input_output_aliases={0: 0, 1: 1, 2: 2},
            compiler_params=params,
            cost_estimate=work,
            name="edge_water",
        )(*held(water, *sends[:2], old_water, pressed, stressed, hb_water, results[10], uy))


def solution(mesh):
    return jax.shard_map(
        body,
        mesh=mesh,
        in_specs=(
            P(("row", "col"), None, None, None),
            P(("row", "col"), None, None, None),
            P(("row", "col"), None, None),
            P(("row", "col")),
            P(None, "row", "col", None),
            P("row", "col", None),
            P(),
        ),
        out_specs=(
            P(("row", "col"), None, None, None),
            P(("row", "col"), None, None, None),
            P(None, "row", "col", None),
        ),
        check_vma=False,
    )
```

```python
import functools

import jax
import jax.numpy as jnp
from jax import lax
from jax.experimental import pallas as pl
from jax.experimental.pallas import tpu as pltpu
from jax.sharding import PartitionSpec as P

STEPS = 3
LANES = 128
SUB = 8
PAD = 8
VX, VY, VZ, XX, YY, ZZ, XY, XZ, YZ = range(9)
HB, LAME, SHEAR, RETAIN, SPRING_LAME, SPRING_SHEAR, ALIVE = 0, 1, 2, 3, 6, 7, 8
ALONG_X = (XX, XY, XZ)
ALONG_Y = (XY, YY, YZ)
ALONG_Z = (XZ, YZ, ZZ)
M_P, M_U, M_BRICK, M_CORNER, M_CONST = 0, 32, 64, 96, 112


def lane_ids():
    return lax.broadcasted_iota(jnp.int32, (SUB, LANES), 1)


def roll(value, shift):
    shift = shift % LANES
    return value if shift == 0 else pltpu.roll(value, shift, 1)


def roll_row(row, shift):
    shift = shift % LANES
    if shift == 0:
        return row
    return pltpu.roll(jnp.broadcast_to(row, (SUB, LANES)), shift, 1)[0:1, :]


def pick(values, indices):
    return jnp.take_along_axis(values, indices, axis=1, mode="promise_in_bounds")


def aligned(start, size=SUB):
    return pl.ds(start if isinstance(start, int) else pl.multiple_of(start, SUB), size)


class Grid:
    def __init__(self, nx, ny, edge):
        self.nx, self.ny, self.edge = nx, ny, edge
        self.plane = nx * ny
        self.across = ny * edge // LANES
        self.yper = LANES // edge
        self.half = self.across // 2
        self.xtiles, self.ytiles = nx // SUB, ny // SUB
        self.per = edge // SUB

    def slot(self, ti, tj):
        return 2 * (ti // self.per) + tj // self.half

    def place(self, ti, tj):
        return aligned((ti % self.per) * SUB), pl.ds((tj % self.half) * LANES, LANES)


def zero_press_pads(g, press):
    zero = jnp.zeros((SUB, LANES), jnp.float32)
    for t in range(g.ytiles):
        press[0, pl.ds(PAD + SUB * t, SUB), :] = zero
        press[g.nx + 1, pl.ds(PAD + SUB * t, SUB), :] = zero

    @pl.loop(1, g.nx + 1)
    def _(x):
        press[x, pl.ds(0, SUB), :] = zero
        press[x, pl.ds(PAD + g.ny, SUB), :] = zero


def zero_stress_pads(g, stress):
    zero = jnp.zeros((SUB, LANES), jnp.float32)
    for field in ALONG_X:
        for tj in range(g.across):
            key = (field - XX) * g.across + tj
            stress[key, pl.ds(0, SUB), :] = zero
            stress[key, pl.ds(PAD + g.nx, SUB), :] = zero


def shifted_top(g, load, ys, lane):
    top = None
    for k, y in enumerate(ys):
        value = roll(load(y), g.edge * k + g.edge - 1)
        top = value if top is None else jnp.where(lane >= g.edge * k, value, top)
    return top


def along_y(g, rolled, tj, lane):
    zero = jnp.zeros((SUB, LANES), jnp.float32)
    after = rolled[tj + 1][1] if tj + 1 < len(rolled) else zero
    before = rolled[tj - 1][0] if tj > 0 else zero
    ahead = jnp.where(lane < LANES - g.edge, rolled[tj][1], after)
    behind = jnp.where(lane >= g.edge, rolled[tj][0], before)
    return ahead - behind


def along_z(g, value, beyond, depth):
    zero = jnp.zeros((SUB, LANES), jnp.float32)
    return jnp.where(depth == g.edge - 1, beyond, roll(value, -1)) - jnp.where(depth == 0, zero, roll(value, 1))


def water_z(g, value, below, lane):
    zero = jnp.zeros((SUB, LANES), jnp.float32)
    return jnp.where(lane == LANES - 1, zero, roll(value, -1)) - jnp.where(lane == 0, below, roll(value, 1))


def surface_pick():
    return lax.broadcasted_iota(jnp.int32, (SUB, LANES), 0)


def water_velocity(g, layers, water_out, press, surface_row, load_hb, load_u):
    lane = lane_ids()
    top_pick = surface_pick() * g.edge + (g.edge - 1)

    def water_layer(x):
        results = []
        for t in range(g.ytiles):
            rows = pl.ds(PAD + SUB * t, SUB)
            here = press[x + 1, rows, :]
            dx = press[x + 2, rows, :] - press[x, rows, :]
            dy = press[x + 1, pl.ds(PAD + SUB * t + 1, SUB), :] - press[x + 1, pl.ds(PAD + SUB * t - 1, SUB), :]
            surface = jnp.broadcast_to(surface_row(t, x), (SUB, LANES))
            dz = water_z(g, here, -pick(surface, top_pick), lane)
            own = x * g.ny + SUB * t
            hb = load_hb(x, t)
            for k, change in ((1, dx), (2, dy), (3, dz)):
                results.append((k * g.plane + own, load_u(k, x, t) - hb * change))
        return results

    turns, layer = layers

    @pl.loop(0, turns)
    def _(turn):
        x = layer(turn)
        for row, value in water_layer(x) + water_layer(x + 1):
            water_out[aligned(row), :] = value


def brick_velocity(g, water_out, stress, load_v, bricks_out, load_hb):
    lane = lane_ids()
    depth = lane % g.edge
    zero = jnp.zeros((SUB, LANES), jnp.float32)
    across, ny = g.across, g.ny

    @pl.loop(0, g.xtiles)
    def _(ti):
        row = pl.multiple_of(SUB * ti, SUB)
        here = pl.ds(pl.multiple_of(row + PAD, SUB), SUB)

        def load(field, tj):
            return stress[(field - XX) * across + tj, here, :]

        def along_x(field, tj):
            key = (field - XX) * across + tj
            return stress[key, pl.ds(row + PAD + 1, SUB), :] - stress[key, pl.ds(row + PAD - 1, SUB), :]

        results = []
        for target, fx, fy, fz in zip((VX, VY, VZ), ALONG_X, ALONG_Y, ALONG_Z):
            rolled = [(roll(value, g.edge), roll(value, -g.edge)) for value in (load(fy, tj) for tj in range(across))]
            for tj in range(across):
                beyond = zero
                if fz == ZZ:
                    ys = [g.yper * tj + k for k in range(g.yper)]
                    beyond = -shifted_top(g, lambda y: water_out[pl.ds(row * ny + y, SUB, stride=ny), :], ys, lane)
                change = along_x(fx, tj) + along_y(g, rolled, tj, lane) + along_z(g, load(fz, tj), beyond, depth)
                results.append((target * across + tj, load_v(target, ti, tj) + load_hb(ti, tj) * change))
        for key, value in results:
            bricks_out[key, pl.ds(row, SUB), :] = value


def brick_stress(g, ti, first, bricks, memory, params, speed, tops, store):
    edge, across = g.edge, g.across
    wide = across + 2
    lane = lane_ids()
    depth = lane % edge
    row = SUB * ti if isinstance(ti, int) else pl.multiple_of(SUB * ti, SUB)
    here, inner = aligned(row), aligned(row + PAD)
    rolled = []
    for field in (VX, VY, VZ):
        values = [speed[field * wide + tj, inner, :] for tj in range(wide)]
        rolled.append([(roll(value, edge), roll(value, -edge)) for value in values])
    for tj in range(across):
        ys = [g.yper * tj + k for k in range(g.yper)]
        dx, dy, dz, speeds = [], [], [], []
        for field in (VX, VY, VZ):
            key = field * wide + 1 + tj
            value = speed[key, inner, :]
            speeds.append(value)
            dx.append(speed[key, pl.ds(row + PAD + 1, SUB), :] - speed[key, pl.ds(row + PAD - 1, SUB), :])
            dy.append(along_y(g, rolled[field], tj + 1, lane))
            dz.append(along_z(g, value, shifted_top(g, tops[field], ys, lane), depth))
        strain = [dx[0], dy[1], dz[2], dy[0] + dx[1], dz[0] + dx[2], dz[1] + dy[2]]
        dilation = strain[0] + strain[1] + strain[2]

        def param(c):
            return params[c * across + tj, here, :]

        lame, shear = param(LAME) * dilation, param(SHEAR)
        spring_lame, spring_shear = param(SPRING_LAME) * dilation, param(SPRING_SHEAR)
        retain = [param(RETAIN + l) for l in range(3)]
        half_shear, half_spring = 0.5 * shear, 0.5 * spring_shear
        slot = g.slot(ti, tj)
        rows, lanes = g.place(ti, tj)
        if first:
            alive = param(ALIVE)
        stresses, memories = [], {}
        for comp in range(6):
            if comp < 3:
                elastic = shear * strain[comp] + lame
                relaxed = spring_shear * strain[comp] + spring_lame
            else:
                elastic = half_shear * strain[comp]
                relaxed = half_spring * strain[comp]
            summed = None
            for l in range(3):
                place = 6 * l + comp
                if first:
                    old = memory[slot, place, rows, lanes] * alive
                else:
                    old = memory[place * across + tj, here, :]
                new = relaxed + retain[l] * (old - relaxed)
                memories[place] = new
                summed = new if summed is None else summed + new
            stresses.append(bricks[(XX + comp) * across + tj, here, :] + elastic - summed)
        store(ti, tj, here, inner, speeds, stresses, memories)


def store_planes(g, bricks_out, memory_out, stress):
    def store(ti, tj, here, inner, speeds, stresses, memories):
        for place, value in memories.items():
            memory_out[place * g.across + tj, here, :] = value
        for comp, value in enumerate(stresses):
            bricks_out[(XX + comp) * g.across + tj, here, :] = value
            stress[comp * g.across + tj, inner, :] = value

    return store


def store_slots(g, motion, memory):
    def store(ti, tj, here, inner, speeds, stresses, memories):
        slot = g.slot(ti, tj)
        rows, lanes = g.place(ti, tj)
        for place, value in memories.items():
            memory[slot, place, rows, lanes] = value
        for field, value in enumerate(speeds + stresses):
            motion[slot, field, rows, lanes] = value

    return store


def route(odd, first, last, out_far, out_near):
    for start in range(0, out_far.shape[0], SUB):
        rows = pl.ds(start, SUB)
        one, other = first[rows, :], last[rows, :]
        out_far[rows, :] = jnp.where(odd, other, one)
        out_near[rows, :] = jnp.where(odd, one, other)


def unroute(odd, from_far, from_near, before, after):
    for start in range(0, from_far.shape[0], SUB):
        rows = pl.ds(start, SUB)
        far, near = from_far[rows, :], from_near[rows, :]
        before[rows, :] = jnp.where(odd, near, far)
        after[rows, :] = jnp.where(odd, far, near)


def pack(g, water, bricks, params, edges, odd, buffers, sends, first):
    row_u, row_hb, col_u, col_hb = edges
    row_first, row_last, col_first, col_last = buffers
    row_odd, col_odd = odd[0] > 0.0, odd[1] > 0.0
    nx, ny, across, edge = g.nx, g.ny, g.across, g.edge
    lane = lane_ids()
    for side, (out, x, inward, sign) in enumerate(((row_first, 0, 1, 1.0), (row_last, nx - 1, nx - 2, -1.0))):
        for t in range(g.ytiles):
            own = x * ny + SUB * t
            hb = row_hb(side, t)
            out[pl.ds(M_P + SUB * t, SUB), :] = water[pl.ds(own, SUB), :]
            out[pl.ds(M_U + SUB * t, SUB), :] = row_u(side, t) - sign * hb * water[pl.ds(inward * ny + SUB * t, SUB), :]
            if first:
                out[pl.ds(M_CONST + SUB * t, SUB), :] = hb
        for tj in range(across):
            block = M_BRICK + SUB * tj
            for k, field in enumerate(ALONG_X + (VX, VY, VZ)):
                out[pl.ds(block + k, 1), :] = bricks[field * across + tj, pl.ds(x, 1), :]
            out[pl.ds(block + 6, 1), :] = params[HB * across + tj, pl.ds(x, 1), :]
            out[pl.ds(block + 7, 1), :] = jnp.zeros((1, LANES), jnp.float32)
        out[pl.ds(M_CORNER, 2 * SUB), :] = jnp.zeros((2 * SUB, LANES), jnp.float32)
    sides = ((col_first, 0, 1, 0, 1.0), (col_last, ny - 1, ny - 2, across - 1, -1.0))
    for side, (out, y, inward, tj, sign) in enumerate(sides):
        for t in range(g.xtiles):
            own = SUB * t * ny + y
            hb = col_hb(side, t)
            out[pl.ds(M_P + SUB * t, SUB), :] = water[pl.ds(own, SUB, stride=ny), :]
            out[pl.ds(M_U + SUB * t, SUB), :] = (
                col_u(side, t) - sign * hb * water[pl.ds(SUB * t * ny + inward, SUB, stride=ny), :]
            )
            if first:
                out[pl.ds(M_CONST + SUB * t, SUB), :] = hb
            rows = pl.ds(SUB * t, SUB)
            pieces = [bricks[field * across + tj, rows, :] for field in ALONG_Y + (VX, VY, VZ)]
            pieces.append(params[HB * across + tj, rows, :])
            beside = (1, 0) if t == 0 else (SUB - 2, SUB - 1)
            shear = bricks[XZ * across + tj, rows, :]
            if t == 0 or t == g.xtiles - 1:
                shear = pltpu.roll(shear, 1 if t == 0 else SUB - 1, 0)
            sub = lax.broadcasted_iota(jnp.int32, (SUB, LANES), 0)
            pieces.append(jnp.where(sub == beside[0], shear, bricks[XX * across + tj, rows, :]))
            packed = None
            for k, value in enumerate(pieces):
                moved = roll(value, edge * (k - y % g.yper))
                packed = moved if packed is None else jnp.where(lane >= edge * k, moved, packed)
            out[pl.ds(M_BRICK + SUB * t, SUB), :] = packed
            if t == 0:
                corner = packed
        out[pl.ds(M_CORNER, SUB), :] = jnp.where(row_odd, packed, corner)
        out[pl.ds(M_CORNER + SUB, SUB), :] = jnp.where(row_odd, corner, packed)
    route(row_odd, row_first, row_last, *sends[:2])
    route(col_odd, col_first, col_last, *sends[2:])


def first_kernel(
    g, live_hbm, table_hbm, water_hbm, material_hbm, motion_hbm, kinds_hbm, odd,
    water_out, bricks_out, params, columns, row_far, row_near, col_far, col_near,
    stress, pressure, ux_edge, uy_edge, material_x, material_y, motion, kinds, live, table, sems, *buffers,
):
    nx, ny, across = g.nx, g.ny, g.across
    copies = []

    def fetch(source, target):
        copies.append(pltpu.make_async_copy(source, target, sems.at[len(copies)]))
        copies[-1].start()

    fetch(live_hbm, live)
    fetch(table_hbm, table)
    fetch(kinds_hbm, kinds)
    fetch(motion_hbm, motion)
    fetch(water_hbm.at[0], pressure)
    for side, (x, y) in enumerate(((0, 0), (nx - 1, ny - SUB))):
        fetch(water_hbm.at[1, x], ux_edge.at[side])
        fetch(material_hbm.at[x], material_x.at[side])
        fetch(water_hbm.at[2, :, pl.ds(y, SUB), :], uy_edge.at[side])
        fetch(material_hbm.at[:, pl.ds(y, SUB), :], material_y.at[side])
    lane = lane_ids()
    zero_stress_pads(g, stress)
    copies[0].wait()
    copies[1].wait()
    scales = (0.5, 0.5, 1.0, 1.0, 1.0, 1.0, 0.5, 1.0)
    for c, factor in enumerate(scales):
        column = jnp.zeros((SUB, LANES), jnp.float32)
        for level in range(table.shape[0]):
            column = jnp.where(lane == level, table[level, c], column)
        columns[c] = column * factor
    copies[2].wait()
    copies[3].wait()

    @pl.loop(0, g.xtiles)
    def _(ti):
        for tj in range(across):
            slot = g.slot(ti, tj)
            rows, lanes = g.place(ti, tj)
            alive = live[slot].astype(jnp.float32)
            here = aligned(SUB * ti)
            index = kinds[slot, rows, lanes]
            for c in range(8):
                value = pick(columns[c], index)
                params[c * across + tj, here, :] = value if 3 <= c < 6 else value * alive
            params[ALIVE * across + tj, here, :] = jnp.zeros((SUB, LANES), jnp.float32) + alive
            for field in range(XX, YZ + 1):
                value = motion[slot, field, rows, lanes] * alive
                bricks_out[field * across + tj, here, :] = value
                stress[(field - XX) * across + tj, aligned(PAD + SUB * ti), :] = value

    copies[4].wait()

    @pl.loop(0, nx // 2)
    def _(turn):
        results = []
        for x in (2 * turn, 2 * turn + 1):
            for t in range(g.ytiles):
                results.append((x * ny + SUB * t, pressure[x, pl.ds(SUB * t, SUB), :]))
        for own, value in results:
            water_out[aligned(own), :] = value

    def load_v(field, ti, tj):
        slot = g.slot(ti, tj)
        rows, lanes = g.place(ti, tj)
        return motion[slot, field, rows, lanes] * live[slot].astype(jnp.float32)

    def load_hb(ti, tj):
        return params[HB * across + tj, aligned(SUB * ti), :]

    brick_velocity(g, water_out, stress, load_v, bricks_out, load_hb)
    for copy in copies[5:]:
        copy.wait()

    def rows_of(side, t):
        return side, pl.ds(SUB * t, SUB), side * (SUB - 1)

    edges = (
        lambda side, t: ux_edge[side, pl.ds(SUB * t, SUB), :],
        lambda side, t: pick(columns[0], material_x[side, pl.ds(SUB * t, SUB), :]),
        lambda side, t: uy_edge[(*rows_of(side, t), slice(None))],
        lambda side, t: pick(columns[0], material_y[(*rows_of(side, t), slice(None))]),
    )
    pack(g, water_out, bricks_out, params, edges, odd, buffers, (row_far, row_near, col_far, col_near), True)


def first_water_kernel(
    g, pressure, row_first, row_last, bricks, columns, state, material, water_out, first_same, last_same, hb_water, hk_water, press
):
    nx, ny = g.nx, g.ny
    zero_press_pads(g, press)

    @pl.loop(0, nx // 2)
    def _(turn):
        results = []
        for x in (2 * turn, 2 * turn + 1):
            for t in range(g.ytiles):
                own = x * ny + SUB * t
                index = material[x, pl.ds(SUB * t, SUB), :]
                results.append((x, t, own, pick(columns[0], index), pick(columns[1], index), pressure[aligned(own), :]))
        for x, t, own, hb, hk, value in results:
            hb_water[aligned(own), :] = hb
            hk_water[aligned(own), :] = hk
            press[x + 1, pl.ds(PAD + SUB * t, SUB), :] = value

    water_velocity(
        g,
        (nx // 2, lambda turn: 2 * turn),
        water_out,
        press,
        lambda t, x: bricks[ZZ * g.across + t, pl.ds(x, 1), :],
        lambda x, t: hb_water[aligned(x * ny + SUB * t), :],
        lambda k, x, t: state[k, x, pl.ds(SUB * t, SUB), :],
    )


def edge_water_kernel(
    g, same, row_first, row_last, water, press, stress, hb_water, ux, uy, water_out, first_same, last_same
):
    nx, ny, plane = g.nx, g.ny, g.plane

    def load_u(k, x, t):
        if k == 1:
            layer = x - (x // (nx - SUB)) * (nx - 2 * SUB) + 1
            return ux[aligned(layer * ny + SUB * t), :]
        if k == 2:
            return uy[aligned(x * (ny + 2 * PAD) + PAD + SUB * t), :]
        return water[aligned(3 * plane + x * ny + SUB * t), :]

    water_velocity(
        g,
        (SUB, lambda turn: 2 * turn + (turn // (SUB // 2)) * (nx - 2 * SUB)),
        water_out,
        press,
        lambda t, x: stress[(ZZ - XX) * g.across + t, pl.ds(PAD + x, 1), :],
        lambda x, t: hb_water[aligned(x * ny + SUB * t), :],
        load_u,
    )


def slots_of(g, array, ti):
    slot = g.slot(ti, 0)
    return array.at[pl.ds(slot, 2), :, pl.ds((ti % g.per) * SUB, SUB), :]


class Refs:
    def __init__(self, refs):
        self.refs = list(refs)

    def take(self, count):
        taken, self.refs = self.refs[:count], self.refs[count:]
        return taken


def inner_kernel(g, first, last, *refs):
    refs = Refs(refs)
    water, bricks, memory, params, hb_water, hk_water, odd, col_far, col_near = refs.take(9)
    if not first:
        (const_in,) = refs.take(1)
    uy, speed = refs.take(2)
    if last:
        water_hbm, motion_hbm, memory_hbm = refs.take(3)
    else:
        water_out, press, stress, bricks_out, memory_out = refs.take(5)
    if first:
        (const_out,) = refs.take(1)
    col_before, col_after = refs.take(2)
    if last:
        press_buf, uy_buf, motion_buf, memory_buf, sems = refs.take(5)
    unroute(odd[1] > 0.0, col_far, col_near, col_before, col_after)

    nx, ny, edge, across, plane = g.nx, g.ny, g.edge, g.across, g.plane
    wide = across + 2
    lane = lane_ids()
    top_pick = surface_pick() * edge + (edge - 1)
    py = ny + 2 * PAD
    low, high = SUB, nx - SUB
    copies = []

    def send(source, target):
        copies.append(pltpu.make_async_copy(source, target, sems.at[len(copies)]))
        copies[-1].start()

    def part(component, start, stop):
        return pl.ds(component * plane + start * ny, (stop - start) * ny)

    if last:
        send(water.at[part(3, 0, nx), :], water_hbm.at[part(3, 0, nx), :])
        send(water.at[part(1, 1, nx - 1), :], water_hbm.at[part(1, 1, nx - 1), :])
    else:
        zero_press_pads(g, press)
        zero_stress_pads(g, stress)

    @pl.loop(0, nx)
    def _(x):
        for t in range(g.ytiles):
            own = x * ny + SUB * t
            uy[aligned(x * py + PAD + SUB * t), :] = water[aligned(2 * plane + own), :]
            if last:
                uy_buf[aligned(own), :] = water[aligned(2 * plane + own), :]

    for side, (ref, y, halo, sign) in enumerate(((col_before, 0, -1, 1.0), (col_after, ny - 1, ny, -1.0))):
        for t in range(g.xtiles):
            own = pl.ds(SUB * t * ny + y, SUB, stride=ny)
            here = pl.ds(SUB * t * py + PAD + y, SUB, stride=py)
            place = pl.ds(32 * side + SUB * t, SUB)
            if first:
                theirs = ref[pl.ds(M_CONST + SUB * t, SUB), :]
                const_out[place, :] = theirs
            else:
                theirs = const_in[place, :]
            value = uy[here, :] + sign * hb_water[own, :] * ref[pl.ds(M_P + SUB * t, SUB), :]
            uy[here, :] = value
            if last:
                uy_buf[own, :] = value
            uy[pl.ds(SUB * t * py + PAD + halo, SUB, stride=py), :] = (
                ref[pl.ds(M_U + SUB * t, SUB), :] - sign * theirs * water[own, :]
            )
    if last:
        send(uy_buf, water_hbm.at[part(2, 0, nx), :])

    for field in (VX, VY, VZ):
        for tj in range(across):
            for ti in range(g.xtiles):
                speed[field * wide + 1 + tj, pl.ds(PAD + SUB * ti, SUB), :] = bricks[field * across + tj, pl.ds(SUB * ti, SUB), :]
    for ref, tj, halo, sign in ((col_before, 0, 0, 1.0), (col_after, across - 1, wide - 1, -1.0)):
        near = 0 if tj == 0 else LANES - edge
        far = LANES - edge - near
        inside = (lane >= near) & (lane < near + edge)
        for ti in range(g.xtiles):
            column = ref[pl.ds(M_BRICK + SUB * ti, SUB), :]
            own_hb = jnp.where(inside, sign * params[HB * across + tj, pl.ds(SUB * ti, SUB), :], 0.0)
            their_hb = sign * roll(column, far - 6 * edge)
            here = pl.ds(PAD + SUB * ti, SUB)
            for c in (VX, VY, VZ):
                key = c * wide + 1 + tj
                speed[key, here, :] = bricks[c * across + tj, pl.ds(SUB * ti, SUB), :] - own_hb * roll(column, near - c * edge)
                own = bricks[ALONG_Y[c] * across + tj, pl.ds(SUB * ti, SUB), :]
                speed[c * wide + halo, here, :] = roll(column, far - (3 + c) * edge) + their_hb * roll(own, far - near)

    store = store_slots(g, motion_buf, memory_buf) if last else store_planes(g, bricks_out, memory_out, stress)

    @pl.loop(1, g.xtiles - 1)
    def _(ti):
        row = pl.multiple_of(SUB * ti, SUB)
        tops = (
            lambda y: water[pl.ds(plane + row * ny + y, SUB, stride=ny), :],
            lambda y: uy[pl.ds(row * py + PAD + y, SUB, stride=py), :],
            lambda y: water[pl.ds(3 * plane + row * ny + y, SUB, stride=ny), :],
        )
        brick_stress(g, ti, first, bricks, memory, params, speed, tops, store)

    if last:
        for ti in range(1, g.xtiles - 1):
            send(slots_of(g, motion_buf, ti), slots_of(g, motion_hbm, ti))
            send(slots_of(g, memory_buf, ti), slots_of(g, memory_hbm, ti))

    def layer(x):
        results = []
        for t in range(g.ytiles):
            own = x * ny + SUB * t
            dx = water[aligned(plane + own + ny), :] - water[aligned(plane + own - ny), :]
            results.append(
                (x, t, own, water_stress(g, x, t, dx, water, uy, speed, hk_water, lane, top_pick))
            )
        return results

    @pl.loop(0, (nx - 4) // 2)
    def _(turn):
        for x, t, own, value in layer(2 + 2 * turn) + layer(3 + 2 * turn):
            if last:
                press_buf[aligned(own), :] = value
            else:
                water_out[aligned(own), :] = value
                press[x + 1, pl.ds(PAD + SUB * t, SUB), :] = value

    if last:
        send(press_buf.at[part(0, 2, nx - 2), :], water_hbm.at[part(0, 2, nx - 2), :])
        for copy in copies:
            copy.wait()
    else:
        def load_u(k, x, t):
            if k == 2:
                return uy[aligned(x * py + PAD + SUB * t), :]
            return water[aligned(k * plane + x * ny + SUB * t), :]

        layers = ((high - low) // 2, lambda turn: low + 2 * turn)
        water_velocity(
            g,
            layers,
            water_out,
            press,
            lambda t, x: stress[(ZZ - XX) * across + t, pl.ds(PAD + x, 1), :],
            lambda x, t: hb_water[aligned(x * ny + SUB * t), :],
            load_u,
        )


def water_stress(g, x, t, dx, water, uy, speed, hk_water, lane, top_pick):
    row = x * (g.ny + 2 * PAD) + PAD + SUB * t
    own = x * g.ny + SUB * t
    dy = uy[pl.ds(row + 1, SUB), :] - uy[pl.ds(row - 1, SUB), :]
    surface = jnp.broadcast_to(speed[VZ * (g.across + 2) + 1 + t, pl.ds(PAD + x, 1), :], (SUB, LANES))
    dz = water_z(g, water[aligned(3 * g.plane + own), :], pick(surface, top_pick), lane)
    return water[aligned(own), :] - hk_water[aligned(own), :] * (dx + dy + dz)


def edge_kernel(g, first, last, *refs):
    refs = Refs(refs)
    water, bricks, memory, params, hb_water, hk_water, odd, col_far, col_near, row_far, row_near = refs.take(11)
    if not first:
        (const_in,) = refs.take(1)
    (uy,) = refs.take(1)
    refs.take(4 if last else 6)
    (speed,) = refs.take(1)
    if last:
        water_hbm, motion_hbm, memory_hbm = refs.take(3)
    else:
        water_out, press, stress, bricks_out, memory_out = refs.take(5)
        sends = refs.take(4)
    (ux,) = refs.take(1)
    if first:
        (const_out,) = refs.take(1)
    col_before, col_after, row_before, row_after = refs.take(4)
    if last:
        press_buf, motion_buf, memory_buf, sems = refs.take(4)
    else:
        buffers = refs.take(4)
    unroute(odd[1] > 0.0, col_far, col_near, col_before, col_after)
    unroute(odd[0] > 0.0, row_far, row_near, row_before, row_after)
    for ref in (row_before, row_after):
        far, near = ref[pl.ds(M_CORNER, SUB), :], ref[pl.ds(M_CORNER + SUB, SUB), :]
        ref[pl.ds(M_CORNER, SUB), :] = jnp.where(odd[1] > 0.0, near, far)
        ref[pl.ds(M_CORNER + SUB, SUB), :] = jnp.where(odd[1] > 0.0, far, near)

    nx, ny, edge, across, plane = g.nx, g.ny, g.edge, g.across, g.plane
    wide = across + 2
    lane = lane_ids()
    top_pick = surface_pick() * edge + (edge - 1)
    py = ny + 2 * PAD
    copies = []

    def send(source, target):
        copies.append(pltpu.make_async_copy(source, target, sems.at[len(copies)]))
        copies[-1].start()

    @pl.loop(0, SUB)
    def _(x):
        for t in range(g.ytiles):
            own = x * ny + SUB * t
            ux[aligned(ny + own), :] = water[aligned(plane + own), :]
            ux[aligned((1 + SUB) * ny + own), :] = water[aligned(plane + (nx - SUB) * ny + own), :]

    sides = ((row_before, 0, -1, 1.0, 1, 0), (row_after, nx - 1, nx, -1.0, 2 * SUB, 2 * SUB + 1))
    for side, (ref, x, halo, sign, own_layer, halo_layer) in enumerate(sides):
        for t in range(g.ytiles):
            own = pl.ds(x * ny + SUB * t, SUB)
            place = pl.ds(32 * side + SUB * t, SUB)
            if first:
                theirs = ref[pl.ds(M_CONST + SUB * t, SUB), :]
                const_out[place, :] = theirs
            else:
                theirs = const_in[place, :]
            here = pl.ds(own_layer * ny + SUB * t, SUB)
            ux[here, :] = ux[here, :] + sign * hb_water[own, :] * ref[pl.ds(M_P + SUB * t, SUB), :]
            ux[pl.ds(halo_layer * ny + SUB * t, SUB), :] = ref[pl.ds(M_U + SUB * t, SUB), :] - sign * theirs * water[own, :]
    if last:
        for layer, x in ((1, 0), (2 * SUB, nx - 1)):
            send(ux.at[pl.ds(layer * ny, ny), :], water_hbm.at[pl.ds(plane + x * ny, ny), :])

    for ref, x, halo, sign, _, _ in sides:
        for tj in range(across):
            block = M_BRICK + SUB * tj
            own_hb = sign * params[HB * across + tj, pl.ds(x, 1), :]
            their_hb = sign * ref[pl.ds(block + 6, 1), :]
            for c in (VX, VY, VZ):
                here = pl.ds(PAD + x, 1)
                key = c * wide + 1 + tj
                speed[key, here, :] = speed[key, here, :] - own_hb * ref[pl.ds(block + c, 1), :]
                speed[key, pl.ds(PAD + halo, 1), :] = (
                    ref[pl.ds(block + 3 + c, 1), :] + their_hb * bricks[ALONG_X[c] * across + tj, pl.ds(x, 1), :]
                )
        edge_row = SUB - 1 if x == 0 else 0
        beside_row = SUB - 2 if x == 0 else 1
        for k, (col_ref, tj, col_halo, col_sign) in enumerate(((col_before, 0, 0, 1.0), (col_after, across - 1, wide - 1, -1.0))):
            near = 0 if tj == 0 else LANES - edge
            far = LANES - edge - near
            inside = (lane[0:1, :] >= near) & (lane[0:1, :] < near + edge)
            corner = ref[pl.ds(M_CORNER + SUB * k + edge_row, 1), :]
            beside = ref[pl.ds(M_CORNER + SUB * k + beside_row, 1), :]
            across_y = [roll_row(corner, near - c * edge) for c in range(3)]
            across_x = (roll_row(corner, far - 7 * edge), roll_row(corner, far), roll_row(beside, far - 7 * edge))
            row_hb = jnp.where(inside, col_sign * ref[pl.ds(M_BRICK + SUB * tj + 6, 1), :], 0.0)
            col_hb = sign * roll_row(col_ref[pl.ds(M_BRICK + x, 1), :], far - 6 * edge)
            for c in (VX, VY, VZ):
                key, here = c * wide + 1 + tj, pl.ds(PAD + halo, 1)
                speed[key, here, :] = speed[key, here, :] - row_hb * across_y[c]
                key, here = c * wide + col_halo, pl.ds(PAD + x, 1)
                speed[key, here, :] = speed[key, here, :] - col_hb * across_x[c]

    store = store_slots(g, motion_buf, memory_buf) if last else store_planes(g, bricks_out, memory_out, stress)

    @pl.loop(0, 2)
    def _(turn):
        ti = turn * (g.xtiles - 1)
        row = pl.multiple_of(SUB * ti, SUB)
        above = pl.multiple_of((1 + SUB * turn) * ny, SUB)
        tops = (
            lambda y: ux[pl.ds(above + y, SUB, stride=ny), :],
            lambda y: uy[pl.ds(row * py + PAD + y, SUB, stride=py), :],
            lambda y: water[pl.ds(3 * plane + row * ny + y, SUB, stride=ny), :],
        )
        brick_stress(g, ti, first, bricks, memory, params, speed, tops, store)

    if last:
        for ti in (0, g.xtiles - 1):
            send(slots_of(g, motion_buf, ti), slots_of(g, motion_hbm, ti))
            send(slots_of(g, memory_buf, ti), slots_of(g, memory_hbm, ti))

    for pair, (x, layer) in enumerate(((0, 1), (nx - 2, 2 * SUB - 1))):
        for step in range(2):
            for t in range(g.ytiles):
                dx = (
                    ux[pl.ds((layer + step + 1) * ny + SUB * t, SUB), :] - ux[pl.ds((layer + step - 1) * ny + SUB * t, SUB), :]
                )
                value = water_stress(g, x + step, t, dx, water, uy, speed, hk_water, lane, top_pick)
                if last:
                    press_buf[pl.ds((2 * pair + step) * ny + SUB * t, SUB), :] = value
                else:
                    water_out[pl.ds((x + step) * ny + SUB * t, SUB), :] = value
                    press[x + step + 1, pl.ds(PAD + SUB * t, SUB), :] = value

    if last:
        for pair, x in enumerate((0, nx - 2)):
            send(press_buf.at[pl.ds(2 * pair * ny, 2 * ny), :], water_hbm.at[pl.ds(x * ny, 2 * ny), :])
        for copy in copies:
            copy.wait()
    else:
        def load_v(field, ti, tj):
            return speed[field * wide + 1 + tj, aligned(PAD + SUB * ti), :]

        def load_hb(ti, tj):
            return params[HB * across + tj, aligned(SUB * ti), :]

        def column(side, t):
            return pl.ds(SUB * t * ny + side * (ny - 1), SUB, stride=ny)

        faces = (
            lambda side, t: ux[pl.ds((1 + side * (2 * SUB - 1)) * ny + SUB * t, SUB), :],
            lambda side, t: hb_water[pl.ds(side * (nx - 1) * ny + SUB * t, SUB), :],
            lambda side, t: uy[pl.ds(SUB * t * py + PAD + side * (ny - 1), SUB, stride=py), :],
            lambda side, t: hb_water[column(side, t), :],
        )
        brick_velocity(g, water_out, stress, load_v, bricks_out, load_hb)
        pack(g, water_out, bricks_out, params, faces, odd, buffers, sends, False)


def swap(value, axis, start):
    pairs = [(i, i + 1) for i in range(start, lax.axis_size(axis) - 1, 2)]
    return lax.ppermute(value, axis, pairs + [(j, i) for i, j in pairs])


def exchange(sends):
    row_far, row_near, col_far, col_near = sends
    col_far = swap(col_far, "col", 1)
    col_near = swap(col_near, "col", 0)

    def with_corners(message, start):
        corners = jnp.concatenate([col_far[start : start + SUB], col_near[start : start + SUB]])
        return lax.dynamic_update_slice(message, corners, (M_CORNER, 0))

    row_far = swap(with_corners(row_far, M_CORNER), "row", 1)
    row_near = swap(with_corners(row_near, M_CORNER + SUB), "row", 0)
    return col_far, col_near, row_far, row_near


def body(
    brick_velocity_stress,
    brick_relaxation_memory,
    brick_cell_material,
    brick_live,
    water_state,
    water_material,
    material_table,
):
    _, nx, ny, nz = water_state.shape
    g = Grid(nx, ny, brick_cell_material.shape[1])
    across, plane = g.across, g.plane

    def f32(*shape):
        return jax.ShapeDtypeStruct(shape, jnp.float32)

    vmem = pl.BlockSpec(memory_space=pltpu.VMEM)
    hbm = pl.BlockSpec(memory_space=pltpu.HBM)
    params = pltpu.CompilerParams(vmem_limit_bytes=24 * 1024 * 1024)
    def messages(first):
        return [f32(M_CONST + (32 if first else 0), LANES)] * 4

    def buffer(*shape):
        return pltpu.VMEM(shape, jnp.float32)

    def held(*values):
        return [pltpu.with_memory_space_constraint(value, pltpu.VMEM) for value in values]

    def pinned(*values):
        return [pltpu.with_memory_space_constraint(value, pltpu.HBM) for value in values]

    def message_buffers(count, first):
        return [buffer(M_CONST + (32 if first else 0), LANES)] * count

    odd = jnp.stack([lax.axis_index(axis) & 1 for axis in ("row", "col")]).astype(jnp.float32)
    odd = jnp.broadcast_to(odd[:, None, None], (2, SUB, LANES))
    press = buffer(nx + 2, ny + 2 * PAD, nz)
    stress = buffer(6 * across, nx + 2 * PAD, LANES)
    work = pl.CostEstimate(flops=20_000_000, bytes_accessed=8_000_000, transcendentals=0)
    water, bricks, coefficients, columns, *sends = pl.pallas_call(
        functools.partial(first_kernel, g),
        out_shape=[
            buffer(4 * plane, nz), f32(9 * across, nx, LANES), f32(9 * across, nx, LANES), f32(8, SUB, LANES),
        ] + messages(True),
        in_specs=[hbm] * 6 + [vmem],
        out_specs=[vmem] * 8,
        scratch_shapes=[
            stress,
            buffer(nx, ny, nz),
            buffer(2, ny, nz),
            buffer(2, nx, SUB, nz),
            pltpu.VMEM((2, ny, nz), jnp.int32),
            pltpu.VMEM((2, nx, SUB, nz), jnp.int32),
            pltpu.VMEM(brick_velocity_stress.shape, jnp.float32),
            pltpu.VMEM(brick_cell_material.shape, jnp.int32),
            pltpu.SMEM(brick_live.shape, jnp.int32),
            pltpu.SMEM(material_table.shape, jnp.float32),
            pltpu.SemaphoreType.DMA((13,)),
        ]
        + message_buffers(4, True),
        compiler_params=params,
        name="first_bricks",
    )(*pinned(brick_live, material_table, water_state, water_material, brick_velocity_stress, brick_cell_material), odd)

    def passed(*messages):
        return [buffer(*message.shape) for message in messages]

    water, sends[0], sends[1], hb_water, hk_water = pl.pallas_call(
        functools.partial(first_water_kernel, g),
        out_shape=[buffer(4 * plane, nz)] + passed(*sends[:2]) + [f32(plane, nz), f32(plane, nz)],
        in_specs=[vmem] * 7,
        out_specs=[vmem] * 5,
        input_output_aliases={0: 0, 1: 1, 2: 2},
        scratch_shapes=[press],
        compiler_params=params,
        cost_estimate=work,
        name="first_water",
    )(*held(water, *sends[:2], bricks, columns, water_state, water_material))
    memory = brick_relaxation_memory
    col_const, row_const = (), ()
    uy_shape = (nx * (ny + 2 * PAD), nz)
    speed_shape = (3 * (across + 2), nx + 2 * PAD, LANES)
    ux_buffer = buffer((2 * SUB + 2) * ny, nz)
    slot_buffers = [
        pltpu.VMEM(brick_velocity_stress.shape, jnp.float32),
        pltpu.VMEM(brick_relaxation_memory.shape, jnp.float32),
    ]
    finals = [f32(4 * plane, nz), f32(*brick_velocity_stress.shape), f32(*brick_relaxation_memory.shape)]
    planes = [
        buffer(4 * plane, nz),
        buffer(nx + 2, ny + 2 * PAD, nz),
        buffer(6 * across, nx + 2 * PAD, LANES),
        buffer(9 * across, nx, LANES),
        buffer(18 * across, nx, LANES),
    ]
    for step in range(STEPS):
        first, last = step == 0, step == STEPS - 1
        *columns, row_far, row_near = exchange(sends)
        state = (water, bricks, memory, coefficients, hb_water, hk_water, odd)
        shapes = finals if last else planes
        spaces = [hbm if last else vmem] * len(shapes)
        inner = pl.pallas_call(
            functools.partial(inner_kernel, g, first, last),
            out_shape=[buffer(*uy_shape), buffer(*speed_shape)] + shapes + ([buffer(64, LANES)] if first else []),
            in_specs=[vmem] * (9 + len(col_const)),
            out_specs=[vmem] * 2 + spaces + ([vmem] if first else []),
            scratch_shapes=message_buffers(2, first)
            + ([buffer(plane, nz), buffer(plane, nz)] + slot_buffers + [pltpu.SemaphoreType.DMA((8,))] if last else []),
            compiler_params=params,
            cost_estimate=work,
            name="inner",
        )(*held(*state), *columns, *col_const)
        if first:
            col_const = (inner[-1],)
            inner = inner[:-1]
        uy, *partial = inner
        count = 11 + len(row_const) + 1
        results = pl.pallas_call(
            functools.partial(edge_kernel, g, first, last),
            out_shape=[buffer(*speed_shape)]
            + shapes
            + ([] if last else messages(False) + [ux_buffer])
            + ([buffer(64, LANES)] if first else []),
            in_specs=[vmem] * (count + 1) + spaces,
            out_specs=[vmem] + spaces + [vmem] * (0 if last else 5) + ([vmem] if first else []),
            input_output_aliases={count + k: k for k in range(1 + len(shapes))},
            scratch_shapes=([ux_buffer] if last else [])
            + message_buffers(4, first)
            + (
                [buffer(4 * ny, nz)] + slot_buffers + [pltpu.SemaphoreType.DMA((8,))]
                if last
                else message_buffers(4, False)
            ),
            compiler_params=params,
            name="edges",
        )(*held(*state), *columns, row_far, row_near, *row_const, *held(uy), *(held(partial[0]) + (list(partial[1:]) if last else held(*partial[1:]))))
        if last:
            return results[2], results[3], results[1].reshape(water_state.shape)
        old_water = water
        _, water, pressed, stressed, bricks, memory = results[:6]
        sends = list(results[6:10])
        if first:
            row_const = (results[11],)
        water, sends[0], sends[1] = pl.pallas_call(
            functools.partial(edge_water_kernel, g),
            out_shape=[buffer(4 * plane, nz)] + passed(*sends[:2]),
            in_specs=[vmem] * 9,
            out_specs=[vmem] * 3,
            input_output_aliases={0: 0, 1: 1, 2: 2},
            compiler_params=params,
            cost_estimate=work,
            name="edge_water",
        )(*held(water, *sends[:2], old_water, pressed, stressed, hb_water, results[10], uy))


def solution(mesh):
    return jax.shard_map(
        body,
        mesh=mesh,
        in_specs=(
            P(("row", "col"), None, None, None),
            P(("row", "col"), None, None, None),
            P(("row", "col"), None, None),
            P(("row", "col")),
            P(None, "row", "col", None),
            P("row", "col", None),
            P(),
        ),
        out_specs=(
            P(("row", "col"), None, None, None),
            P(("row", "col"), None, None, None),
            P(None, "row", "col", None),
        ),
        check_vma=False,
    )
```

```python
import functools

import jax
import jax.numpy as jnp
from jax import lax
from jax.experimental import pallas as pl
from jax.experimental.pallas import tpu as pltpu
from jax.sharding import PartitionSpec as P

STEPS = 3
LANES = 128
SUB = 8
PAD = 8
VX, VY, VZ, XX, YY, ZZ, XY, XZ, YZ = range(9)
HB, LAME, SHEAR, RETAIN, SPRING_LAME, SPRING_SHEAR, ALIVE = 0, 1, 2, 3, 6, 7, 8
ALONG_X = (XX, XY, XZ)
ALONG_Y = (XY, YY, YZ)
ALONG_Z = (XZ, YZ, ZZ)
M_P, M_U, M_BRICK, M_CORNER, M_CONST = 0, 32, 64, 96, 112


def lane_ids():
    return lax.broadcasted_iota(jnp.int32, (SUB, LANES), 1)


def roll(value, shift):
    shift = shift % LANES
    return value if shift == 0 else pltpu.roll(value, shift, 1)


def roll_row(row, shift):
    shift = shift % LANES
    if shift == 0:
        return row
    return pltpu.roll(jnp.broadcast_to(row, (SUB, LANES)), shift, 1)[0:1, :]


def pick(values, indices):
    return jnp.take_along_axis(values, indices, axis=1, mode="promise_in_bounds")


def aligned(start, size=SUB):
    return pl.ds(start if isinstance(start, int) else pl.multiple_of(start, SUB), size)


class Grid:
    def __init__(self, nx, ny, edge):
        self.nx, self.ny, self.edge = nx, ny, edge
        self.plane = nx * ny
        self.across = ny * edge // LANES
        self.yper = LANES // edge
        self.half = self.across // 2
        self.xtiles, self.ytiles = nx // SUB, ny // SUB
        self.per = edge // SUB

    def slot(self, ti, tj):
        return 2 * (ti // self.per) + tj // self.half

    def place(self, ti, tj):
        return aligned((ti % self.per) * SUB), pl.ds((tj % self.half) * LANES, LANES)


def zero_press_pads(g, press):
    zero = jnp.zeros((SUB, LANES), jnp.float32)
    for t in range(g.ytiles):
        press[0, pl.ds(PAD + SUB * t, SUB), :] = zero
        press[g.nx + 1, pl.ds(PAD + SUB * t, SUB), :] = zero

    @pl.loop(1, g.nx + 1)
    def _(x):
        press[x, pl.ds(0, SUB), :] = zero
        press[x, pl.ds(PAD + g.ny, SUB), :] = zero


def zero_stress_pads(g, stress):
    zero = jnp.zeros((SUB, LANES), jnp.float32)
    for field in ALONG_X:
        for tj in range(g.across):
            key = (field - XX) * g.across + tj
            stress[key, pl.ds(0, SUB), :] = zero
            stress[key, pl.ds(PAD + g.nx, SUB), :] = zero


def shifted_top(g, load, ys, lane):
    top = None
    for k, y in enumerate(ys):
        value = roll(load(y), g.edge * k + g.edge - 1)
        top = value if top is None else jnp.where(lane >= g.edge * k, value, top)
    return top


def along_y(g, rolled, tj, lane):
    zero = jnp.zeros((SUB, LANES), jnp.float32)
    after = rolled[tj + 1][1] if tj + 1 < len(rolled) else zero
    before = rolled[tj - 1][0] if tj > 0 else zero
    ahead = jnp.where(lane < LANES - g.edge, rolled[tj][1], after)
    behind = jnp.where(lane >= g.edge, rolled[tj][0], before)
    return ahead - behind


def along_z(g, value, beyond, depth):
    zero = jnp.zeros((SUB, LANES), jnp.float32)
    return jnp.where(depth == g.edge - 1, beyond, roll(value, -1)) - jnp.where(depth == 0, zero, roll(value, 1))


def water_z(g, value, below, lane):
    zero = jnp.zeros((SUB, LANES), jnp.float32)
    return jnp.where(lane == LANES - 1, zero, roll(value, -1)) - jnp.where(lane == 0, below, roll(value, 1))


def surface_pick():
    return lax.broadcasted_iota(jnp.int32, (SUB, LANES), 0)


def water_velocity(g, layers, water_out, press, surface_row, load_hb, load_u):
    lane = lane_ids()
    top_pick = surface_pick() * g.edge + (g.edge - 1)

    def water_layer(x):
        results = []
        for t in range(g.ytiles):
            rows = pl.ds(PAD + SUB * t, SUB)
            here = press[x + 1, rows, :]
            dx = press[x + 2, rows, :] - press[x, rows, :]
            dy = press[x + 1, pl.ds(PAD + SUB * t + 1, SUB), :] - press[x + 1, pl.ds(PAD + SUB * t - 1, SUB), :]
            surface = jnp.broadcast_to(surface_row(t, x), (SUB, LANES))
            dz = water_z(g, here, -pick(surface, top_pick), lane)
            own = x * g.ny + SUB * t
            hb = load_hb(x, t)
            for k, change in ((1, dx), (2, dy), (3, dz)):
                results.append((k * g.plane + own, load_u(k, x, t) - hb * change))
        return results

    turns, layer = layers

    @pl.loop(0, turns)
    def _(turn):
        x = layer(turn)
        for row, value in water_layer(x) + water_layer(x + 1):
            water_out[aligned(row), :] = value


def brick_velocity(g, water_out, stress, load_v, bricks_out, load_hb):
    lane = lane_ids()
    depth = lane % g.edge
    zero = jnp.zeros((SUB, LANES), jnp.float32)
    across, ny = g.across, g.ny

    @pl.loop(0, g.xtiles)
    def _(ti):
        row = pl.multiple_of(SUB * ti, SUB)
        here = pl.ds(pl.multiple_of(row + PAD, SUB), SUB)

        def load(field, tj):
            return stress[(field - XX) * across + tj, here, :]

        def along_x(field, tj):
            key = (field - XX) * across + tj
            return stress[key, pl.ds(row + PAD + 1, SUB), :] - stress[key, pl.ds(row + PAD - 1, SUB), :]

        results = []
        for target, fx, fy, fz in zip((VX, VY, VZ), ALONG_X, ALONG_Y, ALONG_Z):
            rolled = [(roll(value, g.edge), roll(value, -g.edge)) for value in (load(fy, tj) for tj in range(across))]
            for tj in range(across):
                beyond = zero
                if fz == ZZ:
                    ys = [g.yper * tj + k for k in range(g.yper)]
                    beyond = -shifted_top(g, lambda y: water_out[pl.ds(row * ny + y, SUB, stride=ny), :], ys, lane)
                change = along_x(fx, tj) + along_y(g, rolled, tj, lane) + along_z(g, load(fz, tj), beyond, depth)
                results.append((target * across + tj, load_v(target, ti, tj) + load_hb(ti, tj) * change))
        for key, value in results:
            bricks_out[key, pl.ds(row, SUB), :] = value


def brick_stress(g, ti, first, bricks, memory, params, speed, tops, store):
    edge, across = g.edge, g.across
    wide = across + 2
    lane = lane_ids()
    depth = lane % edge
    row = SUB * ti if isinstance(ti, int) else pl.multiple_of(SUB * ti, SUB)
    here, inner = aligned(row), aligned(row + PAD)
    rolled = []
    for field in (VX, VY, VZ):
        values = [speed[field * wide + tj, inner, :] for tj in range(wide)]
        rolled.append([(roll(value, edge), roll(value, -edge)) for value in values])
    for tj in range(across):
        ys = [g.yper * tj + k for k in range(g.yper)]
        dx, dy, dz, speeds = [], [], [], []
        for field in (VX, VY, VZ):
            key = field * wide + 1 + tj
            value = speed[key, inner, :]
            speeds.append(value)
            dx.append(speed[key, pl.ds(row + PAD + 1, SUB), :] - speed[key, pl.ds(row + PAD - 1, SUB), :])
            dy.append(along_y(g, rolled[field], tj + 1, lane))
            dz.append(along_z(g, value, shifted_top(g, tops[field], ys, lane), depth))
        strain = [dx[0], dy[1], dz[2], dy[0] + dx[1], dz[0] + dx[2], dz[1] + dy[2]]
        dilation = strain[0] + strain[1] + strain[2]

        def param(c):
            return params[c * across + tj, here, :]

        lame, shear = param(LAME) * dilation, param(SHEAR)
        spring_lame, spring_shear = param(SPRING_LAME) * dilation, param(SPRING_SHEAR)
        retain = [param(RETAIN + l) for l in range(3)]
        half_shear, half_spring = 0.5 * shear, 0.5 * spring_shear
        slot = g.slot(ti, tj)
        rows, lanes = g.place(ti, tj)
        if first:
            alive = param(ALIVE)
        stresses, memories = [], {}
        for comp in range(6):
            if comp < 3:
                elastic = shear * strain[comp] + lame
                relaxed = spring_shear * strain[comp] + spring_lame
            else:
                elastic = half_shear * strain[comp]
                relaxed = half_spring * strain[comp]
            summed = None
            for l in range(3):
                place = 6 * l + comp
                if first:
                    old = memory[slot, place, rows, lanes] * alive
                else:
                    old = memory[place * across + tj, here, :]
                new = relaxed + retain[l] * (old - relaxed)
                memories[place] = new
                summed = new if summed is None else summed + new
            stresses.append(bricks[(XX + comp) * across + tj, here, :] + elastic - summed)
        store(ti, tj, here, inner, speeds, stresses, memories)


def store_planes(g, bricks_out, memory_out, stress):
    def store(ti, tj, here, inner, speeds, stresses, memories):
        for place, value in memories.items():
            memory_out[place * g.across + tj, here, :] = value
        for comp, value in enumerate(stresses):
            bricks_out[(XX + comp) * g.across + tj, here, :] = value
            stress[comp * g.across + tj, inner, :] = value

    return store


def store_slots(g, motion, memory):
    def store(ti, tj, here, inner, speeds, stresses, memories):
        slot = g.slot(ti, tj)
        rows, lanes = g.place(ti, tj)
        for place, value in memories.items():
            memory[slot, place, rows, lanes] = value
        for field, value in enumerate(speeds + stresses):
            motion[slot, field, rows, lanes] = value

    return store


def route(odd, first, last, out_far, out_near):
    for start in range(0, out_far.shape[0], SUB):
        rows = pl.ds(start, SUB)
        one, other = first[rows, :], last[rows, :]
        out_far[rows, :] = jnp.where(odd, other, one)
        out_near[rows, :] = jnp.where(odd, one, other)


def unroute(odd, from_far, from_near, before, after):
    for start in range(0, from_far.shape[0], SUB):
        rows = pl.ds(start, SUB)
        far, near = from_far[rows, :], from_near[rows, :]
        before[rows, :] = jnp.where(odd, near, far)
        after[rows, :] = jnp.where(odd, far, near)


def pack(g, water, bricks, params, edges, odd, buffers, sends, first):
    row_u, row_hb, col_u, col_hb = edges
    row_first, row_last, col_first, col_last = buffers
    row_odd, col_odd = odd[0] > 0.0, odd[1] > 0.0
    nx, ny, across, edge = g.nx, g.ny, g.across, g.edge
    lane = lane_ids()
    for side, (out, x, inward, sign) in enumerate(((row_first, 0, 1, 1.0), (row_last, nx - 1, nx - 2, -1.0))):
        for t in range(g.ytiles):
            own = x * ny + SUB * t
            hb = row_hb(side, t)
            out[pl.ds(M_P + SUB * t, SUB), :] = water[pl.ds(own, SUB), :]
            out[pl.ds(M_U + SUB * t, SUB), :] = row_u(side, t) - sign * hb * water[pl.ds(inward * ny + SUB * t, SUB), :]
            if first:
                out[pl.ds(M_CONST + SUB * t, SUB), :] = hb
        for tj in range(across):
            block = M_BRICK + SUB * tj
            for k, field in enumerate(ALONG_X + (VX, VY, VZ)):
                out[pl.ds(block + k, 1), :] = bricks[field * across + tj, pl.ds(x, 1), :]
            out[pl.ds(block + 6, 1), :] = params[HB * across + tj, pl.ds(x, 1), :]
            out[pl.ds(block + 7, 1), :] = jnp.zeros((1, LANES), jnp.float32)
        out[pl.ds(M_CORNER, 2 * SUB), :] = jnp.zeros((2 * SUB, LANES), jnp.float32)
    sides = ((col_first, 0, 1, 0, 1.0), (col_last, ny - 1, ny - 2, across - 1, -1.0))
    for side, (out, y, inward, tj, sign) in enumerate(sides):
        for t in range(g.xtiles):
            own = SUB * t * ny + y
            hb = col_hb(side, t)
            out[pl.ds(M_P + SUB * t, SUB), :] = water[pl.ds(own, SUB, stride=ny), :]
            out[pl.ds(M_U + SUB * t, SUB), :] = (
                col_u(side, t) - sign * hb * water[pl.ds(SUB * t * ny + inward, SUB, stride=ny), :]
            )
            if first:
                out[pl.ds(M_CONST + SUB * t, SUB), :] = hb
            rows = pl.ds(SUB * t, SUB)
            pieces = [bricks[field * across + tj, rows, :] for field in ALONG_Y + (VX, VY, VZ)]
            pieces.append(params[HB * across + tj, rows, :])
            beside = (1, 0) if t == 0 else (SUB - 2, SUB - 1)
            shear = bricks[XZ * across + tj, rows, :]
            if t == 0 or t == g.xtiles - 1:
                shear = pltpu.roll(shear, 1 if t == 0 else SUB - 1, 0)
            sub = lax.broadcasted_iota(jnp.int32, (SUB, LANES), 0)
            pieces.append(jnp.where(sub == beside[0], shear, bricks[XX * across + tj, rows, :]))
            packed = None
            for k, value in enumerate(pieces):
                moved = roll(value, edge * (k - y % g.yper))
                packed = moved if packed is None else jnp.where(lane >= edge * k, moved, packed)
            out[pl.ds(M_BRICK + SUB * t, SUB), :] = packed
            if t == 0:
                corner = packed
        out[pl.ds(M_CORNER, SUB), :] = jnp.where(row_odd, packed, corner)
        out[pl.ds(M_CORNER + SUB, SUB), :] = jnp.where(row_odd, corner, packed)
    route(row_odd, row_first, row_last, *sends[:2])
    route(col_odd, col_first, col_last, *sends[2:])


def first_kernel(
    g, live_hbm, table_hbm, water_hbm, material_hbm, motion_hbm, kinds_hbm, odd,
    water_out, bricks_out, params, columns, row_far, row_near, col_far, col_near,
    stress, pressure, ux_edge, uy_edge, material_x, material_y, motion, kinds, live, table, sems, *buffers,
):
    nx, ny, across = g.nx, g.ny, g.across
    copies = []

    def fetch(source, target):
        copies.append(pltpu.make_async_copy(source, target, sems.at[len(copies)]))
        copies[-1].start()

    fetch(live_hbm, live)
    fetch(table_hbm, table)
    fetch(kinds_hbm, kinds)
    fetch(motion_hbm, motion)
    fetch(water_hbm.at[0], pressure)
    for side, (x, y) in enumerate(((0, 0), (nx - 1, ny - SUB))):
        fetch(water_hbm.at[1, x], ux_edge.at[side])
        fetch(material_hbm.at[x], material_x.at[side])
        fetch(water_hbm.at[2, :, pl.ds(y, SUB), :], uy_edge.at[side])
        fetch(material_hbm.at[:, pl.ds(y, SUB), :], material_y.at[side])
    lane = lane_ids()
    zero_stress_pads(g, stress)
    copies[0].wait()
    copies[1].wait()
    scales = (0.5, 0.5, 1.0, 1.0, 1.0, 1.0, 0.5, 1.0)
    for c, factor in enumerate(scales):
        column = jnp.zeros((SUB, LANES), jnp.float32)
        for level in range(table.shape[0]):
            column = jnp.where(lane == level, table[level, c], column)
        columns[c] = column * factor
    copies[2].wait()
    copies[3].wait()

    @pl.loop(0, g.xtiles)
    def _(ti):
        for tj in range(across):
            slot = g.slot(ti, tj)
            rows, lanes = g.place(ti, tj)
            alive = live[slot].astype(jnp.float32)
            here = aligned(SUB * ti)
            index = kinds[slot, rows, lanes]
            for c in range(8):
                value = pick(columns[c], index)
                params[c * across + tj, here, :] = value if 3 <= c < 6 else value * alive
            params[ALIVE * across + tj, here, :] = jnp.zeros((SUB, LANES), jnp.float32) + alive
            for field in range(XX, YZ + 1):
                value = motion[slot, field, rows, lanes] * alive
                bricks_out[field * across + tj, here, :] = value
                stress[(field - XX) * across + tj, aligned(PAD + SUB * ti), :] = value

    copies[4].wait()

    @pl.loop(0, nx // 2)
    def _(turn):
        results = []
        for x in (2 * turn, 2 * turn + 1):
            for t in range(g.ytiles):
                results.append((x * ny + SUB * t, pressure[x, pl.ds(SUB * t, SUB), :]))
        for own, value in results:
            water_out[aligned(own), :] = value

    def load_v(field, ti, tj):
        slot = g.slot(ti, tj)
        rows, lanes = g.place(ti, tj)
        return motion[slot, field, rows, lanes] * live[slot].astype(jnp.float32)

    def load_hb(ti, tj):
        return params[HB * across + tj, aligned(SUB * ti), :]

    brick_velocity(g, water_out, stress, load_v, bricks_out, load_hb)
    for copy in copies[5:]:
        copy.wait()

    def rows_of(side, t):
        return side, pl.ds(SUB * t, SUB), side * (SUB - 1)

    edges = (
        lambda side, t: ux_edge[side, pl.ds(SUB * t, SUB), :],
        lambda side, t: pick(columns[0], material_x[side, pl.ds(SUB * t, SUB), :]),
        lambda side, t: uy_edge[(*rows_of(side, t), slice(None))],
        lambda side, t: pick(columns[0], material_y[(*rows_of(side, t), slice(None))]),
    )
    pack(g, water_out, bricks_out, params, edges, odd, buffers, (row_far, row_near, col_far, col_near), True)


def first_water_kernel(
    g, pressure, row_first, row_last, bricks, columns, state, material, water_out, first_same, last_same, hb_water, hk_water, press
):
    nx, ny = g.nx, g.ny
    zero_press_pads(g, press)

    @pl.loop(0, nx // 2)
    def _(turn):
        results = []
        for x in (2 * turn, 2 * turn + 1):
            for t in range(g.ytiles):
                own = x * ny + SUB * t
                index = material[x, pl.ds(SUB * t, SUB), :]
                results.append((x, t, own, pick(columns[0], index), pick(columns[1], index), pressure[aligned(own), :]))
        for x, t, own, hb, hk, value in results:
            hb_water[aligned(own), :] = hb
            hk_water[aligned(own), :] = hk
            press[x + 1, pl.ds(PAD + SUB * t, SUB), :] = value

    water_velocity(
        g,
        (nx // 2, lambda turn: 2 * turn),
        water_out,
        press,
        lambda t, x: bricks[ZZ * g.across + t, pl.ds(x, 1), :],
        lambda x, t: hb_water[aligned(x * ny + SUB * t), :],
        lambda k, x, t: state[k, x, pl.ds(SUB * t, SUB), :],
    )


def edge_water_kernel(
    g, same, row_first, row_last, water, press, stress, hb_water, ux, uy, water_out, first_same, last_same
):
    nx, ny, plane = g.nx, g.ny, g.plane

    def load_u(k, x, t):
        if k == 1:
            layer = x - (x // (nx - SUB)) * (nx - 2 * SUB) + 1
            return ux[aligned(layer * ny + SUB * t), :]
        if k == 2:
            return uy[aligned(x * (ny + 2 * PAD) + PAD + SUB * t), :]
        return water[aligned(3 * plane + x * ny + SUB * t), :]

    water_velocity(
        g,
        (SUB, lambda turn: 2 * turn + (turn // (SUB // 2)) * (nx - 2 * SUB)),
        water_out,
        press,
        lambda t, x: stress[(ZZ - XX) * g.across + t, pl.ds(PAD + x, 1), :],
        lambda x, t: hb_water[aligned(x * ny + SUB * t), :],
        load_u,
    )


def slots_of(g, array, ti):
    slot = g.slot(ti, 0)
    return array.at[pl.ds(slot, 2), :, pl.ds((ti % g.per) * SUB, SUB), :]


class Refs:
    def __init__(self, refs):
        self.refs = list(refs)

    def take(self, count):
        taken, self.refs = self.refs[:count], self.refs[count:]
        return taken


def inner_kernel(g, first, last, *refs):
    refs = Refs(refs)
    water, bricks, memory, params, hb_water, hk_water, odd, col_far, col_near = refs.take(9)
    if not first:
        (const_in,) = refs.take(1)
    uy, speed = refs.take(2)
    if last:
        water_hbm, motion_hbm, memory_hbm = refs.take(3)
    else:
        water_out, press, stress, bricks_out, memory_out = refs.take(5)
    if first:
        (const_out,) = refs.take(1)
    col_before, col_after = refs.take(2)
    if last:
        press_buf, uy_buf, motion_buf, memory_buf, sems = refs.take(5)
    unroute(odd[1] > 0.0, col_far, col_near, col_before, col_after)

    nx, ny, edge, across, plane = g.nx, g.ny, g.edge, g.across, g.plane
    wide = across + 2
    lane = lane_ids()
    top_pick = surface_pick() * edge + (edge - 1)
    py = ny + 2 * PAD
    low, high = SUB, nx - SUB
    copies = []

    def send(source, target):
        copies.append(pltpu.make_async_copy(source, target, sems.at[len(copies)]))
        copies[-1].start()

    def part(component, start, stop):
        return pl.ds(component * plane + start * ny, (stop - start) * ny)

    if last:
        send(water.at[part(3, 0, nx), :], water_hbm.at[part(3, 0, nx), :])
        send(water.at[part(1, 1, nx - 1), :], water_hbm.at[part(1, 1, nx - 1), :])
    else:
        zero_press_pads(g, press)
        zero_stress_pads(g, stress)

    @pl.loop(0, nx)
    def _(x):
        for t in range(g.ytiles):
            own = x * ny + SUB * t
            uy[aligned(x * py + PAD + SUB * t), :] = water[aligned(2 * plane + own), :]
            if last:
                uy_buf[aligned(own), :] = water[aligned(2 * plane + own), :]

    for side, (ref, y, halo, sign) in enumerate(((col_before, 0, -1, 1.0), (col_after, ny - 1, ny, -1.0))):
        for t in range(g.xtiles):
            own = pl.ds(SUB * t * ny + y, SUB, stride=ny)
            here = pl.ds(SUB * t * py + PAD + y, SUB, stride=py)
            place = pl.ds(32 * side + SUB * t, SUB)
            if first:
                theirs = ref[pl.ds(M_CONST + SUB * t, SUB), :]
                const_out[place, :] = theirs
            else:
                theirs = const_in[place, :]
            value = uy[here, :] + sign * hb_water[own, :] * ref[pl.ds(M_P + SUB * t, SUB), :]
            uy[here, :] = value
            if last:
                uy_buf[own, :] = value
            uy[pl.ds(SUB * t * py + PAD + halo, SUB, stride=py), :] = (
                ref[pl.ds(M_U + SUB * t, SUB), :] - sign * theirs * water[own, :]
            )
    if last:
        send(uy_buf, water_hbm.at[part(2, 0, nx), :])

    for field in (VX, VY, VZ):
        for tj in range(across):
            for ti in range(g.xtiles):
                speed[field * wide + 1 + tj, pl.ds(PAD + SUB * ti, SUB), :] = bricks[field * across + tj, pl.ds(SUB * ti, SUB), :]
    for ref, tj, halo, sign in ((col_before, 0, 0, 1.0), (col_after, across - 1, wide - 1, -1.0)):
        near = 0 if tj == 0 else LANES - edge
        far = LANES - edge - near
        inside = (lane >= near) & (lane < near + edge)
        for ti in range(g.xtiles):
            column = ref[pl.ds(M_BRICK + SUB * ti, SUB), :]
            own_hb = jnp.where(inside, sign * params[HB * across + tj, pl.ds(SUB * ti, SUB), :], 0.0)
            their_hb = sign * roll(column, far - 6 * edge)
            here = pl.ds(PAD + SUB * ti, SUB)
            for c in (VX, VY, VZ):
                key = c * wide + 1 + tj
                speed[key, here, :] = bricks[c * across + tj, pl.ds(SUB * ti, SUB), :] - own_hb * roll(column, near - c * edge)
                own = bricks[ALONG_Y[c] * across + tj, pl.ds(SUB * ti, SUB), :]
                speed[c * wide + halo, here, :] = roll(column, far - (3 + c) * edge) + their_hb * roll(own, far - near)

    store = store_slots(g, motion_buf, memory_buf) if last else store_planes(g, bricks_out, memory_out, stress)

    @pl.loop(1, g.xtiles - 1)
    def _(ti):
        row = pl.multiple_of(SUB * ti, SUB)
        tops = (
            lambda y: water[pl.ds(plane + row * ny + y, SUB, stride=ny), :],
            lambda y: uy[pl.ds(row * py + PAD + y, SUB, stride=py), :],
            lambda y: water[pl.ds(3 * plane + row * ny + y, SUB, stride=ny), :],
        )
        brick_stress(g, ti, first, bricks, memory, params, speed, tops, store)

    if last:
        for ti in range(1, g.xtiles - 1):
            send(slots_of(g, motion_buf, ti), slots_of(g, motion_hbm, ti))
            send(slots_of(g, memory_buf, ti), slots_of(g, memory_hbm, ti))

    def layer(x):
        results = []
        for t in range(g.ytiles):
            own = x * ny + SUB * t
            dx = water[aligned(plane + own + ny), :] - water[aligned(plane + own - ny), :]
            results.append(
                (x, t, own, water_stress(g, x, t, dx, water, uy, speed, hk_water, lane, top_pick))
            )
        return results

    @pl.loop(0, (nx - 4) // 2)
    def _(turn):
        for x, t, own, value in layer(2 + 2 * turn) + layer(3 + 2 * turn):
            if last:
                press_buf[aligned(own), :] = value
            else:
                water_out[aligned(own), :] = value
                press[x + 1, pl.ds(PAD + SUB * t, SUB), :] = value

    if last:
        send(press_buf.at[part(0, 2, nx - 2), :], water_hbm.at[part(0, 2, nx - 2), :])
        for copy in copies:
            copy.wait()
    else:
        def load_u(k, x, t):
            if k == 2:
                return uy[aligned(x * py + PAD + SUB * t), :]
            return water[aligned(k * plane + x * ny + SUB * t), :]

        layers = ((high - low) // 2, lambda turn: low + 2 * turn)
        water_velocity(
            g,
            layers,
            water_out,
            press,
            lambda t, x: stress[(ZZ - XX) * across + t, pl.ds(PAD + x, 1), :],
            lambda x, t: hb_water[aligned(x * ny + SUB * t), :],
            load_u,
        )


def water_stress(g, x, t, dx, water, uy, speed, hk_water, lane, top_pick):
    row = x * (g.ny + 2 * PAD) + PAD + SUB * t
    own = x * g.ny + SUB * t
    dy = uy[pl.ds(row + 1, SUB), :] - uy[pl.ds(row - 1, SUB), :]
    surface = jnp.broadcast_to(speed[VZ * (g.across + 2) + 1 + t, pl.ds(PAD + x, 1), :], (SUB, LANES))
    dz = water_z(g, water[aligned(3 * g.plane + own), :], pick(surface, top_pick), lane)
    return water[aligned(own), :] - hk_water[aligned(own), :] * (dx + dy + dz)


def edge_kernel(g, first, last, *refs):
    refs = Refs(refs)
    water, bricks, memory, params, hb_water, hk_water, odd, col_far, col_near, row_far, row_near = refs.take(11)
    if not first:
        (const_in,) = refs.take(1)
    (uy,) = refs.take(1)
    refs.take(4 if last else 6)
    (speed,) = refs.take(1)
    if last:
        water_hbm, motion_hbm, memory_hbm = refs.take(3)
    else:
        water_out, press, stress, bricks_out, memory_out = refs.take(5)
        sends = refs.take(4)
    (ux,) = refs.take(1)
    if first:
        (const_out,) = refs.take(1)
    col_before, col_after, row_before, row_after = refs.take(4)
    if last:
        press_buf, motion_buf, memory_buf, sems = refs.take(4)
    else:
        buffers = refs.take(4)
    unroute(odd[1] > 0.0, col_far, col_near, col_before, col_after)
    unroute(odd[0] > 0.0, row_far, row_near, row_before, row_after)
    for ref in (row_before, row_after):
        far, near = ref[pl.ds(M_CORNER, SUB), :], ref[pl.ds(M_CORNER + SUB, SUB), :]
        ref[pl.ds(M_CORNER, SUB), :] = jnp.where(odd[1] > 0.0, near, far)
        ref[pl.ds(M_CORNER + SUB, SUB), :] = jnp.where(odd[1] > 0.0, far, near)

    nx, ny, edge, across, plane = g.nx, g.ny, g.edge, g.across, g.plane
    wide = across + 2
    lane = lane_ids()
    top_pick = surface_pick() * edge + (edge - 1)
    py = ny + 2 * PAD
    copies = []

    def send(source, target):
        copies.append(pltpu.make_async_copy(source, target, sems.at[len(copies)]))
        copies[-1].start()

    @pl.loop(0, SUB)
    def _(x):
        for t in range(g.ytiles):
            own = x * ny + SUB * t
            ux[aligned(ny + own), :] = water[aligned(plane + own), :]
            ux[aligned((1 + SUB) * ny + own), :] = water[aligned(plane + (nx - SUB) * ny + own), :]

    sides = ((row_before, 0, -1, 1.0, 1, 0), (row_after, nx - 1, nx, -1.0, 2 * SUB, 2 * SUB + 1))
    for side, (ref, x, halo, sign, own_layer, halo_layer) in enumerate(sides):
        for t in range(g.ytiles):
            own = pl.ds(x * ny + SUB * t, SUB)
            place = pl.ds(32 * side + SUB * t, SUB)
            if first:
                theirs = ref[pl.ds(M_CONST + SUB * t, SUB), :]
                const_out[place, :] = theirs
            else:
                theirs = const_in[place, :]
            here = pl.ds(own_layer * ny + SUB * t, SUB)
            ux[here, :] = ux[here, :] + sign * hb_water[own, :] * ref[pl.ds(M_P + SUB * t, SUB), :]
            ux[pl.ds(halo_layer * ny + SUB * t, SUB), :] = ref[pl.ds(M_U + SUB * t, SUB), :] - sign * theirs * water[own, :]
    if last:
        for layer, x in ((1, 0), (2 * SUB, nx - 1)):
            send(ux.at[pl.ds(layer * ny, ny), :], water_hbm.at[pl.ds(plane + x * ny, ny), :])

    for ref, x, halo, sign, _, _ in sides:
        for tj in range(across):
            block = M_BRICK + SUB * tj
            own_hb = sign * params[HB * across + tj, pl.ds(x, 1), :]
            their_hb = sign * ref[pl.ds(block + 6, 1), :]
            for c in (VX, VY, VZ):
                here = pl.ds(PAD + x, 1)
                key = c * wide + 1 + tj
                speed[key, here, :] = speed[key, here, :] - own_hb * ref[pl.ds(block + c, 1), :]
                speed[key, pl.ds(PAD + halo, 1), :] = (
                    ref[pl.ds(block + 3 + c, 1), :] + their_hb * bricks[ALONG_X[c] * across + tj, pl.ds(x, 1), :]
                )
        edge_row = SUB - 1 if x == 0 else 0
        beside_row = SUB - 2 if x == 0 else 1
        for k, (col_ref, tj, col_halo, col_sign) in enumerate(((col_before, 0, 0, 1.0), (col_after, across - 1, wide - 1, -1.0))):
            near = 0 if tj == 0 else LANES - edge
            far = LANES - edge - near
            inside = (lane[0:1, :] >= near) & (lane[0:1, :] < near + edge)
            corner = ref[pl.ds(M_CORNER + SUB * k + edge_row, 1), :]
            beside = ref[pl.ds(M_CORNER + SUB * k + beside_row, 1), :]
            across_y = [roll_row(corner, near - c * edge) for c in range(3)]
            across_x = (roll_row(corner, far - 7 * edge), roll_row(corner, far), roll_row(beside, far - 7 * edge))
            row_hb = jnp.where(inside, col_sign * ref[pl.ds(M_BRICK + SUB * tj + 6, 1), :], 0.0)
            col_hb = sign * roll_row(col_ref[pl.ds(M_BRICK + x, 1), :], far - 6 * edge)
            for c in (VX, VY, VZ):
                key, here = c * wide + 1 + tj, pl.ds(PAD + halo, 1)
                speed[key, here, :] = speed[key, here, :] - row_hb * across_y[c]
                key, here = c * wide + col_halo, pl.ds(PAD + x, 1)
                speed[key, here, :] = speed[key, here, :] - col_hb * across_x[c]

    store = store_slots(g, motion_buf, memory_buf) if last else store_planes(g, bricks_out, memory_out, stress)

    @pl.loop(0, 2)
    def _(turn):
        ti = turn * (g.xtiles - 1)
        row = pl.multiple_of(SUB * ti, SUB)
        above = pl.multiple_of((1 + SUB * turn) * ny, SUB)
        tops = (
            lambda y: ux[pl.ds(above + y, SUB, stride=ny), :],
            lambda y: uy[pl.ds(row * py + PAD + y, SUB, stride=py), :],
            lambda y: water[pl.ds(3 * plane + row * ny + y, SUB, stride=ny), :],
        )
        brick_stress(g, ti, first, bricks, memory, params, speed, tops, store)

    if last:
        for ti in (0, g.xtiles - 1):
            send(slots_of(g, motion_buf, ti), slots_of(g, motion_hbm, ti))
            send(slots_of(g, memory_buf, ti), slots_of(g, memory_hbm, ti))

    for pair, (x, layer) in enumerate(((0, 1), (nx - 2, 2 * SUB - 1))):
        for step in range(2):
            for t in range(g.ytiles):
                dx = (
                    ux[pl.ds((layer + step + 1) * ny + SUB * t, SUB), :] - ux[pl.ds((layer + step - 1) * ny + SUB * t, SUB), :]
                )
                value = water_stress(g, x + step, t, dx, water, uy, speed, hk_water, lane, top_pick)
                if last:
                    press_buf[pl.ds((2 * pair + step) * ny + SUB * t, SUB), :] = value
                else:
                    water_out[pl.ds((x + step) * ny + SUB * t, SUB), :] = value
                    press[x + step + 1, pl.ds(PAD + SUB * t, SUB), :] = value

    if last:
        for pair, x in enumerate((0, nx - 2)):
            send(press_buf.at[pl.ds(2 * pair * ny, 2 * ny), :], water_hbm.at[pl.ds(x * ny, 2 * ny), :])
        for copy in copies:
            copy.wait()
    else:
        def load_v(field, ti, tj):
            return speed[field * wide + 1 + tj, aligned(PAD + SUB * ti), :]

        def load_hb(ti, tj):
            return params[HB * across + tj, aligned(SUB * ti), :]

        def column(side, t):
            return pl.ds(SUB * t * ny + side * (ny - 1), SUB, stride=ny)

        faces = (
            lambda side, t: ux[pl.ds((1 + side * (2 * SUB - 1)) * ny + SUB * t, SUB), :],
            lambda side, t: hb_water[pl.ds(side * (nx - 1) * ny + SUB * t, SUB), :],
            lambda side, t: uy[pl.ds(SUB * t * py + PAD + side * (ny - 1), SUB, stride=py), :],
            lambda side, t: hb_water[column(side, t), :],
        )
        brick_velocity(g, water_out, stress, load_v, bricks_out, load_hb)
        pack(g, water_out, bricks_out, params, faces, odd, buffers, sends, False)


def swap(value, axis, start):
    pairs = [(i, i + 1) for i in range(start, lax.axis_size(axis) - 1, 2)]
    return lax.ppermute(value, axis, pairs + [(j, i) for i, j in pairs])


def exchange(sends):
    row_far, row_near, col_far, col_near = sends
    col_far = swap(col_far, "col", 1)
    col_near = swap(col_near, "col", 0)

    def with_corners(message, start):
        corners = jnp.concatenate([col_far[start : start + SUB], col_near[start : start + SUB]])
        return lax.dynamic_update_slice(message, corners, (M_CORNER, 0))

    row_far, row_near = lax.optimization_barrier(
        (with_corners(row_far, M_CORNER), with_corners(row_near, M_CORNER + SUB))
    )
    row_far = swap(row_far, "row", 1)
    row_near = swap(row_near, "row", 0)
    return col_far, col_near, row_far, row_near


def body(
    brick_velocity_stress,
    brick_relaxation_memory,
    brick_cell_material,
    brick_live,
    water_state,
    water_material,
    material_table,
):
    _, nx, ny, nz = water_state.shape
    g = Grid(nx, ny, brick_cell_material.shape[1])
    across, plane = g.across, g.plane

    def f32(*shape):
        return jax.ShapeDtypeStruct(shape, jnp.float32)

    vmem = pl.BlockSpec(memory_space=pltpu.VMEM)
    hbm = pl.BlockSpec(memory_space=pltpu.HBM)
    params = pltpu.CompilerParams(vmem_limit_bytes=24 * 1024 * 1024)
    def messages(first):
        return [f32(M_CONST + (32 if first else 0), LANES)] * 4

    def buffer(*shape):
        return pltpu.VMEM(shape, jnp.float32)

    def held(*values):
        return [pltpu.with_memory_space_constraint(value, pltpu.VMEM) for value in values]

    def pinned(*values):
        return [pltpu.with_memory_space_constraint(value, pltpu.HBM) for value in values]

    def message_buffers(count, first):
        return [buffer(M_CONST + (32 if first else 0), LANES)] * count

    odd = jnp.stack([lax.axis_index(axis) & 1 for axis in ("row", "col")]).astype(jnp.float32)
    odd = jnp.broadcast_to(odd[:, None, None], (2, SUB, LANES))
    press = buffer(nx + 2, ny + 2 * PAD, nz)
    stress = buffer(6 * across, nx + 2 * PAD, LANES)
    work = pl.CostEstimate(flops=20_000_000, bytes_accessed=8_000_000, transcendentals=0)
    water, bricks, coefficients, columns, *sends = pl.pallas_call(
        functools.partial(first_kernel, g),
        out_shape=[
            buffer(4 * plane, nz), f32(9 * across, nx, LANES), f32(9 * across, nx, LANES), f32(8, SUB, LANES),
        ] + messages(True),
        in_specs=[hbm] * 6 + [vmem],
        out_specs=[vmem] * 8,
        scratch_shapes=[
            stress,
            buffer(nx, ny, nz),
            buffer(2, ny, nz),
            buffer(2, nx, SUB, nz),
            pltpu.VMEM((2, ny, nz), jnp.int32),
            pltpu.VMEM((2, nx, SUB, nz), jnp.int32),
            pltpu.VMEM(brick_velocity_stress.shape, jnp.float32),
            pltpu.VMEM(brick_cell_material.shape, jnp.int32),
            pltpu.SMEM(brick_live.shape, jnp.int32),
            pltpu.SMEM(material_table.shape, jnp.float32),
            pltpu.SemaphoreType.DMA((13,)),
        ]
        + message_buffers(4, True),
        compiler_params=params,
        name="first_bricks",
    )(*pinned(brick_live, material_table, water_state, water_material, brick_velocity_stress, brick_cell_material), odd)

    def passed(*messages):
        return [buffer(*message.shape) for message in messages]

    water, sends[0], sends[1], hb_water, hk_water = pl.pallas_call(
        functools.partial(first_water_kernel, g),
        out_shape=[buffer(4 * plane, nz)] + passed(*sends[:2]) + [f32(plane, nz), f32(plane, nz)],
        in_specs=[vmem] * 7,
        out_specs=[vmem] * 5,
        input_output_aliases={0: 0, 1: 1, 2: 2},
        scratch_shapes=[press],
        compiler_params=params,
        cost_estimate=work,
        name="first_water",
    )(*held(water, *sends[:2], bricks, columns, water_state, water_material))
    memory = brick_relaxation_memory
    col_const, row_const = (), ()
    uy_shape = (nx * (ny + 2 * PAD), nz)
    speed_shape = (3 * (across + 2), nx + 2 * PAD, LANES)
    ux_buffer = buffer((2 * SUB + 2) * ny, nz)
    slot_buffers = [
        pltpu.VMEM(brick_velocity_stress.shape, jnp.float32),
        pltpu.VMEM(brick_relaxation_memory.shape, jnp.float32),
    ]
    finals = [f32(4 * plane, nz), f32(*brick_velocity_stress.shape), f32(*brick_relaxation_memory.shape)]
    planes = [
        buffer(4 * plane, nz),
        buffer(nx + 2, ny + 2 * PAD, nz),
        buffer(6 * across, nx + 2 * PAD, LANES),
        buffer(9 * across, nx, LANES),
        buffer(18 * across, nx, LANES),
    ]
    for step in range(STEPS):
        first, last = step == 0, step == STEPS - 1
        *columns, row_far, row_near = exchange(sends)
        state = (water, bricks, memory, coefficients, hb_water, hk_water, odd)
        shapes = finals if last else planes
        spaces = [hbm if last else vmem] * len(shapes)
        inner = pl.pallas_call(
            functools.partial(inner_kernel, g, first, last),
            out_shape=[buffer(*uy_shape), buffer(*speed_shape)] + shapes + ([buffer(64, LANES)] if first else []),
            in_specs=[vmem] * (9 + len(col_const)),
            out_specs=[vmem] * 2 + spaces + ([vmem] if first else []),
            scratch_shapes=message_buffers(2, first)
            + ([buffer(plane, nz), buffer(plane, nz)] + slot_buffers + [pltpu.SemaphoreType.DMA((8,))] if last else []),
            compiler_params=params,
            cost_estimate=work,
            name="inner",
        )(*held(*state), *columns, *col_const)
        if first:
            col_const = (inner[-1],)
            inner = inner[:-1]
        uy, *partial = inner
        count = 11 + len(row_const) + 1
        results = pl.pallas_call(
            functools.partial(edge_kernel, g, first, last),
            out_shape=[buffer(*speed_shape)]
            + shapes
            + ([] if last else messages(False) + [ux_buffer])
            + ([buffer(64, LANES)] if first else []),
            in_specs=[vmem] * (count + 1) + spaces,
            out_specs=[vmem] + spaces + [vmem] * (0 if last else 5) + ([vmem] if first else []),
            input_output_aliases={count + k: k for k in range(1 + len(shapes))},
            scratch_shapes=([ux_buffer] if last else [])
            + message_buffers(4, first)
            + (
                [buffer(4 * ny, nz)] + slot_buffers + [pltpu.SemaphoreType.DMA((8,))]
                if last
                else message_buffers(4, False)
            ),
            compiler_params=params,
            name="edges",
        )(*held(*state), *columns, row_far, row_near, *row_const, *held(uy), *(held(partial[0]) + (list(partial[1:]) if last else held(*partial[1:]))))
        if last:
            return results[2], results[3], results[1].reshape(water_state.shape)
        old_water = water
        _, water, pressed, stressed, bricks, memory = results[:6]
        sends = list(results[6:10])
        if first:
            row_const = (results[11],)
        water, sends[0], sends[1] = pl.pallas_call(
            functools.partial(edge_water_kernel, g),
            out_shape=[buffer(4 * plane, nz)] + passed(*sends[:2]),
            in_specs=[vmem] * 9,
            out_specs=[vmem] * 3,
            input_output_aliases={0: 0, 1: 1, 2: 2},
            compiler_params=params,
            cost_estimate=work,
            name="edge_water",
        )(*held(water, *sends[:2], old_water, pressed, stressed, hb_water, results[10], uy))


def solution(mesh):
    return jax.shard_map(
        body,
        mesh=mesh,
        in_specs=(
            P(("row", "col"), None, None, None),
            P(("row", "col"), None, None, None),
            P(("row", "col"), None, None),
            P(("row", "col")),
            P(None, "row", "col", None),
            P("row", "col", None),
            P(),
        ),
        out_specs=(
            P(("row", "col"), None, None, None),
            P(("row", "col"), None, None, None),
            P(None, "row", "col", None),
        ),
        check_vma=False,
    )
```

```python
import functools

import jax
import jax.numpy as jnp
from jax import lax
from jax.experimental import pallas as pl
from jax.experimental.pallas import tpu as pltpu
from jax.sharding import PartitionSpec as P

STEPS = 3
LANES = 128
SUB = 8
PAD = 8
VX, VY, VZ, XX, YY, ZZ, XY, XZ, YZ = range(9)
HB, LAME, SHEAR, RETAIN, SPRING_LAME, SPRING_SHEAR, ALIVE = 0, 1, 2, 3, 6, 7, 8
ALONG_X = (XX, XY, XZ)
ALONG_Y = (XY, YY, YZ)
ALONG_Z = (XZ, YZ, ZZ)
M_P, M_U, M_BRICK, M_CORNER, M_CONST = 0, 32, 64, 96, 112


def lane_ids():
    return lax.broadcasted_iota(jnp.int32, (SUB, LANES), 1)


def roll(value, shift):
    shift = shift % LANES
    return value if shift == 0 else pltpu.roll(value, shift, 1)


def roll_row(row, shift):
    shift = shift % LANES
    if shift == 0:
        return row
    return pltpu.roll(jnp.broadcast_to(row, (SUB, LANES)), shift, 1)[0:1, :]


def pick(values, indices):
    return jnp.take_along_axis(values, indices, axis=1, mode="promise_in_bounds")


def aligned(start, size=SUB):
    return pl.ds(start if isinstance(start, int) else pl.multiple_of(start, SUB), size)


class Grid:
    def __init__(self, nx, ny, edge):
        self.nx, self.ny, self.edge = nx, ny, edge
        self.plane = nx * ny
        self.across = ny * edge // LANES
        self.yper = LANES // edge
        self.half = self.across // 2
        self.xtiles, self.ytiles = nx // SUB, ny // SUB
        self.per = edge // SUB

    def slot(self, ti, tj):
        return 2 * (ti // self.per) + tj // self.half

    def place(self, ti, tj):
        return aligned((ti % self.per) * SUB), pl.ds((tj % self.half) * LANES, LANES)


def zero_press_pads(g, press):
    zero = jnp.zeros((SUB, LANES), jnp.float32)
    for t in range(g.ytiles):
        press[0, pl.ds(PAD + SUB * t, SUB), :] = zero
        press[g.nx + 1, pl.ds(PAD + SUB * t, SUB), :] = zero

    @pl.loop(0, g.nx // SUB)
    def _(turn):
        for step in range(SUB):
            x = SUB * turn + step + 1
            press[x, pl.ds(0, SUB), :] = zero
            press[x, pl.ds(PAD + g.ny, SUB), :] = zero


def zero_stress_pads(g, stress):
    zero = jnp.zeros((SUB, LANES), jnp.float32)
    for field in ALONG_X:
        for tj in range(g.across):
            key = (field - XX) * g.across + tj
            stress[key, pl.ds(0, SUB), :] = zero
            stress[key, pl.ds(PAD + g.nx, SUB), :] = zero


def shifted_top(g, load, ys, lane):
    top = None
    for k, y in enumerate(ys):
        value = roll(load(y), g.edge * k + g.edge - 1)
        top = value if top is None else jnp.where(lane >= g.edge * k, value, top)
    return top


def along_y(g, rolled, tj, lane):
    zero = jnp.zeros((SUB, LANES), jnp.float32)
    after = rolled[tj + 1][1] if tj + 1 < len(rolled) else zero
    before = rolled[tj - 1][0] if tj > 0 else zero
    ahead = jnp.where(lane < LANES - g.edge, rolled[tj][1], after)
    behind = jnp.where(lane >= g.edge, rolled[tj][0], before)
    return ahead - behind


def along_z(g, value, beyond, depth):
    zero = jnp.zeros((SUB, LANES), jnp.float32)
    return jnp.where(depth == g.edge - 1, beyond, roll(value, -1)) - jnp.where(depth == 0, zero, roll(value, 1))


def water_z(g, value, below, lane):
    zero = jnp.zeros((SUB, LANES), jnp.float32)
    return jnp.where(lane == LANES - 1, zero, roll(value, -1)) - jnp.where(lane == 0, below, roll(value, 1))


def surface_pick():
    return lax.broadcasted_iota(jnp.int32, (SUB, LANES), 0)


def water_velocity(g, layers, water_out, press, surface_row, load_hb, load_u):
    lane = lane_ids()
    top_pick = surface_pick() * g.edge + (g.edge - 1)

    def water_layer(x):
        results = []
        for t in range(g.ytiles):
            rows = pl.ds(PAD + SUB * t, SUB)
            here = press[x + 1, rows, :]
            dx = press[x + 2, rows, :] - press[x, rows, :]
            dy = press[x + 1, pl.ds(PAD + SUB * t + 1, SUB), :] - press[x + 1, pl.ds(PAD + SUB * t - 1, SUB), :]
            surface = jnp.broadcast_to(surface_row(t, x), (SUB, LANES))
            dz = water_z(g, here, -pick(surface, top_pick), lane)
            own = x * g.ny + SUB * t
            hb = load_hb(x, t)
            for k, change in ((1, dx), (2, dy), (3, dz)):
                results.append((k * g.plane + own, load_u(k, x, t) - hb * change))
        return results

    turns, layer = layers

    @pl.loop(0, turns)
    def _(turn):
        x = layer(turn)
        for row, value in water_layer(x) + water_layer(x + 1):
            water_out[aligned(row), :] = value


def brick_velocity(g, water_out, stress, load_v, bricks_out, load_hb):
    lane = lane_ids()
    depth = lane % g.edge
    zero = jnp.zeros((SUB, LANES), jnp.float32)
    across, ny = g.across, g.ny

    @pl.loop(0, g.xtiles)
    def _(ti):
        row = pl.multiple_of(SUB * ti, SUB)
        here = pl.ds(pl.multiple_of(row + PAD, SUB), SUB)

        def load(field, tj):
            return stress[(field - XX) * across + tj, here, :]

        def along_x(field, tj):
            key = (field - XX) * across + tj
            return stress[key, pl.ds(row + PAD + 1, SUB), :] - stress[key, pl.ds(row + PAD - 1, SUB), :]

        results = []
        for target, fx, fy, fz in zip((VX, VY, VZ), ALONG_X, ALONG_Y, ALONG_Z):
            rolled = [(roll(value, g.edge), roll(value, -g.edge)) for value in (load(fy, tj) for tj in range(across))]
            for tj in range(across):
                beyond = zero
                if fz == ZZ:
                    ys = [g.yper * tj + k for k in range(g.yper)]
                    beyond = -shifted_top(g, lambda y: water_out[pl.ds(row * ny + y, SUB, stride=ny), :], ys, lane)
                change = along_x(fx, tj) + along_y(g, rolled, tj, lane) + along_z(g, load(fz, tj), beyond, depth)
                results.append((target * across + tj, load_v(target, ti, tj) + load_hb(ti, tj) * change))
        for key, value in results:
            bricks_out[key, pl.ds(row, SUB), :] = value


def brick_stress(g, ti, first, bricks, memory, params, speed, tops, store):
    edge, across = g.edge, g.across
    wide = across + 2
    lane = lane_ids()
    depth = lane % edge
    row = SUB * ti if isinstance(ti, int) else pl.multiple_of(SUB * ti, SUB)
    here, inner = aligned(row), aligned(row + PAD)
    rolled = []
    for field in (VX, VY, VZ):
        values = [speed[field * wide + tj, inner, :] for tj in range(wide)]
        rolled.append([(roll(value, edge), roll(value, -edge)) for value in values])
    for tj in range(across):
        ys = [g.yper * tj + k for k in range(g.yper)]
        dx, dy, dz, speeds = [], [], [], []
        for field in (VX, VY, VZ):
            key = field * wide + 1 + tj
            value = speed[key, inner, :]
            speeds.append(value)
            dx.append(speed[key, pl.ds(row + PAD + 1, SUB), :] - speed[key, pl.ds(row + PAD - 1, SUB), :])
            dy.append(along_y(g, rolled[field], tj + 1, lane))
            dz.append(along_z(g, value, shifted_top(g, tops[field], ys, lane), depth))
        strain = [dx[0], dy[1], dz[2], dy[0] + dx[1], dz[0] + dx[2], dz[1] + dy[2]]
        dilation = strain[0] + strain[1] + strain[2]

        def param(c):
            return params[c * across + tj, here, :]

        lame, shear = param(LAME) * dilation, param(SHEAR)
        spring_lame, spring_shear = param(SPRING_LAME) * dilation, param(SPRING_SHEAR)
        retain = [param(RETAIN + l) for l in range(3)]
        half_shear, half_spring = 0.5 * shear, 0.5 * spring_shear
        slot = g.slot(ti, tj)
        rows, lanes = g.place(ti, tj)
        if first:
            alive = param(ALIVE)
        stresses, memories = [], {}
        for comp in range(6):
            if comp < 3:
                elastic = shear * strain[comp] + lame
                relaxed = spring_shear * strain[comp] + spring_lame
            else:
                elastic = half_shear * strain[comp]
                relaxed = half_spring * strain[comp]
            summed = None
            for l in range(3):
                place = 6 * l + comp
                if first:
                    old = memory[slot, place, rows, lanes] * alive
                else:
                    old = memory[place * across + tj, here, :]
                new = relaxed + retain[l] * (old - relaxed)
                memories[place] = new
                summed = new if summed is None else summed + new
            stresses.append(bricks[(XX + comp) * across + tj, here, :] + elastic - summed)
        store(ti, tj, here, inner, speeds, stresses, memories)


def store_planes(g, bricks_out, memory_out, stress):
    def store(ti, tj, here, inner, speeds, stresses, memories):
        for place, value in memories.items():
            memory_out[place * g.across + tj, here, :] = value
        for comp, value in enumerate(stresses):
            bricks_out[(XX + comp) * g.across + tj, here, :] = value
            stress[comp * g.across + tj, inner, :] = value

    return store


def store_slots(g, motion, memory):
    def store(ti, tj, here, inner, speeds, stresses, memories):
        slot = g.slot(ti, tj)
        rows, lanes = g.place(ti, tj)
        for place, value in memories.items():
            memory[slot, place, rows, lanes] = value
        for field, value in enumerate(speeds + stresses):
            motion[slot, field, rows, lanes] = value

    return store


def route(odd, first, last, out_far, out_near):
    for start in range(0, out_far.shape[0], SUB):
        rows = pl.ds(start, SUB)
        one, other = first[rows, :], last[rows, :]
        out_far[rows, :] = jnp.where(odd, other, one)
        out_near[rows, :] = jnp.where(odd, one, other)


def unroute(odd, from_far, from_near, before, after, starts=None):
    for start in starts or range(0, from_far.shape[0], SUB):
        rows = pl.ds(start, SUB)
        far, near = from_far[rows, :], from_near[rows, :]
        before[rows, :] = jnp.where(odd, near, far)
        after[rows, :] = jnp.where(odd, far, near)


def pack(g, water, bricks, params, edges, odd, buffers, sends, first):
    row_u, row_hb, col_u, col_hb = edges
    row_first, row_last, col_first, col_last = buffers
    row_odd, col_odd = odd[0] > 0.0, odd[1] > 0.0
    nx, ny, across, edge = g.nx, g.ny, g.across, g.edge
    lane = lane_ids()
    for side, (out, x, inward, sign) in enumerate(((row_first, 0, 1, 1.0), (row_last, nx - 1, nx - 2, -1.0))):
        for t in range(g.ytiles):
            own = x * ny + SUB * t
            hb = row_hb(side, t)
            out[pl.ds(M_P + SUB * t, SUB), :] = water[pl.ds(own, SUB), :]
            out[pl.ds(M_U + SUB * t, SUB), :] = row_u(side, t) - sign * hb * water[pl.ds(inward * ny + SUB * t, SUB), :]
            if first:
                out[pl.ds(M_CONST + SUB * t, SUB), :] = hb
        for tj in range(across):
            block = M_BRICK + SUB * tj
            for k, field in enumerate(ALONG_X + (VX, VY, VZ)):
                out[pl.ds(block + k, 1), :] = bricks[field * across + tj, pl.ds(x, 1), :]
            out[pl.ds(block + 6, 1), :] = params[HB * across + tj, pl.ds(x, 1), :]
            out[pl.ds(block + 7, 1), :] = jnp.zeros((1, LANES), jnp.float32)
        out[pl.ds(M_CORNER, 2 * SUB), :] = jnp.zeros((2 * SUB, LANES), jnp.float32)
    sides = ((col_first, 0, 1, 0, 1.0), (col_last, ny - 1, ny - 2, across - 1, -1.0))
    for side, (out, y, inward, tj, sign) in enumerate(sides):
        for t in range(g.xtiles):
            own = SUB * t * ny + y
            hb = col_hb(side, t)
            out[pl.ds(M_P + SUB * t, SUB), :] = water[pl.ds(own, SUB, stride=ny), :]
            out[pl.ds(M_U + SUB * t, SUB), :] = (
                col_u(side, t) - sign * hb * water[pl.ds(SUB * t * ny + inward, SUB, stride=ny), :]
            )
            if first:
                out[pl.ds(M_CONST + SUB * t, SUB), :] = hb
            rows = pl.ds(SUB * t, SUB)
            pieces = [bricks[field * across + tj, rows, :] for field in ALONG_Y + (VX, VY, VZ)]
            pieces.append(params[HB * across + tj, rows, :])
            beside = (1, 0) if t == 0 else (SUB - 2, SUB - 1)
            shear = bricks[XZ * across + tj, rows, :]
            if t == 0 or t == g.xtiles - 1:
                shear = pltpu.roll(shear, 1 if t == 0 else SUB - 1, 0)
            sub = lax.broadcasted_iota(jnp.int32, (SUB, LANES), 0)
            pieces.append(jnp.where(sub == beside[0], shear, bricks[XX * across + tj, rows, :]))
            packed = None
            for k, value in enumerate(pieces):
                moved = roll(value, edge * (k - y % g.yper))
                packed = moved if packed is None else jnp.where(lane >= edge * k, moved, packed)
            out[pl.ds(M_BRICK + SUB * t, SUB), :] = packed
            if t == 0:
                corner = packed
        out[pl.ds(M_CORNER, SUB), :] = jnp.where(row_odd, packed, corner)
        out[pl.ds(M_CORNER + SUB, SUB), :] = jnp.where(row_odd, corner, packed)
    route(row_odd, row_first, row_last, *sends[:2])
    route(col_odd, col_first, col_last, *sends[2:])


def first_kernel(
    g, live_hbm, table_hbm, water_hbm, material_hbm, motion_hbm, kinds_hbm, odd,
    water_out, bricks_out, params, columns, row_far, row_near, col_far, col_near,
    stress, pressure, ux_edge, uy_edge, material_x, material_y, motion, kinds, live, table, sems, *buffers,
):
    nx, ny, across = g.nx, g.ny, g.across
    copies = []

    def fetch(source, target):
        copies.append(pltpu.make_async_copy(source, target, sems.at[len(copies)]))
        copies[-1].start()

    fetch(live_hbm, live)
    fetch(table_hbm, table)
    fetch(kinds_hbm, kinds)
    fetch(motion_hbm, motion)
    fetch(water_hbm.at[0], pressure)
    for side, (x, y) in enumerate(((0, 0), (nx - 1, ny - SUB))):
        fetch(water_hbm.at[1, x], ux_edge.at[side])
        fetch(material_hbm.at[x], material_x.at[side])
        fetch(water_hbm.at[2, :, pl.ds(y, SUB), :], uy_edge.at[side])
        fetch(material_hbm.at[:, pl.ds(y, SUB), :], material_y.at[side])
    lane = lane_ids()
    zero_stress_pads(g, stress)
    copies[0].wait()
    copies[1].wait()
    scales = (0.5, 0.5, 1.0, 1.0, 1.0, 1.0, 0.5, 1.0)
    for c, factor in enumerate(scales):
        column = jnp.zeros((SUB, LANES), jnp.float32)
        for level in range(table.shape[0]):
            column = jnp.where(lane == level, table[level, c], column)
        columns[c] = column * factor
    copies[2].wait()
    copies[3].wait()

    @pl.loop(0, g.xtiles)
    def _(ti):
        for tj in range(across):
            slot = g.slot(ti, tj)
            rows, lanes = g.place(ti, tj)
            alive = live[slot].astype(jnp.float32)
            here = aligned(SUB * ti)
            index = kinds[slot, rows, lanes]
            for c in range(8):
                value = pick(columns[c], index)
                params[c * across + tj, here, :] = value if 3 <= c < 6 else value * alive
            params[ALIVE * across + tj, here, :] = jnp.zeros((SUB, LANES), jnp.float32) + alive
            for field in range(XX, YZ + 1):
                value = motion[slot, field, rows, lanes] * alive
                bricks_out[field * across + tj, here, :] = value
                stress[(field - XX) * across + tj, aligned(PAD + SUB * ti), :] = value

    copies[4].wait()

    @pl.loop(0, nx // 2)
    def _(turn):
        results = []
        for x in (2 * turn, 2 * turn + 1):
            for t in range(g.ytiles):
                results.append((x * ny + SUB * t, pressure[x, pl.ds(SUB * t, SUB), :]))
        for own, value in results:
            water_out[aligned(own), :] = value

    def load_v(field, ti, tj):
        slot = g.slot(ti, tj)
        rows, lanes = g.place(ti, tj)
        return motion[slot, field, rows, lanes] * live[slot].astype(jnp.float32)

    def load_hb(ti, tj):
        return params[HB * across + tj, aligned(SUB * ti), :]

    brick_velocity(g, water_out, stress, load_v, bricks_out, load_hb)
    for copy in copies[5:]:
        copy.wait()

    def rows_of(side, t):
        return side, pl.ds(SUB * t, SUB), side * (SUB - 1)

    edges = (
        lambda side, t: ux_edge[side, pl.ds(SUB * t, SUB), :],
        lambda side, t: pick(columns[0], material_x[side, pl.ds(SUB * t, SUB), :]),
        lambda side, t: uy_edge[(*rows_of(side, t), slice(None))],
        lambda side, t: pick(columns[0], material_y[(*rows_of(side, t), slice(None))]),
    )
    pack(g, water_out, bricks_out, params, edges, odd, buffers, (row_far, row_near, col_far, col_near), True)


def first_water_kernel(
    g, pressure, row_first, row_last, bricks, columns, state, material, water_out, first_same, last_same, hb_water, hk_water, press
):
    nx, ny = g.nx, g.ny
    zero_press_pads(g, press)

    @pl.loop(0, nx // 2)
    def _(turn):
        results = []
        for x in (2 * turn, 2 * turn + 1):
            for t in range(g.ytiles):
                own = x * ny + SUB * t
                index = material[x, pl.ds(SUB * t, SUB), :]
                results.append((x, t, own, pick(columns[0], index), pick(columns[1], index), pressure[aligned(own), :]))
        for x, t, own, hb, hk, value in results:
            hb_water[aligned(own), :] = hb
            hk_water[aligned(own), :] = hk
            press[x + 1, pl.ds(PAD + SUB * t, SUB), :] = value

    water_velocity(
        g,
        (nx // 2, lambda turn: 2 * turn),
        water_out,
        press,
        lambda t, x: bricks[ZZ * g.across + t, pl.ds(x, 1), :],
        lambda x, t: hb_water[aligned(x * ny + SUB * t), :],
        lambda k, x, t: state[k, x, pl.ds(SUB * t, SUB), :],
    )


def edge_water_kernel(
    g, same, row_first, row_last, water, press, stress, hb_water, ux, uy, water_out, first_same, last_same
):
    nx, ny, plane = g.nx, g.ny, g.plane

    def water_layers(layers, ux_row):
        def load_u(k, x, t):
            if k == 1:
                return ux_row(x, t)
            if k == 2:
                return uy[aligned(x * (ny + 2 * PAD) + PAD + SUB * t), :]
            return water[aligned(3 * plane + x * ny + SUB * t), :]

        water_velocity(
            g,
            layers,
            water_out,
            press,
            lambda t, x: stress[(ZZ - XX) * g.across + t, pl.ds(PAD + x, 1), :],
            lambda x, t: hb_water[aligned(x * ny + SUB * t), :],
            load_u,
        )

    def near_face(x, t):
        layer = x - (x // (nx - SUB)) * (nx - 2 * SUB) + 1
        return ux[aligned(layer * ny + SUB * t), :]

    water_layers((SUB, lambda turn: 2 * turn + (turn // (SUB // 2)) * (nx - 2 * SUB)), near_face)
    water_layers(
        ((nx - 2 * SUB) // 2, lambda turn: SUB + 2 * turn),
        lambda x, t: water[aligned(plane + x * ny + SUB * t), :],
    )


def slots_of(g, array, ti):
    slot = g.slot(ti, 0)
    return array.at[pl.ds(slot, 2), :, pl.ds((ti % g.per) * SUB, SUB), :]


class Refs:
    def __init__(self, refs):
        self.refs = list(refs)

    def take(self, count):
        taken, self.refs = self.refs[:count], self.refs[count:]
        return taken


def inner_kernel(g, first, last, *refs):
    refs = Refs(refs)
    water, bricks, memory, params, hb_water, hk_water, odd, col_far, col_near = refs.take(9)
    if not first:
        (const_in,) = refs.take(1)
    uy, speed = refs.take(2)
    if last:
        water_hbm, motion_hbm, memory_hbm = refs.take(3)
    else:
        water_out, press, stress, bricks_out, memory_out = refs.take(5)
    if first:
        (const_out,) = refs.take(1)
    col_before, col_after = refs.take(2)
    if last:
        press_buf, uy_buf, motion_buf, memory_buf, sems = refs.take(5)
    unroute(odd[1] > 0.0, col_far, col_near, col_before, col_after)

    nx, ny, edge, across, plane = g.nx, g.ny, g.edge, g.across, g.plane
    wide = across + 2
    lane = lane_ids()
    top_pick = surface_pick() * edge + (edge - 1)
    py = ny + 2 * PAD
    copies = []

    def send(source, target):
        copies.append(pltpu.make_async_copy(source, target, sems.at[len(copies)]))
        copies[-1].start()

    def part(component, start, stop):
        return pl.ds(component * plane + start * ny, (stop - start) * ny)

    if last:
        send(water.at[part(3, 0, nx), :], water_hbm.at[part(3, 0, nx), :])
        send(water.at[part(1, 1, nx - 1), :], water_hbm.at[part(1, 1, nx - 1), :])
    else:
        zero_press_pads(g, press)
        zero_stress_pads(g, stress)

    @pl.loop(0, nx // 4)
    def _(turn):
        results = []
        for x in (4 * turn + step for step in range(4)):
            for t in range(g.ytiles):
                own = x * ny + SUB * t
                results.append((own, x * py + PAD + SUB * t, water[aligned(2 * plane + own), :]))
        for own, row, value in results:
            uy[aligned(row), :] = value
            if last:
                uy_buf[aligned(own), :] = value

    for side, (ref, y, halo, sign) in enumerate(((col_before, 0, -1, 1.0), (col_after, ny - 1, ny, -1.0))):
        for t in range(g.xtiles):
            own = pl.ds(SUB * t * ny + y, SUB, stride=ny)
            here = pl.ds(SUB * t * py + PAD + y, SUB, stride=py)
            place = pl.ds(32 * side + SUB * t, SUB)
            if first:
                theirs = ref[pl.ds(M_CONST + SUB * t, SUB), :]
                const_out[place, :] = theirs
            else:
                theirs = const_in[place, :]
            value = uy[here, :] + sign * hb_water[own, :] * ref[pl.ds(M_P + SUB * t, SUB), :]
            uy[here, :] = value
            if last:
                uy_buf[own, :] = value
            uy[pl.ds(SUB * t * py + PAD + halo, SUB, stride=py), :] = (
                ref[pl.ds(M_U + SUB * t, SUB), :] - sign * theirs * water[own, :]
            )
    if last:
        send(uy_buf, water_hbm.at[part(2, 0, nx), :])

    for field in (VX, VY, VZ):
        for tj in range(across):
            for ti in range(g.xtiles):
                speed[field * wide + 1 + tj, pl.ds(PAD + SUB * ti, SUB), :] = bricks[field * across + tj, pl.ds(SUB * ti, SUB), :]
    for ref, tj, halo, sign in ((col_before, 0, 0, 1.0), (col_after, across - 1, wide - 1, -1.0)):
        near = 0 if tj == 0 else LANES - edge
        far = LANES - edge - near
        inside = (lane >= near) & (lane < near + edge)
        for ti in range(g.xtiles):
            column = ref[pl.ds(M_BRICK + SUB * ti, SUB), :]
            own_hb = jnp.where(inside, sign * params[HB * across + tj, pl.ds(SUB * ti, SUB), :], 0.0)
            their_hb = sign * roll(column, far - 6 * edge)
            here = pl.ds(PAD + SUB * ti, SUB)
            for c in (VX, VY, VZ):
                key = c * wide + 1 + tj
                speed[key, here, :] = bricks[c * across + tj, pl.ds(SUB * ti, SUB), :] - own_hb * roll(column, near - c * edge)
                own = bricks[ALONG_Y[c] * across + tj, pl.ds(SUB * ti, SUB), :]
                speed[c * wide + halo, here, :] = roll(column, far - (3 + c) * edge) + their_hb * roll(own, far - near)

    store = store_slots(g, motion_buf, memory_buf) if last else store_planes(g, bricks_out, memory_out, stress)

    @pl.loop(1, g.xtiles - 1)
    def _(ti):
        row = pl.multiple_of(SUB * ti, SUB)
        tops = (
            lambda y: water[pl.ds(plane + row * ny + y, SUB, stride=ny), :],
            lambda y: uy[pl.ds(row * py + PAD + y, SUB, stride=py), :],
            lambda y: water[pl.ds(3 * plane + row * ny + y, SUB, stride=ny), :],
        )
        brick_stress(g, ti, first, bricks, memory, params, speed, tops, store)

    if last:
        for ti in range(1, g.xtiles - 1):
            send(slots_of(g, motion_buf, ti), slots_of(g, motion_hbm, ti))
            send(slots_of(g, memory_buf, ti), slots_of(g, memory_hbm, ti))

    def layer(x):
        results = []
        for t in range(g.ytiles):
            own = x * ny + SUB * t
            dx = water[aligned(plane + own + ny), :] - water[aligned(plane + own - ny), :]
            results.append(
                (x, t, own, water_stress(g, x, t, dx, water, uy, speed, hk_water, lane, top_pick))
            )
        return results

    @pl.loop(0, (nx - 4) // 2)
    def _(turn):
        for x, t, own, value in layer(2 + 2 * turn) + layer(3 + 2 * turn):
            if last:
                press_buf[aligned(own), :] = value
            else:
                water_out[aligned(own), :] = value
                press[x + 1, pl.ds(PAD + SUB * t, SUB), :] = value

    if last:
        send(press_buf.at[part(0, 2, nx - 2), :], water_hbm.at[part(0, 2, nx - 2), :])
        for copy in copies:
            copy.wait()


def water_stress(g, x, t, dx, water, uy, speed, hk_water, lane, top_pick):
    row = x * (g.ny + 2 * PAD) + PAD + SUB * t
    own = x * g.ny + SUB * t
    dy = uy[pl.ds(row + 1, SUB), :] - uy[pl.ds(row - 1, SUB), :]
    surface = jnp.broadcast_to(speed[VZ * (g.across + 2) + 1 + t, pl.ds(PAD + x, 1), :], (SUB, LANES))
    dz = water_z(g, water[aligned(3 * g.plane + own), :], pick(surface, top_pick), lane)
    return water[aligned(own), :] - hk_water[aligned(own), :] * (dx + dy + dz)


def edge_kernel(g, first, last, *refs):
    refs = Refs(refs)
    water, bricks, memory, params, hb_water, hk_water, odd, col_far, col_near, row_far, row_near = refs.take(11)
    if not first:
        (const_in,) = refs.take(1)
    (uy,) = refs.take(1)
    refs.take(4 if last else 6)
    (speed,) = refs.take(1)
    if last:
        water_hbm, motion_hbm, memory_hbm = refs.take(3)
    else:
        water_out, press, stress, bricks_out, memory_out = refs.take(5)
        sends = refs.take(4)
    (ux,) = refs.take(1)
    if first:
        (const_out,) = refs.take(1)
    col_before, col_after, row_before, row_after = refs.take(4)
    if last:
        press_buf, motion_buf, memory_buf, sems = refs.take(4)
    else:
        buffers = refs.take(4)
    unroute(odd[1] > 0.0, col_far, col_near, col_before, col_after, (M_BRICK, M_BRICK + g.nx - SUB))
    unroute(odd[0] > 0.0, row_far, row_near, row_before, row_after)
    for ref in (row_before, row_after):
        far, near = ref[pl.ds(M_CORNER, SUB), :], ref[pl.ds(M_CORNER + SUB, SUB), :]
        ref[pl.ds(M_CORNER, SUB), :] = jnp.where(odd[1] > 0.0, near, far)
        ref[pl.ds(M_CORNER + SUB, SUB), :] = jnp.where(odd[1] > 0.0, far, near)

    nx, ny, edge, across, plane = g.nx, g.ny, g.edge, g.across, g.plane
    wide = across + 2
    lane = lane_ids()
    top_pick = surface_pick() * edge + (edge - 1)
    py = ny + 2 * PAD
    copies = []

    def send(source, target):
        copies.append(pltpu.make_async_copy(source, target, sems.at[len(copies)]))
        copies[-1].start()

    @pl.loop(0, SUB)
    def _(x):
        for t in range(g.ytiles):
            own = x * ny + SUB * t
            ux[aligned(ny + own), :] = water[aligned(plane + own), :]
            ux[aligned((1 + SUB) * ny + own), :] = water[aligned(plane + (nx - SUB) * ny + own), :]

    sides = ((row_before, 0, -1, 1.0, 1, 0), (row_after, nx - 1, nx, -1.0, 2 * SUB, 2 * SUB + 1))
    for side, (ref, x, halo, sign, own_layer, halo_layer) in enumerate(sides):
        for t in range(g.ytiles):
            own = pl.ds(x * ny + SUB * t, SUB)
            place = pl.ds(32 * side + SUB * t, SUB)
            if first:
                theirs = ref[pl.ds(M_CONST + SUB * t, SUB), :]
                const_out[place, :] = theirs
            else:
                theirs = const_in[place, :]
            here = pl.ds(own_layer * ny + SUB * t, SUB)
            ux[here, :] = ux[here, :] + sign * hb_water[own, :] * ref[pl.ds(M_P + SUB * t, SUB), :]
            ux[pl.ds(halo_layer * ny + SUB * t, SUB), :] = ref[pl.ds(M_U + SUB * t, SUB), :] - sign * theirs * water[own, :]
    if last:
        for layer, x in ((1, 0), (2 * SUB, nx - 1)):
            send(ux.at[pl.ds(layer * ny, ny), :], water_hbm.at[pl.ds(plane + x * ny, ny), :])

    speed_rows = {}

    def speed_row(key, x):
        if (key, x) not in speed_rows:
            speed_rows[key, x] = speed[key, pl.ds(PAD + x, 1), :]
        return speed_rows[key, x]

    for ref, x, halo, sign, _, _ in sides:
        for tj in range(across):
            block = M_BRICK + SUB * tj
            own_hb = sign * params[HB * across + tj, pl.ds(x, 1), :]
            their_hb = sign * ref[pl.ds(block + 6, 1), :]
            for c in (VX, VY, VZ):
                key = c * wide + 1 + tj
                speed_rows[key, x] = speed_row(key, x) - own_hb * ref[pl.ds(block + c, 1), :]
                speed_rows[key, halo] = (
                    ref[pl.ds(block + 3 + c, 1), :] + their_hb * bricks[ALONG_X[c] * across + tj, pl.ds(x, 1), :]
                )
        edge_row = SUB - 1 if x == 0 else 0
        beside_row = SUB - 2 if x == 0 else 1
        for k, (col_ref, tj, col_halo, col_sign) in enumerate(((col_before, 0, 0, 1.0), (col_after, across - 1, wide - 1, -1.0))):
            near = 0 if tj == 0 else LANES - edge
            far = LANES - edge - near
            inside = (lane[0:1, :] >= near) & (lane[0:1, :] < near + edge)
            corner = ref[pl.ds(M_CORNER + SUB * k + edge_row, 1), :]
            beside = ref[pl.ds(M_CORNER + SUB * k + beside_row, 1), :]
            across_y = [roll_row(corner, near - c * edge) for c in range(3)]
            across_x = (roll_row(corner, far - 7 * edge), roll_row(corner, far), roll_row(beside, far - 7 * edge))
            row_hb = jnp.where(inside, col_sign * ref[pl.ds(M_BRICK + SUB * tj + 6, 1), :], 0.0)
            col_hb = sign * roll_row(col_ref[pl.ds(M_BRICK + x, 1), :], far - 6 * edge)
            for c in (VX, VY, VZ):
                key = c * wide + 1 + tj
                speed_rows[key, halo] = speed_row(key, halo) - row_hb * across_y[c]
                key = c * wide + col_halo
                speed_rows[key, x] = speed_row(key, x) - col_hb * across_x[c]
    for (key, x), value in speed_rows.items():
        speed[key, pl.ds(PAD + x, 1), :] = value

    store = store_slots(g, motion_buf, memory_buf) if last else store_planes(g, bricks_out, memory_out, stress)

    @pl.loop(0, 2)
    def _(turn):
        ti = turn * (g.xtiles - 1)
        row = pl.multiple_of(SUB * ti, SUB)
        above = pl.multiple_of((1 + SUB * turn) * ny, SUB)
        tops = (
            lambda y: ux[pl.ds(above + y, SUB, stride=ny), :],
            lambda y: uy[pl.ds(row * py + PAD + y, SUB, stride=py), :],
            lambda y: water[pl.ds(3 * plane + row * ny + y, SUB, stride=ny), :],
        )
        brick_stress(g, ti, first, bricks, memory, params, speed, tops, store)

    if last:
        for ti in (0, g.xtiles - 1):
            send(slots_of(g, motion_buf, ti), slots_of(g, motion_hbm, ti))
            send(slots_of(g, memory_buf, ti), slots_of(g, memory_hbm, ti))

    for pair, (x, layer) in enumerate(((0, 1), (nx - 2, 2 * SUB - 1))):
        for step in range(2):
            for t in range(g.ytiles):
                dx = (
                    ux[pl.ds((layer + step + 1) * ny + SUB * t, SUB), :] - ux[pl.ds((layer + step - 1) * ny + SUB * t, SUB), :]
                )
                value = water_stress(g, x + step, t, dx, water, uy, speed, hk_water, lane, top_pick)
                if last:
                    press_buf[pl.ds((2 * pair + step) * ny + SUB * t, SUB), :] = value
                else:
                    water_out[pl.ds((x + step) * ny + SUB * t, SUB), :] = value
                    press[x + step + 1, pl.ds(PAD + SUB * t, SUB), :] = value

    if last:
        for pair, x in enumerate((0, nx - 2)):
            send(press_buf.at[pl.ds(2 * pair * ny, 2 * ny), :], water_hbm.at[pl.ds(x * ny, 2 * ny), :])
        for copy in copies:
            copy.wait()
    else:
        def load_v(field, ti, tj):
            return speed[field * wide + 1 + tj, aligned(PAD + SUB * ti), :]

        def load_hb(ti, tj):
            return params[HB * across + tj, aligned(SUB * ti), :]

        def column(side, t):
            return pl.ds(SUB * t * ny + side * (ny - 1), SUB, stride=ny)

        faces = (
            lambda side, t: ux[pl.ds((1 + side * (2 * SUB - 1)) * ny + SUB * t, SUB), :],
            lambda side, t: hb_water[pl.ds(side * (nx - 1) * ny + SUB * t, SUB), :],
            lambda side, t: uy[pl.ds(SUB * t * py + PAD + side * (ny - 1), SUB, stride=py), :],
            lambda side, t: hb_water[column(side, t), :],
        )
        brick_velocity(g, water_out, stress, load_v, bricks_out, load_hb)
        pack(g, water_out, bricks_out, params, faces, odd, buffers, sends, False)


def swap(value, axis, start):
    pairs = [(i, i + 1) for i in range(start, lax.axis_size(axis) - 1, 2)]
    return lax.ppermute(value, axis, pairs + [(j, i) for i, j in pairs])


def exchange(sends):
    row_far, row_near, col_far, col_near = sends
    col_far = swap(col_far, "col", 1)
    col_near = swap(col_near, "col", 0)

    def with_corners(message, start):
        corners = jnp.concatenate([col_far[start : start + SUB], col_near[start : start + SUB]])
        return lax.dynamic_update_slice(message, corners, (M_CORNER, 0))

    row_far = swap(with_corners(row_far, M_CORNER), "row", 1)
    row_near = swap(with_corners(row_near, M_CORNER + SUB), "row", 0)
    return col_far, col_near, row_far, row_near


def body(
    brick_velocity_stress,
    brick_relaxation_memory,
    brick_cell_material,
    brick_live,
    water_state,
    water_material,
    material_table,
):
    _, nx, ny, nz = water_state.shape
    g = Grid(nx, ny, brick_cell_material.shape[1])
    across, plane = g.across, g.plane

    def f32(*shape):
        return jax.ShapeDtypeStruct(shape, jnp.float32)

    vmem = pl.BlockSpec(memory_space=pltpu.VMEM)
    hbm = pl.BlockSpec(memory_space=pltpu.HBM)
    params = pltpu.CompilerParams(vmem_limit_bytes=24 * 1024 * 1024)
    def messages(first):
        return [f32(M_CONST + (32 if first else 0), LANES)] * 4

    def buffer(*shape):
        return pltpu.VMEM(shape, jnp.float32)

    def held(*values):
        return [pltpu.with_memory_space_constraint(value, pltpu.VMEM) for value in values]

    def pinned(*values):
        return [pltpu.with_memory_space_constraint(value, pltpu.HBM) for value in values]

    def message_buffers(count, first):
        return [buffer(M_CONST + (32 if first else 0), LANES)] * count

    odd = jnp.stack([lax.axis_index(axis) & 1 for axis in ("row", "col")]).astype(jnp.float32)
    odd = jnp.broadcast_to(odd[:, None, None], (2, SUB, LANES))
    press = buffer(nx + 2, ny + 2 * PAD, nz)
    stress = buffer(6 * across, nx + 2 * PAD, LANES)
    work = pl.CostEstimate(flops=20_000_000, bytes_accessed=8_000_000, transcendentals=0)
    water, bricks, coefficients, columns, *sends = pl.pallas_call(
        functools.partial(first_kernel, g),
        out_shape=[
            buffer(4 * plane, nz), f32(9 * across, nx, LANES), f32(9 * across, nx, LANES), f32(8, SUB, LANES),
        ] + messages(True),
        in_specs=[hbm] * 6 + [vmem],
        out_specs=[vmem] * 8,
        scratch_shapes=[
            stress,
            buffer(nx, ny, nz),
            buffer(2, ny, nz),
            buffer(2, nx, SUB, nz),
            pltpu.VMEM((2, ny, nz), jnp.int32),
            pltpu.VMEM((2, nx, SUB, nz), jnp.int32),
            pltpu.VMEM(brick_velocity_stress.shape, jnp.float32),
            pltpu.VMEM(brick_cell_material.shape, jnp.int32),
            pltpu.SMEM(brick_live.shape, jnp.int32),
            pltpu.SMEM(material_table.shape, jnp.float32),
            pltpu.SemaphoreType.DMA((13,)),
        ]
        + message_buffers(4, True),
        compiler_params=params,
        name="first_bricks",
    )(*pinned(brick_live, material_table, water_state, water_material, brick_velocity_stress, brick_cell_material), odd)

    def passed(*messages):
        return [buffer(*message.shape) for message in messages]

    water, sends[0], sends[1], hb_water, hk_water = pl.pallas_call(
        functools.partial(first_water_kernel, g),
        out_shape=[buffer(4 * plane, nz)] + passed(*sends[:2]) + [f32(plane, nz), f32(plane, nz)],
        in_specs=[vmem] * 7,
        out_specs=[vmem] * 5,
        input_output_aliases={0: 0, 1: 1, 2: 2},
        scratch_shapes=[press],
        compiler_params=params,
        cost_estimate=work,
        name="first_water",
    )(*held(water, *sends[:2], bricks, columns, water_state, water_material))
    memory = brick_relaxation_memory
    col_const, row_const = (), ()
    uy_shape = (nx * (ny + 2 * PAD), nz)
    speed_shape = (3 * (across + 2), nx + 2 * PAD, LANES)
    ux_buffer = buffer((2 * SUB + 2) * ny, nz)
    slot_buffers = [
        pltpu.VMEM(brick_velocity_stress.shape, jnp.float32),
        pltpu.VMEM(brick_relaxation_memory.shape, jnp.float32),
    ]
    finals = [f32(4 * plane, nz), f32(*brick_velocity_stress.shape), f32(*brick_relaxation_memory.shape)]
    planes = [
        buffer(4 * plane, nz),
        buffer(nx + 2, ny + 2 * PAD, nz),
        buffer(6 * across, nx + 2 * PAD, LANES),
        buffer(9 * across, nx, LANES),
        buffer(18 * across, nx, LANES),
    ]
    for step in range(STEPS):
        first, last = step == 0, step == STEPS - 1
        *columns, row_far, row_near = exchange(sends)
        state = (water, bricks, memory, coefficients, hb_water, hk_water, odd)
        shapes = finals if last else planes
        spaces = [hbm if last else vmem] * len(shapes)
        inner = pl.pallas_call(
            functools.partial(inner_kernel, g, first, last),
            out_shape=[buffer(*uy_shape), buffer(*speed_shape)] + shapes + ([buffer(64, LANES)] if first else []),
            in_specs=[vmem] * (9 + len(col_const)),
            out_specs=[vmem] * 2 + spaces + ([vmem] if first else []),
            scratch_shapes=message_buffers(2, first)
            + ([buffer(plane, nz), buffer(plane, nz)] + slot_buffers + [pltpu.SemaphoreType.DMA((8,))] if last else []),
            compiler_params=params,
            cost_estimate=work,
            name="inner",
        )(*held(*state), *columns, *col_const)
        if first:
            col_const = (inner[-1],)
            inner = inner[:-1]
        uy, *partial = inner
        count = 11 + len(row_const) + 1
        results = pl.pallas_call(
            functools.partial(edge_kernel, g, first, last),
            out_shape=[buffer(*speed_shape)]
            + shapes
            + ([] if last else messages(False) + [ux_buffer])
            + ([buffer(64, LANES)] if first else []),
            in_specs=[vmem] * (count + 1) + spaces,
            out_specs=[vmem] + spaces + [vmem] * (0 if last else 5) + ([vmem] if first else []),
            input_output_aliases={count + k: k for k in range(1 + len(shapes))},
            scratch_shapes=([ux_buffer] if last else [])
            + message_buffers(4, first)
            + (
                [buffer(4 * ny, nz)] + slot_buffers + [pltpu.SemaphoreType.DMA((8,))]
                if last
                else message_buffers(4, False)
            ),
            compiler_params=params,
            name="edges",
        )(*held(*state), *columns, row_far, row_near, *row_const, *held(uy), *(held(partial[0]) + (list(partial[1:]) if last else held(*partial[1:]))))
        if last:
            return results[2], results[3], results[1].reshape(water_state.shape)
        old_water = water
        _, water, pressed, stressed, bricks, memory = results[:6]
        sends = list(results[6:10])
        if first:
            row_const = (results[11],)
        water, sends[0], sends[1] = pl.pallas_call(
            functools.partial(edge_water_kernel, g),
            out_shape=[buffer(4 * plane, nz)] + passed(*sends[:2]),
            in_specs=[vmem] * 9,
            out_specs=[vmem] * 3,
            input_output_aliases={0: 0, 1: 1, 2: 2},
            compiler_params=params,
            cost_estimate=work,
            name="edge_water",
        )(*held(water, *sends[:2], old_water, pressed, stressed, hb_water, results[10], uy))


def solution(mesh):
    return jax.shard_map(
        body,
        mesh=mesh,
        in_specs=(
            P(("row", "col"), None, None, None),
            P(("row", "col"), None, None, None),
            P(("row", "col"), None, None),
            P(("row", "col")),
            P(None, "row", "col", None),
            P("row", "col", None),
            P(),
        ),
        out_specs=(
            P(("row", "col"), None, None, None),
            P(("row", "col"), None, None, None),
            P(None, "row", "col", None),
        ),
        check_vma=False,
    )
```

```python
import functools

import jax
import jax.numpy as jnp
from jax import lax
from jax.experimental import pallas as pl
from jax.experimental.pallas import tpu as pltpu
from jax.sharding import PartitionSpec as P

STEPS = 3
LANES = 128
SUB = 8
PAD = 8
VX, VY, VZ, XX, YY, ZZ, XY, XZ, YZ = range(9)
HB, LAME, SHEAR, RETAIN, SPRING_LAME, SPRING_SHEAR, ALIVE = 0, 1, 2, 3, 6, 7, 8
ALONG_X = (XX, XY, XZ)
ALONG_Y = (XY, YY, YZ)
ALONG_Z = (XZ, YZ, ZZ)
M_P, M_U, M_BRICK, M_CORNER, M_RELAY = 0, 32, 64, 92, 96
ROW_CONST, COL_CONST = 96, 104


def lane_ids():
    return lax.broadcasted_iota(jnp.int32, (SUB, LANES), 1)


def roll(value, shift):
    shift = shift % LANES
    return value if shift == 0 else pltpu.roll(value, shift, 1)


def roll_row(row, shift):
    shift = shift % LANES
    if shift == 0:
        return row
    return pltpu.roll(jnp.broadcast_to(row, (SUB, LANES)), shift, 1)[0:1, :]


def pick(values, indices):
    return jnp.take_along_axis(values, indices, axis=1, mode="promise_in_bounds")


def aligned(start, size=SUB):
    return pl.ds(start if isinstance(start, int) else pl.multiple_of(start, SUB), size)


class Grid:
    def __init__(self, nx, ny, edge):
        self.nx, self.ny, self.edge = nx, ny, edge
        self.plane = nx * ny
        self.across = ny * edge // LANES
        self.yper = LANES // edge
        self.half = self.across // 2
        self.xtiles, self.ytiles = nx // SUB, ny // SUB
        self.per = edge // SUB

    def slot(self, ti, tj):
        return 2 * (ti // self.per) + tj // self.half

    def place(self, ti, tj):
        return aligned((ti % self.per) * SUB), pl.ds((tj % self.half) * LANES, LANES)


def zero_press_pads(g, press):
    zero = jnp.zeros((SUB, LANES), jnp.float32)
    for t in range(g.ytiles):
        press[0, pl.ds(PAD + SUB * t, SUB), :] = zero
        press[g.nx + 1, pl.ds(PAD + SUB * t, SUB), :] = zero

    @pl.loop(0, g.nx // SUB)
    def _(turn):
        for step in range(SUB):
            x = SUB * turn + step + 1
            press[x, pl.ds(0, SUB), :] = zero
            press[x, pl.ds(PAD + g.ny, SUB), :] = zero


def zero_stress_pads(g, stress):
    zero = jnp.zeros((SUB, LANES), jnp.float32)
    for field in ALONG_X:
        for tj in range(g.across):
            key = (field - XX) * g.across + tj
            stress[key, pl.ds(0, SUB), :] = zero
            stress[key, pl.ds(PAD + g.nx, SUB), :] = zero


def shifted_top(g, load, ys, lane):
    top = None
    for k, y in enumerate(ys):
        value = roll(load(y), g.edge * k + g.edge - 1)
        top = value if top is None else jnp.where(lane >= g.edge * k, value, top)
    return top


def along_y(g, rolled, tj, lane):
    zero = jnp.zeros((SUB, LANES), jnp.float32)
    after = rolled[tj + 1][1] if tj + 1 < len(rolled) else zero
    before = rolled[tj - 1][0] if tj > 0 else zero
    ahead = jnp.where(lane < LANES - g.edge, rolled[tj][1], after)
    behind = jnp.where(lane >= g.edge, rolled[tj][0], before)
    return ahead - behind


def along_z(g, value, beyond, depth):
    zero = jnp.zeros((SUB, LANES), jnp.float32)
    return jnp.where(depth == g.edge - 1, beyond, roll(value, -1)) - jnp.where(depth == 0, zero, roll(value, 1))


def water_z(g, value, below, lane):
    zero = jnp.zeros((SUB, LANES), jnp.float32)
    return jnp.where(lane == LANES - 1, zero, roll(value, -1)) - jnp.where(lane == 0, below, roll(value, 1))


def surface_pick():
    return lax.broadcasted_iota(jnp.int32, (SUB, LANES), 0)


def water_velocity(g, layers, water_out, press, surface_row, load_hb, load_u):
    lane = lane_ids()
    top_pick = surface_pick() * g.edge + (g.edge - 1)

    def water_layer(x):
        results = []
        for t in range(g.ytiles):
            rows = pl.ds(PAD + SUB * t, SUB)
            here = press[x + 1, rows, :]
            dx = press[x + 2, rows, :] - press[x, rows, :]
            dy = press[x + 1, pl.ds(PAD + SUB * t + 1, SUB), :] - press[x + 1, pl.ds(PAD + SUB * t - 1, SUB), :]
            surface = jnp.broadcast_to(surface_row(t, x), (SUB, LANES))
            dz = water_z(g, here, -pick(surface, top_pick), lane)
            own = x * g.ny + SUB * t
            hb = load_hb(x, t)
            for k, change in ((1, dx), (2, dy), (3, dz)):
                results.append((k * g.plane + own, load_u(k, x, t) - hb * change))
        return results

    turns, layer = layers

    @pl.loop(0, turns)
    def _(turn):
        x = layer(turn)
        for row, value in water_layer(x) + water_layer(x + 1):
            water_out[aligned(row), :] = value


def brick_velocity(g, water_out, stress, load_v, bricks_out, load_hb):
    lane = lane_ids()
    depth = lane % g.edge
    zero = jnp.zeros((SUB, LANES), jnp.float32)
    across, ny = g.across, g.ny

    @pl.loop(0, g.xtiles)
    def _(ti):
        row = pl.multiple_of(SUB * ti, SUB)
        here = pl.ds(pl.multiple_of(row + PAD, SUB), SUB)

        def load(field, tj):
            return stress[(field - XX) * across + tj, here, :]

        def along_x(field, tj):
            key = (field - XX) * across + tj
            return stress[key, pl.ds(row + PAD + 1, SUB), :] - stress[key, pl.ds(row + PAD - 1, SUB), :]

        results = []
        for target, fx, fy, fz in zip((VX, VY, VZ), ALONG_X, ALONG_Y, ALONG_Z):
            rolled = [(roll(value, g.edge), roll(value, -g.edge)) for value in (load(fy, tj) for tj in range(across))]
            for tj in range(across):
                beyond = zero
                if fz == ZZ:
                    ys = [g.yper * tj + k for k in range(g.yper)]
                    beyond = -shifted_top(g, lambda y: water_out[pl.ds(row * ny + y, SUB, stride=ny), :], ys, lane)
                change = along_x(fx, tj) + along_y(g, rolled, tj, lane) + along_z(g, load(fz, tj), beyond, depth)
                results.append((target * across + tj, load_v(target, ti, tj) + load_hb(ti, tj) * change))
        for key, value in results:
            bricks_out[key, pl.ds(row, SUB), :] = value


def brick_stress(g, ti, first, bricks, memory, params, speed, tops, store):
    edge, across = g.edge, g.across
    wide = across + 2
    lane = lane_ids()
    depth = lane % edge
    row = SUB * ti if isinstance(ti, int) else pl.multiple_of(SUB * ti, SUB)
    here, inner = aligned(row), aligned(row + PAD)
    rolled = []
    for field in (VX, VY, VZ):
        values = [speed[field * wide + tj, inner, :] for tj in range(wide)]
        rolled.append([(roll(value, edge), roll(value, -edge)) for value in values])
    for tj in range(across):
        ys = [g.yper * tj + k for k in range(g.yper)]
        dx, dy, dz, speeds = [], [], [], []
        for field in (VX, VY, VZ):
            key = field * wide + 1 + tj
            value = speed[key, inner, :]
            speeds.append(value)
            dx.append(speed[key, pl.ds(row + PAD + 1, SUB), :] - speed[key, pl.ds(row + PAD - 1, SUB), :])
            dy.append(along_y(g, rolled[field], tj + 1, lane))
            dz.append(along_z(g, value, shifted_top(g, tops[field], ys, lane), depth))
        strain = [dx[0], dy[1], dz[2], dy[0] + dx[1], dz[0] + dx[2], dz[1] + dy[2]]
        dilation = strain[0] + strain[1] + strain[2]

        def param(c):
            return params[c * across + tj, here, :]

        lame, shear = param(LAME) * dilation, param(SHEAR)
        spring_lame, spring_shear = param(SPRING_LAME) * dilation, param(SPRING_SHEAR)
        retain = [param(RETAIN + l) for l in range(3)]
        half_shear, half_spring = 0.5 * shear, 0.5 * spring_shear
        slot = g.slot(ti, tj)
        rows, lanes = g.place(ti, tj)
        if first:
            alive = param(ALIVE)
        stresses, memories = [], {}
        for comp in range(6):
            if comp < 3:
                elastic = shear * strain[comp] + lame
                relaxed = spring_shear * strain[comp] + spring_lame
            else:
                elastic = half_shear * strain[comp]
                relaxed = half_spring * strain[comp]
            summed = None
            for l in range(3):
                place = 6 * l + comp
                if first:
                    old = memory[slot, place, rows, lanes] * alive
                else:
                    old = memory[place * across + tj, here, :]
                new = relaxed + retain[l] * (old - relaxed)
                memories[place] = new
                summed = new if summed is None else summed + new
            stresses.append(bricks[(XX + comp) * across + tj, here, :] + elastic - summed)
        store(ti, tj, here, inner, speeds, stresses, memories)


def store_planes(g, bricks_out, memory_out, stress):
    def store(ti, tj, here, inner, speeds, stresses, memories):
        for place, value in memories.items():
            memory_out[place * g.across + tj, here, :] = value
        for comp, value in enumerate(stresses):
            bricks_out[(XX + comp) * g.across + tj, here, :] = value
            stress[comp * g.across + tj, inner, :] = value

    return store


def store_slots(g, motion, memory):
    def store(ti, tj, here, inner, speeds, stresses, memories):
        slot = g.slot(ti, tj)
        rows, lanes = g.place(ti, tj)
        for place, value in memories.items():
            memory[slot, place, rows, lanes] = value
        for field, value in enumerate(speeds + stresses):
            motion[slot, field, rows, lanes] = value

    return store


def route(odd, first, last, out_far, out_near):
    for start in range(0, out_far.shape[0], SUB):
        rows = pl.ds(start, SUB)
        one, other = first[rows, :], last[rows, :]
        out_far[rows, :] = jnp.where(odd, other, one)
        out_near[rows, :] = jnp.where(odd, one, other)


def unroute(odd, from_far, from_near, before, after, starts=None):
    for start in starts or range(0, from_far.shape[0], SUB):
        rows = pl.ds(start, SUB)
        far, near = from_far[rows, :], from_near[rows, :]
        before[rows, :] = jnp.where(odd, near, far)
        after[rows, :] = jnp.where(odd, far, near)


def pack(g, water, bricks, params, edges, odd, buffers, sends, first):
    row_u, row_hb, col_u, col_hb = edges
    row_first, row_last, col_first, col_last = buffers
    row_odd, col_odd = odd[0] > 0.0, odd[1] > 0.0
    nx, ny, across, edge = g.nx, g.ny, g.across, g.edge
    lane = lane_ids()
    for side, (out, x, inward, sign) in enumerate(((row_first, 0, 1, 1.0), (row_last, nx - 1, nx - 2, -1.0))):
        for t in range(g.ytiles):
            own = x * ny + SUB * t
            hb = row_hb(side, t)
            out[pl.ds(M_P + SUB * t, SUB), :] = water[pl.ds(own, SUB), :]
            out[pl.ds(M_U + SUB * t, SUB), :] = row_u(side, t) - sign * hb * water[pl.ds(inward * ny + SUB * t, SUB), :]
            if first:
                out[pl.ds(ROW_CONST + SUB * t, SUB), :] = hb
        for tj in range(across):
            for k, field in enumerate(ALONG_X + (VX, VY, VZ)):
                out[pl.ds(M_BRICK + k * across + tj, 1), :] = bricks[field * across + tj, pl.ds(x, 1), :]
            out[pl.ds(M_BRICK + 6 * across + tj, 1), :] = params[HB * across + tj, pl.ds(x, 1), :]
        out[pl.ds(M_CORNER, 4), :] = jnp.zeros((4, LANES), jnp.float32)
    sides = ((col_first, 0, 1, 0, 1.0), (col_last, ny - 1, ny - 2, across - 1, -1.0))
    for side, (out, y, inward, tj, sign) in enumerate(sides):
        for t in range(g.xtiles):
            own = SUB * t * ny + y
            hb = col_hb(side, t)
            out[pl.ds(M_P + SUB * t, SUB), :] = water[pl.ds(own, SUB, stride=ny), :]
            out[pl.ds(M_U + SUB * t, SUB), :] = (
                col_u(side, t) - sign * hb * water[pl.ds(SUB * t * ny + inward, SUB, stride=ny), :]
            )
            if first:
                out[pl.ds(COL_CONST + SUB * t, SUB), :] = hb
            rows = pl.ds(SUB * t, SUB)
            pieces = [bricks[field * across + tj, rows, :] for field in ALONG_Y + (VX, VY, VZ)]
            pieces.append(params[HB * across + tj, rows, :])
            beside = (1, 0) if t == 0 else (SUB - 2, SUB - 1)
            shear = bricks[XZ * across + tj, rows, :]
            if t == 0 or t == g.xtiles - 1:
                shear = pltpu.roll(shear, 1 if t == 0 else SUB - 1, 0)
            sub = lax.broadcasted_iota(jnp.int32, (SUB, LANES), 0)
            pieces.append(jnp.where(sub == beside[0], shear, bricks[XX * across + tj, rows, :]))
            packed = None
            for k, value in enumerate(pieces):
                moved = roll(value, edge * (k - y % g.yper))
                packed = moved if packed is None else jnp.where(lane >= edge * k, moved, packed)
            out[pl.ds(M_BRICK + SUB * t, SUB), :] = packed
            if t == 0:
                corner = packed
        one = (corner[0:1, :], corner[1:2, :])
        other = (packed[SUB - 1 : SUB, :], packed[SUB - 2 : SUB - 1, :])
        out[pl.ds(M_RELAY, SUB), :] = jnp.zeros((SUB, LANES), jnp.float32)
        for k in range(2):
            out[pl.ds(M_RELAY + k, 1), :] = jnp.where(row_odd[0:1, :], other[k], one[k])
            out[pl.ds(M_RELAY + 2 + k, 1), :] = jnp.where(row_odd[0:1, :], one[k], other[k])
    route(row_odd, row_first, row_last, *sends[:2])
    route(col_odd, col_first, col_last, *sends[2:])


def first_kernel(
    g, live_hbm, table_hbm, water_hbm, material_hbm, motion_hbm, kinds_hbm, odd,
    water_out, bricks_out, params, columns, row_far, row_near, col_far, col_near,
    stress, pressure, ux_edge, uy_edge, material_x, material_y, motion, kinds, live, table, sems, *buffers,
):
    nx, ny, across = g.nx, g.ny, g.across
    copies = []

    def fetch(source, target):
        copies.append(pltpu.make_async_copy(source, target, sems.at[len(copies)]))
        copies[-1].start()

    fetch(live_hbm, live)
    fetch(table_hbm, table)
    fetch(kinds_hbm, kinds)
    fetch(motion_hbm, motion)
    fetch(water_hbm.at[0], pressure)
    for side, (x, y) in enumerate(((0, 0), (nx - 1, ny - SUB))):
        fetch(water_hbm.at[1, x], ux_edge.at[side])
        fetch(material_hbm.at[x], material_x.at[side])
        fetch(water_hbm.at[2, :, pl.ds(y, SUB), :], uy_edge.at[side])
        fetch(material_hbm.at[:, pl.ds(y, SUB), :], material_y.at[side])
    lane = lane_ids()
    zero_stress_pads(g, stress)
    copies[0].wait()
    copies[1].wait()
    scales = (0.5, 0.5, 1.0, 1.0, 1.0, 1.0, 0.5, 1.0)
    for c, factor in enumerate(scales):
        column = jnp.zeros((SUB, LANES), jnp.float32)
        for level in range(table.shape[0]):
            column = jnp.where(lane == level, table[level, c], column)
        columns[c] = column * factor
    copies[2].wait()
    copies[3].wait()

    @pl.loop(0, g.xtiles)
    def _(ti):
        for tj in range(across):
            slot = g.slot(ti, tj)
            rows, lanes = g.place(ti, tj)
            alive = live[slot].astype(jnp.float32)
            here = aligned(SUB * ti)
            index = kinds[slot, rows, lanes]
            for c in range(8):
                value = pick(columns[c], index)
                params[c * across + tj, here, :] = value if 3 <= c < 6 else value * alive
            params[ALIVE * across + tj, here, :] = jnp.zeros((SUB, LANES), jnp.float32) + alive
            for field in range(XX, YZ + 1):
                value = motion[slot, field, rows, lanes] * alive
                bricks_out[field * across + tj, here, :] = value
                stress[(field - XX) * across + tj, aligned(PAD + SUB * ti), :] = value

    copies[4].wait()

    @pl.loop(0, nx // 2)
    def _(turn):
        results = []
        for x in (2 * turn, 2 * turn + 1):
            for t in range(g.ytiles):
                results.append((x * ny + SUB * t, pressure[x, pl.ds(SUB * t, SUB), :]))
        for own, value in results:
            water_out[aligned(own), :] = value

    def load_v(field, ti, tj):
        slot = g.slot(ti, tj)
        rows, lanes = g.place(ti, tj)
        return motion[slot, field, rows, lanes] * live[slot].astype(jnp.float32)

    def load_hb(ti, tj):
        return params[HB * across + tj, aligned(SUB * ti), :]

    brick_velocity(g, water_out, stress, load_v, bricks_out, load_hb)
    for copy in copies[5:]:
        copy.wait()

    def rows_of(side, t):
        return side, pl.ds(SUB * t, SUB), side * (SUB - 1)

    edges = (
        lambda side, t: ux_edge[side, pl.ds(SUB * t, SUB), :],
        lambda side, t: pick(columns[0], material_x[side, pl.ds(SUB * t, SUB), :]),
        lambda side, t: uy_edge[(*rows_of(side, t), slice(None))],
        lambda side, t: pick(columns[0], material_y[(*rows_of(side, t), slice(None))]),
    )
    pack(g, water_out, bricks_out, params, edges, odd, buffers, (row_far, row_near, col_far, col_near), True)


def first_water_kernel(
    g, pressure, row_first, row_last, bricks, columns, state, material, water_out, first_same, last_same, hb_water, hk_water, press
):
    nx, ny = g.nx, g.ny
    zero_press_pads(g, press)

    @pl.loop(0, nx // 2)
    def _(turn):
        results = []
        for x in (2 * turn, 2 * turn + 1):
            for t in range(g.ytiles):
                own = x * ny + SUB * t
                index = material[x, pl.ds(SUB * t, SUB), :]
                results.append((x, t, own, pick(columns[0], index), pick(columns[1], index), pressure[aligned(own), :]))
        for x, t, own, hb, hk, value in results:
            hb_water[aligned(own), :] = hb
            hk_water[aligned(own), :] = hk
            press[x + 1, pl.ds(PAD + SUB * t, SUB), :] = value

    water_velocity(
        g,
        (nx // 2, lambda turn: 2 * turn),
        water_out,
        press,
        lambda t, x: bricks[ZZ * g.across + t, pl.ds(x, 1), :],
        lambda x, t: hb_water[aligned(x * ny + SUB * t), :],
        lambda k, x, t: state[k, x, pl.ds(SUB * t, SUB), :],
    )


def edge_water_kernel(
    g, same, row_first, row_last, water, press, stress, hb_water, ux, uy, water_out, first_same, last_same
):
    nx, ny, plane = g.nx, g.ny, g.plane

    def water_layers(layers, ux_row):
        def load_u(k, x, t):
            if k == 1:
                return ux_row(x, t)
            if k == 2:
                return uy[aligned(x * (ny + 2 * PAD) + PAD + SUB * t), :]
            return water[aligned(3 * plane + x * ny + SUB * t), :]

        water_velocity(
            g,
            layers,
            water_out,
            press,
            lambda t, x: stress[(ZZ - XX) * g.across + t, pl.ds(PAD + x, 1), :],
            lambda x, t: hb_water[aligned(x * ny + SUB * t), :],
            load_u,
        )

    def near_face(x, t):
        layer = x - (x // (nx - SUB)) * (nx - 2 * SUB) + 1
        return ux[aligned(layer * ny + SUB * t), :]

    water_layers((SUB, lambda turn: 2 * turn + (turn // (SUB // 2)) * (nx - 2 * SUB)), near_face)
    water_layers(
        ((nx - 2 * SUB) // 2, lambda turn: SUB + 2 * turn),
        lambda x, t: water[aligned(plane + x * ny + SUB * t), :],
    )


def slots_of(g, array, ti):
    slot = g.slot(ti, 0)
    return array.at[pl.ds(slot, 2), :, pl.ds((ti % g.per) * SUB, SUB), :]


class Refs:
    def __init__(self, refs):
        self.refs = list(refs)

    def take(self, count):
        taken, self.refs = self.refs[:count], self.refs[count:]
        return taken


def inner_kernel(g, first, last, *refs):
    refs = Refs(refs)
    water, bricks, memory, params, hb_water, hk_water, odd, col_far, col_near = refs.take(9)
    if not first:
        (const_in,) = refs.take(1)
    uy, speed = refs.take(2)
    if last:
        water_hbm, press_buf, motion_buf, memory_buf = refs.take(4)
    else:
        water_out, press, stress, bricks_out, memory_out = refs.take(5)
    if first:
        (const_out,) = refs.take(1)
    col_before, col_after = refs.take(2)
    if last:
        uy_buf, sems = refs.take(2)
    unroute(odd[1] > 0.0, col_far, col_near, col_before, col_after)

    nx, ny, edge, across, plane = g.nx, g.ny, g.edge, g.across, g.plane
    wide = across + 2
    lane = lane_ids()
    top_pick = surface_pick() * edge + (edge - 1)
    py = ny + 2 * PAD
    copies = []

    def send(source, target):
        copies.append(pltpu.make_async_copy(source, target, sems.at[len(copies)]))
        copies[-1].start()

    def part(component, start, stop):
        return pl.ds(component * plane + start * ny, (stop - start) * ny)

    if last:
        send(water.at[part(3, 0, nx), :], water_hbm.at[part(3, 0, nx), :])
        send(water.at[part(1, 1, nx - 1), :], water_hbm.at[part(1, 1, nx - 1), :])
    else:
        zero_press_pads(g, press)
        zero_stress_pads(g, stress)

    @pl.loop(0, nx // 4)
    def _(turn):
        results = []
        for x in (4 * turn + step for step in range(4)):
            for t in range(g.ytiles):
                own = x * ny + SUB * t
                results.append((own, x * py + PAD + SUB * t, water[aligned(2 * plane + own), :]))
        for own, row, value in results:
            uy[aligned(row), :] = value
            if last:
                uy_buf[aligned(own), :] = value

    for side, (ref, y, halo, sign) in enumerate(((col_before, 0, -1, 1.0), (col_after, ny - 1, ny, -1.0))):
        for t in range(g.xtiles):
            own = pl.ds(SUB * t * ny + y, SUB, stride=ny)
            here = pl.ds(SUB * t * py + PAD + y, SUB, stride=py)
            place = pl.ds(32 * side + SUB * t, SUB)
            if first:
                theirs = ref[pl.ds(COL_CONST + SUB * t, SUB), :]
                const_out[place, :] = theirs
            else:
                theirs = const_in[place, :]
            value = uy[here, :] + sign * hb_water[own, :] * ref[pl.ds(M_P + SUB * t, SUB), :]
            uy[here, :] = value
            if last:
                uy_buf[own, :] = value
            uy[pl.ds(SUB * t * py + PAD + halo, SUB, stride=py), :] = (
                ref[pl.ds(M_U + SUB * t, SUB), :] - sign * theirs * water[own, :]
            )
    if last:
        send(uy_buf, water_hbm.at[part(2, 0, nx), :])

    for field in (VX, VY, VZ):
        for tj in range(across):
            for ti in range(g.xtiles):
                speed[field * wide + 1 + tj, pl.ds(PAD + SUB * ti, SUB), :] = bricks[field * across + tj, pl.ds(SUB * ti, SUB), :]
    for ref, tj, halo, sign in ((col_before, 0, 0, 1.0), (col_after, across - 1, wide - 1, -1.0)):
        near = 0 if tj == 0 else LANES - edge
        far = LANES - edge - near
        inside = (lane >= near) & (lane < near + edge)
        for ti in range(g.xtiles):
            column = ref[pl.ds(M_BRICK + SUB * ti, SUB), :]
            own_hb = jnp.where(inside, sign * params[HB * across + tj, pl.ds(SUB * ti, SUB), :], 0.0)
            their_hb = sign * roll(column, far - 6 * edge)
            here = pl.ds(PAD + SUB * ti, SUB)
            for c in (VX, VY, VZ):
                key = c * wide + 1 + tj
                speed[key, here, :] = bricks[c * across + tj, pl.ds(SUB * ti, SUB), :] - own_hb * roll(column, near - c * edge)
                own = bricks[ALONG_Y[c] * across + tj, pl.ds(SUB * ti, SUB), :]
                speed[c * wide + halo, here, :] = roll(column, far - (3 + c) * edge) + their_hb * roll(own, far - near)

    store = store_slots(g, motion_buf, memory_buf) if last else store_planes(g, bricks_out, memory_out, stress)

    @pl.loop(1, g.xtiles - 1)
    def _(ti):
        row = pl.multiple_of(SUB * ti, SUB)
        tops = (
            lambda y: water[pl.ds(plane + row * ny + y, SUB, stride=ny), :],
            lambda y: uy[pl.ds(row * py + PAD + y, SUB, stride=py), :],
            lambda y: water[pl.ds(3 * plane + row * ny + y, SUB, stride=ny), :],
        )
        brick_stress(g, ti, first, bricks, memory, params, speed, tops, store)

    def layer(x):
        results = []
        for t in range(g.ytiles):
            own = x * ny + SUB * t
            dx = water[aligned(plane + own + ny), :] - water[aligned(plane + own - ny), :]
            results.append(
                (x, t, own, water_stress(g, x, t, dx, water, uy, speed, hk_water, lane, top_pick))
            )
        return results

    @pl.loop(0, (nx - 4) // 2)
    def _(turn):
        for x, t, own, value in layer(2 + 2 * turn) + layer(3 + 2 * turn):
            if last:
                press_buf[aligned(own), :] = value
            else:
                water_out[aligned(own), :] = value
                press[x + 1, pl.ds(PAD + SUB * t, SUB), :] = value

    if last:
        for copy in copies:
            copy.wait()


def water_stress(g, x, t, dx, water, uy, speed, hk_water, lane, top_pick):
    row = x * (g.ny + 2 * PAD) + PAD + SUB * t
    own = x * g.ny + SUB * t
    dy = uy[pl.ds(row + 1, SUB), :] - uy[pl.ds(row - 1, SUB), :]
    surface = jnp.broadcast_to(speed[VZ * (g.across + 2) + 1 + t, pl.ds(PAD + x, 1), :], (SUB, LANES))
    dz = water_z(g, water[aligned(3 * g.plane + own), :], pick(surface, top_pick), lane)
    return water[aligned(own), :] - hk_water[aligned(own), :] * (dx + dy + dz)


def edge_kernel(g, first, last, *refs):
    refs = Refs(refs)
    water, bricks, memory, params, hb_water, hk_water, odd, col_far, col_near, row_far, row_near = refs.take(11)
    if not first:
        (const_in,) = refs.take(1)
    (uy,) = refs.take(1)
    if last:
        inner_press, inner_motion, inner_memory = refs.take(3)
    refs.take(2 if last else 6)
    (speed,) = refs.take(1)
    if last:
        water_hbm, motion_hbm, memory_hbm = refs.take(3)
    else:
        water_out, press, stress, bricks_out, memory_out = refs.take(5)
        sends = refs.take(4)
    (ux,) = refs.take(1)
    if first:
        (const_out,) = refs.take(1)
    col_before, col_after, row_before, row_after = refs.take(4)
    if last:
        press_buf, motion_buf, memory_buf, sems = refs.take(4)
    else:
        buffers = refs.take(4)
    unroute(odd[1] > 0.0, col_far, col_near, col_before, col_after, (M_BRICK, M_BRICK + g.nx - SUB))
    unroute(odd[0] > 0.0, row_far, row_near, row_before, row_after)
    col_odd = odd[1, pl.ds(0, 1), :] > 0.0

    nx, ny, edge, across, plane = g.nx, g.ny, g.edge, g.across, g.plane
    wide = across + 2
    lane = lane_ids()
    top_pick = surface_pick() * edge + (edge - 1)
    py = ny + 2 * PAD
    copies = []

    def send(source, target):
        copies.append(pltpu.make_async_copy(source, target, sems.at[len(copies)]))
        copies[-1].start()

    if last:
        middle = pl.ds(2 * ny, (nx - 4) * ny)
        send(inner_press.at[middle, :], water_hbm.at[middle, :])
        for ti in range(1, g.xtiles - 1):
            send(slots_of(g, inner_memory, ti), slots_of(g, memory_hbm, ti))
            send(slots_of(g, inner_motion, ti), slots_of(g, motion_hbm, ti))

    @pl.loop(0, SUB)
    def _(x):
        for t in range(g.ytiles):
            own = x * ny + SUB * t
            ux[aligned(ny + own), :] = water[aligned(plane + own), :]
            ux[aligned((1 + SUB) * ny + own), :] = water[aligned(plane + (nx - SUB) * ny + own), :]

    sides = ((row_before, 0, -1, 1.0, 1, 0), (row_after, nx - 1, nx, -1.0, 2 * SUB, 2 * SUB + 1))
    for side, (ref, x, halo, sign, own_layer, halo_layer) in enumerate(sides):
        for t in range(g.ytiles):
            own = pl.ds(x * ny + SUB * t, SUB)
            place = pl.ds(32 * side + SUB * t, SUB)
            if first:
                theirs = ref[pl.ds(ROW_CONST + SUB * t, SUB), :]
                const_out[place, :] = theirs
            else:
                theirs = const_in[place, :]
            here = pl.ds(own_layer * ny + SUB * t, SUB)
            ux[here, :] = ux[here, :] + sign * hb_water[own, :] * ref[pl.ds(M_P + SUB * t, SUB), :]
            ux[pl.ds(halo_layer * ny + SUB * t, SUB), :] = ref[pl.ds(M_U + SUB * t, SUB), :] - sign * theirs * water[own, :]
    if last:
        for layer, x in ((1, 0), (2 * SUB, nx - 1)):
            send(ux.at[pl.ds(layer * ny, ny), :], water_hbm.at[pl.ds(plane + x * ny, ny), :])

    speed_rows = {}

    def speed_row(key, x):
        if (key, x) not in speed_rows:
            speed_rows[key, x] = speed[key, pl.ds(PAD + x, 1), :]
        return speed_rows[key, x]

    for ref, x, halo, sign, _, _ in sides:
        for tj in range(across):
            own_hb = sign * params[HB * across + tj, pl.ds(x, 1), :]
            their_hb = sign * ref[pl.ds(M_BRICK + 6 * across + tj, 1), :]
            for c in (VX, VY, VZ):
                key = c * wide + 1 + tj
                speed_rows[key, x] = speed_row(key, x) - own_hb * ref[pl.ds(M_BRICK + c * across + tj, 1), :]
                speed_rows[key, halo] = (
                    ref[pl.ds(M_BRICK + (3 + c) * across + tj, 1), :] + their_hb * bricks[ALONG_X[c] * across + tj, pl.ds(x, 1), :]
                )
        relayed = [ref[pl.ds(M_CORNER + k, 1), :] for k in range(4)]
        for k, (col_ref, tj, col_halo, col_sign) in enumerate(((col_before, 0, 0, 1.0), (col_after, across - 1, wide - 1, -1.0))):
            near = 0 if tj == 0 else LANES - edge
            far = LANES - edge - near
            inside = (lane[0:1, :] >= near) & (lane[0:1, :] < near + edge)
            corner = jnp.where(col_odd, relayed[2 - 2 * k], relayed[2 * k])
            beside = jnp.where(col_odd, relayed[3 - 2 * k], relayed[2 * k + 1])
            across_y = [roll_row(corner, near - c * edge) for c in range(3)]
            across_x = (roll_row(corner, far - 7 * edge), roll_row(corner, far), roll_row(beside, far - 7 * edge))
            row_hb = jnp.where(inside, col_sign * ref[pl.ds(M_BRICK + 6 * across + tj, 1), :], 0.0)
            col_hb = sign * roll_row(col_ref[pl.ds(M_BRICK + x, 1), :], far - 6 * edge)
            for c in (VX, VY, VZ):
                key = c * wide + 1 + tj
                speed_rows[key, halo] = speed_row(key, halo) - row_hb * across_y[c]
                key = c * wide + col_halo
                speed_rows[key, x] = speed_row(key, x) - col_hb * across_x[c]
    for (key, x), value in speed_rows.items():
        speed[key, pl.ds(PAD + x, 1), :] = value

    store = store_slots(g, motion_buf, memory_buf) if last else store_planes(g, bricks_out, memory_out, stress)

    @pl.loop(0, 2)
    def _(turn):
        ti = turn * (g.xtiles - 1)
        row = pl.multiple_of(SUB * ti, SUB)
        above = pl.multiple_of((1 + SUB * turn) * ny, SUB)
        tops = (
            lambda y: ux[pl.ds(above + y, SUB, stride=ny), :],
            lambda y: uy[pl.ds(row * py + PAD + y, SUB, stride=py), :],
            lambda y: water[pl.ds(3 * plane + row * ny + y, SUB, stride=ny), :],
        )
        brick_stress(g, ti, first, bricks, memory, params, speed, tops, store)

    if last:
        for ti in (0, g.xtiles - 1):
            send(slots_of(g, motion_buf, ti), slots_of(g, motion_hbm, ti))
            send(slots_of(g, memory_buf, ti), slots_of(g, memory_hbm, ti))

    for pair, (x, layer) in enumerate(((0, 1), (nx - 2, 2 * SUB - 1))):
        for step in range(2):
            for t in range(g.ytiles):
                dx = (
                    ux[pl.ds((layer + step + 1) * ny + SUB * t, SUB), :] - ux[pl.ds((layer + step - 1) * ny + SUB * t, SUB), :]
                )
                value = water_stress(g, x + step, t, dx, water, uy, speed, hk_water, lane, top_pick)
                if last:
                    press_buf[pl.ds((2 * pair + step) * ny + SUB * t, SUB), :] = value
                else:
                    water_out[pl.ds((x + step) * ny + SUB * t, SUB), :] = value
                    press[x + step + 1, pl.ds(PAD + SUB * t, SUB), :] = value

    if last:
        for pair, x in enumerate((0, nx - 2)):
            send(press_buf.at[pl.ds(2 * pair * ny, 2 * ny), :], water_hbm.at[pl.ds(x * ny, 2 * ny), :])
        for copy in copies:
            copy.wait()
    else:
        def load_v(field, ti, tj):
            return speed[field * wide + 1 + tj, aligned(PAD + SUB * ti), :]

        def load_hb(ti, tj):
            return params[HB * across + tj, aligned(SUB * ti), :]

        def column(side, t):
            return pl.ds(SUB * t * ny + side * (ny - 1), SUB, stride=ny)

        faces = (
            lambda side, t: ux[pl.ds((1 + side * (2 * SUB - 1)) * ny + SUB * t, SUB), :],
            lambda side, t: hb_water[pl.ds(side * (nx - 1) * ny + SUB * t, SUB), :],
            lambda side, t: uy[pl.ds(SUB * t * py + PAD + side * (ny - 1), SUB, stride=py), :],
            lambda side, t: hb_water[column(side, t), :],
        )
        brick_velocity(g, water_out, stress, load_v, bricks_out, load_hb)
        pack(g, water_out, bricks_out, params, faces, odd, buffers, sends, False)


def swap(value, axis, start):
    pairs = [(i, i + 1) for i in range(start, lax.axis_size(axis) - 1, 2)]
    return lax.ppermute(value, axis, pairs + [(j, i) for i, j in pairs])


def exchange(sends):
    row_far, row_near, col_far, col_near = sends
    col_far = swap(col_far, "col", 1)
    col_near = swap(col_near, "col", 0)

    def with_corners(message, start):
        corners = jnp.concatenate([col_far[start : start + 2], col_near[start : start + 2]])
        return lax.dynamic_update_slice(message, corners, (M_CORNER, 0))

    row_far = swap(with_corners(row_far, M_RELAY), "row", 1)
    row_near = swap(with_corners(row_near, M_RELAY + 2), "row", 0)
    return col_far, col_near, row_far, row_near


def body(
    brick_velocity_stress,
    brick_relaxation_memory,
    brick_cell_material,
    brick_live,
    water_state,
    water_material,
    material_table,
):
    _, nx, ny, nz = water_state.shape
    g = Grid(nx, ny, brick_cell_material.shape[1])
    across, plane = g.across, g.plane

    def f32(*shape):
        return jax.ShapeDtypeStruct(shape, jnp.float32)

    vmem = pl.BlockSpec(memory_space=pltpu.VMEM)
    hbm = pl.BlockSpec(memory_space=pltpu.HBM)
    params = pltpu.CompilerParams(vmem_limit_bytes=24 * 1024 * 1024)
    def messages(first):
        return [f32(start + (32 if first else 0), LANES) for start in (ROW_CONST, ROW_CONST, COL_CONST, COL_CONST)]

    def buffer(*shape):
        return pltpu.VMEM(shape, jnp.float32)

    def held(*values):
        return [pltpu.with_memory_space_constraint(value, pltpu.VMEM) for value in values]

    def pinned(*values):
        return [pltpu.with_memory_space_constraint(value, pltpu.HBM) for value in values]

    def message_buffers(kinds, first):
        starts = {"row": ROW_CONST, "col": COL_CONST}
        return [buffer(starts[kind] + (32 if first else 0), LANES) for kind in kinds for _ in range(2)]

    odd = jnp.stack([lax.axis_index(axis) & 1 for axis in ("row", "col")]).astype(jnp.float32)
    odd = jnp.broadcast_to(odd[:, None, None], (2, SUB, LANES))
    press = buffer(nx + 2, ny + 2 * PAD, nz)
    stress = buffer(6 * across, nx + 2 * PAD, LANES)
    work = pl.CostEstimate(flops=20_000_000, bytes_accessed=8_000_000, transcendentals=0)
    water, bricks, coefficients, columns, *sends = pl.pallas_call(
        functools.partial(first_kernel, g),
        out_shape=[
            buffer(4 * plane, nz), f32(9 * across, nx, LANES), f32(9 * across, nx, LANES), f32(8, SUB, LANES),
        ] + messages(True),
        in_specs=[hbm] * 6 + [vmem],
        out_specs=[vmem] * 8,
        scratch_shapes=[
            stress,
            buffer(nx, ny, nz),
            buffer(2, ny, nz),
            buffer(2, nx, SUB, nz),
            pltpu.VMEM((2, ny, nz), jnp.int32),
            pltpu.VMEM((2, nx, SUB, nz), jnp.int32),
            pltpu.VMEM(brick_velocity_stress.shape, jnp.float32),
            pltpu.VMEM(brick_cell_material.shape, jnp.int32),
            pltpu.SMEM(brick_live.shape, jnp.int32),
            pltpu.SMEM(material_table.shape, jnp.float32),
            pltpu.SemaphoreType.DMA((13,)),
        ]
        + message_buffers(("row", "col"), True),
        compiler_params=params,
        name="first_bricks",
    )(*pinned(brick_live, material_table, water_state, water_material, brick_velocity_stress, brick_cell_material), odd)

    def passed(*messages):
        return [buffer(*message.shape) for message in messages]

    water, sends[0], sends[1], hb_water, hk_water = pl.pallas_call(
        functools.partial(first_water_kernel, g),
        out_shape=[buffer(4 * plane, nz)] + passed(*sends[:2]) + [f32(plane, nz), f32(plane, nz)],
        in_specs=[vmem] * 7,
        out_specs=[vmem] * 5,
        input_output_aliases={0: 0, 1: 1, 2: 2},
        scratch_shapes=[press],
        compiler_params=params,
        cost_estimate=work,
        name="first_water",
    )(*held(water, *sends[:2], bricks, columns, water_state, water_material))
    memory = brick_relaxation_memory
    col_const, row_const = (), ()
    uy_shape = (nx * (ny + 2 * PAD), nz)
    speed_shape = (3 * (across + 2), nx + 2 * PAD, LANES)
    ux_buffer = buffer((2 * SUB + 2) * ny, nz)
    slot_buffers = [
        pltpu.VMEM(brick_velocity_stress.shape, jnp.float32),
        pltpu.VMEM(brick_relaxation_memory.shape, jnp.float32),
    ]
    finals = [f32(4 * plane, nz), f32(*brick_velocity_stress.shape), f32(*brick_relaxation_memory.shape)]
    planes = [
        buffer(4 * plane, nz),
        buffer(nx + 2, ny + 2 * PAD, nz),
        buffer(6 * across, nx + 2 * PAD, LANES),
        buffer(9 * across, nx, LANES),
        buffer(18 * across, nx, LANES),
    ]
    for step in range(STEPS):
        first, last = step == 0, step == STEPS - 1
        *columns, row_far, row_near = exchange(sends)
        state = (water, bricks, memory, coefficients, hb_water, hk_water, odd)
        held_out = [buffer(plane, nz)] + slot_buffers if last else planes
        inner = pl.pallas_call(
            functools.partial(inner_kernel, g, first, last),
            out_shape=[buffer(*uy_shape), buffer(*speed_shape)]
            + finals[: 1 if last else 0]
            + held_out
            + ([buffer(64, LANES)] if first else []),
            in_specs=[vmem] * (9 + len(col_const)),
            out_specs=[vmem] * 2 + [hbm] * (1 if last else 0) + [vmem] * (len(held_out) + (1 if first else 0)),
            scratch_shapes=message_buffers(("col",), first)
            + ([buffer(plane, nz), pltpu.SemaphoreType.DMA((3,))] if last else []),
            compiler_params=params,
            cost_estimate=work,
            name="inner",
        )(*held(*state), *columns, *col_const)
        if first:
            col_const = (inner[-1],)
            inner = inner[:-1]
        inputs = held(*state) + list(columns) + [row_far, row_near] + list(row_const)
        if last:
            uy, speed, partial, *rest = inner
            inputs += held(uy, *rest)
            same, spaces, out_shape = [*held(speed), partial], [vmem, hbm], [buffer(*speed_shape)] + finals
        else:
            uy, *partial = inner
            inputs += held(uy)
            same, spaces, out_shape = held(*partial), [vmem] * len(partial), [buffer(*speed_shape)] + planes
        rest_shape = ([] if last else messages(False) + [ux_buffer]) + ([buffer(64, LANES)] if first else [])
        results = pl.pallas_call(
            functools.partial(edge_kernel, g, first, last),
            out_shape=out_shape + rest_shape,
            in_specs=[vmem] * len(inputs) + spaces,
            out_specs=[vmem] + [hbm if last else vmem] * (len(out_shape) - 1) + [vmem] * len(rest_shape),
            input_output_aliases={len(inputs) + k: k for k in range(len(same))},
            scratch_shapes=([ux_buffer] if last else [])
            + message_buffers(("col", "row"), first)
            + (
                [buffer(4 * ny, nz)] + slot_buffers + [pltpu.SemaphoreType.DMA((13,))]
                if last
                else message_buffers(("row", "col"), False)
            ),
            compiler_params=params,
            name="edges",
        )(*inputs, *same)
        if last:
            return results[2], results[3], results[1].reshape(water_state.shape)
        old_water = water
        _, water, pressed, stressed, bricks, memory = results[:6]
        sends = list(results[6:10])
        if first:
            row_const = (results[11],)
        water, sends[0], sends[1] = pl.pallas_call(
            functools.partial(edge_water_kernel, g),
            out_shape=[buffer(4 * plane, nz)] + passed(*sends[:2]),
            in_specs=[vmem] * 9,
            out_specs=[vmem] * 3,
            input_output_aliases={0: 0, 1: 1, 2: 2},
            compiler_params=params,
            cost_estimate=work,
            name="edge_water",
        )(*held(water, *sends[:2], old_water, pressed, stressed, hb_water, results[10], uy))


def solution(mesh):
    return jax.shard_map(
        body,
        mesh=mesh,
        in_specs=(
            P(("row", "col"), None, None, None),
            P(("row", "col"), None, None, None),
            P(("row", "col"), None, None),
            P(("row", "col")),
            P(None, "row", "col", None),
            P("row", "col", None),
            P(),
        ),
        out_specs=(
            P(("row", "col"), None, None, None),
            P(("row", "col"), None, None, None),
            P(None, "row", "col", None),
        ),
        check_vma=False,
    )
```

```python
import functools

import jax
import jax.numpy as jnp
from jax import lax
from jax.experimental import pallas as pl
from jax.experimental.pallas import tpu as pltpu
from jax.sharding import PartitionSpec as P

STEPS = 3
LANES = 128
SUB = 8
PAD = 8
VX, VY, VZ, XX, YY, ZZ, XY, XZ, YZ = range(9)
HB, LAME, SHEAR, RETAIN, SPRING_LAME, SPRING_SHEAR, ALIVE = 0, 1, 2, 3, 6, 7, 8
ALONG_X = (XX, XY, XZ)
ALONG_Y = (XY, YY, YZ)
ALONG_Z = (XZ, YZ, ZZ)
M_P, M_U, M_BRICK, M_CORNER, M_RELAY = 0, 32, 64, 92, 96
ROW_CONST, COL_CONST = 96, 104


def lane_ids():
    return lax.broadcasted_iota(jnp.int32, (SUB, LANES), 1)


def roll(value, shift):
    shift = shift % LANES
    return value if shift == 0 else pltpu.roll(value, shift, 1)


def roll_row(row, shift):
    shift = shift % LANES
    if shift == 0:
        return row
    return pltpu.roll(jnp.broadcast_to(row, (SUB, LANES)), shift, 1)[0:1, :]


def pick(values, indices):
    return jnp.take_along_axis(values, indices, axis=1, mode="promise_in_bounds")


def aligned(start, size=SUB):
    return pl.ds(start if isinstance(start, int) else pl.multiple_of(start, SUB), size)


class Grid:
    def __init__(self, nx, ny, edge):
        self.nx, self.ny, self.edge = nx, ny, edge
        self.plane = nx * ny
        self.across = ny * edge // LANES
        self.yper = LANES // edge
        self.half = self.across // 2
        self.xtiles, self.ytiles = nx // SUB, ny // SUB
        self.per = edge // SUB

    def slot(self, ti, tj):
        return 2 * (ti // self.per) + tj // self.half

    def place(self, ti, tj):
        return aligned((ti % self.per) * SUB), pl.ds((tj % self.half) * LANES, LANES)


def zero_press_pads(g, press):
    zero = jnp.zeros((SUB, LANES), jnp.float32)
    for t in range(g.ytiles):
        press[0, pl.ds(PAD + SUB * t, SUB), :] = zero
        press[g.nx + 1, pl.ds(PAD + SUB * t, SUB), :] = zero

    @pl.loop(0, g.nx // SUB)
    def _(turn):
        for step in range(SUB):
            x = SUB * turn + step + 1
            press[x, pl.ds(0, SUB), :] = zero
            press[x, pl.ds(PAD + g.ny, SUB), :] = zero


def zero_stress_pads(g, stress):
    zero = jnp.zeros((SUB, LANES), jnp.float32)
    for field in ALONG_X:
        for tj in range(g.across):
            key = (field - XX) * g.across + tj
            stress[key, pl.ds(0, SUB), :] = zero
            stress[key, pl.ds(PAD + g.nx, SUB), :] = zero


def shifted_top(g, load, ys, lane):
    top = None
    for k, y in enumerate(ys):
        value = roll(load(y), g.edge * k + g.edge - 1)
        top = value if top is None else jnp.where(lane >= g.edge * k, value, top)
    return top


def along_y(g, rolled, tj, lane):
    zero = jnp.zeros((SUB, LANES), jnp.float32)
    after = rolled[tj + 1][1] if tj + 1 < len(rolled) else zero
    before = rolled[tj - 1][0] if tj > 0 else zero
    ahead = jnp.where(lane < LANES - g.edge, rolled[tj][1], after)
    behind = jnp.where(lane >= g.edge, rolled[tj][0], before)
    return ahead - behind


def along_z(g, value, beyond, depth):
    zero = jnp.zeros((SUB, LANES), jnp.float32)
    return jnp.where(depth == g.edge - 1, beyond, roll(value, -1)) - jnp.where(depth == 0, zero, roll(value, 1))


def water_z(g, value, below, lane):
    zero = jnp.zeros((SUB, LANES), jnp.float32)
    return jnp.where(lane == LANES - 1, zero, roll(value, -1)) - jnp.where(lane == 0, below, roll(value, 1))


def surface_pick():
    return lax.broadcasted_iota(jnp.int32, (SUB, LANES), 0)


def water_velocity(g, layers, water_out, press, surface_row, load_hb, load_u):
    lane = lane_ids()
    top_pick = surface_pick() * g.edge + (g.edge - 1)

    def water_layer(x):
        results = []
        for t in range(g.ytiles):
            rows = pl.ds(PAD + SUB * t, SUB)
            here = press[x + 1, rows, :]
            dx = press[x + 2, rows, :] - press[x, rows, :]
            dy = press[x + 1, pl.ds(PAD + SUB * t + 1, SUB), :] - press[x + 1, pl.ds(PAD + SUB * t - 1, SUB), :]
            surface = jnp.broadcast_to(surface_row(t, x), (SUB, LANES))
            dz = water_z(g, here, -pick(surface, top_pick), lane)
            own = x * g.ny + SUB * t
            hb = load_hb(x, t)
            for k, change in ((1, dx), (2, dy), (3, dz)):
                results.append((k * g.plane + own, load_u(k, x, t) - hb * change))
        return results

    turns, layer = layers

    @pl.loop(0, turns)
    def _(turn):
        x = layer(turn)
        for row, value in water_layer(x) + water_layer(x + 1):
            water_out[aligned(row), :] = value


def brick_velocity(g, tiles, water_out, stress, load_v, bricks_out, load_hb):
    lane = lane_ids()
    depth = lane % g.edge
    zero = jnp.zeros((SUB, LANES), jnp.float32)
    across, ny = g.across, g.ny

    turns, tile = tiles

    @pl.loop(0, turns)
    def _(turn):
        ti = tile(turn)
        row = pl.multiple_of(SUB * ti, SUB)
        here = pl.ds(pl.multiple_of(row + PAD, SUB), SUB)

        def load(field, tj):
            return stress[(field - XX) * across + tj, here, :]

        def along_x(field, tj):
            key = (field - XX) * across + tj
            return stress[key, pl.ds(row + PAD + 1, SUB), :] - stress[key, pl.ds(row + PAD - 1, SUB), :]

        results = []
        for target, fx, fy, fz in zip((VX, VY, VZ), ALONG_X, ALONG_Y, ALONG_Z):
            rolled = [(roll(value, g.edge), roll(value, -g.edge)) for value in (load(fy, tj) for tj in range(across))]
            for tj in range(across):
                beyond = zero
                if fz == ZZ:
                    ys = [g.yper * tj + k for k in range(g.yper)]
                    beyond = -shifted_top(g, lambda y: water_out[pl.ds(row * ny + y, SUB, stride=ny), :], ys, lane)
                change = along_x(fx, tj) + along_y(g, rolled, tj, lane) + along_z(g, load(fz, tj), beyond, depth)
                results.append((target * across + tj, load_v(target, ti, tj) + load_hb(ti, tj) * change))
        for key, value in results:
            bricks_out[key, pl.ds(row, SUB), :] = value


def window(row):
    def read(ref, key, offset=0):
        return ref[key, pl.ds(row + offset, SUB), :]

    return read


def both_faces(g):
    lower = lax.broadcasted_iota(jnp.int32, (SUB, LANES), 0) < SUB // 2

    def read(ref, key, offset=0):
        return jnp.where(lower, ref[key, pl.ds(offset, SUB), :], ref[key, pl.ds(g.nx - SUB + offset, SUB), :])

    return read


def brick_stress(g, read, bricks, memory, params, speed, tops, store):
    edge, across = g.edge, g.across
    wide = across + 2
    lane = lane_ids()
    depth = lane % edge
    rolled = []
    for field in (VX, VY, VZ):
        values = [read(speed, field * wide + tj, PAD) for tj in range(wide)]
        rolled.append([(roll(value, edge), roll(value, -edge)) for value in values])
    for tj in range(across):
        ys = [g.yper * tj + k for k in range(g.yper)]
        dx, dy, dz, speeds = [], [], [], []
        for field in (VX, VY, VZ):
            key = field * wide + 1 + tj
            value = read(speed, key, PAD)
            speeds.append(value)
            dx.append(read(speed, key, PAD + 1) - read(speed, key, PAD - 1))
            dy.append(along_y(g, rolled[field], tj + 1, lane))
            dz.append(along_z(g, value, shifted_top(g, tops[field], ys, lane), depth))
        strain = [dx[0], dy[1], dz[2], dy[0] + dx[1], dz[0] + dx[2], dz[1] + dy[2]]
        dilation = strain[0] + strain[1] + strain[2]

        def param(c):
            return read(params, c * across + tj)

        lame, shear = param(LAME) * dilation, param(SHEAR)
        spring_lame, spring_shear = param(SPRING_LAME) * dilation, param(SPRING_SHEAR)
        retain = [param(RETAIN + l) for l in range(3)]
        half_shear, half_spring = 0.5 * shear, 0.5 * spring_shear
        stresses, memories = [], {}
        for comp in range(6):
            if comp < 3:
                elastic = shear * strain[comp] + lame
                relaxed = spring_shear * strain[comp] + spring_lame
            else:
                elastic = half_shear * strain[comp]
                relaxed = half_spring * strain[comp]
            summed = None
            for l in range(3):
                place = 6 * l + comp
                old = read(memory, place * across + tj)
                new = relaxed + retain[l] * (old - relaxed)
                memories[place] = new
                summed = new if summed is None else summed + new
            stresses.append(read(bricks, (XX + comp) * across + tj) + elastic - summed)
        store(tj, speeds, stresses, memories)


def store_planes(g, bricks_out, memory_out, stress, pieces):
    def store(tj, speeds, stresses, memories):
        for first, count, row in pieces:
            for place, value in memories.items():
                memory_out[place * g.across + tj, pl.ds(row, count), :] = value[first : first + count, :]
            for comp, value in enumerate(stresses):
                value = value[first : first + count, :]
                bricks_out[(XX + comp) * g.across + tj, pl.ds(row, count), :] = value
                stress[comp * g.across + tj, pl.ds(row + PAD, count), :] = value

    return store


def store_slots(g, motion, memory, ti):
    def store(tj, speeds, stresses, memories):
        slot = g.slot(ti, tj)
        rows, lanes = g.place(ti, tj)
        for place, value in memories.items():
            memory[slot, place, rows, lanes] = value
        for field, value in enumerate(speeds + stresses):
            motion[slot, field, rows, lanes] = value

    return store


def route(odd, first, last, out_far, out_near):
    for start in range(0, out_far.shape[0], SUB):
        rows = pl.ds(start, SUB)
        one, other = first[rows, :], last[rows, :]
        out_far[rows, :] = jnp.where(odd, other, one)
        out_near[rows, :] = jnp.where(odd, one, other)


def unroute(odd, from_far, from_near, before, after, starts=None):
    for start in starts or range(0, from_far.shape[0], SUB):
        rows = pl.ds(start, SUB)
        far, near = from_far[rows, :], from_near[rows, :]
        before[rows, :] = jnp.where(odd, near, far)
        after[rows, :] = jnp.where(odd, far, near)


def pack(g, water, bricks, params, edges, odd, buffers, sends, first):
    row_u, row_hb, col_u, col_hb = edges
    row_first, row_last, col_first, col_last = buffers
    row_odd, col_odd = odd[0] > 0.0, odd[1] > 0.0
    nx, ny, across, edge = g.nx, g.ny, g.across, g.edge
    lane = lane_ids()
    for side, (out, x, inward, sign) in enumerate(((row_first, 0, 1, 1.0), (row_last, nx - 1, nx - 2, -1.0))):
        for t in range(g.ytiles):
            own = x * ny + SUB * t
            hb = row_hb(side, t)
            out[pl.ds(M_P + SUB * t, SUB), :] = water[pl.ds(own, SUB), :]
            out[pl.ds(M_U + SUB * t, SUB), :] = row_u(side, t) - sign * hb * water[pl.ds(inward * ny + SUB * t, SUB), :]
            if first:
                out[pl.ds(ROW_CONST + SUB * t, SUB), :] = hb
        for tj in range(across):
            for k, field in enumerate(ALONG_X + (VX, VY, VZ)):
                out[pl.ds(M_BRICK + k * across + tj, 1), :] = bricks[field * across + tj, pl.ds(x, 1), :]
            out[pl.ds(M_BRICK + 6 * across + tj, 1), :] = params[HB * across + tj, pl.ds(x, 1), :]
        out[pl.ds(M_CORNER, 4), :] = jnp.zeros((4, LANES), jnp.float32)
    sides = ((col_first, 0, 1, 0, 1.0), (col_last, ny - 1, ny - 2, across - 1, -1.0))
    for side, (out, y, inward, tj, sign) in enumerate(sides):
        for t in range(g.xtiles):
            own = SUB * t * ny + y
            hb = col_hb(side, t)
            out[pl.ds(M_P + SUB * t, SUB), :] = water[pl.ds(own, SUB, stride=ny), :]
            out[pl.ds(M_U + SUB * t, SUB), :] = (
                col_u(side, t) - sign * hb * water[pl.ds(SUB * t * ny + inward, SUB, stride=ny), :]
            )
            if first:
                out[pl.ds(COL_CONST + SUB * t, SUB), :] = hb
            rows = pl.ds(SUB * t, SUB)
            pieces = [bricks[field * across + tj, rows, :] for field in ALONG_Y + (VX, VY, VZ)]
            pieces.append(params[HB * across + tj, rows, :])
            beside = (1, 0) if t == 0 else (SUB - 2, SUB - 1)
            shear = bricks[XZ * across + tj, rows, :]
            if t == 0 or t == g.xtiles - 1:
                shear = pltpu.roll(shear, 1 if t == 0 else SUB - 1, 0)
            sub = lax.broadcasted_iota(jnp.int32, (SUB, LANES), 0)
            pieces.append(jnp.where(sub == beside[0], shear, bricks[XX * across + tj, rows, :]))
            packed = None
            for k, value in enumerate(pieces):
                moved = roll(value, edge * (k - y % g.yper))
                packed = moved if packed is None else jnp.where(lane >= edge * k, moved, packed)
            out[pl.ds(M_BRICK + SUB * t, SUB), :] = packed
            if t == 0:
                corner = packed
        one = (corner[0:1, :], corner[1:2, :])
        other = (packed[SUB - 1 : SUB, :], packed[SUB - 2 : SUB - 1, :])
        out[pl.ds(M_RELAY, SUB), :] = jnp.zeros((SUB, LANES), jnp.float32)
        for k in range(2):
            out[pl.ds(M_RELAY + k, 1), :] = jnp.where(row_odd[0:1, :], other[k], one[k])
            out[pl.ds(M_RELAY + 2 + k, 1), :] = jnp.where(row_odd[0:1, :], one[k], other[k])
    route(row_odd, row_first, row_last, *sends[:2])
    route(col_odd, col_first, col_last, *sends[2:])


def first_kernel(
    g, live_hbm, table_hbm, water_hbm, material_hbm, motion_hbm, kinds_hbm, memory_hbm, odd,
    water_out, bricks_out, params, columns, memory, row_far, row_near, col_far, col_near,
    stress, pressure, ux_edge, uy_edge, material_x, material_y, motion, kinds, live, table, sems, *buffers,
):
    nx, ny, across = g.nx, g.ny, g.across
    copies = []

    def fetch(source, target):
        copies.append(pltpu.make_async_copy(source, target, sems.at[len(copies)]))
        copies[-1].start()

    fetch(live_hbm, live)
    fetch(table_hbm, table)
    fetch(kinds_hbm, kinds)
    fetch(motion_hbm, motion)
    fetch(water_hbm.at[0], pressure)
    for side, (x, y) in enumerate(((0, 0), (nx - 1, ny - SUB))):
        fetch(water_hbm.at[1, x], ux_edge.at[side])
        fetch(material_hbm.at[x], material_x.at[side])
        fetch(water_hbm.at[2, :, pl.ds(y, SUB), :], uy_edge.at[side])
        fetch(material_hbm.at[:, pl.ds(y, SUB), :], material_y.at[side])
    fetch(memory_hbm, memory)
    lane = lane_ids()
    zero_stress_pads(g, stress)
    copies[0].wait()
    copies[1].wait()
    scales = (0.5, 0.5, 1.0, 1.0, 1.0, 1.0, 0.5, 1.0)
    for c, factor in enumerate(scales):
        column = jnp.zeros((SUB, LANES), jnp.float32)
        for level in range(table.shape[0]):
            column = jnp.where(lane == level, table[level, c], column)
        columns[c] = column * factor
    copies[2].wait()
    copies[3].wait()

    @pl.loop(0, g.xtiles)
    def _(ti):
        for tj in range(across):
            slot = g.slot(ti, tj)
            rows, lanes = g.place(ti, tj)
            alive = live[slot].astype(jnp.float32)
            here = aligned(SUB * ti)
            index = kinds[slot, rows, lanes]
            for c in range(8):
                value = pick(columns[c], index)
                params[c * across + tj, here, :] = value if 3 <= c < 6 else value * alive
            params[ALIVE * across + tj, here, :] = jnp.zeros((SUB, LANES), jnp.float32) + alive
            for field in range(XX, YZ + 1):
                value = motion[slot, field, rows, lanes] * alive
                bricks_out[field * across + tj, here, :] = value
                stress[(field - XX) * across + tj, aligned(PAD + SUB * ti), :] = value

    copies[4].wait()

    @pl.loop(0, nx // 2)
    def _(turn):
        results = []
        for x in (2 * turn, 2 * turn + 1):
            for t in range(g.ytiles):
                results.append((x * ny + SUB * t, pressure[x, pl.ds(SUB * t, SUB), :]))
        for own, value in results:
            water_out[aligned(own), :] = value

    def load_v(field, ti, tj):
        slot = g.slot(ti, tj)
        rows, lanes = g.place(ti, tj)
        return motion[slot, field, rows, lanes] * live[slot].astype(jnp.float32)

    def load_hb(ti, tj):
        return params[HB * across + tj, aligned(SUB * ti), :]

    brick_velocity(g, (g.xtiles, lambda turn: turn), water_out, stress, load_v, bricks_out, load_hb)
    for copy in copies[5:-1]:
        copy.wait()

    def rows_of(side, t):
        return side, pl.ds(SUB * t, SUB), side * (SUB - 1)

    edges = (
        lambda side, t: ux_edge[side, pl.ds(SUB * t, SUB), :],
        lambda side, t: pick(columns[0], material_x[side, pl.ds(SUB * t, SUB), :]),
        lambda side, t: uy_edge[(*rows_of(side, t), slice(None))],
        lambda side, t: pick(columns[0], material_y[(*rows_of(side, t), slice(None))]),
    )
    pack(g, water_out, bricks_out, params, edges, odd, buffers, (row_far, row_near, col_far, col_near), True)
    copies[-1].wait()


def first_water_kernel(
    g, pressure, row_first, row_last, bricks, columns, state, material, params, memory,
    water_out, first_same, last_same, hb_water, hk_water, memory_out, press,
):
    nx, ny = g.nx, g.ny

    @pl.loop(0, 18)
    def _(place):
        results = []
        for ti in range(g.xtiles):
            for tj in range(g.across):
                rows, lanes = g.place(ti, tj)
                value = memory[g.slot(ti, tj), place, rows, lanes]
                results.append((tj, ti, value * params[ALIVE * g.across + tj, pl.ds(SUB * ti, SUB), :]))
        for tj, ti, value in results:
            memory_out[place * g.across + tj, pl.ds(SUB * ti, SUB), :] = value

    zero_press_pads(g, press)

    @pl.loop(0, nx // 2)
    def _(turn):
        results = []
        for x in (2 * turn, 2 * turn + 1):
            for t in range(g.ytiles):
                own = x * ny + SUB * t
                index = material[x, pl.ds(SUB * t, SUB), :]
                results.append((x, t, own, pick(columns[0], index), pick(columns[1], index), pressure[aligned(own), :]))
        for x, t, own, hb, hk, value in results:
            hb_water[aligned(own), :] = hb
            hk_water[aligned(own), :] = hk
            press[x + 1, pl.ds(PAD + SUB * t, SUB), :] = value

    water_velocity(
        g,
        (nx // 2, lambda turn: 2 * turn),
        water_out,
        press,
        lambda t, x: bricks[ZZ * g.across + t, pl.ds(x, 1), :],
        lambda x, t: hb_water[aligned(x * ny + SUB * t), :],
        lambda k, x, t: state[k, x, pl.ds(SUB * t, SUB), :],
    )


def edge_water_kernel(
    g, same, row_first, row_last, water, press, stress, hb_water, ux, uy, water_out, first_same, last_same
):
    nx, ny, plane = g.nx, g.ny, g.plane

    def water_layers(layers, ux_row):
        def load_u(k, x, t):
            if k == 1:
                return ux_row(x, t)
            if k == 2:
                return uy[aligned(x * (ny + 2 * PAD) + PAD + SUB * t), :]
            return water[aligned(3 * plane + x * ny + SUB * t), :]

        water_velocity(
            g,
            layers,
            water_out,
            press,
            lambda t, x: stress[(ZZ - XX) * g.across + t, pl.ds(PAD + x, 1), :],
            lambda x, t: hb_water[aligned(x * ny + SUB * t), :],
            load_u,
        )

    def near_face(x, t):
        layer = x - (x // (nx - SUB)) * (nx - 2 * SUB) + 1
        return ux[aligned(layer * ny + SUB * t), :]

    water_layers((SUB, lambda turn: 2 * turn + (turn // (SUB // 2)) * (nx - 2 * SUB)), near_face)
    water_layers(
        ((nx - 2 * SUB) // 2, lambda turn: SUB + 2 * turn),
        lambda x, t: water[aligned(plane + x * ny + SUB * t), :],
    )


def slots_of(g, array, ti):
    slot = g.slot(ti, 0)
    return array.at[pl.ds(slot, 2), :, pl.ds((ti % g.per) * SUB, SUB), :]


class Refs:
    def __init__(self, refs):
        self.refs = list(refs)

    def take(self, count):
        taken, self.refs = self.refs[:count], self.refs[count:]
        return taken


def inner_kernel(g, first, last, *refs):
    refs = Refs(refs)
    water, bricks, memory, params, hb_water, hk_water, odd, col_far, col_near = refs.take(9)
    if not first:
        (const_in,) = refs.take(1)
    uy, speed = refs.take(2)
    if last:
        water_hbm, press_buf, motion_buf, memory_buf = refs.take(4)
    else:
        water_out, press, stress, bricks_out, memory_out = refs.take(5)
    if first:
        (const_out,) = refs.take(1)
    col_before, col_after = refs.take(2)
    if last:
        uy_buf, sems = refs.take(2)
    unroute(odd[1] > 0.0, col_far, col_near, col_before, col_after)

    nx, ny, edge, across, plane = g.nx, g.ny, g.edge, g.across, g.plane
    wide = across + 2
    lane = lane_ids()
    top_pick = surface_pick() * edge + (edge - 1)
    py = ny + 2 * PAD
    copies = []

    def send(source, target):
        copies.append(pltpu.make_async_copy(source, target, sems.at[len(copies)]))
        copies[-1].start()

    def part(component, start, stop):
        return pl.ds(component * plane + start * ny, (stop - start) * ny)

    if last:
        send(water.at[part(3, 0, nx), :], water_hbm.at[part(3, 0, nx), :])
        send(water.at[part(1, 1, nx - 1), :], water_hbm.at[part(1, 1, nx - 1), :])
    else:
        zero_press_pads(g, press)
        zero_stress_pads(g, stress)

    @pl.loop(0, nx // 4)
    def _(turn):
        results = []
        for x in (4 * turn + step for step in range(4)):
            for t in range(g.ytiles):
                own = x * ny + SUB * t
                results.append((own, x * py + PAD + SUB * t, water[aligned(2 * plane + own), :]))
        for own, row, value in results:
            uy[aligned(row), :] = value
            if last:
                uy_buf[aligned(own), :] = value

    for side, (ref, y, halo, sign) in enumerate(((col_before, 0, -1, 1.0), (col_after, ny - 1, ny, -1.0))):
        for t in range(g.xtiles):
            own = pl.ds(SUB * t * ny + y, SUB, stride=ny)
            here = pl.ds(SUB * t * py + PAD + y, SUB, stride=py)
            place = pl.ds(32 * side + SUB * t, SUB)
            if first:
                theirs = ref[pl.ds(COL_CONST + SUB * t, SUB), :]
                const_out[place, :] = theirs
            else:
                theirs = const_in[place, :]
            value = uy[here, :] + sign * hb_water[own, :] * ref[pl.ds(M_P + SUB * t, SUB), :]
            uy[here, :] = value
            if last:
                uy_buf[own, :] = value
            uy[pl.ds(SUB * t * py + PAD + halo, SUB, stride=py), :] = (
                ref[pl.ds(M_U + SUB * t, SUB), :] - sign * theirs * water[own, :]
            )
    if last:
        send(uy_buf, water_hbm.at[part(2, 0, nx), :])

    for field in (VX, VY, VZ):
        for tj in range(across):
            for ti in range(g.xtiles):
                speed[field * wide + 1 + tj, pl.ds(PAD + SUB * ti, SUB), :] = bricks[field * across + tj, pl.ds(SUB * ti, SUB), :]
    for ref, tj, halo, sign in ((col_before, 0, 0, 1.0), (col_after, across - 1, wide - 1, -1.0)):
        near = 0 if tj == 0 else LANES - edge
        far = LANES - edge - near
        inside = (lane >= near) & (lane < near + edge)
        for ti in range(g.xtiles):
            column = ref[pl.ds(M_BRICK + SUB * ti, SUB), :]
            own_hb = jnp.where(inside, sign * params[HB * across + tj, pl.ds(SUB * ti, SUB), :], 0.0)
            their_hb = sign * roll(column, far - 6 * edge)
            here = pl.ds(PAD + SUB * ti, SUB)
            for c in (VX, VY, VZ):
                key = c * wide + 1 + tj
                speed[key, here, :] = bricks[c * across + tj, pl.ds(SUB * ti, SUB), :] - own_hb * roll(column, near - c * edge)
                own = bricks[ALONG_Y[c] * across + tj, pl.ds(SUB * ti, SUB), :]
                speed[c * wide + halo, here, :] = roll(column, far - (3 + c) * edge) + their_hb * roll(own, far - near)

    windows = g.xtiles - 2 if last else g.xtiles

    @pl.loop(0, windows)
    def _(turn):
        if last:
            row = pl.multiple_of(SUB * (turn + 1), SUB)
            store = store_slots(g, motion_buf, memory_buf, turn + 1)
        else:
            row = 2 + SUB * turn - 4 * (turn // (g.xtiles - 1))
            store = store_planes(g, bricks_out, memory_out, stress, [(0, SUB, row)])
        tops = (
            lambda y: water[pl.ds(plane + row * ny + y, SUB, stride=ny), :],
            lambda y: uy[pl.ds(row * py + PAD + y, SUB, stride=py), :],
            lambda y: water[pl.ds(3 * plane + row * ny + y, SUB, stride=ny), :],
        )
        brick_stress(g, window(row), bricks, memory, params, speed, tops, store)

    def layer(x):
        results = []
        for t in range(g.ytiles):
            own = x * ny + SUB * t
            dx = water[aligned(plane + own + ny), :] - water[aligned(plane + own - ny), :]
            results.append(
                (x, t, own, water_stress(g, x, t, dx, water, uy, speed, hk_water, lane, top_pick))
            )
        return results

    @pl.loop(0, (nx - 4) // 2)
    def _(turn):
        for x, t, own, value in layer(2 + 2 * turn) + layer(3 + 2 * turn):
            if last:
                press_buf[aligned(own), :] = value
            else:
                water_out[aligned(own), :] = value
                press[x + 1, pl.ds(PAD + SUB * t, SUB), :] = value

    if last:
        for copy in copies:
            copy.wait()
    else:
        def load_v(field, ti, tj):
            return speed[field * wide + 1 + tj, aligned(PAD + SUB * ti), :]

        def load_hb(ti, tj):
            return params[HB * across + tj, aligned(SUB * ti), :]

        brick_velocity(g, (g.xtiles - 2, lambda turn: turn + 1), water_out, stress, load_v, bricks_out, load_hb)


def water_stress(g, x, t, dx, water, uy, speed, hk_water, lane, top_pick):
    row = x * (g.ny + 2 * PAD) + PAD + SUB * t
    own = x * g.ny + SUB * t
    dy = uy[pl.ds(row + 1, SUB), :] - uy[pl.ds(row - 1, SUB), :]
    surface = jnp.broadcast_to(speed[VZ * (g.across + 2) + 1 + t, pl.ds(PAD + x, 1), :], (SUB, LANES))
    dz = water_z(g, water[aligned(3 * g.plane + own), :], pick(surface, top_pick), lane)
    return water[aligned(own), :] - hk_water[aligned(own), :] * (dx + dy + dz)


def edge_kernel(g, first, last, *refs):
    refs = Refs(refs)
    water, bricks, memory, params, hb_water, hk_water, odd, col_far, col_near, row_far, row_near = refs.take(11)
    if not first:
        (const_in,) = refs.take(1)
    (uy,) = refs.take(1)
    if last:
        inner_press, inner_motion, inner_memory = refs.take(3)
    refs.take(2 if last else 6)
    (speed,) = refs.take(1)
    if last:
        water_hbm, motion_hbm, memory_hbm = refs.take(3)
    else:
        water_out, press, stress, bricks_out, memory_out = refs.take(5)
        sends = refs.take(4)
    (ux,) = refs.take(1)
    if first:
        (const_out,) = refs.take(1)
    col_before, col_after, row_before, row_after = refs.take(4)
    if last:
        press_buf, motion_buf, memory_buf, sems = refs.take(4)
    else:
        buffers = refs.take(4)
    unroute(odd[1] > 0.0, col_far, col_near, col_before, col_after, (M_BRICK, M_BRICK + g.nx - SUB))
    unroute(odd[0] > 0.0, row_far, row_near, row_before, row_after)
    col_odd = odd[1, pl.ds(0, 1), :] > 0.0

    nx, ny, edge, across, plane = g.nx, g.ny, g.edge, g.across, g.plane
    wide = across + 2
    lane = lane_ids()
    top_pick = surface_pick() * edge + (edge - 1)
    py = ny + 2 * PAD
    copies = []

    def send(source, target):
        copies.append(pltpu.make_async_copy(source, target, sems.at[len(copies)]))
        copies[-1].start()

    if last:
        middle = pl.ds(2 * ny, (nx - 4) * ny)
        send(inner_press.at[middle, :], water_hbm.at[middle, :])
        for ti in range(1, g.xtiles - 1):
            send(slots_of(g, inner_memory, ti), slots_of(g, memory_hbm, ti))
            send(slots_of(g, inner_motion, ti), slots_of(g, motion_hbm, ti))

    @pl.loop(0, SUB)
    def _(x):
        for t in range(g.ytiles):
            own = x * ny + SUB * t
            ux[aligned(ny + own), :] = water[aligned(plane + own), :]
            ux[aligned((1 + SUB) * ny + own), :] = water[aligned(plane + (nx - SUB) * ny + own), :]

    sides = ((row_before, 0, -1, 1.0, 1, 0), (row_after, nx - 1, nx, -1.0, 2 * SUB, 2 * SUB + 1))
    for side, (ref, x, halo, sign, own_layer, halo_layer) in enumerate(sides):
        for t in range(g.ytiles):
            own = pl.ds(x * ny + SUB * t, SUB)
            place = pl.ds(32 * side + SUB * t, SUB)
            if first:
                theirs = ref[pl.ds(ROW_CONST + SUB * t, SUB), :]
                const_out[place, :] = theirs
            else:
                theirs = const_in[place, :]
            here = pl.ds(own_layer * ny + SUB * t, SUB)
            ux[here, :] = ux[here, :] + sign * hb_water[own, :] * ref[pl.ds(M_P + SUB * t, SUB), :]
            ux[pl.ds(halo_layer * ny + SUB * t, SUB), :] = ref[pl.ds(M_U + SUB * t, SUB), :] - sign * theirs * water[own, :]
    if last:
        for layer, x in ((1, 0), (2 * SUB, nx - 1)):
            send(ux.at[pl.ds(layer * ny, ny), :], water_hbm.at[pl.ds(plane + x * ny, ny), :])

    speed_rows = {}

    def speed_row(key, x):
        if (key, x) not in speed_rows:
            speed_rows[key, x] = speed[key, pl.ds(PAD + x, 1), :]
        return speed_rows[key, x]

    for ref, x, halo, sign, _, _ in sides:
        for tj in range(across):
            own_hb = sign * params[HB * across + tj, pl.ds(x, 1), :]
            their_hb = sign * ref[pl.ds(M_BRICK + 6 * across + tj, 1), :]
            for c in (VX, VY, VZ):
                key = c * wide + 1 + tj
                speed_rows[key, x] = speed_row(key, x) - own_hb * ref[pl.ds(M_BRICK + c * across + tj, 1), :]
                speed_rows[key, halo] = (
                    ref[pl.ds(M_BRICK + (3 + c) * across + tj, 1), :] + their_hb * bricks[ALONG_X[c] * across + tj, pl.ds(x, 1), :]
                )
        relayed = [ref[pl.ds(M_CORNER + k, 1), :] for k in range(4)]
        for k, (col_ref, tj, col_halo, col_sign) in enumerate(((col_before, 0, 0, 1.0), (col_after, across - 1, wide - 1, -1.0))):
            near = 0 if tj == 0 else LANES - edge
            far = LANES - edge - near
            inside = (lane[0:1, :] >= near) & (lane[0:1, :] < near + edge)
            corner = jnp.where(col_odd, relayed[2 - 2 * k], relayed[2 * k])
            beside = jnp.where(col_odd, relayed[3 - 2 * k], relayed[2 * k + 1])
            across_y = [roll_row(corner, near - c * edge) for c in range(3)]
            across_x = (roll_row(corner, far - 7 * edge), roll_row(corner, far), roll_row(beside, far - 7 * edge))
            row_hb = jnp.where(inside, col_sign * ref[pl.ds(M_BRICK + 6 * across + tj, 1), :], 0.0)
            col_hb = sign * roll_row(col_ref[pl.ds(M_BRICK + x, 1), :], far - 6 * edge)
            for c in (VX, VY, VZ):
                key = c * wide + 1 + tj
                speed_rows[key, halo] = speed_row(key, halo) - row_hb * across_y[c]
                key = c * wide + col_halo
                speed_rows[key, x] = speed_row(key, x) - col_hb * across_x[c]
    for (key, x), value in speed_rows.items():
        speed[key, pl.ds(PAD + x, 1), :] = value

    def tops_at(row, above):
        return (
            lambda y: ux[pl.ds(above + y, SUB, stride=ny), :],
            lambda y: uy[pl.ds(row * py + PAD + y, SUB, stride=py), :],
            lambda y: water[pl.ds(3 * plane + row * ny + y, SUB, stride=ny), :],
        )

    if last:
        @pl.loop(0, 2)
        def _(turn):
            ti = turn * (g.xtiles - 1)
            row = pl.multiple_of(SUB * ti, SUB)
            tops = tops_at(row, pl.multiple_of((1 + SUB * turn) * ny, SUB))
            brick_stress(g, window(row), bricks, memory, params, speed, tops, store_slots(g, motion_buf, memory_buf, ti))
    else:
        lower = lax.broadcasted_iota(jnp.int32, (SUB, LANES), 0) < SUB // 2

        def joined(one, other):
            return lambda y: jnp.where(lower, one(y), other(y))

        tops = [joined(*pair) for pair in zip(tops_at(0, ny), tops_at(nx - SUB, (1 + SUB) * ny))]
        store = store_planes(g, bricks_out, memory_out, stress, [(0, SUB // 2, 0), (SUB // 2, SUB // 2, nx - SUB // 2)])
        brick_stress(g, both_faces(g), bricks, memory, params, speed, tops, store)

    if last:
        for ti in (0, g.xtiles - 1):
            send(slots_of(g, motion_buf, ti), slots_of(g, motion_hbm, ti))
            send(slots_of(g, memory_buf, ti), slots_of(g, memory_hbm, ti))

    for pair, (x, layer) in enumerate(((0, 1), (nx - 2, 2 * SUB - 1))):
        for step in range(2):
            for t in range(g.ytiles):
                dx = (
                    ux[pl.ds((layer + step + 1) * ny + SUB * t, SUB), :] - ux[pl.ds((layer + step - 1) * ny + SUB * t, SUB), :]
                )
                value = water_stress(g, x + step, t, dx, water, uy, speed, hk_water, lane, top_pick)
                if last:
                    press_buf[pl.ds((2 * pair + step) * ny + SUB * t, SUB), :] = value
                else:
                    water_out[pl.ds((x + step) * ny + SUB * t, SUB), :] = value
                    press[x + step + 1, pl.ds(PAD + SUB * t, SUB), :] = value

    if last:
        for pair, x in enumerate((0, nx - 2)):
            send(press_buf.at[pl.ds(2 * pair * ny, 2 * ny), :], water_hbm.at[pl.ds(x * ny, 2 * ny), :])
        for copy in copies:
            copy.wait()
    else:
        def load_v(field, ti, tj):
            return speed[field * wide + 1 + tj, aligned(PAD + SUB * ti), :]

        def load_hb(ti, tj):
            return params[HB * across + tj, aligned(SUB * ti), :]

        def column(side, t):
            return pl.ds(SUB * t * ny + side * (ny - 1), SUB, stride=ny)

        faces = (
            lambda side, t: ux[pl.ds((1 + side * (2 * SUB - 1)) * ny + SUB * t, SUB), :],
            lambda side, t: hb_water[pl.ds(side * (nx - 1) * ny + SUB * t, SUB), :],
            lambda side, t: uy[pl.ds(SUB * t * py + PAD + side * (ny - 1), SUB, stride=py), :],
            lambda side, t: hb_water[column(side, t), :],
        )
        brick_velocity(g, (2, lambda turn: turn * (g.xtiles - 1)), water_out, stress, load_v, bricks_out, load_hb)
        pack(g, water_out, bricks_out, params, faces, odd, buffers, sends, False)


def swap(value, axis, start):
    pairs = [(i, i + 1) for i in range(start, lax.axis_size(axis) - 1, 2)]
    return lax.ppermute(value, axis, pairs + [(j, i) for i, j in pairs])


def exchange(sends):
    row_far, row_near, col_far, col_near = sends
    col_far = swap(col_far, "col", 1)
    col_near = swap(col_near, "col", 0)

    def with_corners(message, start):
        corners = jnp.concatenate([col_far[start : start + 2], col_near[start : start + 2]])
        return lax.dynamic_update_slice(message, corners, (M_CORNER, 0))

    row_far = swap(with_corners(row_far, M_RELAY), "row", 1)
    row_near = swap(with_corners(row_near, M_RELAY + 2), "row", 0)
    return col_far, col_near, row_far, row_near


def body(
    brick_velocity_stress,
    brick_relaxation_memory,
    brick_cell_material,
    brick_live,
    water_state,
    water_material,
    material_table,
):
    _, nx, ny, nz = water_state.shape
    g = Grid(nx, ny, brick_cell_material.shape[1])
    across, plane = g.across, g.plane

    def f32(*shape):
        return jax.ShapeDtypeStruct(shape, jnp.float32)

    vmem = pl.BlockSpec(memory_space=pltpu.VMEM)
    hbm = pl.BlockSpec(memory_space=pltpu.HBM)
    params = pltpu.CompilerParams(vmem_limit_bytes=24 * 1024 * 1024)
    def messages(first):
        return [f32(start + (32 if first else 0), LANES) for start in (ROW_CONST, ROW_CONST, COL_CONST, COL_CONST)]

    def buffer(*shape):
        return pltpu.VMEM(shape, jnp.float32)

    def held(*values):
        return [pltpu.with_memory_space_constraint(value, pltpu.VMEM) for value in values]

    def pinned(*values):
        return [pltpu.with_memory_space_constraint(value, pltpu.HBM) for value in values]

    def message_buffers(kinds, first):
        starts = {"row": ROW_CONST, "col": COL_CONST}
        return [buffer(starts[kind] + (32 if first else 0), LANES) for kind in kinds for _ in range(2)]

    odd = jnp.stack([lax.axis_index(axis) & 1 for axis in ("row", "col")]).astype(jnp.float32)
    odd = jnp.broadcast_to(odd[:, None, None], (2, SUB, LANES))
    press = buffer(nx + 2, ny + 2 * PAD, nz)
    stress = buffer(6 * across, nx + 2 * PAD, LANES)
    work = pl.CostEstimate(flops=20_000_000, bytes_accessed=8_000_000, transcendentals=0)
    water, bricks, coefficients, columns, memory, *sends = pl.pallas_call(
        functools.partial(first_kernel, g),
        out_shape=[
            buffer(4 * plane, nz), f32(9 * across, nx, LANES), f32(9 * across, nx, LANES), f32(8, SUB, LANES),
            buffer(*brick_relaxation_memory.shape),
        ] + messages(True),
        in_specs=[hbm] * 7 + [vmem],
        out_specs=[vmem] * 9,
        scratch_shapes=[
            stress,
            buffer(nx, ny, nz),
            buffer(2, ny, nz),
            buffer(2, nx, SUB, nz),
            pltpu.VMEM((2, ny, nz), jnp.int32),
            pltpu.VMEM((2, nx, SUB, nz), jnp.int32),
            pltpu.VMEM(brick_velocity_stress.shape, jnp.float32),
            pltpu.VMEM(brick_cell_material.shape, jnp.int32),
            pltpu.SMEM(brick_live.shape, jnp.int32),
            pltpu.SMEM(material_table.shape, jnp.float32),
            pltpu.SemaphoreType.DMA((14,)),
        ]
        + message_buffers(("row", "col"), True),
        compiler_params=params,
        name="first_bricks",
    )(
        *pinned(
            brick_live, material_table, water_state, water_material,
            brick_velocity_stress, brick_cell_material, brick_relaxation_memory,
        ),
        odd,
    )

    def passed(*messages):
        return [buffer(*message.shape) for message in messages]

    water, sends[0], sends[1], hb_water, hk_water, memory = pl.pallas_call(
        functools.partial(first_water_kernel, g),
        out_shape=[buffer(4 * plane, nz)] + passed(*sends[:2]) + [f32(plane, nz), f32(plane, nz), f32(18 * across, nx, LANES)],
        in_specs=[vmem] * 9,
        out_specs=[vmem] * 6,
        input_output_aliases={0: 0, 1: 1, 2: 2},
        scratch_shapes=[press],
        compiler_params=params,
        cost_estimate=work,
        name="first_water",
    )(*held(water, *sends[:2], bricks, columns, water_state, water_material, coefficients, memory))
    col_const, row_const = (), ()
    uy_shape = (nx * (ny + 2 * PAD), nz)
    speed_shape = (3 * (across + 2), nx + 2 * PAD, LANES)
    ux_buffer = buffer((2 * SUB + 2) * ny, nz)
    slot_buffers = [
        pltpu.VMEM(brick_velocity_stress.shape, jnp.float32),
        pltpu.VMEM(brick_relaxation_memory.shape, jnp.float32),
    ]
    finals = [f32(4 * plane, nz), f32(*brick_velocity_stress.shape), f32(*brick_relaxation_memory.shape)]
    planes = [
        buffer(4 * plane, nz),
        buffer(nx + 2, ny + 2 * PAD, nz),
        buffer(6 * across, nx + 2 * PAD, LANES),
        buffer(9 * across, nx, LANES),
        buffer(18 * across, nx, LANES),
    ]
    for step in range(STEPS):
        first, last = step == 0, step == STEPS - 1
        *columns, row_far, row_near = exchange(sends)
        state = (water, bricks, memory, coefficients, hb_water, hk_water, odd)
        held_out = [buffer(plane, nz)] + slot_buffers if last else planes
        inner = pl.pallas_call(
            functools.partial(inner_kernel, g, first, last),
            out_shape=[buffer(*uy_shape), buffer(*speed_shape)]
            + finals[: 1 if last else 0]
            + held_out
            + ([buffer(64, LANES)] if first else []),
            in_specs=[vmem] * (9 + len(col_const)),
            out_specs=[vmem] * 2 + [hbm] * (1 if last else 0) + [vmem] * (len(held_out) + (1 if first else 0)),
            scratch_shapes=message_buffers(("col",), first)
            + ([buffer(plane, nz), pltpu.SemaphoreType.DMA((3,))] if last else []),
            compiler_params=params,
            cost_estimate=work,
            name="inner",
        )(*held(*state), *columns, *col_const)
        if first:
            col_const = (inner[-1],)
            inner = inner[:-1]
        inputs = held(*state) + list(columns) + [row_far, row_near] + list(row_const)
        if last:
            uy, speed, partial, *rest = inner
            inputs += held(uy, *rest)
            same, spaces, out_shape = [*held(speed), partial], [vmem, hbm], [buffer(*speed_shape)] + finals
        else:
            uy, *partial = inner
            inputs += held(uy)
            same, spaces, out_shape = held(*partial), [vmem] * len(partial), [buffer(*speed_shape)] + planes
        rest_shape = ([] if last else messages(False) + [ux_buffer]) + ([buffer(64, LANES)] if first else [])
        results = pl.pallas_call(
            functools.partial(edge_kernel, g, first, last),
            out_shape=out_shape + rest_shape,
            in_specs=[vmem] * len(inputs) + spaces,
            out_specs=[vmem] + [hbm if last else vmem] * (len(out_shape) - 1) + [vmem] * len(rest_shape),
            input_output_aliases={len(inputs) + k: k for k in range(len(same))},
            scratch_shapes=([ux_buffer] if last else [])
            + message_buffers(("col", "row"), first)
            + (
                [buffer(4 * ny, nz)] + slot_buffers + [pltpu.SemaphoreType.DMA((13,))]
                if last
                else message_buffers(("row", "col"), False)
            ),
            compiler_params=params,
            name="edges",
        )(*inputs, *same)
        if last:
            return results[2], results[3], results[1].reshape(water_state.shape)
        old_water = water
        _, water, pressed, stressed, bricks, memory = results[:6]
        sends = list(results[6:10])
        if first:
            row_const = (results[11],)
        water, sends[0], sends[1] = pl.pallas_call(
            functools.partial(edge_water_kernel, g),
            out_shape=[buffer(4 * plane, nz)] + passed(*sends[:2]),
            in_specs=[vmem] * 9,
            out_specs=[vmem] * 3,
            input_output_aliases={0: 0, 1: 1, 2: 2},
            compiler_params=params,
            cost_estimate=work,
            name="edge_water",
        )(*held(water, *sends[:2], old_water, pressed, stressed, hb_water, results[10], uy))


def solution(mesh):
    return jax.shard_map(
        body,
        mesh=mesh,
        in_specs=(
            P(("row", "col"), None, None, None),
            P(("row", "col"), None, None, None),
            P(("row", "col"), None, None),
            P(("row", "col")),
            P(None, "row", "col", None),
            P("row", "col", None),
            P(),
        ),
        out_specs=(
            P(("row", "col"), None, None, None),
            P(("row", "col"), None, None, None),
            P(None, "row", "col", None),
        ),
        check_vma=False,
    )
```

```python
import functools

import jax
import jax.numpy as jnp
from jax import lax
from jax.experimental import pallas as pl
from jax.experimental.pallas import tpu as pltpu
from jax.sharding import PartitionSpec as P

STEPS = 3
LANES = 128
SUB = 8
PAD = 8
VX, VY, VZ, XX, YY, ZZ, XY, XZ, YZ = range(9)
HB, LAME, SHEAR, RETAIN, SPRING_LAME, SPRING_SHEAR, ALIVE = 0, 1, 2, 3, 6, 7, 8
ALONG_X = (XX, XY, XZ)
ALONG_Y = (XY, YY, YZ)
ALONG_Z = (XZ, YZ, ZZ)
M_P, M_U, M_BRICK, M_CORNER, M_RELAY = 0, 32, 64, 92, 96
ROW_CONST, COL_CONST = 96, 104


def lane_ids():
    return lax.broadcasted_iota(jnp.int32, (SUB, LANES), 1)


def roll(value, shift):
    shift = shift % LANES
    return value if shift == 0 else pltpu.roll(value, shift, 1)


def roll_row(row, shift):
    shift = shift % LANES
    if shift == 0:
        return row
    return pltpu.roll(jnp.broadcast_to(row, (SUB, LANES)), shift, 1)[0:1, :]


def pick(values, indices):
    return jnp.take_along_axis(values, indices, axis=1, mode="promise_in_bounds")


def aligned(start, size=SUB):
    return pl.ds(start if isinstance(start, int) else pl.multiple_of(start, SUB), size)


class Grid:
    def __init__(self, nx, ny, edge):
        self.nx, self.ny, self.edge = nx, ny, edge
        self.plane = nx * ny
        self.across = ny * edge // LANES
        self.yper = LANES // edge
        self.half = self.across // 2
        self.xtiles, self.ytiles = nx // SUB, ny // SUB
        self.per = edge // SUB

    def slot(self, ti, tj):
        return 2 * (ti // self.per) + tj // self.half

    def place(self, ti, tj):
        return aligned((ti % self.per) * SUB), pl.ds((tj % self.half) * LANES, LANES)


def zero_press_pads(g, press):
    zero = jnp.zeros((SUB, LANES), jnp.float32)
    for t in range(g.ytiles):
        press[0, pl.ds(PAD + SUB * t, SUB), :] = zero
        press[g.nx + 1, pl.ds(PAD + SUB * t, SUB), :] = zero

    @pl.loop(0, g.nx // SUB)
    def _(turn):
        for step in range(SUB):
            x = SUB * turn + step + 1
            press[x, pl.ds(0, SUB), :] = zero
            press[x, pl.ds(PAD + g.ny, SUB), :] = zero


def zero_stress_pads(g, stress):
    zero = jnp.zeros((SUB, LANES), jnp.float32)
    for field in ALONG_X:
        for tj in range(g.across):
            key = (field - XX) * g.across + tj
            stress[key, pl.ds(0, SUB), :] = zero
            stress[key, pl.ds(PAD + g.nx, SUB), :] = zero


def shifted_top(g, load, ys, lane):
    top = None
    for k, y in enumerate(ys):
        value = roll(load(y), g.edge * k + g.edge - 1)
        top = value if top is None else jnp.where(lane >= g.edge * k, value, top)
    return top


def along_y(g, rolled, tj, lane):
    zero = jnp.zeros((SUB, LANES), jnp.float32)
    after = rolled[tj + 1][1] if tj + 1 < len(rolled) else zero
    before = rolled[tj - 1][0] if tj > 0 else zero
    ahead = jnp.where(lane < LANES - g.edge, rolled[tj][1], after)
    behind = jnp.where(lane >= g.edge, rolled[tj][0], before)
    return ahead - behind


def along_z(g, value, beyond, depth):
    zero = jnp.zeros((SUB, LANES), jnp.float32)
    return jnp.where(depth == g.edge - 1, beyond, roll(value, -1)) - jnp.where(depth == 0, zero, roll(value, 1))


def water_z(g, value, below, lane):
    zero = jnp.zeros((SUB, LANES), jnp.float32)
    return jnp.where(lane == LANES - 1, zero, roll(value, -1)) - jnp.where(lane == 0, below, roll(value, 1))


def surface_pick():
    return lax.broadcasted_iota(jnp.int32, (SUB, LANES), 0)


def water_velocity(g, layers, water_out, press, surface_row, load_hb, load_u):
    lane = lane_ids()
    top_pick = surface_pick() * g.edge + (g.edge - 1)

    def water_layer(x):
        results = []
        for t in range(g.ytiles):
            rows = pl.ds(PAD + SUB * t, SUB)
            here = press[x + 1, rows, :]
            dx = press[x + 2, rows, :] - press[x, rows, :]
            dy = press[x + 1, pl.ds(PAD + SUB * t + 1, SUB), :] - press[x + 1, pl.ds(PAD + SUB * t - 1, SUB), :]
            surface = jnp.broadcast_to(surface_row(t, x), (SUB, LANES))
            dz = water_z(g, here, -pick(surface, top_pick), lane)
            own = x * g.ny + SUB * t
            hb = load_hb(x, t)
            for k, change in ((1, dx), (2, dy), (3, dz)):
                results.append((k * g.plane + own, load_u(k, x, t) - hb * change))
        return results

    turns, layer = layers

    @pl.loop(0, turns)
    def _(turn):
        x = layer(turn)
        for row, value in water_layer(x) + water_layer(x + 1):
            water_out[aligned(row), :] = value


def brick_velocity(g, tiles, water_out, stress, load_v, bricks_out, load_hb):
    lane = lane_ids()
    depth = lane % g.edge
    zero = jnp.zeros((SUB, LANES), jnp.float32)
    across, ny = g.across, g.ny

    turns, tile = tiles

    @pl.loop(0, turns)
    def _(turn):
        ti = tile(turn)
        row = pl.multiple_of(SUB * ti, SUB)
        here = pl.ds(pl.multiple_of(row + PAD, SUB), SUB)

        def load(field, tj):
            return stress[(field - XX) * across + tj, here, :]

        def along_x(field, tj):
            key = (field - XX) * across + tj
            return stress[key, pl.ds(row + PAD + 1, SUB), :] - stress[key, pl.ds(row + PAD - 1, SUB), :]

        results = []
        for target, fx, fy, fz in zip((VX, VY, VZ), ALONG_X, ALONG_Y, ALONG_Z):
            rolled = [(roll(value, g.edge), roll(value, -g.edge)) for value in (load(fy, tj) for tj in range(across))]
            for tj in range(across):
                beyond = zero
                if fz == ZZ:
                    ys = [g.yper * tj + k for k in range(g.yper)]
                    beyond = -shifted_top(g, lambda y: water_out[pl.ds(row * ny + y, SUB, stride=ny), :], ys, lane)
                change = along_x(fx, tj) + along_y(g, rolled, tj, lane) + along_z(g, load(fz, tj), beyond, depth)
                results.append((target * across + tj, load_v(target, ti, tj) + load_hb(ti, tj) * change))
        for key, value in results:
            bricks_out[key, pl.ds(row, SUB), :] = value


def window(row):
    def read(ref, key, offset=0):
        return ref[key, pl.ds(row + offset, SUB), :]

    return read


def both_faces(g):
    lower = lax.broadcasted_iota(jnp.int32, (SUB, LANES), 0) < SUB // 2

    def read(ref, key, offset=0):
        return jnp.where(lower, ref[key, pl.ds(offset, SUB), :], ref[key, pl.ds(g.nx - SUB + offset, SUB), :])

    return read


def brick_stress(g, read, bricks, memory, params, speed, tops, store):
    edge, across = g.edge, g.across
    wide = across + 2
    lane = lane_ids()
    depth = lane % edge
    rolled = []
    for field in (VX, VY, VZ):
        values = [read(speed, field * wide + tj, PAD) for tj in range(wide)]
        rolled.append([(roll(value, edge), roll(value, -edge)) for value in values])
    for tj in range(across):
        ys = [g.yper * tj + k for k in range(g.yper)]
        dx, dy, dz, speeds = [], [], [], []
        for field in (VX, VY, VZ):
            key = field * wide + 1 + tj
            value = read(speed, key, PAD)
            speeds.append(value)
            dx.append(read(speed, key, PAD + 1) - read(speed, key, PAD - 1))
            dy.append(along_y(g, rolled[field], tj + 1, lane))
            dz.append(along_z(g, value, shifted_top(g, tops[field], ys, lane), depth))
        strain = [dx[0], dy[1], dz[2], dy[0] + dx[1], dz[0] + dx[2], dz[1] + dy[2]]
        dilation = strain[0] + strain[1] + strain[2]

        def param(c):
            return read(params, c * across + tj)

        lame, shear = param(LAME) * dilation, param(SHEAR)
        spring_lame, spring_shear = param(SPRING_LAME) * dilation, param(SPRING_SHEAR)
        retain = [param(RETAIN + l) for l in range(3)]
        half_shear, half_spring = 0.5 * shear, 0.5 * spring_shear
        stresses, memories = [], {}
        for comp in range(6):
            if comp < 3:
                elastic = shear * strain[comp] + lame
                relaxed = spring_shear * strain[comp] + spring_lame
            else:
                elastic = half_shear * strain[comp]
                relaxed = half_spring * strain[comp]
            summed = None
            for l in range(3):
                place = 6 * l + comp
                old = read(memory, place * across + tj)
                new = relaxed + retain[l] * (old - relaxed)
                memories[place] = new
                summed = new if summed is None else summed + new
            stresses.append(read(bricks, (XX + comp) * across + tj) + elastic - summed)
        store(tj, speeds, stresses, memories)


def store_planes(g, bricks_out, memory_out, stress, pieces):
    def store(tj, speeds, stresses, memories):
        for first, count, row in pieces:
            for place, value in memories.items():
                memory_out[place * g.across + tj, pl.ds(row, count), :] = value[first : first + count, :]
            for comp, value in enumerate(stresses):
                value = value[first : first + count, :]
                bricks_out[(XX + comp) * g.across + tj, pl.ds(row, count), :] = value
                stress[comp * g.across + tj, pl.ds(row + PAD, count), :] = value

    return store


def store_slots(g, motion, memory, ti):
    def store(tj, speeds, stresses, memories):
        slot = g.slot(ti, tj)
        rows, lanes = g.place(ti, tj)
        for place, value in memories.items():
            memory[slot, place, rows, lanes] = value
        for field, value in enumerate(speeds + stresses):
            motion[slot, field, rows, lanes] = value

    return store


def route(odd, first, last, out_far, out_near):
    for start in range(0, out_far.shape[0], SUB):
        rows = pl.ds(start, SUB)
        one, other = first[rows, :], last[rows, :]
        out_far[rows, :] = jnp.where(odd, other, one)
        out_near[rows, :] = jnp.where(odd, one, other)


def unroute(odd, from_far, from_near, before, after, starts=None):
    for start in starts or range(0, from_far.shape[0], SUB):
        rows = pl.ds(start, SUB)
        far, near = from_far[rows, :], from_near[rows, :]
        before[rows, :] = jnp.where(odd, near, far)
        after[rows, :] = jnp.where(odd, far, near)


def pack(g, water, bricks, params, edges, odd, buffers, sends, first):
    row_u, row_hb, col_u, col_hb = edges
    row_first, row_last, col_first, col_last = buffers
    row_odd, col_odd = odd[0] > 0.0, odd[1] > 0.0
    nx, ny, across, edge = g.nx, g.ny, g.across, g.edge
    lane = lane_ids()
    for side, (out, x, inward, sign) in enumerate(((row_first, 0, 1, 1.0), (row_last, nx - 1, nx - 2, -1.0))):
        for t in range(g.ytiles):
            own = x * ny + SUB * t
            hb = row_hb(side, t)
            out[pl.ds(M_P + SUB * t, SUB), :] = water[pl.ds(own, SUB), :]
            out[pl.ds(M_U + SUB * t, SUB), :] = row_u(side, t) - sign * hb * water[pl.ds(inward * ny + SUB * t, SUB), :]
            if first:
                out[pl.ds(ROW_CONST + SUB * t, SUB), :] = hb
        for tj in range(across):
            for k, field in enumerate(ALONG_X + (VX, VY, VZ)):
                out[pl.ds(M_BRICK + k * across + tj, 1), :] = bricks[field * across + tj, pl.ds(x, 1), :]
            out[pl.ds(M_BRICK + 6 * across + tj, 1), :] = params[HB * across + tj, pl.ds(x, 1), :]
        out[pl.ds(M_CORNER, 4), :] = jnp.zeros((4, LANES), jnp.float32)
    sides = ((col_first, 0, 1, 0, 1.0), (col_last, ny - 1, ny - 2, across - 1, -1.0))
    for side, (out, y, inward, tj, sign) in enumerate(sides):
        for t in range(g.xtiles):
            own = SUB * t * ny + y
            hb = col_hb(side, t)
            out[pl.ds(M_P + SUB * t, SUB), :] = water[pl.ds(own, SUB, stride=ny), :]
            out[pl.ds(M_U + SUB * t, SUB), :] = (
                col_u(side, t) - sign * hb * water[pl.ds(SUB * t * ny + inward, SUB, stride=ny), :]
            )
            if first:
                out[pl.ds(COL_CONST + SUB * t, SUB), :] = hb
            rows = pl.ds(SUB * t, SUB)
            pieces = [bricks[field * across + tj, rows, :] for field in ALONG_Y + (VX, VY, VZ)]
            pieces.append(params[HB * across + tj, rows, :])
            beside = (1, 0) if t == 0 else (SUB - 2, SUB - 1)
            shear = bricks[XZ * across + tj, rows, :]
            if t == 0 or t == g.xtiles - 1:
                shear = pltpu.roll(shear, 1 if t == 0 else SUB - 1, 0)
            sub = lax.broadcasted_iota(jnp.int32, (SUB, LANES), 0)
            pieces.append(jnp.where(sub == beside[0], shear, bricks[XX * across + tj, rows, :]))
            packed = None
            for k, value in enumerate(pieces):
                moved = roll(value, edge * (k - y % g.yper))
                packed = moved if packed is None else jnp.where(lane >= edge * k, moved, packed)
            out[pl.ds(M_BRICK + SUB * t, SUB), :] = packed
            if t == 0:
                corner = packed
        one = (corner[0:1, :], corner[1:2, :])
        other = (packed[SUB - 1 : SUB, :], packed[SUB - 2 : SUB - 1, :])
        out[pl.ds(M_RELAY, SUB), :] = jnp.zeros((SUB, LANES), jnp.float32)
        for k in range(2):
            out[pl.ds(M_RELAY + k, 1), :] = jnp.where(row_odd[0:1, :], other[k], one[k])
            out[pl.ds(M_RELAY + 2 + k, 1), :] = jnp.where(row_odd[0:1, :], one[k], other[k])
    route(row_odd, row_first, row_last, *sends[:2])
    route(col_odd, col_first, col_last, *sends[2:])


def first_kernel(
    g, live_hbm, table_hbm, water_hbm, material_hbm, motion_hbm, kinds_hbm, memory_hbm, odd,
    water_out, bricks_out, params, columns, memory, row_far, row_near, col_far, col_near,
    stress, pressure, ux_edge, uy_edge, material_x, material_y, motion, kinds, live, table, sems, *buffers,
):
    nx, ny, across = g.nx, g.ny, g.across
    copies = []

    def fetch(source, target):
        copies.append(pltpu.make_async_copy(source, target, sems.at[len(copies)]))
        copies[-1].start()

    fetch(live_hbm, live)
    fetch(table_hbm, table)
    fetch(kinds_hbm, kinds)
    fetch(motion_hbm, motion)
    fetch(water_hbm.at[0], pressure)
    for side, (x, y) in enumerate(((0, 0), (nx - 1, ny - SUB))):
        fetch(water_hbm.at[1, x], ux_edge.at[side])
        fetch(material_hbm.at[x], material_x.at[side])
        fetch(water_hbm.at[2, :, pl.ds(y, SUB), :], uy_edge.at[side])
        fetch(material_hbm.at[:, pl.ds(y, SUB), :], material_y.at[side])
    fetch(memory_hbm, memory)
    lane = lane_ids()
    zero_stress_pads(g, stress)
    copies[0].wait()
    copies[1].wait()
    scales = (0.5, 0.5, 1.0, 1.0, 1.0, 1.0, 0.5, 1.0)
    for c, factor in enumerate(scales):
        column = jnp.zeros((SUB, LANES), jnp.float32)
        for level in range(table.shape[0]):
            column = jnp.where(lane == level, table[level, c], column)
        columns[c] = column * factor
    copies[2].wait()
    copies[3].wait()

    @pl.loop(0, g.xtiles)
    def _(ti):
        for tj in range(across):
            slot = g.slot(ti, tj)
            rows, lanes = g.place(ti, tj)
            alive = live[slot].astype(jnp.float32)
            here = aligned(SUB * ti)
            index = kinds[slot, rows, lanes]
            for c in range(8):
                value = pick(columns[c], index)
                params[c * across + tj, here, :] = value if 3 <= c < 6 else value * alive
            params[ALIVE * across + tj, here, :] = jnp.zeros((SUB, LANES), jnp.float32) + alive
            for field in range(XX, YZ + 1):
                value = motion[slot, field, rows, lanes] * alive
                bricks_out[field * across + tj, here, :] = value
                stress[(field - XX) * across + tj, aligned(PAD + SUB * ti), :] = value

    copies[4].wait()

    @pl.loop(0, nx // 2)
    def _(turn):
        results = []
        for x in (2 * turn, 2 * turn + 1):
            for t in range(g.ytiles):
                results.append((x * ny + SUB * t, pressure[x, pl.ds(SUB * t, SUB), :]))
        for own, value in results:
            water_out[aligned(own), :] = value

    def load_v(field, ti, tj):
        slot = g.slot(ti, tj)
        rows, lanes = g.place(ti, tj)
        return motion[slot, field, rows, lanes] * live[slot].astype(jnp.float32)

    def load_hb(ti, tj):
        return params[HB * across + tj, aligned(SUB * ti), :]

    brick_velocity(g, (g.xtiles, lambda turn: turn), water_out, stress, load_v, bricks_out, load_hb)
    for copy in copies[5:-1]:
        copy.wait()

    def rows_of(side, t):
        return side, pl.ds(SUB * t, SUB), side * (SUB - 1)

    edges = (
        lambda side, t: ux_edge[side, pl.ds(SUB * t, SUB), :],
        lambda side, t: pick(columns[0], material_x[side, pl.ds(SUB * t, SUB), :]),
        lambda side, t: uy_edge[(*rows_of(side, t), slice(None))],
        lambda side, t: pick(columns[0], material_y[(*rows_of(side, t), slice(None))]),
    )
    pack(g, water_out, bricks_out, params, edges, odd, buffers, (row_far, row_near, col_far, col_near), True)
    copies[-1].wait()


def first_water_kernel(
    g, pressure, row_first, row_last, bricks, columns, state, material, params, memory,
    water_out, first_same, last_same, hb_water, hk_water, memory_out, press,
):
    nx, ny = g.nx, g.ny

    @pl.loop(0, 18)
    def _(place):
        results = []
        for ti in range(g.xtiles):
            for tj in range(g.across):
                rows, lanes = g.place(ti, tj)
                value = memory[g.slot(ti, tj), place, rows, lanes]
                results.append((tj, ti, value * params[ALIVE * g.across + tj, pl.ds(SUB * ti, SUB), :]))
        for tj, ti, value in results:
            memory_out[place * g.across + tj, pl.ds(SUB * ti, SUB), :] = value

    zero_press_pads(g, press)

    @pl.loop(0, nx // 2)
    def _(turn):
        results = []
        for x in (2 * turn, 2 * turn + 1):
            for t in range(g.ytiles):
                own = x * ny + SUB * t
                index = material[x, pl.ds(SUB * t, SUB), :]
                results.append((x, t, own, pick(columns[0], index), pick(columns[1], index), pressure[aligned(own), :]))
        for x, t, own, hb, hk, value in results:
            hb_water[aligned(own), :] = hb
            hk_water[aligned(own), :] = hk
            press[x + 1, pl.ds(PAD + SUB * t, SUB), :] = value

    water_velocity(
        g,
        (nx // 2, lambda turn: 2 * turn),
        water_out,
        press,
        lambda t, x: bricks[ZZ * g.across + t, pl.ds(x, 1), :],
        lambda x, t: hb_water[aligned(x * ny + SUB * t), :],
        lambda k, x, t: state[k, x, pl.ds(SUB * t, SUB), :],
    )


def edge_water_kernel(
    g, same, row_first, row_last, water, press, stress, hb_water, ux, uy, water_out, first_same, last_same
):
    nx, ny, plane = g.nx, g.ny, g.plane

    def water_layers(layers, ux_row):
        def load_u(k, x, t):
            if k == 1:
                return ux_row(x, t)
            if k == 2:
                return uy[aligned(x * (ny + 2 * PAD) + PAD + SUB * t), :]
            return water[aligned(3 * plane + x * ny + SUB * t), :]

        water_velocity(
            g,
            layers,
            water_out,
            press,
            lambda t, x: stress[(ZZ - XX) * g.across + t, pl.ds(PAD + x, 1), :],
            lambda x, t: hb_water[aligned(x * ny + SUB * t), :],
            load_u,
        )

    def near_face(x, t):
        layer = x - (x // (nx - SUB)) * (nx - 2 * SUB) + 1
        return ux[aligned(layer * ny + SUB * t), :]

    water_layers((SUB, lambda turn: 2 * turn + (turn // (SUB // 2)) * (nx - 2 * SUB)), near_face)
    water_layers(
        ((nx - 2 * SUB) // 2, lambda turn: SUB + 2 * turn),
        lambda x, t: water[aligned(plane + x * ny + SUB * t), :],
    )


def slots_of(g, array, ti):
    slot = g.slot(ti, 0)
    return array.at[pl.ds(slot, 2), :, pl.ds((ti % g.per) * SUB, SUB), :]


class Refs:
    def __init__(self, refs):
        self.refs = list(refs)

    def take(self, count):
        taken, self.refs = self.refs[:count], self.refs[count:]
        return taken


def inner_kernel(g, first, last, *refs):
    refs = Refs(refs)
    water, bricks, memory, params, hb_water, hk_water, odd, col_far, col_near = refs.take(9)
    if not first:
        (const_in,) = refs.take(1)
    uy, speed = refs.take(2)
    if last:
        water_hbm, press_buf, motion_buf, memory_buf = refs.take(4)
    else:
        water_out, press, stress, bricks_out, memory_out = refs.take(5)
    if first:
        (const_out,) = refs.take(1)
    col_before, col_after = refs.take(2)
    if last:
        uy_buf, sems = refs.take(2)
    unroute(odd[1] > 0.0, col_far, col_near, col_before, col_after)

    nx, ny, edge, across, plane = g.nx, g.ny, g.edge, g.across, g.plane
    wide = across + 2
    lane = lane_ids()
    top_pick = surface_pick() * edge + (edge - 1)
    py = ny + 2 * PAD
    copies = []

    def send(source, target):
        copies.append(pltpu.make_async_copy(source, target, sems.at[len(copies)]))
        copies[-1].start()

    def part(component, start, stop):
        return pl.ds(component * plane + start * ny, (stop - start) * ny)

    if last:
        send(water.at[part(3, 0, nx), :], water_hbm.at[part(3, 0, nx), :])
        send(water.at[part(1, 1, nx - 1), :], water_hbm.at[part(1, 1, nx - 1), :])
    else:
        zero_press_pads(g, press)
        zero_stress_pads(g, stress)

    @pl.loop(0, nx // 4)
    def _(turn):
        results = []
        for x in (4 * turn + step for step in range(4)):
            for t in range(g.ytiles):
                own = x * ny + SUB * t
                results.append((own, x * py + PAD + SUB * t, water[aligned(2 * plane + own), :]))
        for own, row, value in results:
            uy[aligned(row), :] = value
            if last:
                uy_buf[aligned(own), :] = value

    for side, (ref, y, halo, sign) in enumerate(((col_before, 0, -1, 1.0), (col_after, ny - 1, ny, -1.0))):
        for t in range(g.xtiles):
            own = pl.ds(SUB * t * ny + y, SUB, stride=ny)
            here = pl.ds(SUB * t * py + PAD + y, SUB, stride=py)
            place = pl.ds(32 * side + SUB * t, SUB)
            if first:
                theirs = ref[pl.ds(COL_CONST + SUB * t, SUB), :]
                const_out[place, :] = theirs
            else:
                theirs = const_in[place, :]
            value = uy[here, :] + sign * hb_water[own, :] * ref[pl.ds(M_P + SUB * t, SUB), :]
            uy[here, :] = value
            if last:
                uy_buf[own, :] = value
            uy[pl.ds(SUB * t * py + PAD + halo, SUB, stride=py), :] = (
                ref[pl.ds(M_U + SUB * t, SUB), :] - sign * theirs * water[own, :]
            )
    if last:
        send(uy_buf, water_hbm.at[part(2, 0, nx), :])

    for field in (VX, VY, VZ):
        for tj in range(across):
            for ti in range(g.xtiles):
                speed[field * wide + 1 + tj, pl.ds(PAD + SUB * ti, SUB), :] = bricks[field * across + tj, pl.ds(SUB * ti, SUB), :]
    for ref, tj, halo, sign in ((col_before, 0, 0, 1.0), (col_after, across - 1, wide - 1, -1.0)):
        near = 0 if tj == 0 else LANES - edge
        far = LANES - edge - near
        inside = (lane >= near) & (lane < near + edge)
        for ti in range(g.xtiles):
            column = ref[pl.ds(M_BRICK + SUB * ti, SUB), :]
            own_hb = jnp.where(inside, sign * params[HB * across + tj, pl.ds(SUB * ti, SUB), :], 0.0)
            their_hb = sign * roll(column, far - 6 * edge)
            here = pl.ds(PAD + SUB * ti, SUB)
            for c in (VX, VY, VZ):
                key = c * wide + 1 + tj
                speed[key, here, :] = bricks[c * across + tj, pl.ds(SUB * ti, SUB), :] - own_hb * roll(column, near - c * edge)
                own = bricks[ALONG_Y[c] * across + tj, pl.ds(SUB * ti, SUB), :]
                speed[c * wide + halo, here, :] = roll(column, far - (3 + c) * edge) + their_hb * roll(own, far - near)

    windows = g.xtiles - 2 if last else g.xtiles

    @pl.loop(0, windows)
    def _(turn):
        if last:
            row = pl.multiple_of(SUB * (turn + 1), SUB)
            store = store_slots(g, motion_buf, memory_buf, turn + 1)
        else:
            row = 2 + SUB * turn - 4 * (turn // (g.xtiles - 1))
            store = store_planes(g, bricks_out, memory_out, stress, [(0, SUB, row)])
        tops = (
            lambda y: water[pl.ds(plane + row * ny + y, SUB, stride=ny), :],
            lambda y: uy[pl.ds(row * py + PAD + y, SUB, stride=py), :],
            lambda y: water[pl.ds(3 * plane + row * ny + y, SUB, stride=ny), :],
        )
        brick_stress(g, window(row), bricks, memory, params, speed, tops, store)

    def layer(x):
        results = []
        for t in range(g.ytiles):
            own = x * ny + SUB * t
            dx = water[aligned(plane + own + ny), :] - water[aligned(plane + own - ny), :]
            results.append(
                (x, t, own, water_stress(g, x, t, dx, water, uy, speed, hk_water, lane, top_pick))
            )
        return results

    @pl.loop(0, (nx - 4) // 2)
    def _(turn):
        for x, t, own, value in layer(2 + 2 * turn) + layer(3 + 2 * turn):
            if last:
                press_buf[aligned(own), :] = value
            else:
                water_out[aligned(own), :] = value
                press[x + 1, pl.ds(PAD + SUB * t, SUB), :] = value

    if last:
        for copy in copies:
            copy.wait()
    else:
        def load_v(field, ti, tj):
            return speed[field * wide + 1 + tj, aligned(PAD + SUB * ti), :]

        def load_hb(ti, tj):
            return params[HB * across + tj, aligned(SUB * ti), :]

        brick_velocity(g, (g.xtiles - 2, lambda turn: turn + 1), water_out, stress, load_v, bricks_out, load_hb)


def water_stress(g, x, t, dx, water, uy, speed, hk_water, lane, top_pick):
    row = x * (g.ny + 2 * PAD) + PAD + SUB * t
    own = x * g.ny + SUB * t
    dy = uy[pl.ds(row + 1, SUB), :] - uy[pl.ds(row - 1, SUB), :]
    surface = jnp.broadcast_to(speed[VZ * (g.across + 2) + 1 + t, pl.ds(PAD + x, 1), :], (SUB, LANES))
    dz = water_z(g, water[aligned(3 * g.plane + own), :], pick(surface, top_pick), lane)
    return water[aligned(own), :] - hk_water[aligned(own), :] * (dx + dy + dz)


def edge_kernel(g, first, last, *refs):
    refs = Refs(refs)
    water, bricks, memory, params, hb_water, hk_water, odd, col_far, col_near, row_far, row_near = refs.take(11)
    if not first:
        (const_in,) = refs.take(1)
    (uy,) = refs.take(1)
    if last:
        inner_press, inner_motion, inner_memory = refs.take(3)
    refs.take(2 if last else 6)
    (speed,) = refs.take(1)
    if last:
        water_hbm, motion_hbm, memory_hbm = refs.take(3)
    else:
        water_out, press, stress, bricks_out, memory_out = refs.take(5)
        sends = refs.take(4)
    (ux,) = refs.take(1)
    if first:
        (const_out,) = refs.take(1)
    col_before, col_after, row_before, row_after = refs.take(4)
    if last:
        press_buf, motion_buf, memory_buf, sems = refs.take(4)
    else:
        buffers = refs.take(4)
    unroute(odd[1] > 0.0, col_far, col_near, col_before, col_after, (M_BRICK, M_BRICK + g.nx - SUB))
    unroute(odd[0] > 0.0, row_far, row_near, row_before, row_after)
    col_odd = odd[1, pl.ds(0, 1), :] > 0.0

    nx, ny, edge, across, plane = g.nx, g.ny, g.edge, g.across, g.plane
    wide = across + 2
    lane = lane_ids()
    top_pick = surface_pick() * edge + (edge - 1)
    py = ny + 2 * PAD
    copies = []

    def send(source, target):
        copies.append(pltpu.make_async_copy(source, target, sems.at[len(copies)]))
        copies[-1].start()

    if last:
        middle = pl.ds(2 * ny, (nx - 4) * ny)
        send(inner_press.at[middle, :], water_hbm.at[middle, :])
        for ti in range(1, g.xtiles - 1):
            send(slots_of(g, inner_memory, ti), slots_of(g, memory_hbm, ti))
            send(slots_of(g, inner_motion, ti), slots_of(g, motion_hbm, ti))

    @pl.loop(0, SUB)
    def _(x):
        for t in range(g.ytiles):
            own = x * ny + SUB * t
            ux[aligned(ny + own), :] = water[aligned(plane + own), :]
            ux[aligned((1 + SUB) * ny + own), :] = water[aligned(plane + (nx - SUB) * ny + own), :]

    sides = ((row_before, 0, -1, 1.0, 1, 0), (row_after, nx - 1, nx, -1.0, 2 * SUB, 2 * SUB + 1))
    for side, (ref, x, halo, sign, own_layer, halo_layer) in enumerate(sides):
        for t in range(g.ytiles):
            own = pl.ds(x * ny + SUB * t, SUB)
            place = pl.ds(32 * side + SUB * t, SUB)
            if first:
                theirs = ref[pl.ds(ROW_CONST + SUB * t, SUB), :]
                const_out[place, :] = theirs
            else:
                theirs = const_in[place, :]
            here = pl.ds(own_layer * ny + SUB * t, SUB)
            ux[here, :] = ux[here, :] + sign * hb_water[own, :] * ref[pl.ds(M_P + SUB * t, SUB), :]
            ux[pl.ds(halo_layer * ny + SUB * t, SUB), :] = ref[pl.ds(M_U + SUB * t, SUB), :] - sign * theirs * water[own, :]
    if last:
        for layer, x in ((1, 0), (2 * SUB, nx - 1)):
            send(ux.at[pl.ds(layer * ny, ny), :], water_hbm.at[pl.ds(plane + x * ny, ny), :])

    speed_rows = {}

    def speed_row(key, x):
        if (key, x) not in speed_rows:
            speed_rows[key, x] = speed[key, pl.ds(PAD + x, 1), :]
        return speed_rows[key, x]

    for ref, x, halo, sign, _, _ in sides:
        for tj in range(across):
            own_hb = sign * params[HB * across + tj, pl.ds(x, 1), :]
            their_hb = sign * ref[pl.ds(M_BRICK + 6 * across + tj, 1), :]
            for c in (VX, VY, VZ):
                key = c * wide + 1 + tj
                speed_rows[key, x] = speed_row(key, x) - own_hb * ref[pl.ds(M_BRICK + c * across + tj, 1), :]
                speed_rows[key, halo] = (
                    ref[pl.ds(M_BRICK + (3 + c) * across + tj, 1), :] + their_hb * bricks[ALONG_X[c] * across + tj, pl.ds(x, 1), :]
                )
        relayed = [ref[pl.ds(M_CORNER + k, 1), :] for k in range(4)]
        for k, (col_ref, tj, col_halo, col_sign) in enumerate(((col_before, 0, 0, 1.0), (col_after, across - 1, wide - 1, -1.0))):
            near = 0 if tj == 0 else LANES - edge
            far = LANES - edge - near
            inside = (lane[0:1, :] >= near) & (lane[0:1, :] < near + edge)
            corner = jnp.where(col_odd, relayed[2 - 2 * k], relayed[2 * k])
            beside = jnp.where(col_odd, relayed[3 - 2 * k], relayed[2 * k + 1])
            across_y = [roll_row(corner, near - c * edge) for c in range(3)]
            across_x = (roll_row(corner, far - 7 * edge), roll_row(corner, far), roll_row(beside, far - 7 * edge))
            row_hb = jnp.where(inside, col_sign * ref[pl.ds(M_BRICK + 6 * across + tj, 1), :], 0.0)
            col_hb = sign * roll_row(col_ref[pl.ds(M_BRICK + x, 1), :], far - 6 * edge)
            for c in (VX, VY, VZ):
                key = c * wide + 1 + tj
                speed_rows[key, halo] = speed_row(key, halo) - row_hb * across_y[c]
                key = c * wide + col_halo
                speed_rows[key, x] = speed_row(key, x) - col_hb * across_x[c]
    for (key, x), value in speed_rows.items():
        speed[key, pl.ds(PAD + x, 1), :] = value

    for pair, (x, layer) in enumerate(((0, 1), (nx - 2, 2 * SUB - 1))):
        for step in range(2):
            for t in range(g.ytiles):
                dx = (
                    ux[pl.ds((layer + step + 1) * ny + SUB * t, SUB), :] - ux[pl.ds((layer + step - 1) * ny + SUB * t, SUB), :]
                )
                value = water_stress(g, x + step, t, dx, water, uy, speed, hk_water, lane, top_pick)
                if last:
                    press_buf[pl.ds((2 * pair + step) * ny + SUB * t, SUB), :] = value
                else:
                    water_out[pl.ds((x + step) * ny + SUB * t, SUB), :] = value
                    press[x + step + 1, pl.ds(PAD + SUB * t, SUB), :] = value

    if last:
        for pair, x in enumerate((0, nx - 2)):
            send(press_buf.at[pl.ds(2 * pair * ny, 2 * ny), :], water_hbm.at[pl.ds(x * ny, 2 * ny), :])

    def tops_at(row, above):
        return (
            lambda y: ux[pl.ds(above + y, SUB, stride=ny), :],
            lambda y: uy[pl.ds(row * py + PAD + y, SUB, stride=py), :],
            lambda y: water[pl.ds(3 * plane + row * ny + y, SUB, stride=ny), :],
        )

    if last:
        for turn, ti in enumerate((0, g.xtiles - 1)):
            tops = tops_at(SUB * ti, (1 + SUB * turn) * ny)
            store = store_slots(g, motion_buf, memory_buf, ti)
            brick_stress(g, window(SUB * ti), bricks, memory, params, speed, tops, store)
            send(slots_of(g, memory_buf, ti), slots_of(g, memory_hbm, ti))
            send(slots_of(g, motion_buf, ti), slots_of(g, motion_hbm, ti))
    else:
        lower = lax.broadcasted_iota(jnp.int32, (SUB, LANES), 0) < SUB // 2

        def joined(one, other):
            return lambda y: jnp.where(lower, one(y), other(y))

        tops = [joined(*pair) for pair in zip(tops_at(0, ny), tops_at(nx - SUB, (1 + SUB) * ny))]
        store = store_planes(g, bricks_out, memory_out, stress, [(0, SUB // 2, 0), (SUB // 2, SUB // 2, nx - SUB // 2)])
        brick_stress(g, both_faces(g), bricks, memory, params, speed, tops, store)

    if last:
        for copy in copies:
            copy.wait()
    else:
        def load_v(field, ti, tj):
            return speed[field * wide + 1 + tj, aligned(PAD + SUB * ti), :]

        def load_hb(ti, tj):
            return params[HB * across + tj, aligned(SUB * ti), :]

        def column(side, t):
            return pl.ds(SUB * t * ny + side * (ny - 1), SUB, stride=ny)

        faces = (
            lambda side, t: ux[pl.ds((1 + side * (2 * SUB - 1)) * ny + SUB * t, SUB), :],
            lambda side, t: hb_water[pl.ds(side * (nx - 1) * ny + SUB * t, SUB), :],
            lambda side, t: uy[pl.ds(SUB * t * py + PAD + side * (ny - 1), SUB, stride=py), :],
            lambda side, t: hb_water[column(side, t), :],
        )
        brick_velocity(g, (2, lambda turn: turn * (g.xtiles - 1)), water_out, stress, load_v, bricks_out, load_hb)
        pack(g, water_out, bricks_out, params, faces, odd, buffers, sends, False)


def swap(value, axis, start):
    pairs = [(i, i + 1) for i in range(start, lax.axis_size(axis) - 1, 2)]
    return lax.ppermute(value, axis, pairs + [(j, i) for i, j in pairs])


def exchange(sends):
    row_far, row_near, col_far, col_near = sends
    col_far = swap(col_far, "col", 1)
    col_near = swap(col_near, "col", 0)

    def with_corners(message, start):
        corners = jnp.concatenate([col_far[start : start + 2], col_near[start : start + 2]])
        return lax.dynamic_update_slice(message, corners, (M_CORNER, 0))

    row_far = swap(with_corners(row_far, M_RELAY), "row", 1)
    row_near = swap(with_corners(row_near, M_RELAY + 2), "row", 0)
    return col_far, col_near, row_far, row_near


def body(
    brick_velocity_stress,
    brick_relaxation_memory,
    brick_cell_material,
    brick_live,
    water_state,
    water_material,
    material_table,
):
    _, nx, ny, nz = water_state.shape
    g = Grid(nx, ny, brick_cell_material.shape[1])
    across, plane = g.across, g.plane

    def f32(*shape):
        return jax.ShapeDtypeStruct(shape, jnp.float32)

    vmem = pl.BlockSpec(memory_space=pltpu.VMEM)
    hbm = pl.BlockSpec(memory_space=pltpu.HBM)
    params = pltpu.CompilerParams(vmem_limit_bytes=24 * 1024 * 1024)
    def messages(first):
        return [f32(start + (32 if first else 0), LANES) for start in (ROW_CONST, ROW_CONST, COL_CONST, COL_CONST)]

    def buffer(*shape):
        return pltpu.VMEM(shape, jnp.float32)

    def held(*values):
        return [pltpu.with_memory_space_constraint(value, pltpu.VMEM) for value in values]

    def pinned(*values):
        return [pltpu.with_memory_space_constraint(value, pltpu.HBM) for value in values]

    def message_buffers(kinds, first):
        starts = {"row": ROW_CONST, "col": COL_CONST}
        return [buffer(starts[kind] + (32 if first else 0), LANES) for kind in kinds for _ in range(2)]

    odd = jnp.stack([lax.axis_index(axis) & 1 for axis in ("row", "col")]).astype(jnp.float32)
    odd = jnp.broadcast_to(odd[:, None, None], (2, SUB, LANES))
    press = buffer(nx + 2, ny + 2 * PAD, nz)
    stress = buffer(6 * across, nx + 2 * PAD, LANES)
    work = pl.CostEstimate(flops=20_000_000, bytes_accessed=8_000_000, transcendentals=0)
    water, bricks, coefficients, columns, memory, *sends = pl.pallas_call(
        functools.partial(first_kernel, g),
        out_shape=[
            buffer(4 * plane, nz), f32(9 * across, nx, LANES), f32(9 * across, nx, LANES), f32(8, SUB, LANES),
            buffer(*brick_relaxation_memory.shape),
        ] + messages(True),
        in_specs=[hbm] * 7 + [vmem],
        out_specs=[vmem] * 9,
        scratch_shapes=[
            stress,
            buffer(nx, ny, nz),
            buffer(2, ny, nz),
            buffer(2, nx, SUB, nz),
            pltpu.VMEM((2, ny, nz), jnp.int32),
            pltpu.VMEM((2, nx, SUB, nz), jnp.int32),
            pltpu.VMEM(brick_velocity_stress.shape, jnp.float32),
            pltpu.VMEM(brick_cell_material.shape, jnp.int32),
            pltpu.SMEM(brick_live.shape, jnp.int32),
            pltpu.SMEM(material_table.shape, jnp.float32),
            pltpu.SemaphoreType.DMA((14,)),
        ]
        + message_buffers(("row", "col"), True),
        compiler_params=params,
        name="first_bricks",
    )(
        *pinned(
            brick_live, material_table, water_state, water_material,
            brick_velocity_stress, brick_cell_material, brick_relaxation_memory,
        ),
        odd,
    )

    def passed(*messages):
        return [buffer(*message.shape) for message in messages]

    water, sends[0], sends[1], hb_water, hk_water, memory = pl.pallas_call(
        functools.partial(first_water_kernel, g),
        out_shape=[buffer(4 * plane, nz)] + passed(*sends[:2]) + [f32(plane, nz), f32(plane, nz), f32(18 * across, nx, LANES)],
        in_specs=[vmem] * 9,
        out_specs=[vmem] * 6,
        input_output_aliases={0: 0, 1: 1, 2: 2},
        scratch_shapes=[press],
        compiler_params=params,
        cost_estimate=work,
        name="first_water",
    )(*held(water, *sends[:2], bricks, columns, water_state, water_material, coefficients, memory))
    col_const, row_const = (), ()
    uy_shape = (nx * (ny + 2 * PAD), nz)
    speed_shape = (3 * (across + 2), nx + 2 * PAD, LANES)
    ux_buffer = buffer((2 * SUB + 2) * ny, nz)
    slot_buffers = [
        pltpu.VMEM(brick_velocity_stress.shape, jnp.float32),
        pltpu.VMEM(brick_relaxation_memory.shape, jnp.float32),
    ]
    finals = [f32(4 * plane, nz), f32(*brick_velocity_stress.shape), f32(*brick_relaxation_memory.shape)]
    planes = [
        buffer(4 * plane, nz),
        buffer(nx + 2, ny + 2 * PAD, nz),
        buffer(6 * across, nx + 2 * PAD, LANES),
        buffer(9 * across, nx, LANES),
        buffer(18 * across, nx, LANES),
    ]
    for step in range(STEPS):
        first, last = step == 0, step == STEPS - 1
        *columns, row_far, row_near = exchange(sends)
        state = (water, bricks, memory, coefficients, hb_water, hk_water, odd)
        held_out = [buffer(plane, nz)] + slot_buffers if last else planes
        inner = pl.pallas_call(
            functools.partial(inner_kernel, g, first, last),
            out_shape=[buffer(*uy_shape), buffer(*speed_shape)]
            + finals[: 1 if last else 0]
            + held_out
            + ([buffer(64, LANES)] if first else []),
            in_specs=[vmem] * (9 + len(col_const)),
            out_specs=[vmem] * 2 + [hbm] * (1 if last else 0) + [vmem] * (len(held_out) + (1 if first else 0)),
            scratch_shapes=message_buffers(("col",), first)
            + ([buffer(plane, nz), pltpu.SemaphoreType.DMA((3,))] if last else []),
            compiler_params=params,
            cost_estimate=work,
            name="inner",
        )(*held(*state), *columns, *col_const)
        if first:
            col_const = (inner[-1],)
            inner = inner[:-1]
        inputs = held(*state) + list(columns) + [row_far, row_near] + list(row_const)
        if last:
            uy, speed, partial, *rest = inner
            inputs += held(uy, *rest)
            same, spaces, out_shape = [*held(speed), partial], [vmem, hbm], [buffer(*speed_shape)] + finals
        else:
            uy, *partial = inner
            inputs += held(uy)
            same, spaces, out_shape = held(*partial), [vmem] * len(partial), [buffer(*speed_shape)] + planes
        rest_shape = ([] if last else messages(False) + [ux_buffer]) + ([buffer(64, LANES)] if first else [])
        results = pl.pallas_call(
            functools.partial(edge_kernel, g, first, last),
            out_shape=out_shape + rest_shape,
            in_specs=[vmem] * len(inputs) + spaces,
            out_specs=[vmem] + [hbm if last else vmem] * (len(out_shape) - 1) + [vmem] * len(rest_shape),
            input_output_aliases={len(inputs) + k: k for k in range(len(same))},
            scratch_shapes=([ux_buffer] if last else [])
            + message_buffers(("col", "row"), first)
            + (
                [buffer(4 * ny, nz)] + slot_buffers + [pltpu.SemaphoreType.DMA((13,))]
                if last
                else message_buffers(("row", "col"), False)
            ),
            compiler_params=params,
            name="edges",
        )(*inputs, *same)
        if last:
            return results[2], results[3], results[1].reshape(water_state.shape)
        old_water = water
        _, water, pressed, stressed, bricks, memory = results[:6]
        sends = list(results[6:10])
        if first:
            row_const = (results[11],)
        water, sends[0], sends[1] = pl.pallas_call(
            functools.partial(edge_water_kernel, g),
            out_shape=[buffer(4 * plane, nz)] + passed(*sends[:2]),
            in_specs=[vmem] * 9,
            out_specs=[vmem] * 3,
            input_output_aliases={0: 0, 1: 1, 2: 2},
            compiler_params=params,
            cost_estimate=work,
            name="edge_water",
        )(*held(water, *sends[:2], old_water, pressed, stressed, hb_water, results[10], uy))


def solution(mesh):
    return jax.shard_map(
        body,
        mesh=mesh,
        in_specs=(
            P(("row", "col"), None, None, None),
            P(("row", "col"), None, None, None),
            P(("row", "col"), None, None),
            P(("row", "col")),
            P(None, "row", "col", None),
            P("row", "col", None),
            P(),
        ),
        out_specs=(
            P(("row", "col"), None, None, None),
            P(("row", "col"), None, None, None),
            P(None, "row", "col", None),
        ),
        check_vma=False,
    )
```

```python
import functools

import jax
import jax.numpy as jnp
from jax import lax
from jax.experimental import pallas as pl
from jax.experimental.pallas import tpu as pltpu
from jax.sharding import PartitionSpec as P

STEPS = 3
LANES = 128
SUB = 8
PAD = 8
VX, VY, VZ, XX, YY, ZZ, XY, XZ, YZ = range(9)
HB, LAME, SHEAR, RETAIN, SPRING_LAME, SPRING_SHEAR, ALIVE = 0, 1, 2, 3, 6, 7, 8
ALONG_X = (XX, XY, XZ)
ALONG_Y = (XY, YY, YZ)
ALONG_Z = (XZ, YZ, ZZ)
M_P, M_U, M_BRICK, M_CORNER, M_RELAY = 0, 32, 64, 92, 96
ROW_CONST, COL_CONST = 96, 104


def lane_ids():
    return lax.broadcasted_iota(jnp.int32, (SUB, LANES), 1)


def roll(value, shift):
    shift = shift % LANES
    return value if shift == 0 else pltpu.roll(value, shift, 1)


def roll_row(row, shift):
    shift = shift % LANES
    if shift == 0:
        return row
    return pltpu.roll(jnp.broadcast_to(row, (SUB, LANES)), shift, 1)[0:1, :]


def pick(values, indices):
    return jnp.take_along_axis(values, indices, axis=1, mode="promise_in_bounds")


def aligned(start, size=SUB):
    return pl.ds(start if isinstance(start, int) else pl.multiple_of(start, SUB), size)


class Grid:
    def __init__(self, nx, ny, edge):
        self.nx, self.ny, self.edge = nx, ny, edge
        self.plane = nx * ny
        self.across = ny * edge // LANES
        self.yper = LANES // edge
        self.half = self.across // 2
        self.xtiles, self.ytiles = nx // SUB, ny // SUB
        self.per = edge // SUB

    def slot(self, ti, tj):
        return 2 * (ti // self.per) + tj // self.half

    def place(self, ti, tj):
        return aligned((ti % self.per) * SUB), pl.ds((tj % self.half) * LANES, LANES)


def zero_press_pads(g, press):
    zero = jnp.zeros((SUB, LANES), jnp.float32)
    for t in range(g.ytiles):
        press[0, pl.ds(PAD + SUB * t, SUB), :] = zero
        press[g.nx + 1, pl.ds(PAD + SUB * t, SUB), :] = zero

    @pl.loop(0, g.nx // SUB)
    def _(turn):
        for step in range(SUB):
            x = SUB * turn + step + 1
            press[x, pl.ds(0, SUB), :] = zero
            press[x, pl.ds(PAD + g.ny, SUB), :] = zero


def zero_stress_pads(g, stress):
    zero = jnp.zeros((SUB, LANES), jnp.float32)
    for field in ALONG_X:
        for tj in range(g.across):
            key = (field - XX) * g.across + tj
            stress[key, pl.ds(0, SUB), :] = zero
            stress[key, pl.ds(PAD + g.nx, SUB), :] = zero


def shifted_top(g, load, ys, lane):
    top = None
    for k, y in enumerate(ys):
        value = roll(load(y), g.edge * k + g.edge - 1)
        top = value if top is None else jnp.where(lane >= g.edge * k, value, top)
    return top


def along_y(g, rolled, tj, lane):
    zero = jnp.zeros((SUB, LANES), jnp.float32)
    after = rolled[tj + 1][1] if tj + 1 < len(rolled) else zero
    before = rolled[tj - 1][0] if tj > 0 else zero
    ahead = jnp.where(lane < LANES - g.edge, rolled[tj][1], after)
    behind = jnp.where(lane >= g.edge, rolled[tj][0], before)
    return ahead - behind


def along_z(g, value, beyond, depth):
    zero = jnp.zeros((SUB, LANES), jnp.float32)
    return jnp.where(depth == g.edge - 1, beyond, roll(value, -1)) - jnp.where(depth == 0, zero, roll(value, 1))


def water_z(g, value, below, lane):
    zero = jnp.zeros((SUB, LANES), jnp.float32)
    return jnp.where(lane == LANES - 1, zero, roll(value, -1)) - jnp.where(lane == 0, below, roll(value, 1))


def surface_pick():
    return lax.broadcasted_iota(jnp.int32, (SUB, LANES), 0)


def water_velocity(g, layers, water_out, press, surface_row, load_hb, load_u):
    lane = lane_ids()
    top_pick = surface_pick() * g.edge + (g.edge - 1)

    def water_layer(x):
        results = []
        for t in range(g.ytiles):
            rows = pl.ds(PAD + SUB * t, SUB)
            here = press[x + 1, rows, :]
            dx = press[x + 2, rows, :] - press[x, rows, :]
            dy = press[x + 1, pl.ds(PAD + SUB * t + 1, SUB), :] - press[x + 1, pl.ds(PAD + SUB * t - 1, SUB), :]
            surface = jnp.broadcast_to(surface_row(t, x), (SUB, LANES))
            dz = water_z(g, here, -pick(surface, top_pick), lane)
            own = x * g.ny + SUB * t
            hb = load_hb(x, t)
            for k, change in ((1, dx), (2, dy), (3, dz)):
                results.append((k * g.plane + own, load_u(k, x, t) - hb * change))
        return results

    turns, layer, count = layers

    @pl.loop(0, turns)
    def _(turn):
        x = layer(turn)
        for row, value in [result for step in range(count) for result in water_layer(x + step)]:
            water_out[aligned(row), :] = value


def brick_velocity(g, tiles, water_out, stress, load_v, bricks_out, load_hb):
    lane = lane_ids()
    depth = lane % g.edge
    zero = jnp.zeros((SUB, LANES), jnp.float32)
    across, ny = g.across, g.ny

    turns, tile = tiles

    @pl.loop(0, turns)
    def _(turn):
        ti = tile(turn)
        row = pl.multiple_of(SUB * ti, SUB)
        here = pl.ds(pl.multiple_of(row + PAD, SUB), SUB)

        def load(field, tj):
            return stress[(field - XX) * across + tj, here, :]

        def along_x(field, tj):
            key = (field - XX) * across + tj
            return stress[key, pl.ds(row + PAD + 1, SUB), :] - stress[key, pl.ds(row + PAD - 1, SUB), :]

        results = []
        for target, fx, fy, fz in zip((VX, VY, VZ), ALONG_X, ALONG_Y, ALONG_Z):
            rolled = [(roll(value, g.edge), roll(value, -g.edge)) for value in (load(fy, tj) for tj in range(across))]
            for tj in range(across):
                beyond = zero
                if fz == ZZ:
                    ys = [g.yper * tj + k for k in range(g.yper)]
                    beyond = -shifted_top(g, lambda y: water_out[pl.ds(row * ny + y, SUB, stride=ny), :], ys, lane)
                change = along_x(fx, tj) + along_y(g, rolled, tj, lane) + along_z(g, load(fz, tj), beyond, depth)
                results.append((target * across + tj, load_v(target, ti, tj) + load_hb(ti, tj) * change))
        for key, value in results:
            bricks_out[key, pl.ds(row, SUB), :] = value


def window(row):
    def read(ref, key, offset=0):
        return ref[key, pl.ds(row + offset, SUB), :]

    return read


def both_faces(g):
    lower = lax.broadcasted_iota(jnp.int32, (SUB, LANES), 0) < SUB // 2

    def read(ref, key, offset=0):
        return jnp.where(lower, ref[key, pl.ds(offset, SUB), :], ref[key, pl.ds(g.nx - SUB + offset, SUB), :])

    return read


def brick_stress(g, read, bricks, memory, params, speed, tops, store):
    edge, across = g.edge, g.across
    wide = across + 2
    lane = lane_ids()
    depth = lane % edge
    rolled = []
    for field in (VX, VY, VZ):
        values = [read(speed, field * wide + tj, PAD) for tj in range(wide)]
        rolled.append([(roll(value, edge), roll(value, -edge)) for value in values])
    for tj in range(across):
        ys = [g.yper * tj + k for k in range(g.yper)]
        dx, dy, dz, speeds = [], [], [], []
        for field in (VX, VY, VZ):
            key = field * wide + 1 + tj
            value = read(speed, key, PAD)
            speeds.append(value)
            dx.append(read(speed, key, PAD + 1) - read(speed, key, PAD - 1))
            dy.append(along_y(g, rolled[field], tj + 1, lane))
            dz.append(along_z(g, value, shifted_top(g, tops[field], ys, lane), depth))
        strain = [dx[0], dy[1], dz[2], dy[0] + dx[1], dz[0] + dx[2], dz[1] + dy[2]]
        dilation = strain[0] + strain[1] + strain[2]

        def param(c):
            return read(params, c * across + tj)

        lame, shear = param(LAME) * dilation, param(SHEAR)
        spring_lame, spring_shear = param(SPRING_LAME) * dilation, param(SPRING_SHEAR)
        retain = [param(RETAIN + l) for l in range(3)]
        half_shear, half_spring = 0.5 * shear, 0.5 * spring_shear
        stresses, memories = [], {}
        for comp in range(6):
            if comp < 3:
                elastic = shear * strain[comp] + lame
                relaxed = spring_shear * strain[comp] + spring_lame
            else:
                elastic = half_shear * strain[comp]
                relaxed = half_spring * strain[comp]
            summed = None
            for l in range(3):
                place = 6 * l + comp
                old = read(memory, place * across + tj)
                new = relaxed + retain[l] * (old - relaxed)
                memories[place] = new
                summed = new if summed is None else summed + new
            stresses.append(read(bricks, (XX + comp) * across + tj) + elastic - summed)
        store(tj, speeds, stresses, memories)


def store_planes(g, bricks_out, memory_out, stress, pieces):
    def store(tj, speeds, stresses, memories):
        for first, count, row in pieces:
            for place, value in memories.items():
                memory_out[place * g.across + tj, pl.ds(row, count), :] = value[first : first + count, :]
            for comp, value in enumerate(stresses):
                value = value[first : first + count, :]
                bricks_out[(XX + comp) * g.across + tj, pl.ds(row, count), :] = value
                stress[comp * g.across + tj, pl.ds(row + PAD, count), :] = value

    return store


def store_slots(g, motion, memory, ti):
    def store(tj, speeds, stresses, memories):
        slot = g.slot(ti, tj)
        rows, lanes = g.place(ti, tj)
        for place, value in memories.items():
            memory[slot, place, rows, lanes] = value
        for field, value in enumerate(speeds + stresses):
            motion[slot, field, rows, lanes] = value

    return store


def route(odd, first, last, out_far, out_near):
    for start in range(0, out_far.shape[0], SUB):
        rows = pl.ds(start, SUB)
        one, other = first[rows, :], last[rows, :]
        out_far[rows, :] = jnp.where(odd, other, one)
        out_near[rows, :] = jnp.where(odd, one, other)


def unroute(odd, from_far, from_near, before, after, starts=None):
    for start in starts or range(0, from_far.shape[0], SUB):
        rows = pl.ds(start, SUB)
        far, near = from_far[rows, :], from_near[rows, :]
        before[rows, :] = jnp.where(odd, near, far)
        after[rows, :] = jnp.where(odd, far, near)


def pack(g, water, bricks, params, edges, odd, buffers, sends, first):
    row_u, row_hb, col_u, col_hb = edges
    row_first, row_last, col_first, col_last = buffers
    row_odd, col_odd = odd[0] > 0.0, odd[1] > 0.0
    nx, ny, across, edge = g.nx, g.ny, g.across, g.edge
    lane = lane_ids()
    for side, (out, x, inward, sign) in enumerate(((row_first, 0, 1, 1.0), (row_last, nx - 1, nx - 2, -1.0))):
        for t in range(g.ytiles):
            own = x * ny + SUB * t
            hb = row_hb(side, t)
            out[pl.ds(M_P + SUB * t, SUB), :] = water[pl.ds(own, SUB), :]
            out[pl.ds(M_U + SUB * t, SUB), :] = row_u(side, t) - sign * hb * water[pl.ds(inward * ny + SUB * t, SUB), :]
            if first:
                out[pl.ds(ROW_CONST + SUB * t, SUB), :] = hb
        for tj in range(across):
            for k, field in enumerate(ALONG_X + (VX, VY, VZ)):
                out[pl.ds(M_BRICK + k * across + tj, 1), :] = bricks[field * across + tj, pl.ds(x, 1), :]
            out[pl.ds(M_BRICK + 6 * across + tj, 1), :] = params[HB * across + tj, pl.ds(x, 1), :]
        out[pl.ds(M_CORNER, 4), :] = jnp.zeros((4, LANES), jnp.float32)
    sides = ((col_first, 0, 1, 0, 1.0), (col_last, ny - 1, ny - 2, across - 1, -1.0))
    for side, (out, y, inward, tj, sign) in enumerate(sides):
        for t in range(g.xtiles):
            own = SUB * t * ny + y
            hb = col_hb(side, t)
            out[pl.ds(M_P + SUB * t, SUB), :] = water[pl.ds(own, SUB, stride=ny), :]
            out[pl.ds(M_U + SUB * t, SUB), :] = (
                col_u(side, t) - sign * hb * water[pl.ds(SUB * t * ny + inward, SUB, stride=ny), :]
            )
            if first:
                out[pl.ds(COL_CONST + SUB * t, SUB), :] = hb
            rows = pl.ds(SUB * t, SUB)
            pieces = [bricks[field * across + tj, rows, :] for field in ALONG_Y + (VX, VY, VZ)]
            pieces.append(params[HB * across + tj, rows, :])
            beside = (1, 0) if t == 0 else (SUB - 2, SUB - 1)
            shear = bricks[XZ * across + tj, rows, :]
            if t == 0 or t == g.xtiles - 1:
                shear = pltpu.roll(shear, 1 if t == 0 else SUB - 1, 0)
            sub = lax.broadcasted_iota(jnp.int32, (SUB, LANES), 0)
            pieces.append(jnp.where(sub == beside[0], shear, bricks[XX * across + tj, rows, :]))
            packed = None
            for k, value in enumerate(pieces):
                moved = roll(value, edge * (k - y % g.yper))
                packed = moved if packed is None else jnp.where(lane >= edge * k, moved, packed)
            out[pl.ds(M_BRICK + SUB * t, SUB), :] = packed
            if t == 0:
                corner = packed
        one = (corner[0:1, :], corner[1:2, :])
        other = (packed[SUB - 1 : SUB, :], packed[SUB - 2 : SUB - 1, :])
        out[pl.ds(M_RELAY, SUB), :] = jnp.zeros((SUB, LANES), jnp.float32)
        for k in range(2):
            out[pl.ds(M_RELAY + k, 1), :] = jnp.where(row_odd[0:1, :], other[k], one[k])
            out[pl.ds(M_RELAY + 2 + k, 1), :] = jnp.where(row_odd[0:1, :], one[k], other[k])
    route(row_odd, row_first, row_last, *sends[:2])
    route(col_odd, col_first, col_last, *sends[2:])


def first_kernel(
    g, live_hbm, table_hbm, water_hbm, material_hbm, motion_hbm, kinds_hbm, memory_hbm, odd,
    water_out, bricks_out, params, columns, memory, row_far, row_near, col_far, col_near,
    stress, pressure, ux_edge, uy_edge, material_x, material_y, motion, kinds, live, table, sems, *buffers,
):
    nx, ny, across = g.nx, g.ny, g.across
    copies = []

    def fetch(source, target):
        copies.append(pltpu.make_async_copy(source, target, sems.at[len(copies)]))
        copies[-1].start()

    fetch(live_hbm, live)
    fetch(table_hbm, table)
    fetch(kinds_hbm, kinds)
    fetch(motion_hbm, motion)
    fetch(water_hbm.at[0], pressure)
    for side, (x, y) in enumerate(((0, 0), (nx - 1, ny - SUB))):
        fetch(water_hbm.at[1, x], ux_edge.at[side])
        fetch(material_hbm.at[x], material_x.at[side])
        fetch(water_hbm.at[2, :, pl.ds(y, SUB), :], uy_edge.at[side])
        fetch(material_hbm.at[:, pl.ds(y, SUB), :], material_y.at[side])
    fetch(memory_hbm, memory)
    lane = lane_ids()
    zero_stress_pads(g, stress)
    copies[0].wait()
    copies[1].wait()
    scales = (0.5, 0.5, 1.0, 1.0, 1.0, 1.0, 0.5, 1.0)
    for c, factor in enumerate(scales):
        column = jnp.zeros((SUB, LANES), jnp.float32)
        for level in range(table.shape[0]):
            column = jnp.where(lane == level, table[level, c], column)
        columns[c] = column * factor
    copies[2].wait()
    copies[3].wait()

    @pl.loop(0, g.xtiles)
    def _(ti):
        for tj in range(across):
            slot = g.slot(ti, tj)
            rows, lanes = g.place(ti, tj)
            alive = live[slot].astype(jnp.float32)
            here = aligned(SUB * ti)
            index = kinds[slot, rows, lanes]
            for c in range(8):
                value = pick(columns[c], index)
                params[c * across + tj, here, :] = value if 3 <= c < 6 else value * alive
            params[ALIVE * across + tj, here, :] = jnp.zeros((SUB, LANES), jnp.float32) + alive
            for field in range(XX, YZ + 1):
                value = motion[slot, field, rows, lanes] * alive
                bricks_out[field * across + tj, here, :] = value
                stress[(field - XX) * across + tj, aligned(PAD + SUB * ti), :] = value

    copies[4].wait()

    @pl.loop(0, nx // 2)
    def _(turn):
        results = []
        for x in (2 * turn, 2 * turn + 1):
            for t in range(g.ytiles):
                results.append((x * ny + SUB * t, pressure[x, pl.ds(SUB * t, SUB), :]))
        for own, value in results:
            water_out[aligned(own), :] = value

    def load_v(field, ti, tj):
        slot = g.slot(ti, tj)
        rows, lanes = g.place(ti, tj)
        return motion[slot, field, rows, lanes] * live[slot].astype(jnp.float32)

    def load_hb(ti, tj):
        return params[HB * across + tj, aligned(SUB * ti), :]

    brick_velocity(g, (g.xtiles, lambda turn: turn), water_out, stress, load_v, bricks_out, load_hb)
    for copy in copies[5:-1]:
        copy.wait()

    def rows_of(side, t):
        return side, pl.ds(SUB * t, SUB), side * (SUB - 1)

    edges = (
        lambda side, t: ux_edge[side, pl.ds(SUB * t, SUB), :],
        lambda side, t: pick(columns[0], material_x[side, pl.ds(SUB * t, SUB), :]),
        lambda side, t: uy_edge[(*rows_of(side, t), slice(None))],
        lambda side, t: pick(columns[0], material_y[(*rows_of(side, t), slice(None))]),
    )
    pack(g, water_out, bricks_out, params, edges, odd, buffers, (row_far, row_near, col_far, col_near), True)
    copies[-1].wait()


def first_water_kernel(
    g, pressure, row_first, row_last, bricks, columns, state, material, params, memory,
    water_out, first_same, last_same, hb_water, hk_water, memory_out, press,
):
    nx, ny = g.nx, g.ny

    @pl.loop(0, 18)
    def _(place):
        results = []
        for ti in range(g.xtiles):
            for tj in range(g.across):
                rows, lanes = g.place(ti, tj)
                value = memory[g.slot(ti, tj), place, rows, lanes]
                results.append((tj, ti, value * params[ALIVE * g.across + tj, pl.ds(SUB * ti, SUB), :]))
        for tj, ti, value in results:
            memory_out[place * g.across + tj, pl.ds(SUB * ti, SUB), :] = value

    zero_press_pads(g, press)

    @pl.loop(0, nx // 2)
    def _(turn):
        results = []
        for x in (2 * turn, 2 * turn + 1):
            for t in range(g.ytiles):
                own = x * ny + SUB * t
                index = material[x, pl.ds(SUB * t, SUB), :]
                results.append((x, t, own, pick(columns[0], index), pick(columns[1], index), pressure[aligned(own), :]))
        for x, t, own, hb, hk, value in results:
            hb_water[aligned(own), :] = hb
            hk_water[aligned(own), :] = hk
            press[x + 1, pl.ds(PAD + SUB * t, SUB), :] = value

    water_velocity(
        g,
        (nx // 4, lambda turn: 4 * turn, 4),
        water_out,
        press,
        lambda t, x: bricks[ZZ * g.across + t, pl.ds(x, 1), :],
        lambda x, t: hb_water[aligned(x * ny + SUB * t), :],
        lambda k, x, t: state[k, x, pl.ds(SUB * t, SUB), :],
    )


def edge_water_kernel(
    g, same, row_first, row_last, water, press, stress, hb_water, ux, uy, water_out, first_same, last_same
):
    nx, ny, plane = g.nx, g.ny, g.plane

    def water_layers(layers, ux_row):
        def load_u(k, x, t):
            if k == 1:
                return ux_row(x, t)
            if k == 2:
                return uy[aligned(x * (ny + 2 * PAD) + PAD + SUB * t), :]
            return water[aligned(3 * plane + x * ny + SUB * t), :]

        water_velocity(
            g,
            layers,
            water_out,
            press,
            lambda t, x: stress[(ZZ - XX) * g.across + t, pl.ds(PAD + x, 1), :],
            lambda x, t: hb_water[aligned(x * ny + SUB * t), :],
            load_u,
        )

    def near_face(x, t):
        layer = x - (x // (nx - SUB)) * (nx - 2 * SUB) + 1
        return ux[aligned(layer * ny + SUB * t), :]

    water_layers((SUB, lambda turn: 2 * turn + (turn // (SUB // 2)) * (nx - 2 * SUB), 2), near_face)
    water_layers(
        ((nx - 2 * SUB) // 2, lambda turn: SUB + 2 * turn, 2),
        lambda x, t: water[aligned(plane + x * ny + SUB * t), :],
    )


def slots_of(g, array, ti):
    slot = g.slot(ti, 0)
    return array.at[pl.ds(slot, 2), :, pl.ds((ti % g.per) * SUB, SUB), :]


class Refs:
    def __init__(self, refs):
        self.refs = list(refs)

    def take(self, count):
        taken, self.refs = self.refs[:count], self.refs[count:]
        return taken


def inner_kernel(g, first, last, *refs):
    refs = Refs(refs)
    water, bricks, memory, params, hb_water, hk_water, odd, col_far, col_near = refs.take(9)
    if not first:
        (const_in,) = refs.take(1)
    uy, speed = refs.take(2)
    if last:
        water_hbm, press_buf, motion_buf, memory_buf = refs.take(4)
    else:
        water_out, press, stress, bricks_out, memory_out = refs.take(5)
    if first:
        (const_out,) = refs.take(1)
    col_before, col_after = refs.take(2)
    if last:
        uy_buf, sems = refs.take(2)
    unroute(odd[1] > 0.0, col_far, col_near, col_before, col_after)

    nx, ny, edge, across, plane = g.nx, g.ny, g.edge, g.across, g.plane
    wide = across + 2
    lane = lane_ids()
    top_pick = surface_pick() * edge + (edge - 1)
    py = ny + 2 * PAD
    copies = []

    def send(source, target):
        copies.append(pltpu.make_async_copy(source, target, sems.at[len(copies)]))
        copies[-1].start()

    def part(component, start, stop):
        return pl.ds(component * plane + start * ny, (stop - start) * ny)

    if last:
        send(water.at[part(3, 0, nx), :], water_hbm.at[part(3, 0, nx), :])
        send(water.at[part(1, 1, nx - 1), :], water_hbm.at[part(1, 1, nx - 1), :])
    else:
        zero_press_pads(g, press)
        zero_stress_pads(g, stress)

    @pl.loop(0, nx // 4)
    def _(turn):
        results = []
        for x in (4 * turn + step for step in range(4)):
            for t in range(g.ytiles):
                own = x * ny + SUB * t
                results.append((own, x * py + PAD + SUB * t, water[aligned(2 * plane + own), :]))
        for own, row, value in results:
            uy[aligned(row), :] = value
            if last:
                uy_buf[aligned(own), :] = value

    for side, (ref, y, halo, sign) in enumerate(((col_before, 0, -1, 1.0), (col_after, ny - 1, ny, -1.0))):
        for t in range(g.xtiles):
            own = pl.ds(SUB * t * ny + y, SUB, stride=ny)
            here = pl.ds(SUB * t * py + PAD + y, SUB, stride=py)
            place = pl.ds(32 * side + SUB * t, SUB)
            if first:
                theirs = ref[pl.ds(COL_CONST + SUB * t, SUB), :]
                const_out[place, :] = theirs
            else:
                theirs = const_in[place, :]
            value = uy[here, :] + sign * hb_water[own, :] * ref[pl.ds(M_P + SUB * t, SUB), :]
            uy[here, :] = value
            if last:
                uy_buf[own, :] = value
            uy[pl.ds(SUB * t * py + PAD + halo, SUB, stride=py), :] = (
                ref[pl.ds(M_U + SUB * t, SUB), :] - sign * theirs * water[own, :]
            )
    if last:
        send(uy_buf, water_hbm.at[part(2, 0, nx), :])

    for field in (VX, VY, VZ):
        for tj in range(across):
            for ti in range(g.xtiles):
                speed[field * wide + 1 + tj, pl.ds(PAD + SUB * ti, SUB), :] = bricks[field * across + tj, pl.ds(SUB * ti, SUB), :]
    for ref, tj, halo, sign in ((col_before, 0, 0, 1.0), (col_after, across - 1, wide - 1, -1.0)):
        near = 0 if tj == 0 else LANES - edge
        far = LANES - edge - near
        inside = (lane >= near) & (lane < near + edge)
        for ti in range(g.xtiles):
            column = ref[pl.ds(M_BRICK + SUB * ti, SUB), :]
            own_hb = jnp.where(inside, sign * params[HB * across + tj, pl.ds(SUB * ti, SUB), :], 0.0)
            their_hb = sign * roll(column, far - 6 * edge)
            here = pl.ds(PAD + SUB * ti, SUB)
            for c in (VX, VY, VZ):
                key = c * wide + 1 + tj
                speed[key, here, :] = bricks[c * across + tj, pl.ds(SUB * ti, SUB), :] - own_hb * roll(column, near - c * edge)
                own = bricks[ALONG_Y[c] * across + tj, pl.ds(SUB * ti, SUB), :]
                speed[c * wide + halo, here, :] = roll(column, far - (3 + c) * edge) + their_hb * roll(own, far - near)

    windows = g.xtiles - 2 if last else g.xtiles

    @pl.loop(0, windows)
    def _(turn):
        if last:
            row = pl.multiple_of(SUB * (turn + 1), SUB)
            store = store_slots(g, motion_buf, memory_buf, turn + 1)
        else:
            row = 2 + SUB * turn - 4 * (turn // (g.xtiles - 1))
            store = store_planes(g, bricks_out, memory_out, stress, [(0, SUB, row)])
        tops = (
            lambda y: water[pl.ds(plane + row * ny + y, SUB, stride=ny), :],
            lambda y: uy[pl.ds(row * py + PAD + y, SUB, stride=py), :],
            lambda y: water[pl.ds(3 * plane + row * ny + y, SUB, stride=ny), :],
        )
        brick_stress(g, window(row), bricks, memory, params, speed, tops, store)

    def layer(x):
        results = []
        for t in range(g.ytiles):
            own = x * ny + SUB * t
            dx = water[aligned(plane + own + ny), :] - water[aligned(plane + own - ny), :]
            results.append(
                (x, t, own, water_stress(g, x, t, dx, water, uy, speed, hk_water, lane, top_pick))
            )
        return results

    @pl.loop(0, (nx - 4) // 2)
    def _(turn):
        for x, t, own, value in layer(2 + 2 * turn) + layer(3 + 2 * turn):
            if last:
                press_buf[aligned(own), :] = value
            else:
                water_out[aligned(own), :] = value
                press[x + 1, pl.ds(PAD + SUB * t, SUB), :] = value

    if last:
        for copy in copies:
            copy.wait()
    else:
        def load_v(field, ti, tj):
            return speed[field * wide + 1 + tj, aligned(PAD + SUB * ti), :]

        def load_hb(ti, tj):
            return params[HB * across + tj, aligned(SUB * ti), :]

        brick_velocity(g, (g.xtiles - 2, lambda turn: turn + 1), water_out, stress, load_v, bricks_out, load_hb)


def water_stress(g, x, t, dx, water, uy, speed, hk_water, lane, top_pick):
    row = x * (g.ny + 2 * PAD) + PAD + SUB * t
    own = x * g.ny + SUB * t
    dy = uy[pl.ds(row + 1, SUB), :] - uy[pl.ds(row - 1, SUB), :]
    surface = jnp.broadcast_to(speed[VZ * (g.across + 2) + 1 + t, pl.ds(PAD + x, 1), :], (SUB, LANES))
    dz = water_z(g, water[aligned(3 * g.plane + own), :], pick(surface, top_pick), lane)
    return water[aligned(own), :] - hk_water[aligned(own), :] * (dx + dy + dz)


def edge_kernel(g, first, last, *refs):
    refs = Refs(refs)
    water, bricks, memory, params, hb_water, hk_water, odd, col_far, col_near, row_far, row_near = refs.take(11)
    if not first:
        (const_in,) = refs.take(1)
    (uy,) = refs.take(1)
    if last:
        inner_press, inner_motion, inner_memory = refs.take(3)
    refs.take(2 if last else 6)
    (speed,) = refs.take(1)
    if last:
        water_hbm, motion_hbm, memory_hbm = refs.take(3)
    else:
        water_out, press, stress, bricks_out, memory_out = refs.take(5)
        sends = refs.take(4)
    (ux,) = refs.take(1)
    if first:
        (const_out,) = refs.take(1)
    col_before, col_after, row_before, row_after = refs.take(4)
    if last:
        press_buf, motion_buf, memory_buf, sems = refs.take(4)
    else:
        buffers = refs.take(4)
    unroute(odd[1] > 0.0, col_far, col_near, col_before, col_after, (M_BRICK, M_BRICK + g.nx - SUB))
    unroute(odd[0] > 0.0, row_far, row_near, row_before, row_after)
    col_odd = odd[1, pl.ds(0, 1), :] > 0.0

    nx, ny, edge, across, plane = g.nx, g.ny, g.edge, g.across, g.plane
    wide = across + 2
    lane = lane_ids()
    top_pick = surface_pick() * edge + (edge - 1)
    py = ny + 2 * PAD
    copies = []

    def send(source, target):
        copies.append(pltpu.make_async_copy(source, target, sems.at[len(copies)]))
        copies[-1].start()

    if last:
        middle = pl.ds(2 * ny, (nx - 4) * ny)
        send(inner_press.at[middle, :], water_hbm.at[middle, :])
        for ti in range(1, g.xtiles - 1):
            send(slots_of(g, inner_memory, ti), slots_of(g, memory_hbm, ti))
            send(slots_of(g, inner_motion, ti), slots_of(g, motion_hbm, ti))

    @pl.loop(0, SUB)
    def _(x):
        for t in range(g.ytiles):
            own = x * ny + SUB * t
            ux[aligned(ny + own), :] = water[aligned(plane + own), :]
            ux[aligned((1 + SUB) * ny + own), :] = water[aligned(plane + (nx - SUB) * ny + own), :]

    sides = ((row_before, 0, -1, 1.0, 1, 0), (row_after, nx - 1, nx, -1.0, 2 * SUB, 2 * SUB + 1))
    for side, (ref, x, halo, sign, own_layer, halo_layer) in enumerate(sides):
        for t in range(g.ytiles):
            own = pl.ds(x * ny + SUB * t, SUB)
            place = pl.ds(32 * side + SUB * t, SUB)
            if first:
                theirs = ref[pl.ds(ROW_CONST + SUB * t, SUB), :]
                const_out[place, :] = theirs
            else:
                theirs = const_in[place, :]
            here = pl.ds(own_layer * ny + SUB * t, SUB)
            ux[here, :] = ux[here, :] + sign * hb_water[own, :] * ref[pl.ds(M_P + SUB * t, SUB), :]
            ux[pl.ds(halo_layer * ny + SUB * t, SUB), :] = ref[pl.ds(M_U + SUB * t, SUB), :] - sign * theirs * water[own, :]
    if last:
        for layer, x in ((1, 0), (2 * SUB, nx - 1)):
            send(ux.at[pl.ds(layer * ny, ny), :], water_hbm.at[pl.ds(plane + x * ny, ny), :])

    speed_rows = {}

    def speed_row(key, x):
        if (key, x) not in speed_rows:
            speed_rows[key, x] = speed[key, pl.ds(PAD + x, 1), :]
        return speed_rows[key, x]

    for ref, x, halo, sign, _, _ in sides:
        for tj in range(across):
            own_hb = sign * params[HB * across + tj, pl.ds(x, 1), :]
            their_hb = sign * ref[pl.ds(M_BRICK + 6 * across + tj, 1), :]
            for c in (VX, VY, VZ):
                key = c * wide + 1 + tj
                speed_rows[key, x] = speed_row(key, x) - own_hb * ref[pl.ds(M_BRICK + c * across + tj, 1), :]
                speed_rows[key, halo] = (
                    ref[pl.ds(M_BRICK + (3 + c) * across + tj, 1), :] + their_hb * bricks[ALONG_X[c] * across + tj, pl.ds(x, 1), :]
                )
        relayed = [ref[pl.ds(M_CORNER + k, 1), :] for k in range(4)]
        for k, (col_ref, tj, col_halo, col_sign) in enumerate(((col_before, 0, 0, 1.0), (col_after, across - 1, wide - 1, -1.0))):
            near = 0 if tj == 0 else LANES - edge
            far = LANES - edge - near
            inside = (lane[0:1, :] >= near) & (lane[0:1, :] < near + edge)
            corner = jnp.where(col_odd, relayed[2 - 2 * k], relayed[2 * k])
            beside = jnp.where(col_odd, relayed[3 - 2 * k], relayed[2 * k + 1])
            across_y = [roll_row(corner, near - c * edge) for c in range(3)]
            across_x = (roll_row(corner, far - 7 * edge), roll_row(corner, far), roll_row(beside, far - 7 * edge))
            row_hb = jnp.where(inside, col_sign * ref[pl.ds(M_BRICK + 6 * across + tj, 1), :], 0.0)
            col_hb = sign * roll_row(col_ref[pl.ds(M_BRICK + x, 1), :], far - 6 * edge)
            for c in (VX, VY, VZ):
                key = c * wide + 1 + tj
                speed_rows[key, halo] = speed_row(key, halo) - row_hb * across_y[c]
                key = c * wide + col_halo
                speed_rows[key, x] = speed_row(key, x) - col_hb * across_x[c]
    for (key, x), value in speed_rows.items():
        speed[key, pl.ds(PAD + x, 1), :] = value

    for pair, (x, layer) in enumerate(((0, 1), (nx - 2, 2 * SUB - 1))):
        for step in range(2):
            for t in range(g.ytiles):
                dx = (
                    ux[pl.ds((layer + step + 1) * ny + SUB * t, SUB), :] - ux[pl.ds((layer + step - 1) * ny + SUB * t, SUB), :]
                )
                value = water_stress(g, x + step, t, dx, water, uy, speed, hk_water, lane, top_pick)
                if last:
                    press_buf[pl.ds((2 * pair + step) * ny + SUB * t, SUB), :] = value
                else:
                    water_out[pl.ds((x + step) * ny + SUB * t, SUB), :] = value
                    press[x + step + 1, pl.ds(PAD + SUB * t, SUB), :] = value

    if last:
        for pair, x in enumerate((0, nx - 2)):
            send(press_buf.at[pl.ds(2 * pair * ny, 2 * ny), :], water_hbm.at[pl.ds(x * ny, 2 * ny), :])

    def tops_at(row, above):
        return (
            lambda y: ux[pl.ds(above + y, SUB, stride=ny), :],
            lambda y: uy[pl.ds(row * py + PAD + y, SUB, stride=py), :],
            lambda y: water[pl.ds(3 * plane + row * ny + y, SUB, stride=ny), :],
        )

    if last:
        for turn, ti in enumerate((0, g.xtiles - 1)):
            tops = tops_at(SUB * ti, (1 + SUB * turn) * ny)
            store = store_slots(g, motion_buf, memory_buf, ti)
            brick_stress(g, window(SUB * ti), bricks, memory, params, speed, tops, store)
            send(slots_of(g, memory_buf, ti), slots_of(g, memory_hbm, ti))
            send(slots_of(g, motion_buf, ti), slots_of(g, motion_hbm, ti))
    else:
        lower = lax.broadcasted_iota(jnp.int32, (SUB, LANES), 0) < SUB // 2

        def joined(one, other):
            return lambda y: jnp.where(lower, one(y), other(y))

        tops = [joined(*pair) for pair in zip(tops_at(0, ny), tops_at(nx - SUB, (1 + SUB) * ny))]
        store = store_planes(g, bricks_out, memory_out, stress, [(0, SUB // 2, 0), (SUB // 2, SUB // 2, nx - SUB // 2)])
        brick_stress(g, both_faces(g), bricks, memory, params, speed, tops, store)

    if last:
        for copy in copies:
            copy.wait()
    else:
        def load_v(field, ti, tj):
            return speed[field * wide + 1 + tj, aligned(PAD + SUB * ti), :]

        def load_hb(ti, tj):
            return params[HB * across + tj, aligned(SUB * ti), :]

        def column(side, t):
            return pl.ds(SUB * t * ny + side * (ny - 1), SUB, stride=ny)

        faces = (
            lambda side, t: ux[pl.ds((1 + side * (2 * SUB - 1)) * ny + SUB * t, SUB), :],
            lambda side, t: hb_water[pl.ds(side * (nx - 1) * ny + SUB * t, SUB), :],
            lambda side, t: uy[pl.ds(SUB * t * py + PAD + side * (ny - 1), SUB, stride=py), :],
            lambda side, t: hb_water[column(side, t), :],
        )
        brick_velocity(g, (2, lambda turn: turn * (g.xtiles - 1)), water_out, stress, load_v, bricks_out, load_hb)
        pack(g, water_out, bricks_out, params, faces, odd, buffers, sends, False)


def swap(value, axis, start):
    pairs = [(i, i + 1) for i in range(start, lax.axis_size(axis) - 1, 2)]
    return lax.ppermute(value, axis, pairs + [(j, i) for i, j in pairs])


def exchange(sends):
    row_far, row_near, col_far, col_near = sends
    col_far = swap(col_far, "col", 1)
    col_near = swap(col_near, "col", 0)

    def with_corners(message, start):
        corners = jnp.concatenate([col_far[start : start + 2], col_near[start : start + 2]])
        return lax.dynamic_update_slice(message, corners, (M_CORNER, 0))

    row_far = swap(with_corners(row_far, M_RELAY), "row", 1)
    row_near = swap(with_corners(row_near, M_RELAY + 2), "row", 0)
    return col_far, col_near, row_far, row_near


def body(
    brick_velocity_stress,
    brick_relaxation_memory,
    brick_cell_material,
    brick_live,
    water_state,
    water_material,
    material_table,
):
    _, nx, ny, nz = water_state.shape
    g = Grid(nx, ny, brick_cell_material.shape[1])
    across, plane = g.across, g.plane

    def f32(*shape):
        return jax.ShapeDtypeStruct(shape, jnp.float32)

    vmem = pl.BlockSpec(memory_space=pltpu.VMEM)
    hbm = pl.BlockSpec(memory_space=pltpu.HBM)
    params = pltpu.CompilerParams(vmem_limit_bytes=24 * 1024 * 1024)
    def messages(first):
        return [f32(start + (32 if first else 0), LANES) for start in (ROW_CONST, ROW_CONST, COL_CONST, COL_CONST)]

    def buffer(*shape):
        return pltpu.VMEM(shape, jnp.float32)

    def held(*values):
        return [pltpu.with_memory_space_constraint(value, pltpu.VMEM) for value in values]

    def pinned(*values):
        return [pltpu.with_memory_space_constraint(value, pltpu.HBM) for value in values]

    def message_buffers(kinds, first):
        starts = {"row": ROW_CONST, "col": COL_CONST}
        return [buffer(starts[kind] + (32 if first else 0), LANES) for kind in kinds for _ in range(2)]

    odd = jnp.stack([lax.axis_index(axis) & 1 for axis in ("row", "col")]).astype(jnp.float32)
    odd = jnp.broadcast_to(odd[:, None, None], (2, SUB, LANES))
    press = buffer(nx + 2, ny + 2 * PAD, nz)
    stress = buffer(6 * across, nx + 2 * PAD, LANES)
    work = pl.CostEstimate(flops=20_000_000, bytes_accessed=8_000_000, transcendentals=0)
    water, bricks, coefficients, columns, memory, *sends = pl.pallas_call(
        functools.partial(first_kernel, g),
        out_shape=[
            buffer(4 * plane, nz), f32(9 * across, nx, LANES), f32(9 * across, nx, LANES), f32(8, SUB, LANES),
            buffer(*brick_relaxation_memory.shape),
        ] + messages(True),
        in_specs=[hbm] * 7 + [vmem],
        out_specs=[vmem] * 9,
        scratch_shapes=[
            stress,
            buffer(nx, ny, nz),
            buffer(2, ny, nz),
            buffer(2, nx, SUB, nz),
            pltpu.VMEM((2, ny, nz), jnp.int32),
            pltpu.VMEM((2, nx, SUB, nz), jnp.int32),
            pltpu.VMEM(brick_velocity_stress.shape, jnp.float32),
            pltpu.VMEM(brick_cell_material.shape, jnp.int32),
            pltpu.SMEM(brick_live.shape, jnp.int32),
            pltpu.SMEM(material_table.shape, jnp.float32),
            pltpu.SemaphoreType.DMA((14,)),
        ]
        + message_buffers(("row", "col"), True),
        compiler_params=params,
        name="first_bricks",
    )(
        *pinned(
            brick_live, material_table, water_state, water_material,
            brick_velocity_stress, brick_cell_material, brick_relaxation_memory,
        ),
        odd,
    )

    def passed(*messages):
        return [buffer(*message.shape) for message in messages]

    water, sends[0], sends[1], hb_water, hk_water, memory = pl.pallas_call(
        functools.partial(first_water_kernel, g),
        out_shape=[buffer(4 * plane, nz)] + passed(*sends[:2]) + [f32(plane, nz), f32(plane, nz), f32(18 * across, nx, LANES)],
        in_specs=[vmem] * 9,
        out_specs=[vmem] * 6,
        input_output_aliases={0: 0, 1: 1, 2: 2},
        scratch_shapes=[press],
        compiler_params=params,
        cost_estimate=work,
        name="first_water",
    )(*held(water, *sends[:2], bricks, columns, water_state, water_material, coefficients, memory))
    col_const, row_const = (), ()
    uy_shape = (nx * (ny + 2 * PAD), nz)
    speed_shape = (3 * (across + 2), nx + 2 * PAD, LANES)
    ux_buffer = buffer((2 * SUB + 2) * ny, nz)
    slot_buffers = [
        pltpu.VMEM(brick_velocity_stress.shape, jnp.float32),
        pltpu.VMEM(brick_relaxation_memory.shape, jnp.float32),
    ]
    finals = [f32(4 * plane, nz), f32(*brick_velocity_stress.shape), f32(*brick_relaxation_memory.shape)]
    planes = [
        buffer(4 * plane, nz),
        buffer(nx + 2, ny + 2 * PAD, nz),
        buffer(6 * across, nx + 2 * PAD, LANES),
        buffer(9 * across, nx, LANES),
        buffer(18 * across, nx, LANES),
    ]
    for step in range(STEPS):
        first, last = step == 0, step == STEPS - 1
        *columns, row_far, row_near = exchange(sends)
        state = (water, bricks, memory, coefficients, hb_water, hk_water, odd)
        held_out = [buffer(plane, nz)] + slot_buffers if last else planes
        inner = pl.pallas_call(
            functools.partial(inner_kernel, g, first, last),
            out_shape=[buffer(*uy_shape), buffer(*speed_shape)]
            + finals[: 1 if last else 0]
            + held_out
            + ([buffer(64, LANES)] if first else []),
            in_specs=[vmem] * (9 + len(col_const)),
            out_specs=[vmem] * 2 + [hbm] * (1 if last else 0) + [vmem] * (len(held_out) + (1 if first else 0)),
            scratch_shapes=message_buffers(("col",), first)
            + ([buffer(plane, nz), pltpu.SemaphoreType.DMA((3,))] if last else []),
            compiler_params=params,
            cost_estimate=work,
            name="inner",
        )(*held(*state), *columns, *col_const)
        if first:
            col_const = (inner[-1],)
            inner = inner[:-1]
        inputs = held(*state) + list(columns) + [row_far, row_near] + list(row_const)
        if last:
            uy, speed, partial, *rest = inner
            inputs += held(uy, *rest)
            same, spaces, out_shape = [*held(speed), partial], [vmem, hbm], [buffer(*speed_shape)] + finals
        else:
            uy, *partial = inner
            inputs += held(uy)
            same, spaces, out_shape = held(*partial), [vmem] * len(partial), [buffer(*speed_shape)] + planes
        rest_shape = ([] if last else messages(False) + [ux_buffer]) + ([buffer(64, LANES)] if first else [])
        results = pl.pallas_call(
            functools.partial(edge_kernel, g, first, last),
            out_shape=out_shape + rest_shape,
            in_specs=[vmem] * len(inputs) + spaces,
            out_specs=[vmem] + [hbm if last else vmem] * (len(out_shape) - 1) + [vmem] * len(rest_shape),
            input_output_aliases={len(inputs) + k: k for k in range(len(same))},
            scratch_shapes=([ux_buffer] if last else [])
            + message_buffers(("col", "row"), first)
            + (
                [buffer(4 * ny, nz)] + slot_buffers + [pltpu.SemaphoreType.DMA((13,))]
                if last
                else message_buffers(("row", "col"), False)
            ),
            compiler_params=params,
            name="edges",
        )(*inputs, *same)
        if last:
            return results[2], results[3], results[1].reshape(water_state.shape)
        old_water = water
        _, water, pressed, stressed, bricks, memory = results[:6]
        sends = list(results[6:10])
        if first:
            row_const = (results[11],)
        water, sends[0], sends[1] = pl.pallas_call(
            functools.partial(edge_water_kernel, g),
            out_shape=[buffer(4 * plane, nz)] + passed(*sends[:2]),
            in_specs=[vmem] * 9,
            out_specs=[vmem] * 3,
            input_output_aliases={0: 0, 1: 1, 2: 2},
            compiler_params=params,
            cost_estimate=work,
            name="edge_water",
        )(*held(water, *sends[:2], old_water, pressed, stressed, hb_water, results[10], uy))


def solution(mesh):
    return jax.shard_map(
        body,
        mesh=mesh,
        in_specs=(
            P(("row", "col"), None, None, None),
            P(("row", "col"), None, None, None),
            P(("row", "col"), None, None),
            P(("row", "col")),
            P(None, "row", "col", None),
            P("row", "col", None),
            P(),
        ),
        out_specs=(
            P(("row", "col"), None, None, None),
            P(("row", "col"), None, None, None),
            P(None, "row", "col", None),
        ),
        check_vma=False,
    )
```
